32 devices in a mesh: rows: 4 (over x, core), seq: 8 (over z, y).
Axes of the slice: x: 2, y: 2, z: 4, core: 2. Of those that a mesh axis runs over, the one named last changes fastest.
Arguments:
- tokens: bfloat16 [4, 1024, 768], P('rows', 'seq'), may hold values from -6 to 6
- memory: bfloat16 [4, 1024, 768], P('rows', 'seq'), may hold values from -6 to 6
- out_grad: bfloat16 [4, 1024, 768], P('rows', 'seq'), may hold values from -6 to 6
- table_lengths: int32 [4, 2], P('rows'), may hold values from 0 to 1024, as said below
- table_plots: int32 [4, 2], P('rows'), may hold values from 0 to 1, each once within a row
- self_gain: bfloat16 [768], P(('rows', 'seq')), may hold values from 0.099609375 to 1.8984375
- self_query: bfloat16 [768, 768], P(('rows', 'seq')), may hold values from -0.21875 to 0.21875
- self_key: bfloat16 [768, 768], P(('rows', 'seq')), may hold values from -0.21875 to 0.21875
- self_value: bfloat16 [768, 768], P(('rows', 'seq')), may hold values from -0.21875 to 0.21875
- self_output: bfloat16 [768, 768], P(('rows', 'seq')), may hold values from -1.75 to 1.75
- cross_gain: bfloat16 [768], P(('rows', 'seq')), may hold values from 0.099609375 to 1.8984375
- cross_query: bfloat16 [768, 768], P(('rows', 'seq')), may hold values from -0.21875 to 0.21875
- cross_key: bfloat16 [768, 768], P(('rows', 'seq')), may hold values from -0.21875 to 0.21875
- cross_value: bfloat16 [768, 768], P(('rows', 'seq')), may hold values from -0.21875 to 0.21875
- cross_output: bfloat16 [768, 768], P(('rows', 'seq')), may hold values from -1.75 to 1.75
- mlp_gain: bfloat16 [768], P(('rows', 'seq')), may hold values from 0.099609375 to 1.8984375
- mlp_gate: bfloat16 [768, 2048], P(('rows', 'seq')), may hold values from -0.21875 to 0.21875
- mlp_up: bfloat16 [768, 2048], P(('rows', 'seq')), may hold values from -0.21875 to 0.21875
- mlp_down: bfloat16 [2048, 768], P(('rows', 'seq')), may hold values from -0.125 to 0.125
Outputs:
- layer_out: bfloat16 [4, 1024, 768], P('rows', 'seq')
- tokens_grad: bfloat16 [4, 1024, 768], P('rows', 'seq')
- memory_grad: bfloat16 [4, 1024, 768], P('rows', 'seq')
- self_gain_grad: float32 [768], P(('rows', 'seq'))
- self_query_grad: float32 [768, 768], P(('rows', 'seq'))
- self_key_grad: float32 [768, 768], P(('rows', 'seq'))
- self_value_grad: float32 [768, 768], P(('rows', 'seq'))
- self_output_grad: float32 [768, 768], P(('rows', 'seq'))
- cross_gain_grad: float32 [768], P(('rows', 'seq'))
- cross_query_grad: float32 [768, 768], P(('rows', 'seq'))
- cross_key_grad: float32 [768, 768], P(('rows', 'seq'))
- cross_value_grad: float32 [768, 768], P(('rows', 'seq'))
- cross_output_grad: float32 [768, 768], P(('rows', 'seq'))
- mlp_gain_grad: float32 [768], P(('rows', 'seq'))
- mlp_gate_grad: float32 [768, 2048], P(('rows', 'seq'))
- mlp_up_grad: float32 [768, 2048], P(('rows', 'seq'))
- mlp_down_grad: float32 [2048, 768], P(('rows', 'seq'))
The draws below stay inside these ranges and needn't reach their ends.
Inputs may be any that keep to these rules, and one draw needn't show every extreme that they name: `table_lengths`: every row's lengths sum to 1024. The rows come in aligned blocks of four (rows 0 to 3, 4 to 7 and so on); in each block one row drawn from the seed holds a single table over all 1024 positions, the first, and its other tables are empty; in the other three rows of each block every table has 64 to 960 positions. `table_plots`: each row's entries name each of the row's 2 plots once.
All inputs are finite; a program needn't handle non-finite values.
Results may differ from the reference program's by a relative error of at most 0.03.
Values may be sent and summed in bfloat16 or wider, within the bound.
A program may use at most 192 MiB of HBM per device.

```python
import math
import jax
import jax.numpy as jnp
from jax import lax

D = 768
HEADS = 12
FF = 2048
POS_DEV = 128
TABS = 2
ROWS = 4
ROW_LEN = 1024
MEM_ROW = 1024


def draw_table_lengths(key, part):
    key = jax.random.fold_in(key, 11)
    pick_key, split_key, remix_key = jax.random.split(key, 3)
    least_len = POS_DEV // 2
    pair_total = 8 * POS_DEV
    most_len = pair_total - least_len
    pair_count = TABS // 2
    levels = 64
    level_square = levels * levels
    draws_first = jax.random.randint(split_key, (ROWS, pair_count), 0, levels + 1)
    first_part = least_len + (most_len - least_len) * draws_first * draws_first // level_square
    packed = jnp.stack([first_part, pair_total - first_part], axis=2).reshape(ROWS, TABS)
    turned = jnp.roll(packed, -1, axis=1).reshape(ROWS, pair_count, 2)
    totals = turned[:, :, 0] + turned[:, :, 1]
    low_end = jnp.maximum(least_len, totals - most_len)
    high_end = jnp.minimum(most_len, totals - least_len)
    draws_again = jax.random.randint(remix_key, (ROWS, pair_count), 0, levels + 1)
    renewed = low_end + (high_end - low_end) * draws_again * draws_again // level_square
    remixed = jnp.stack([renewed, totals - renewed], axis=2).reshape(ROWS, TABS)
    packed = jnp.roll(remixed, 1, axis=1)
    columns = jnp.arange(TABS, dtype=jnp.int32)[None, :]
    chosen = jax.random.randint(pick_key, (ROWS // 4,), 0, 4)
    row_place = jnp.arange(ROWS, dtype=jnp.int32) % 4
    chosen_row = jnp.repeat(chosen, 4)
    whole_row = (row_place == chosen_row)[:, None]
    single = jnp.where(columns == 0, ROW_LEN, 0)
    return jnp.where(whole_row, single, packed).astype(jnp.int32)


def level_of(rng, dims, cuts, least, top_value):
    loudness, own = 1.0, jax.random.fold_in(rng, 6)
    for axis_at, parts in cuts:
        heights = jnp.exp(jax.random.uniform(jax.random.fold_in(own, axis_at), (parts,), jnp.float32, least / len(cuts), top_value / len(cuts)))
        loudness = loudness * jnp.repeat(heights, dims[axis_at] // parts).reshape([-1 if axis == axis_at else 1 for axis in range(len(dims))])
    return loudness


def gaussian(rng, shape, width, limit, cuts=(), kind=jnp.bfloat16):
    result = jax.random.normal(rng, shape, jnp.float32) * width
    if len(cuts) > 0:
        result = level_of(rng, shape, cuts, -0.22, 0.18) * result
    return jnp.clip(result, min=-limit, max=limit).astype(kind)


def setup_inputs(seed: int = 0) -> dict:
    streams_of = jax.random.split(jax.random.key(seed), 20)
    tokens = gaussian(streams_of[0], (ROWS, ROW_LEN, D), 1.0, 6.0, ((0, 4), (1, 8)))
    memory = gaussian(streams_of[1], (ROWS, MEM_ROW, D), 1.0, 6.0, ((0, 4), (1, 8)))
    out_grad = gaussian(streams_of[2], (ROWS, ROW_LEN, D), 1.0, 6.0, ((0, 4), (1, 8)))
    table_lengths = draw_table_lengths(jax.random.fold_in(streams_of[19], 71), 0)
    table_plots = jax.vmap(lambda own: jax.random.permutation(own, TABS))(jax.random.split(streams_of[4], ROWS)).reshape((ROWS, TABS)).astype(jnp.int32)
    self_gain = jnp.clip(1.0 + 0.18 * jax.random.normal(streams_of[5], (D,), jnp.float32), 0.099609375, 1.8984375).astype(jnp.bfloat16)
    self_query = gaussian(streams_of[6], (D, D), D ** -0.5, 0.21875, ((0, 32),))
    self_key = gaussian(streams_of[7], (D, D), D ** -0.5, 0.21875, ((0, 32),))
    self_value = gaussian(streams_of[8], (D, D), D ** -0.5, 0.21875, ((0, 32),))
    self_output = gaussian(streams_of[9], (D, D), (D // 64) ** -0.5, 1.75, ((0, 32),))
    cross_gain = jnp.clip(1.0 + 0.18 * jax.random.normal(streams_of[10], (D,), jnp.float32), 0.099609375, 1.8984375).astype(jnp.bfloat16)
    cross_query = gaussian(streams_of[11], (D, D), D ** -0.5, 0.21875, ((0, 32),))
    cross_key = gaussian(streams_of[12], (D, D), D ** -0.5, 0.21875, ((0, 32),))
    cross_value = gaussian(streams_of[13], (D, D), D ** -0.5, 0.21875, ((0, 32),))
    cross_output = gaussian(streams_of[14], (D, D), (D // 64) ** -0.5, 1.75, ((0, 32),))
    mlp_gain = jnp.clip(1.0 + 0.18 * jax.random.normal(streams_of[15], (D,), jnp.float32), 0.099609375, 1.8984375).astype(jnp.bfloat16)
    mlp_gate = gaussian(streams_of[16], (D, FF), D ** -0.5, 0.21875, ((0, 32),))
    mlp_up = gaussian(streams_of[17], (D, FF), D ** -0.5, 0.21875, ((0, 32),))
    mlp_down = gaussian(streams_of[18], (FF, D), FF ** -0.5, 0.125, ((0, 32),))
    return dict(tokens=tokens, memory=memory, out_grad=out_grad, table_lengths=table_lengths, table_plots=table_plots, self_gain=self_gain, self_query=self_query, self_key=self_key, self_value=self_value, self_output=self_output, cross_gain=cross_gain, cross_query=cross_query, cross_key=cross_key, cross_value=cross_value, cross_output=cross_output, mlp_gain=mlp_gain, mlp_gate=mlp_gate, mlp_up=mlp_up, mlp_down=mlp_down)


@jax.custom_vjp
def low(v):
    return lax.optimization_barrier(v.astype(jnp.bfloat16)).astype(jnp.float32)

@jax.custom_vjp
def low_back(v):
    return v

def low_keep(v):
    return (low(v), None)

def low_pass(kept, grad):
    return (grad,)

def back_keep(v):
    return (v, None)

def back_low(kept, grad):
    return (low(grad),)
low.defvjp(low_keep, low_pass)
low_back.defvjp(back_keep, back_low)
HIGHEST = lax.Precision.HIGHEST
SCALE = 0.125
EPS = 1e-06
NEG = -1e+30

def matmul(operand, weight):
    return jnp.einsum('rld,de->rle', operand, weight, precision=HIGHEST)

def rms_norm(values, gain_vector):
    return values * lax.rsqrt(lax.optimization_barrier(jnp.mean(values * values, axis=-1, keepdims=True)) + EPS) * gain_vector

def split_heads(values):
    return values.reshape(values.shape[0], values.shape[1], HEADS, values.shape[2] // HEADS)

def attend_row(query_row, key_row, value_row, query_seg, key_seg, causal):
    length = query_row.shape[0]
    block_rows = math.gcd(length, 512)
    block_count = length // block_rows
    query_pos = jnp.arange(length, dtype=jnp.int32)
    key_pos = jnp.arange(key_row.shape[0], dtype=jnp.int32)

    def one_block(block_items):
        query_block, seg_block, pos_block = block_items
        scores = low_back(jnp.einsum('qhd,khd->hqk', query_block, key_row, precision=HIGHEST) * SCALE)
        allowed = seg_block[:, None] == key_seg[None, :]
        if causal:
            allowed = jnp.logical_and(allowed, key_pos[None, :] <= pos_block[:, None])
        scores = jnp.where(allowed[None], scores, NEG)
        row_max = lax.optimization_barrier(jnp.max(scores, axis=-1, keepdims=True))
        log_total = row_max + jnp.log(lax.optimization_barrier(jnp.sum(jnp.exp(scores - row_max), axis=-1, keepdims=True)))
        probabilities = low(jnp.exp(scores - log_total))
        return jnp.einsum('hqk,khd->qhd', probabilities, value_row, precision=HIGHEST)
    blocks_out = lax.map(jax.checkpoint(one_block), (query_row.reshape(block_count, block_rows, HEADS, -1), query_seg.reshape(block_count, block_rows), query_pos.reshape(block_count, block_rows)))
    return blocks_out.reshape(length, -1)

def attention(queries, key_rows, value_rows, query_seg, key_seg, causal):

    def one_row(row_items):
        return attend_row(row_items[0], row_items[1], row_items[2], row_items[3], row_items[4], causal)
    return lax.map(one_row, (split_heads(queries), split_heads(key_rows), split_heads(value_rows), query_seg, key_seg))

def reference(tokens, memory, out_grad, table_lengths, table_plots, self_gain, self_query, self_key, self_value, self_output, cross_gain, cross_query, cross_key, cross_value, cross_output, mlp_gain, mlp_gate, mlp_up, mlp_down):
    table_ends = jnp.cumsum(table_lengths, axis=1).astype(jnp.int32)
    places = jnp.arange(tokens.shape[1], dtype=jnp.int32)
    token_seg = lax.optimization_barrier(jnp.sum((places[None, :, None] >= table_ends[:, None, :]).astype(jnp.int32), axis=2)).astype(jnp.int32)
    table_ids = jnp.arange(table_lengths.shape[1], dtype=jnp.int32)
    token_plot = lax.optimization_barrier(jnp.sum(jnp.where(token_seg[:, :, None] == table_ids[None, None, :], table_plots[:, None, :], 0), axis=2)).astype(jnp.int32)
    plot_width = memory.shape[1] // table_lengths.shape[1]
    memory_places = jnp.arange(memory.shape[1], dtype=jnp.int32) // plot_width
    memory_plot = jnp.broadcast_to(memory_places[None, :], (memory.shape[0], memory.shape[1]))
    params = tuple((weight.astype(jnp.float32) for weight in (self_gain, self_query, self_key, self_value, self_output, cross_gain, cross_query, cross_key, cross_value, cross_output, mlp_gain, mlp_gate, mlp_up, mlp_down)))

    def layer(values, memory_values, weights):
        input_one = low(rms_norm(values, weights[0]))
        queries = low(low_back(matmul(input_one, weights[1])))
        key_rows = low(low_back(matmul(input_one, weights[2])))
        value_rows = low(low_back(matmul(input_one, weights[3])))
        attended = low(low_back(attention(queries, key_rows, value_rows, token_seg, token_seg, True)))
        first_sum = values + low_back(matmul(attended, weights[4]))
        input_two = low(rms_norm(first_sum, weights[5]))
        cross_rows = low(low_back(matmul(input_two, weights[6])))
        memory_keys = low(low_back(matmul(memory_values, weights[7])))
        memory_rows = low(low_back(matmul(memory_values, weights[8])))
        cross_att = low(low_back(attention(cross_rows, memory_keys, memory_rows, token_plot, memory_plot, False)))
        second_sum = first_sum + low_back(matmul(cross_att, weights[9]))
        input_three = low(rms_norm(second_sum, weights[10]))
        gate_pre = low_back(matmul(input_three, weights[11]))
        up_pre = low_back(matmul(input_three, weights[12]))
        hidden = low(jax.nn.gelu(gate_pre, approximate=True) * up_pre)
        return second_sum + low_back(matmul(hidden, weights[13]))
    outputs, pullback = jax.vjp(layer, tokens.astype(jnp.float32), memory.astype(jnp.float32), params)
    value_grad, memory_values_grad, weight_grads = pullback(out_grad.astype(jnp.float32))
    return (outputs.astype(jnp.bfloat16), value_grad.astype(jnp.bfloat16), memory_values_grad.astype(jnp.bfloat16), weight_grads[0], weight_grads[1], weight_grads[2], weight_grads[3], weight_grads[4], weight_grads[5], weight_grads[6], weight_grads[7], weight_grads[8], weight_grads[9], weight_grads[10], weight_grads[11], weight_grads[12], weight_grads[13])
```

```python
import functools

import jax
import jax.numpy as jnp
from jax import lax
from jax.experimental import pallas as pl
from jax.experimental.pallas import tpu as pltpu
from jax.sharding import PartitionSpec as P

HEADS = 12


SCALE = 0.125
EPS = 1e-06
NEG = -1e30


def running_sum(lengths):
    ids = jnp.arange(lengths.shape[1], dtype=jnp.int32)
    upto = (ids[None, :] <= ids[:, None]).astype(lengths.dtype)
    return jnp.sum(lengths[:, None, :] * upto[None], axis=2)


def rms_forward(values, gain_vector):
    inverse = lax.rsqrt(jnp.mean(values * values, axis=-1, keepdims=True) + EPS)
    return (values * inverse * gain_vector, inverse)


def rms_backward(values, inverse, gain_vector, upstream):
    normed = values * inverse
    gain_grad = jnp.sum(upstream * normed, axis=(0, 1))
    scaled = upstream * gain_vector
    input_grad = inverse * (scaled - normed * jnp.mean(scaled * normed, axis=-1, keepdims=True))
    return (input_grad, gain_grad)


def matmul(operand, weight):
    return jnp.einsum("rld,de->rle", operand, weight, preferred_element_type=jnp.float32)


def matmul_back(upstream, weight):
    return jnp.einsum("rle,de->rld", upstream, weight, preferred_element_type=jnp.float32)


def weight_grad(operand, upstream):
    return jnp.einsum("rld,rle->de", operand, upstream, preferred_element_type=jnp.float32)


def split_heads(values):
    return values.reshape(values.shape[0], values.shape[1], HEADS, values.shape[2] // HEADS)


def segment_of(places, table_ends):
    return jnp.sum((places[None, :, None] >= table_ends[:, None, :]).astype(jnp.int32), axis=2)


def pair_mask(query_seg, query_pos, key_seg, key_pos, causal):
    same_pair = query_seg[:, :, None] == key_seg[:, None, :]
    if causal:
        same_pair = jnp.logical_and(same_pair, key_pos[None, None, :] <= query_pos[None, :, None])
    return same_pair


def over_blocks(advance_block, fold_state, arrays, block_width):
    piece_rows = arrays[0].shape[1]
    block_count = piece_rows // block_width
    stacked = tuple(
        (
            jnp.moveaxis(
                member.reshape((member.shape[0], block_count, block_width) + member.shape[2:]), 1, 0
            )
            for member in arrays
        )
    )

    def advance(carried, block_items):
        block_index, block_parts = block_items
        return (advance_block(carried, block_parts, block_index * block_width), None)

    fold_state, ignored = lax.scan(
        advance, fold_state, (jnp.arange(block_count, dtype=jnp.int32), stacked)
    )
    return fold_state


def forward_fold(query_heads, query_seg, query_pos, key_segment, causal, block_width):

    def advance_block(fold_state, parts, first_row):
        key_block, value_block = parts
        key_pos = first_row + jnp.arange(key_block.shape[1], dtype=jnp.int32)
        allowed = pair_mask(query_seg, query_pos, key_segment(key_pos), key_pos, causal)

        def compute(current):
            running_max, running_sum, accumulated = current
            scores = (
                jnp.einsum(
                    "rqhd,rkhd->rhqk",
                    query_heads,
                    split_heads(key_block),
                    preferred_element_type=jnp.float32,
                )
                * SCALE
            )
            scores = jnp.where(allowed[:, None], scores, NEG)
            new_max = jnp.maximum(running_max, jnp.max(scores, axis=-1))
            weights = jnp.where(allowed[:, None], jnp.exp(scores - new_max[..., None]), 0.0)
            factor = jnp.exp(running_max - new_max)
            new_sum = running_sum * factor + jnp.sum(weights, axis=-1)
            update = jnp.einsum(
                "rhqk,rkhd->rqhd",
                weights.astype(jnp.bfloat16),
                split_heads(value_block),
                preferred_element_type=jnp.float32,
            )
            return (
                new_max,
                new_sum,
                accumulated * jnp.transpose(factor, (0, 2, 1))[..., None] + update,
            )

        return compute(fold_state)

    def forward_fold_piece(fold_state, shard_piece, first_row):
        return over_blocks(advance_block, fold_state, shard_piece, block_width)

    return forward_fold_piece


def finish(fold_state):
    running_max, running_sum, accumulated = fold_state
    attended = accumulated / jnp.transpose(running_sum, (0, 2, 1))[..., None]
    return (attended, running_max + jnp.log(running_sum))


def query_grad_fold(
    query_heads,
    out_heads,
    log_total,
    row_delta,
    query_seg,
    query_pos,
    key_segment,
    causal,
    block_width,
):

    def advance_block(fold_state, parts, first_row):
        key_block, value_block = parts
        key_pos = first_row + jnp.arange(key_block.shape[1], dtype=jnp.int32)
        allowed = pair_mask(query_seg, query_pos, key_segment(key_pos), key_pos, causal)

        def compute(current):
            key_heads = split_heads(key_block)
            scores = (
                jnp.einsum(
                    "rqhd,rkhd->rhqk", query_heads, key_heads, preferred_element_type=jnp.float32
                )
                * SCALE
            )
            scores = jnp.where(allowed[:, None], scores, NEG)
            probabilities = jnp.where(allowed[:, None], jnp.exp(scores - log_total[..., None]), 0.0)
            prob_grad = jnp.einsum(
                "rqhd,rkhd->rhqk",
                out_heads,
                split_heads(value_block),
                preferred_element_type=jnp.float32,
            )
            score_grad = (probabilities * (prob_grad - row_delta[..., None])).astype(jnp.bfloat16)
            return current + SCALE * jnp.einsum(
                "rhqk,rkhd->rqhd", score_grad, key_heads, preferred_element_type=jnp.float32
            )

        return compute(fold_state)

    def query_fold_piece(fold_state, shard_piece, first_row):
        return over_blocks(advance_block, fold_state, shard_piece, block_width)

    return query_fold_piece


def key_grad_fold(
    key_heads,
    value_heads,
    key_seg,
    key_pos,
    total_rows,
    delta_rows,
    query_segment,
    causal,
    block_width,
):

    def advance_block(fold_state, parts, first_row):
        query_block, out_block = parts
        piece_rows = query_block.shape[1]
        query_pos = first_row + jnp.arange(piece_rows, dtype=jnp.int32)
        allowed = pair_mask(query_segment(query_pos), query_pos, key_seg, key_pos, causal)
        total_block = lax.dynamic_slice_in_dim(total_rows, first_row, piece_rows, 2)
        delta_block = lax.dynamic_slice_in_dim(delta_rows, first_row, piece_rows, 2)

        def compute(current):
            key_acc, value_acc = current
            query_heads = split_heads(query_block)
            out_heads = split_heads(out_block)
            scores = (
                jnp.einsum(
                    "rqhd,rkhd->rhqk", query_heads, key_heads, preferred_element_type=jnp.float32
                )
                * SCALE
            )
            scores = jnp.where(allowed[:, None], scores, NEG)
            probabilities = jnp.where(
                allowed[:, None], jnp.exp(scores - total_block[..., None]), 0.0
            )
            value_acc = value_acc + jnp.einsum(
                "rhqk,rqhd->rkhd",
                probabilities.astype(jnp.bfloat16),
                out_heads,
                preferred_element_type=jnp.float32,
            )
            prob_grad = jnp.einsum(
                "rqhd,rkhd->rhqk", out_heads, value_heads, preferred_element_type=jnp.float32
            )
            score_grad = (probabilities * (prob_grad - delta_block[..., None])).astype(jnp.bfloat16)
            key_acc = key_acc + SCALE * jnp.einsum(
                "rhqk,rqhd->rkhd", score_grad, query_heads, preferred_element_type=jnp.float32
            )
            return (key_acc, value_acc)

        return compute(fold_state)

    def key_fold_piece(fold_state, shard_piece, first_row):
        return over_blocks(advance_block, fold_state, shard_piece, block_width)

    return key_fold_piece


def body_general(
    tokens,
    memory,
    out_grad,
    table_lengths,
    table_plots,
    self_gain,
    self_query,
    self_key,
    self_value,
    self_output,
    cross_gain,
    cross_query,
    cross_key,
    cross_value,
    cross_output,
    mlp_gain,
    mlp_gate,
    mlp_up,
    mlp_down,
):
    weight_names = (
        "self_gain",
        "self_query",
        "self_key",
        "self_value",
        "self_output",
        "cross_gain",
        "cross_query",
        "cross_key",
        "cross_value",
        "cross_output",
        "mlp_gain",
        "mlp_gate",
        "mlp_up",
        "mlp_down",
    )
    gathered = dict(
        zip(
            weight_names,
            (
                lax.all_gather(self_gain, ("rows", "seq"), axis=0, tiled=True),
                lax.all_gather(self_query, ("rows", "seq"), axis=0, tiled=True),
                lax.all_gather(self_key, ("rows", "seq"), axis=0, tiled=True),
                lax.all_gather(self_value, ("rows", "seq"), axis=0, tiled=True),
                lax.all_gather(self_output, ("rows", "seq"), axis=0, tiled=True),
                lax.all_gather(cross_gain, ("rows", "seq"), axis=0, tiled=True),
                lax.all_gather(cross_query, ("rows", "seq"), axis=0, tiled=True),
                lax.all_gather(cross_key, ("rows", "seq"), axis=0, tiled=True),
                lax.all_gather(cross_value, ("rows", "seq"), axis=0, tiled=True),
                lax.all_gather(cross_output, ("rows", "seq"), axis=0, tiled=True),
                lax.all_gather(mlp_gain, ("rows", "seq"), axis=0, tiled=True),
                lax.all_gather(mlp_gate, ("rows", "seq"), axis=0, tiled=True),
                lax.all_gather(mlp_up, ("rows", "seq"), axis=0, tiled=True),
                lax.all_gather(mlp_down, ("rows", "seq"), axis=0, tiled=True),
            ),
        )
    )
    seq_count = lax.axis_size("seq")
    seq_index = lax.axis_index("seq")
    row_count = tokens.shape[0]
    positions = tokens.shape[1]
    memory_cols = memory.shape[1]
    width = tokens.shape[2]
    head_size = width // HEADS
    query_pos = seq_index * positions + jnp.arange(positions, dtype=jnp.int32)
    memory_pos = seq_index * memory_cols + jnp.arange(memory_cols, dtype=jnp.int32)
    table_ends = running_sum(table_lengths)
    tables = table_lengths.shape[1]
    table_ids = jnp.arange(tables, dtype=jnp.int32)
    plot_width = memory_cols * seq_count // tables

    def token_segment(places):
        return segment_of(places, table_ends)

    def token_plot(places):
        segments = segment_of(places, table_ends)
        return jnp.sum(
            jnp.where(segments[:, :, None] == table_ids[None, None, :], table_plots[:, None, :], 0),
            axis=2,
        )

    def memory_plot(places):
        return (places // plot_width)[None, :]

    def start_state():
        return (
            jnp.full((row_count, HEADS, positions), NEG, jnp.float32),
            jnp.zeros((row_count, HEADS, positions), jnp.float32),
            jnp.zeros((row_count, positions, HEADS, head_size), jnp.float32),
        )

    values = tokens.astype(jnp.float32)
    normed_one, inverse_one = rms_forward(values, gathered["self_gain"].astype(jnp.float32))
    input_one = normed_one.astype(jnp.bfloat16)
    queries = matmul(input_one, gathered["self_query"]).astype(jnp.bfloat16)
    key_rows = matmul(input_one, gathered["self_key"]).astype(jnp.bfloat16)
    value_rows = matmul(input_one, gathered["self_value"]).astype(jnp.bfloat16)
    query_seg = token_segment(query_pos)
    self_fold = forward_fold(
        split_heads(queries), query_seg, query_pos, token_segment, True, positions
    )
    self_out, self_total = finish(
        self_fold(
            start_state(),
            (
                lax.all_gather(key_rows, "seq", axis=1, tiled=True),
                lax.all_gather(value_rows, "seq", axis=1, tiled=True),
            ),
            jnp.int32(0),
        )
    )
    self_att = self_out.reshape(row_count, positions, width).astype(jnp.bfloat16)
    first_sum = values + matmul(self_att, gathered["self_output"])
    normed_two, inverse_two = rms_forward(first_sum, gathered["cross_gain"].astype(jnp.float32))
    input_two = normed_two.astype(jnp.bfloat16)
    cross_rows = matmul(input_two, gathered["cross_query"]).astype(jnp.bfloat16)
    memory_keys = matmul(memory, gathered["cross_key"]).astype(jnp.bfloat16)
    memory_rows = matmul(memory, gathered["cross_value"]).astype(jnp.bfloat16)
    query_plot = token_plot(query_pos)
    cross_fold = forward_fold(
        split_heads(cross_rows), query_plot, query_pos, memory_plot, False, memory_cols
    )
    cross_out, cross_total = finish(
        cross_fold(
            start_state(),
            (
                lax.all_gather(memory_keys, "seq", axis=1, tiled=True),
                lax.all_gather(memory_rows, "seq", axis=1, tiled=True),
            ),
            jnp.int32(0),
        )
    )
    cross_att = cross_out.reshape(row_count, positions, width).astype(jnp.bfloat16)
    second_sum = first_sum + matmul(cross_att, gathered["cross_output"])
    normed_three, inverse_three = rms_forward(second_sum, gathered["mlp_gain"].astype(jnp.float32))
    input_three = normed_three.astype(jnp.bfloat16)
    gate_pre = matmul(input_three, gathered["mlp_gate"])
    up_pre = matmul(input_three, gathered["mlp_up"])

    def gated_unit(gate_value, up_value):
        return jax.nn.gelu(gate_value, approximate=True) * up_value

    hidden_value, gated_back = jax.vjp(gated_unit, gate_pre, up_pre)
    hidden = hidden_value.astype(jnp.bfloat16)
    layer_out = (second_sum + matmul(hidden, gathered["mlp_down"])).astype(jnp.bfloat16)
    backward = dict(
        zip(
            weight_names,
            (
                lax.all_gather(self_gain, ("rows", "seq"), axis=0, tiled=True),
                lax.all_gather(self_query, ("rows", "seq"), axis=0, tiled=True),
                lax.all_gather(self_key, ("rows", "seq"), axis=0, tiled=True),
                lax.all_gather(self_value, ("rows", "seq"), axis=0, tiled=True),
                lax.all_gather(self_output, ("rows", "seq"), axis=0, tiled=True),
                lax.all_gather(cross_gain, ("rows", "seq"), axis=0, tiled=True),
                lax.all_gather(cross_query, ("rows", "seq"), axis=0, tiled=True),
                lax.all_gather(cross_key, ("rows", "seq"), axis=0, tiled=True),
                lax.all_gather(cross_value, ("rows", "seq"), axis=0, tiled=True),
                lax.all_gather(cross_output, ("rows", "seq"), axis=0, tiled=True),
                lax.all_gather(mlp_gain, ("rows", "seq"), axis=0, tiled=True),
                lax.all_gather(mlp_gate, ("rows", "seq"), axis=0, tiled=True),
                lax.all_gather(mlp_up, ("rows", "seq"), axis=0, tiled=True),
                lax.all_gather(mlp_down, ("rows", "seq"), axis=0, tiled=True),
            ),
        )
    )
    upstream = out_grad.astype(jnp.float32)
    grad_down = weight_grad(hidden, out_grad)
    hidden_grad = matmul_back(out_grad, backward["mlp_down"])
    gate_grad, up_grad = gated_back(hidden_grad)
    gate_low = gate_grad.astype(jnp.bfloat16)
    up_low = up_grad.astype(jnp.bfloat16)
    grad_gate = weight_grad(input_three, gate_low)
    grad_up = weight_grad(input_three, up_low)
    three_grad = matmul_back(gate_low, backward["mlp_gate"]) + matmul_back(
        up_low, backward["mlp_up"]
    )
    part_three, grad_gain_three = rms_backward(
        second_sum, inverse_three, backward["mlp_gain"].astype(jnp.float32), three_grad
    )
    second_grad = upstream + part_three
    cross_branch = second_grad.astype(jnp.bfloat16)
    grad_cross_output = weight_grad(cross_att, cross_branch)
    cross_dout = matmul_back(cross_branch, backward["cross_output"]).astype(jnp.bfloat16)
    cross_heads = split_heads(cross_dout)
    cross_delta = jnp.einsum("rqhd,rqhd->rhq", cross_heads.astype(jnp.float32), cross_out)
    cross_total_all, cross_delta_all = (
        lax.all_gather(cross_total, "seq", axis=2, tiled=True),
        lax.all_gather(cross_delta, "seq", axis=2, tiled=True),
    )
    cross_query_fold = query_grad_fold(
        split_heads(cross_rows),
        cross_heads,
        cross_total,
        cross_delta,
        query_plot,
        query_pos,
        memory_plot,
        False,
        memory_cols,
    )
    cross_rows_grad = cross_query_fold(
        jnp.zeros((row_count, positions, HEADS, head_size), jnp.float32),
        (
            lax.all_gather(memory_keys, "seq", axis=1, tiled=True),
            lax.all_gather(memory_rows, "seq", axis=1, tiled=True),
        ),
        jnp.int32(0),
    )
    cross_rows_low = cross_rows_grad.reshape(row_count, positions, width).astype(jnp.bfloat16)
    memory_fold = key_grad_fold(
        split_heads(memory_keys),
        split_heads(memory_rows),
        memory_plot(memory_pos),
        memory_pos,
        cross_total_all,
        cross_delta_all,
        token_plot,
        False,
        positions,
    )
    memory_zero = jnp.zeros((row_count, memory_cols, HEADS, head_size), jnp.float32)
    memory_key_grad, memory_value_grad = memory_fold(
        (memory_zero, memory_zero),
        (
            lax.all_gather(cross_rows, "seq", axis=1, tiled=True),
            lax.all_gather(cross_dout, "seq", axis=1, tiled=True),
        ),
        jnp.int32(0),
    )
    memory_key_low = memory_key_grad.reshape(row_count, memory_cols, width).astype(jnp.bfloat16)
    memory_value_low = memory_value_grad.reshape(row_count, memory_cols, width).astype(jnp.bfloat16)
    grad_cross_query = weight_grad(input_two, cross_rows_low)
    grad_cross_key = weight_grad(memory, memory_key_low)
    grad_cross_value = weight_grad(memory, memory_value_low)
    memory_grad = (
        matmul_back(memory_key_low, backward["cross_key"])
        + matmul_back(memory_value_low, backward["cross_value"])
    ).astype(jnp.bfloat16)
    two_grad = matmul_back(cross_rows_low, backward["cross_query"])
    part_two, grad_gain_two = rms_backward(
        first_sum, inverse_two, backward["cross_gain"].astype(jnp.float32), two_grad
    )
    first_grad = second_grad + part_two
    self_branch = first_grad.astype(jnp.bfloat16)
    grad_self_output = weight_grad(self_att, self_branch)
    self_dout = matmul_back(self_branch, backward["self_output"]).astype(jnp.bfloat16)
    self_heads = split_heads(self_dout)
    self_delta = jnp.einsum("rqhd,rqhd->rhq", self_heads.astype(jnp.float32), self_out)
    self_total_all, self_delta_all = (
        lax.all_gather(self_total, "seq", axis=2, tiled=True),
        lax.all_gather(self_delta, "seq", axis=2, tiled=True),
    )
    self_query_fold = query_grad_fold(
        split_heads(queries),
        self_heads,
        self_total,
        self_delta,
        query_seg,
        query_pos,
        token_segment,
        True,
        positions,
    )
    queries_grad = self_query_fold(
        jnp.zeros((row_count, positions, HEADS, head_size), jnp.float32),
        (
            lax.all_gather(key_rows, "seq", axis=1, tiled=True),
            lax.all_gather(value_rows, "seq", axis=1, tiled=True),
        ),
        jnp.int32(0),
    )
    queries_low = queries_grad.reshape(row_count, positions, width).astype(jnp.bfloat16)
    self_key_fold = key_grad_fold(
        split_heads(key_rows),
        split_heads(value_rows),
        query_seg,
        query_pos,
        self_total_all,
        self_delta_all,
        token_segment,
        True,
        positions,
    )
    token_zero = jnp.zeros((row_count, positions, HEADS, head_size), jnp.float32)
    key_grad, value_grad = self_key_fold(
        (token_zero, token_zero),
        (
            lax.all_gather(queries, "seq", axis=1, tiled=True),
            lax.all_gather(self_dout, "seq", axis=1, tiled=True),
        ),
        jnp.int32(0),
    )
    key_low = key_grad.reshape(row_count, positions, width).astype(jnp.bfloat16)
    value_low = value_grad.reshape(row_count, positions, width).astype(jnp.bfloat16)
    grad_self_query = weight_grad(input_one, queries_low)
    grad_self_key = weight_grad(input_one, key_low)
    grad_self_value = weight_grad(input_one, value_low)
    one_grad = (
        matmul_back(queries_low, backward["self_query"])
        + matmul_back(key_low, backward["self_key"])
        + matmul_back(value_low, backward["self_value"])
    )
    part_one, grad_gain_one = rms_backward(
        values, inverse_one, backward["self_gain"].astype(jnp.float32), one_grad
    )
    tokens_grad = (first_grad + part_one).astype(jnp.bfloat16)
    summed = tuple(
        (
            lax.psum_scatter(grad_gain_one, ("rows", "seq"), scatter_dimension=0, tiled=True),
            lax.psum_scatter(grad_self_query, ("rows", "seq"), scatter_dimension=0, tiled=True),
            lax.psum_scatter(grad_self_key, ("rows", "seq"), scatter_dimension=0, tiled=True),
            lax.psum_scatter(grad_self_value, ("rows", "seq"), scatter_dimension=0, tiled=True),
            lax.psum_scatter(grad_self_output, ("rows", "seq"), scatter_dimension=0, tiled=True),
            lax.psum_scatter(grad_gain_two, ("rows", "seq"), scatter_dimension=0, tiled=True),
            lax.psum_scatter(grad_cross_query, ("rows", "seq"), scatter_dimension=0, tiled=True),
            lax.psum_scatter(grad_cross_key, ("rows", "seq"), scatter_dimension=0, tiled=True),
            lax.psum_scatter(grad_cross_value, ("rows", "seq"), scatter_dimension=0, tiled=True),
            lax.psum_scatter(grad_cross_output, ("rows", "seq"), scatter_dimension=0, tiled=True),
            lax.psum_scatter(grad_gain_three, ("rows", "seq"), scatter_dimension=0, tiled=True),
            lax.psum_scatter(grad_gate, ("rows", "seq"), scatter_dimension=0, tiled=True),
            lax.psum_scatter(grad_up, ("rows", "seq"), scatter_dimension=0, tiled=True),
            lax.psum_scatter(grad_down, ("rows", "seq"), scatter_dimension=0, tiled=True),
        )
    )
    return (layer_out, tokens_grad, memory_grad) + summed


MESH = pl.DeviceIdType.MESH
BF = jnp.bfloat16
F32 = jnp.float32
QW = 1152
VMEM_LIMIT = 60 * 1024 * 1024


def coords():
    r = lax.axis_index("rows")
    s = lax.axis_index("seq")
    return lax.div(r, 2), lax.rem(r, 2), lax.rem(s, 2), lax.div(s, 2)


def dev(x, c, y, z):
    return {"rows": 2 * x + c, "seq": 2 * z + y}


def remote(src, dst, send_sem, recv_sem, to):
    return pltpu.make_async_remote_copy(
        src_ref=src,
        dst_ref=dst,
        send_sem=send_sem,
        recv_sem=recv_sem,
        device_id=dev(*to),
        device_id_type=MESH,
    )


def owner_of(x, c, y, z):
    return lax.div(z, 2), lax.rem(z, 2), y, 2 * c + x


def source_of(x, c, y, z):
    return lax.rem(z, 2), lax.div(z, 2), y, 2 * x + c


def is_fixed(x, c, y, z):
    same = jnp.logical_and(lax.div(z, 2) == x, lax.rem(z, 2) == c)
    return jnp.logical_and(same, 2 * c + x == z)


def greet(me, pairs=(), z_line=False, moves=False):
    x, c, y, z = me
    bar = pltpu.get_barrier_semaphore()

    def hello(to):
        pl.semaphore_signal(bar, 1, device_id=dev(*to), device_id_type=MESH)

    count = len(pairs)
    for to in pairs:
        hello(to)
    if z_line:

        @pl.when(z > 0)
        def _():
            hello((x, c, y, z - 1))

        @pl.when(z < 3)
        def _():
            hello((x, c, y, z + 1))

        count = count + jnp.where(z > 0, 1, 0) + jnp.where(z < 3, 1, 0)
    if moves:
        away = jnp.logical_not(is_fixed(*me))

        @pl.when(away)
        def _():
            hello(owner_of(*me))
            hello(source_of(*me))

        count = count + jnp.where(away, 2, 0)
    pl.semaphore_wait(bar, count)


class Move:
    def __init__(self, me, src, dst, sems, back=False):
        self.me = me
        to = source_of(*me) if back else owner_of(*me)
        self.far = remote(src, dst, sems.at[0], sems.at[1], to)
        self.near = pltpu.make_async_copy(src, dst, sems.at[0])
        self.fixed = is_fixed(*me)

    def start(self):
        @pl.when(self.fixed)
        def _():
            self.near.start()

        @pl.when(jnp.logical_not(self.fixed))
        def _():
            self.far.start()

    def arrive(self):
        @pl.when(self.fixed)
        def _():
            self.near.wait()

        @pl.when(jnp.logical_not(self.fixed))
        def _():
            self.far.wait_recv()

    def finish(self):
        @pl.when(jnp.logical_not(self.fixed))
        def _():
            self.far.wait_send()


class Gather4:
    def __init__(self, me, buf, sems):
        x, c, y, z = me
        g = 2 * x + c
        self.g = g
        xp, cp = (1 - x, c, y, z), (x, 1 - c, y, z)
        far = 2 * (1 - x) + c
        self.x_own = remote(buf.at[g], buf.at[g], sems.at[0], sems.at[1], xp)
        self.c_own = remote(buf.at[g], buf.at[g], sems.at[2], sems.at[3], cp)
        self.c_far = remote(buf.at[far], buf.at[far], sems.at[4], sems.at[5], cp)

    def start(self):
        self.x_own.start()
        self.c_own.start()

    def forward(self):
        self.x_own.wait_recv()
        self.c_far.start()

    def arrive(self):
        self.c_own.wait_recv()
        self.c_far.wait_recv()

    def finish(self):
        self.x_own.wait_send()
        self.c_own.wait_send()
        self.c_far.wait_send()


class Gather8:
    def __init__(self, me, buf, sems):
        x, c, y, z = me
        xp, cp, yp = (1 - x, c, y, z), (x, 1 - c, y, z), (x, c, 1 - y, z)
        self.c = c

        def piece(px, pc, py):
            return buf.at[2 * (2 * px + pc) + py]

        def send(p, k, to):
            return remote(p, p, sems.at[2 * k], sems.at[2 * k + 1], to)

        own, at_x = piece(x, c, y), piece(1 - x, c, y)
        at_y, at_d = piece(x, c, 1 - y), piece(1 - x, c, 1 - y)
        self.x_own = send(own, 0, xp)
        self.y_own = send(own, 1, yp)
        self.c_own = send(own, 2, cp)
        self.c_x = send(at_x, 3, cp)
        self.c_y = send(at_y, 4, cp)
        self.c_d = send(at_d, 5, cp)
        self.d_by_y = send(at_x, 6, yp)
        self.d_by_x = send(at_y, 6, xp)

    def start(self):
        self.x_own.start()
        self.y_own.start()
        self.c_own.start()

    def forward(self):
        self.x_own.wait_recv()

        @pl.when(self.c == 0)
        def _():
            self.d_by_y.start()

        self.c_x.start()
        self.y_own.wait_recv()

        @pl.when(self.c == 1)
        def _():
            self.d_by_x.start()

        self.c_y.start()

    def forward_far(self):
        self.d_by_y.wait_recv()
        self.c_d.start()

    def arrive(self):
        for one in (self.c_own, self.c_x, self.c_y, self.c_d):
            one.wait_recv()

    def finish(self):
        for one in (self.x_own, self.y_own, self.c_own, self.c_x, self.c_y, self.c_d, self.d_by_y):
            one.wait_send()


class GatherPlane:
    def __init__(self, me, buf, sems):
        self.me, self.buf, self.sems = me, buf, sems

    def piece(self, p, own=True):
        y = self.me[2]
        return self.buf.at[2 * p + (y if own else 1 - y)]

    def up(self, p):
        x, c, y, z = self.me
        return remote(self.piece(p), self.piece(p), self.sems.at[0, p], self.sems.at[1, p], (x, c, y, z + 1))

    def down(self, p):
        x, c, y, z = self.me
        return remote(self.piece(p), self.piece(p), self.sems.at[2, p], self.sems.at[3, p], (x, c, y, z - 1))

    def across(self, p):
        x, c, y, z = self.me
        return remote(self.piece(p), self.piece(p), self.sems.at[4, p], self.sems.at[5, p], (x, c, 1 - y, z))

    def start(self):
        z = self.me[3]

        @pl.when(z < 3)
        def _():
            self.up(z).start()

        @pl.when(z > 0)
        def _():
            self.down(z).start()

        self.across(z).start()

    def forward(self, k):
        z = self.me[3]

        @pl.when(z - k >= 0)
        def _():
            p = z - k
            self.up(p).wait_recv()

            @pl.when(z < 3)
            def _():
                self.up(p).start()

            self.across(p).start()

        @pl.when(z + k <= 3)
        def _():
            p = z + k
            self.down(p).wait_recv()

            @pl.when(z > 0)
            def _():
                self.down(p).start()

            self.across(p).start()

    def arrive(self):
        for p in range(4):
            self.across(p).wait_recv()

    def finish(self):
        z = self.me[3]
        for p in range(4):
            self.across(p).wait_send()

            @pl.when(jnp.logical_and(z < 3, p <= z))
            def _():
                self.up(p).wait_send()

            @pl.when(jnp.logical_and(z > 0, p >= z))
            def _():
                self.down(p).wait_send()


def gather_kernel(
    tok, mem, dout, tab, qp, fp, dn,
    X, M, DO, TAB, Q, F, DN,
    move_sems, near_sems, part_sems, x_sems, m_sems, do_sems, q_sems, f_sems, dn_sems, ff_sems,
):
    me = coords()
    x, c, y, z = me
    g = 2 * x + c
    s = 2 * z + y
    group = ((1 - x, c, y, z), (x, 1 - c, y, z), (1 - x, 1 - c, y, z))
    greet(me, group + ((x, c, 1 - y, z),), z_line=True, moves=True)
    there = owner_of(*me)
    slot = 2 * (2 * there[0] + there[1]) + there[2]
    here = 2 * g + y
    moves = (
        Move(me, tok, X.at[slot], move_sems.at[0]),
        Move(me, tab, TAB, move_sems.at[1]),
        Move(me, mem, M.at[slot], move_sems.at[2]),
        Move(me, dout, DO.at[2 * there[0] + there[1]], move_sems.at[3]),
    )
    moves[0].start()
    moves[1].start()
    near = (
        pltpu.make_async_copy(qp.at[g], Q.at[s, g], near_sems.at[0]),
        pltpu.make_async_copy(fp, F.at[g, s], near_sems.at[1]),
        pltpu.make_async_copy(dn, DN.at[s], near_sems.at[2]),
    )
    for one in near:
        one.start()
    parts = [
        remote(qp.at[2 * to[0] + to[1]], Q.at[s, g], part_sems.at[0, i], part_sems.at[1, i], to)
        for i, to in enumerate(group)
    ]
    for one in parts:
        one.start()
    moves[2].start()
    moves[3].start()
    for one in near:
        one.wait()
    gather_x = Gather8(me, X, x_sems)
    gather_m = Gather8(me, M, m_sems)
    gather_do = Gather4(me, DO, do_sems)
    gather_q = GatherPlane(me, Q, q_sems)
    gather_f = GatherPlane(me, F.at[g], f_sems)
    gather_dn = GatherPlane(me, DN, dn_sems)
    gather_ff = Gather4(me, F, ff_sems)
    moves[0].arrive()
    gather_x.start()
    for one in parts:
        one.wait_recv()
    gather_q.start()
    moves[2].arrive()
    gather_m.start()
    moves[3].arrive()
    gather_do.start()
    gather_f.start()
    gather_dn.start()
    gather_x.forward()
    gather_x.forward_far()
    gather_m.forward()
    gather_do.forward()
    for k in (1, 2, 3):
        gather_q.forward(k)
        gather_f.forward(k)
        gather_dn.forward(k)
    gather_m.forward_far()
    gather_f.arrive()
    gather_ff.start()
    gather_ff.forward()
    moves[1].arrive()
    gather_x.arrive()
    gather_m.arrive()
    gather_do.arrive()
    gather_q.arrive()
    gather_dn.arrive()
    gather_ff.arrive()
    for one in moves:
        one.finish()
    for one in parts:
        one.wait_send()
    for one in (gather_x, gather_m, gather_do, gather_q, gather_f, gather_dn, gather_ff):
        one.finish()


def dma(*shape):
    return pltpu.SemaphoreType.DMA(shape)


ANYWHERE = pl.BlockSpec(memory_space=pl.ANY)
IN_VMEM = pl.BlockSpec(memory_space=pltpu.VMEM)


def gather_all(tok, mem, dout, tab, qp, fp, dn):
    n, d = tok.shape
    out = (
        jax.ShapeDtypeStruct((8, n, d), BF),
        jax.ShapeDtypeStruct((8, n, d), BF),
        jax.ShapeDtypeStruct((4, n, d), BF),
        jax.ShapeDtypeStruct(tab.shape, tab.dtype),
        jax.ShapeDtypeStruct((8,) + qp.shape, BF),
        jax.ShapeDtypeStruct((4, 8) + fp.shape, BF),
        jax.ShapeDtypeStruct((8,) + dn.shape, BF),
    )
    return pl.pallas_call(
        gather_kernel,
        out_shape=out,
        in_specs=[ANYWHERE] * 7,
        out_specs=[ANYWHERE] * 7,
        scratch_shapes=[
            dma(4, 2), dma(3), dma(2, 3), dma(14), dma(14), dma(6), dma(6, 4), dma(6, 4), dma(6, 4), dma(6),
        ],
        compiler_params=pltpu.CompilerParams(collective_id=1, has_side_effects=True),
        name="gather_all",
    )(tok, mem, dout, tab, qp, fp, dn)


def share_kernel(piece, out, near_sem, sems):
    me = coords()
    x, c, y, z = me
    greet(me, ((1 - x, c, y, z), (x, 1 - c, y, z)))
    near = pltpu.make_async_copy(piece, out.at[2 * x + c], near_sem)
    near.start()
    near.wait()
    gather = Gather4(me, out, sems)
    gather.start()
    gather.forward()
    gather.arrive()
    gather.finish()


def share(piece, number):
    return pl.pallas_call(
        share_kernel,
        out_shape=jax.ShapeDtypeStruct((4,) + piece.shape, piece.dtype),
        in_specs=[IN_VMEM],
        out_specs=IN_VMEM,
        scratch_shapes=[pltpu.SemaphoreType.DMA, dma(6)],
        compiler_params=pltpu.CompilerParams(
            collective_id=number, has_side_effects=True, vmem_limit_bytes=VMEM_LIMIT
        ),
        name="share",
    )(piece)


def chunks(rows, step, run):
    def one(i, carry):
        run(pl.ds(pl.multiple_of(i * step, step), step))
        return carry

    lax.fori_loop(0, rows // step, one, 0)


def add_into(into, more, step=16):
    def run(rows):
        total = into[rows, :].astype(F32) + more[rows, :].astype(F32)
        into[rows, :] = total.astype(into.dtype)

    chunks(into.shape[0], step, run)


def sum4_kernel(count, *refs):
    parts, outs = refs[:count], refs[count : 2 * count]
    scratch = refs[2 * count :]
    me = coords()
    x, c, y, z = me
    xp, cp = (1 - x, c, y, z), (x, 1 - c, y, z)
    greet(me, (xp, cp))
    first = []
    for i in range(count):
        land, sems = scratch[3 * i], scratch[3 * i + 2]
        for px in range(2):
            one = remote(
                parts[i].at[2 * px + 1 - c], land.at[px], sems.at[0, px], sems.at[1, px], cp
            )
            one.start()
            first.append(one)
    second = []
    for i in range(count):
        land, late, sems = scratch[3 * i : 3 * i + 3]
        first[2 * i].wait_recv()
        first[2 * i + 1].wait_recv()
        add_into(land.at[1 - x], parts[i].at[2 * (1 - x) + c])
        one = remote(land.at[1 - x], late, sems.at[0, 2], sems.at[1, 2], xp)
        one.start()
        second.append(one)
    for i in range(count):
        land, late, sems = scratch[3 * i : 3 * i + 3]
        second[i].wait_recv()
        mine, own, out = parts[i].at[2 * x + c], land.at[x], outs[i]

        def run(rows):
            out[rows, :] = (
                mine[rows, :].astype(F32) + own[rows, :].astype(F32) + late[rows, :].astype(F32)
            )

        chunks(out.shape[0], 16, run)
    for one in first + second:
        one.wait_send()


def sum4(arrays, number):
    scratch = []
    for a in arrays:
        scratch += [
            pltpu.VMEM((2,) + a.shape[1:], BF),
            pltpu.VMEM(a.shape[1:], BF),
            dma(2, 3),
        ]
    return pl.pallas_call(
        functools.partial(sum4_kernel, len(arrays)),
        out_shape=tuple(jax.ShapeDtypeStruct(a.shape[1:], F32) for a in arrays),
        in_specs=[IN_VMEM] * len(arrays),
        out_specs=tuple([IN_VMEM] * len(arrays)),
        scratch_shapes=scratch,
        compiler_params=pltpu.CompilerParams(
            collective_id=number, has_side_effects=True, vmem_limit_bytes=VMEM_LIMIT
        ),
        name="sum4",
    )(*arrays)


def sum8_kernel(count, *refs):
    parts, outs = refs[:count], refs[count : 2 * count]
    scratch = refs[2 * count :]
    me = coords()
    x, c, y, z = me
    xp, cp, yp = (1 - x, c, y, z), (x, 1 - c, y, z), (x, c, 1 - y, z)
    greet(me, (xp, cp, yp))
    sends = []

    def send(src, dst, sems, k, to):
        one = remote(src, dst, sems.at[0, k], sems.at[1, k], to)
        one.start()
        sends.append(one)
        return one

    first, second, third = {}, {}, {}
    for i in range(count):
        by_c, by_y, by_x, sems = scratch[4 * i : 4 * i + 4]
        for px in range(2):
            for py in range(2):
                k = 2 * px + py
                first[i, k] = send(
                    parts[i].at[2 * (2 * px + 1 - c) + py], by_c.at[px, py], sems, k, cp
                )
    for i in range(count):
        by_c, by_y, by_x, sems = scratch[4 * i : 4 * i + 4]
        for k in range(4):
            first[i, k].wait_recv()
        for px in range(2):
            add_into(by_c.at[px, 1 - y], parts[i].at[2 * (2 * px + c) + 1 - y])
            second[i, px] = send(by_c.at[px, 1 - y], by_y.at[px], sems, 4 + px, yp)
    for i in range(count):
        by_c, by_y, by_x, sems = scratch[4 * i : 4 * i + 4]
        for px in range(2):
            second[i, px].wait_recv()
        add_into(by_y.at[1 - x], by_c.at[1 - x, y])
        add_into(by_y.at[1 - x], parts[i].at[2 * (2 * (1 - x) + c) + y])
        third[i] = send(by_y.at[1 - x], by_x, sems, 6, xp)
    for i in range(count):
        by_c, by_y, by_x, sems = scratch[4 * i : 4 * i + 4]
        third[i].wait_recv()
        mine, a, b, out = parts[i].at[2 * (2 * x + c) + y], by_c.at[x, y], by_y.at[x], outs[i]

        def run(rows):
            out[rows, :] = (
                mine[rows, :].astype(F32)
                + a[rows, :].astype(F32)
                + b[rows, :].astype(F32)
                + by_x[rows, :].astype(F32)
            )

        chunks(out.shape[0], 16, run)
    for one in sends:
        one.wait_send()


def sum8(arrays, number):
    scratch = []
    for a in arrays:
        n, m = a.shape[1:]
        scratch += [
            pltpu.VMEM((2, 2, n, m), BF),
            pltpu.VMEM((2, n, m), BF),
            pltpu.VMEM((n, m), BF),
            dma(2, 7),
        ]
    return pl.pallas_call(
        functools.partial(sum8_kernel, len(arrays)),
        out_shape=tuple(jax.ShapeDtypeStruct(a.shape[1:], F32) for a in arrays),
        in_specs=[IN_VMEM] * len(arrays),
        out_specs=tuple([IN_VMEM] * len(arrays)),
        scratch_shapes=scratch,
        compiler_params=pltpu.CompilerParams(
            collective_id=number, has_side_effects=True, vmem_limit_bytes=VMEM_LIMIT
        ),
        name="sum8",
    )(*arrays)


class SumPlane:
    def __init__(self, me, parts, by_y, by_up, by_down, sems):
        self.me, self.parts, self.sems = me, parts, sems
        self.by_y, self.by_up, self.by_down = by_y, by_up, by_down

    def across(self, p):
        x, c, y, z = self.me
        return remote(
            self.parts.at[2 * p + 1 - y], self.by_y.at[p], self.sems.at[4, p], self.sems.at[5, p], (x, c, 1 - y, z)
        )

    def up(self, p):
        x, c, y, z = self.me
        return remote(
            self.parts.at[2 * p + y], self.by_up.at[p], self.sems.at[0, p], self.sems.at[1, p], (x, c, y, z + 1)
        )

    def down(self, p):
        x, c, y, z = self.me
        return remote(
            self.parts.at[2 * p + y], self.by_down.at[p], self.sems.at[2, p], self.sems.at[3, p], (x, c, y, z - 1)
        )

    def start(self):
        for p in (3, 0, 2, 1):
            self.across(p).start()

    def fold(self):
        y = self.me[2]
        for p in (3, 0, 2, 1):
            self.across(p).wait_recv()
            add_into(self.parts.at[2 * p + y], self.by_y.at[p])

    def pass_on(self, k):
        x, c, y, z = self.me
        p, q = 3 - k, k

        @pl.when(z < p)
        def _():
            @pl.when(z > 0)
            def _():
                self.up(p).wait_recv()
                add_into(self.parts.at[2 * p + y], self.by_up.at[p])

            self.up(p).start()

        @pl.when(z > q)
        def _():
            @pl.when(z < 3)
            def _():
                self.down(q).wait_recv()
                add_into(self.parts.at[2 * q + y], self.by_down.at[q])

            self.down(q).start()

    def end(self):
        x, c, y, z = self.me

        @pl.when(z > 0)
        def _():
            self.up(z).wait_recv()
            add_into(self.parts.at[2 * z + y], self.by_up.at[z])

        @pl.when(z < 3)
        def _():
            self.down(z).wait_recv()
            add_into(self.parts.at[2 * z + y], self.by_down.at[z])

    def finish(self):
        z = self.me[3]
        for p in range(4):
            self.across(p).wait_send()

            @pl.when(z < p)
            def _():
                self.up(p).wait_send()

            @pl.when(z > p)
            def _():
                self.down(p).wait_send()


def scatter_kernel(
    ra, rb, rd, b0, b1, b2,
    oa, ob, od, t0, t1, t2,
    wa, wb, wd, ya, ua, da, yb, ub, db, yd, ud, dd,
    near_sems, sa, sb, sd, part_sems, move_sems,
):
    me = coords()
    x, c, y, z = me
    g = 2 * x + c
    s = 2 * z + y
    group = ((1 - x, c, y, z), (x, 1 - c, y, z), (1 - x, 1 - c, y, z))
    greet(me, group + ((x, c, 1 - y, z),), z_line=True, moves=True)
    loads = [
        pltpu.make_async_copy(src, dst, near_sems.at[i])
        for i, (src, dst) in enumerate(((ra, wa), (rb, wb), (rd, wd)))
    ]
    for one in loads:
        one.start()
    moves = [
        Move(me, src, dst, move_sems.at[i], back=True)
        for i, (src, dst) in enumerate(((b0, t0), (b1, t1), (b2, t2)))
    ]
    sums = (
        SumPlane(me, wd, yd, ud, dd, sd),
        SumPlane(me, wa, ya, ua, da, sa),
        SumPlane(me, wb, yb, ub, db, sb),
    )
    loads[2].wait()
    sums[0].start()
    loads[0].wait()
    sums[1].start()
    loads[1].wait()
    sums[2].start()
    for one in moves:
        one.start()
    for one in sums:
        one.fold()
        one.pass_on(0)
    for k in (1, 2):
        for one in sums:
            one.pass_on(k)
    for one in sums:
        one.end()
    parts = [
        remote(
            wa.at[s, pl.ds(pl.multiple_of((2 * to[0] + to[1]) * 48, 16), 48)],
            oa.at[g],
            part_sems.at[0, i],
            part_sems.at[1, i],
            to,
        )
        for i, to in enumerate(group)
    ]
    for one in parts:
        one.start()
    stores = [
        pltpu.make_async_copy(src, dst, near_sems.at[i])
        for i, (src, dst) in enumerate(
            ((wa.at[s, pl.ds(pl.multiple_of(g * 48, 16), 48)], oa.at[g]), (wb.at[s], ob), (wd.at[s], od))
        )
    ]
    for one in stores:
        one.start()
    for one in stores:
        one.wait()
    for one in parts:
        one.wait_recv()
    for one in moves:
        one.arrive()
        one.finish()
    for one in parts:
        one.wait_send()
    for one in sums:
        one.finish()


def scatter_all(ra, rb, rd, blocks):
    def buffers(a):
        return [pltpu.VMEM((4,) + a.shape[1:], BF)] * 3

    out = (
        jax.ShapeDtypeStruct((4, 48, QW), BF),
        jax.ShapeDtypeStruct(rb.shape[1:], BF),
        jax.ShapeDtypeStruct(rd.shape[1:], BF),
    ) + tuple(jax.ShapeDtypeStruct(b.shape, b.dtype) for b in blocks)
    return pl.pallas_call(
        scatter_kernel,
        out_shape=out,
        in_specs=[ANYWHERE] * 6,
        out_specs=tuple([ANYWHERE] * 6),
        scratch_shapes=[pltpu.VMEM(a.shape, BF) for a in (ra, rb, rd)]
        + buffers(ra)
        + buffers(rb)
        + buffers(rd)
        + [dma(3), dma(6, 4), dma(6, 4), dma(6, 4), dma(2, 3), dma(3, 2)],
        compiler_params=pltpu.CompilerParams(
            collective_id=2, has_side_effects=True, vmem_limit_bytes=VMEM_LIMIT
        ),
        name="scatter_all",
    )(ra, rb, rd, *blocks)


QB = 256


def dot(a, b):
    return lax.dot_general(a, b, (((1,), (0,)), ((), ())), preferred_element_type=F32)


def dot_nt(a, b):
    return lax.dot_general(a, b, (((1,), (1,)), ((), ())), preferred_element_type=F32)


def dot_tn(a, b):
    return lax.dot_general(a, b, (((0,), (0,)), ((), ())), preferred_element_type=F32)


def masked(scores, info, lanes, causal):
    keys = scores.shape[0]
    if causal:
        pos = lax.broadcasted_iota(jnp.int32, scores.shape, 0)
        allowed = jnp.logical_and(pos >= info[1:2, lanes], pos <= info[0:1, lanes])
        return jnp.where(allowed, scores, NEG)
    plot = info[2:3, lanes]
    half = keys // 2
    low = jnp.where(plot == 0, 0.0, NEG)
    high = jnp.where(plot == 1, 0.0, NEG)
    return jnp.concatenate([scores[:half] + low, scores[half:] + high], axis=0)


def attend_kernel(causal, info, qt, k, vt, out, lse):
    keys = k.shape[0]
    for h in range(3):
        rows = slice(64 * h, 64 * h + 64)
        for b in range(512 // QB):
            lanes = slice(QB * b, QB * b + QB)
            top = keys * (b + 1) * QB // 512 if causal else keys
            scores = dot(k[:top, rows], qt[rows, lanes])
            scores = masked(scores, info, lanes, causal)
            high = jnp.max(scores, axis=0, keepdims=True)
            weights = jnp.exp(scores - high)
            total = jnp.sum(weights, axis=0, keepdims=True)
            out[rows, lanes] = dot(vt[rows, :top], weights.astype(BF)) / total
            lse[h : h + 1, lanes] = high + jnp.log(total)


def attend(info, qt, k, vt, causal):
    return pl.pallas_call(
        functools.partial(attend_kernel, causal),
        out_shape=(
            jax.ShapeDtypeStruct(qt.shape, F32),
            jax.ShapeDtypeStruct((8, qt.shape[1]), F32),
        ),
        compiler_params=pltpu.CompilerParams(vmem_limit_bytes=VMEM_LIMIT),
        name="attend",
    )(info, qt, k, vt)


def attend_back_kernel(causal, info, qt, k, kt, v, dot_t, out, lse, dq, dk, dv, dk_acc, dv_acc):
    keys = k.shape[0]
    for h in range(3):
        rows = slice(64 * h, 64 * h + 64)
        for b in reversed(range(512 // QB)):
            lanes = slice(QB * b, QB * b + QB)
            top = keys * (b + 1) * QB // 512 if causal else keys
            query, outer = qt[rows, lanes], dot_t[rows, lanes]
            delta = jnp.sum(outer.astype(F32) * out[rows, lanes], axis=0, keepdims=True)
            scores = masked(dot(k[:top, rows], query), info, lanes, causal)
            prob = jnp.exp(scores - lse[h : h + 1, lanes])
            grad = (prob * (dot(v[:top, rows], outer) - delta)).astype(BF)
            dq[rows, lanes] = (SCALE * dot(kt[rows, :top], grad)).astype(BF)
            dk_new = dot_nt(query, grad)
            dv_new = dot_nt(outer, prob.astype(BF))
            if b == 512 // QB - 1:
                dk_acc[...] = dk_new
                dv_acc[...] = dv_new
            else:
                dk_acc[:, :top] += dk_new
                dv_acc[:, :top] += dv_new
        dk[rows, :] = dk_acc[...].astype(BF)
        dv[rows, :] = dv_acc[...].astype(BF)


def attend_back(info, qt, k, kt, v, dot_t, out, lse, causal):
    keys = k.shape[0]
    return pl.pallas_call(
        functools.partial(attend_back_kernel, causal),
        out_shape=(
            jax.ShapeDtypeStruct(qt.shape, BF),
            jax.ShapeDtypeStruct((192, keys), BF),
            jax.ShapeDtypeStruct((192, keys), BF),
        ),
        scratch_shapes=[pltpu.VMEM((64, keys), F32), pltpu.VMEM((64, keys), F32)],
        compiler_params=pltpu.CompilerParams(vmem_limit_bytes=VMEM_LIMIT),
        name="attend_back",
    )(info, qt, k, kt, v, dot_t, out, lse)


def norm(values, gain):
    inverse = lax.rsqrt(jnp.mean(values * values, axis=-1, keepdims=True) + EPS)
    return (values * inverse * gain).astype(BF), inverse


def norm_back(values, inverse, gain, upstream):
    normed = values * inverse
    scaled = upstream * gain
    grad = inverse * (scaled - normed * jnp.mean(scaled * normed, axis=-1, keepdims=True))
    return grad, upstream * normed


def body_planes(
    tokens, memory, out_grad, table_lengths, table_plots,
    self_gain, self_query, self_key, self_value, self_output,
    cross_gain, cross_query, cross_key, cross_value, cross_output,
    mlp_gain, mlp_gate, mlp_up, mlp_down,
):
    x, c, y, z = coords()
    g = 2 * x + c
    n, d = tokens.shape[1:]

    def quarters(w):
        return jnp.moveaxis(w.reshape(w.shape[0], 4, -1), 1, 0)

    attn = [self_query, self_key, self_value, cross_query, cross_key, cross_value]
    attn = jnp.concatenate([quarters(w) for w in attn], axis=2)
    gains = jnp.stack([self_gain, cross_gain, mlp_gain], axis=1)
    gains = jnp.broadcast_to(jnp.pad(gains, ((0, 0), (0, 125)))[None], (4, 24, 128))
    feed = jnp.concatenate([quarters(mlp_gate), quarters(mlp_up), gains], axis=2)
    qp = jnp.concatenate([attn, feed], axis=1)
    fp = jnp.concatenate([self_output, cross_output, cross_query], axis=1)
    fp = jnp.concatenate([fp[:, :QW], fp[:, QW:]], axis=0)
    ends = running_sum(table_lengths)
    tab = jnp.concatenate([ends[0], table_plots[0], jnp.zeros((4,), jnp.int32)])
    tab = jnp.broadcast_to(tab[:, None], (8, 128))
    X, M, DO, TAB, Q, F, DN = gather_all(tokens[0], memory[0], out_grad[0], tab, qp, fp, mlp_down)

    Q = jnp.moveaxis(Q, 1, 0)
    wa = Q[:, :, :24].reshape(768, QW)
    wm = Q[:, :, 24:].reshape(768, QW)
    w_gate, w_up = wm[:, :512], wm[:, 512:1024]
    gain_one, gain_two, gain_three = (wm[:, 1024 + i].astype(F32) for i in range(3))
    full = jnp.concatenate([F[:, :, :24].reshape(768, QW), F[:, :, 24:].reshape(768, QW)], axis=1)
    w_so, w_co, w_cq_full = full[:, :768], full[:, 768:1536], full[:, 1536:]
    w_down = DN.reshape(512, 768)
    end_one, end_two, plot_one, plot_two = (TAB[i, 0] for i in range(4))
    lane = jnp.arange(512, dtype=jnp.int32)
    qpos = (2 * lax.div(lane, 128) + y) * 128 + lax.rem(lane, 128)
    seg = (qpos >= end_one).astype(jnp.int32) + (qpos >= end_two).astype(jnp.int32)
    first_at = jnp.where(seg == 0, 0, jnp.where(seg == 1, end_one, end_two))
    plot = jnp.where(seg == 0, plot_one, 0) + jnp.where(seg == 1, plot_two, 0)
    info = jnp.concatenate([jnp.stack([qpos, first_at, plot]), jnp.zeros((5, 512), jnp.int32)])

    def mine(a):
        a = a.reshape(4, 2, n, a.shape[-1])
        return lax.dynamic_index_in_dim(a, y, 1, keepdims=False).reshape(4 * n, -1)

    def own(a):
        return lax.dynamic_slice_in_dim(a, g * n, n, 0)

    values = X.reshape(8 * n, d).astype(F32)
    mem = M.reshape(8 * n, d)
    douts = DO.reshape(4 * n, d)
    x1, inv1 = norm(values, gain_one)
    x1_mine = mine(x1)
    v_mine = mine(values)
    qt = (SCALE * dot(x1_mine, wa[:, :192])).astype(BF).T
    k = dot(x1, wa[:, 192:384]).astype(BF)
    v = dot(x1, wa[:, 384:576]).astype(BF)
    mk = dot(mem, wa[:, 768:960]).astype(BF)
    mv = dot(mem, wa[:, 960:1152]).astype(BF)
    kt, vt, mkt, mvt = k.T, v.T, mk.T, mv.T
    att_t, lse1 = attend(info, qt, k, vt, True)
    att_low = att_t.astype(BF)
    att_all = share(att_low, 3).reshape(768, 512)
    first = v_mine + dot_tn(att_all, w_so)
    x2, inv2 = norm(first, gain_two)
    cqt = (SCALE * dot(x2, wa[:, 576:768])).astype(BF).T
    catt_t, lse2 = attend(info, cqt, mk, mvt, False)
    catt_low = catt_t.astype(BF)
    catt_all = share(catt_low, 3).reshape(768, 512)
    second = first + dot_tn(catt_all, w_co)
    x3, inv3 = norm(second, gain_three)
    gate, up = dot(x3, w_gate), dot(x3, w_up)

    def gated_unit(gate_value, up_value):
        return jax.nn.gelu(gate_value, approximate=True) * up_value

    hidden, gated_back = jax.vjp(gated_unit, gate, up)
    hidden = hidden.astype(BF)
    out_part = dot(hidden, w_down).astype(BF)
    d_down = dot_tn(hidden, douts).astype(BF)
    gate_grad, up_grad = gated_back(dot_nt(douts, w_down))
    gate_grad, up_grad = gate_grad.astype(BF), up_grad.astype(BF)
    d_gate = dot_tn(x3, gate_grad).astype(BF)
    d_up = dot_tn(x3, up_grad).astype(BF)
    dx3_part = (dot_nt(gate_grad, w_gate) + dot_nt(up_grad, w_up)).astype(BF)
    out_sum, dx3 = sum4((out_part.reshape(4, n, d), dx3_part.reshape(4, n, d)), 4)
    layer_block = (own(second) + out_sum).astype(BF)
    part, g3 = norm_back(own(second), own(inv3), gain_three, dx3)
    gain3 = jnp.sum(g3, axis=0)
    second_grad = own(douts).astype(F32) + part
    dsec = share(second_grad.astype(BF), 5).reshape(4 * n, d)
    w_co_mine = lax.dynamic_slice_in_dim(w_co, g * 192, 192, 0)
    w_so_mine = lax.dynamic_slice_in_dim(w_so, g * 192, 192, 0)
    d_co = dot(catt_low, dsec).astype(BF)
    cdot = dot_nt(w_co_mine, dsec).astype(BF)
    dcq, dmk, dmv = attend_back(info, cqt, mk, mkt, mv, cdot, catt_t, lse2, False)
    dcq_all = share(dcq, 3).reshape(768, 512)
    dx2 = lax.dot_general(dcq_all, w_cq_full, (((0,), (1,)), ((), ())), preferred_element_type=F32)
    part, g2 = norm_back(first, inv2, gain_two, dx2)
    gain2 = jnp.sum(own(g2), axis=0)
    first_grad = dsec.astype(F32) + part
    dfirst = first_grad.astype(BF)

    def grad_of(operand, turned):
        return lax.dot_general(
            operand, turned, (((0,), (1,)), ((), ())), preferred_element_type=F32
        ).astype(BF)

    def back_to(turned, weight):
        return lax.dot_general(
            turned, weight, (((0,), (1,)), ((), ())), preferred_element_type=F32
        )

    d_cq = grad_of(x2, dcq)
    d_ck, d_cv = grad_of(mem, dmk), grad_of(mem, dmv)
    mem_part = (back_to(dmk, wa[:, 768:960]) + back_to(dmv, wa[:, 960:1152])).astype(BF)
    d_so = dot(att_low, dfirst).astype(BF)
    sdot = dot_nt(w_so_mine, dfirst).astype(BF)
    dq, dk, dv = attend_back(info, qt, k, kt, v, sdot, att_t, lse1, True)
    d_q = grad_of(x1_mine, dq)
    d_k, d_v = grad_of(x1, dk), grad_of(x1, dv)
    one_q = back_to(dq, wa[:, :192]).reshape(4, 1, n, d)
    one_kv = (back_to(dk, wa[:, 192:384]) + back_to(dv, wa[:, 384:576])).reshape(4, 2, n, d)
    here = (jnp.arange(2) == y)[None, :, None, None]
    one_part = jnp.where(here, one_kv + one_q, one_kv).astype(BF).reshape(8, n, d)
    mem_sum, dx1 = sum8((mem_part.reshape(8, n, d), one_part), 6)
    values_own = own(v_mine)
    part, g1 = norm_back(values_own, own(mine(inv1)), gain_one, dx1)
    gain1 = jnp.sum(g1, axis=0)
    first_own = second_grad + own(first_grad - dsec.astype(F32))
    tokens_block = (first_own + part).astype(BF)
    memory_block = mem_sum.astype(BF)
    gain_cols = jnp.pad(jnp.stack([gain1, gain2, gain3], axis=1), ((0, 0), (0, 125))).astype(BF)
    da = jnp.concatenate([d_q, d_k, d_v, d_cq, d_ck, d_cv], axis=1).reshape(4, 8, 24, QW)
    dm = jnp.concatenate([d_gate, d_up, gain_cols], axis=1).reshape(4, 8, 24, QW)
    ra = jnp.moveaxis(jnp.concatenate([da, dm], axis=2), 1, 0).reshape(8, 192, QW)
    rb = jnp.concatenate([d_so.reshape(8, 24, d), d_co.reshape(8, 24, d)], axis=1)
    rd = d_down.reshape(8, 64, d)
    oa, ob, od, layer_mine, tokens_mine, memory_mine = scatter_all(
        ra, rb, rd, (layer_block, tokens_block, memory_block)
    )
    oa = oa.astype(F32)

    def columns(top, start, width):
        part = oa[:, 24 * top : 24 * top + 24, start : start + width]
        return jnp.moveaxis(part, 0, 1).reshape(24, 4 * width)

    gain_sum = jnp.sum(oa[:, 24:, 1024:1027], axis=0)
    ob = ob.astype(F32)
    return (
        layer_mine[None],
        tokens_mine[None],
        memory_mine[None],
        gain_sum[:, 0],
        columns(0, 0, 192),
        columns(0, 192, 192),
        columns(0, 384, 192),
        ob[:24],
        gain_sum[:, 1],
        columns(0, 576, 192),
        columns(0, 768, 192),
        columns(0, 960, 192),
        ob[24:],
        gain_sum[:, 2],
        columns(1, 0, 512),
        columns(1, 512, 512),
        od.astype(F32),
    )


def solution(mesh):
    placed = (
        P("rows", "seq", None),
        P("rows", "seq", None),
        P("rows", "seq", None),
        P("rows", None),
        P("rows", None),
        P(("rows", "seq")),
        P(("rows", "seq"), None),
        P(("rows", "seq"), None),
        P(("rows", "seq"), None),
        P(("rows", "seq"), None),
        P(("rows", "seq")),
        P(("rows", "seq"), None),
        P(("rows", "seq"), None),
        P(("rows", "seq"), None),
        P(("rows", "seq"), None),
        P(("rows", "seq")),
        P(("rows", "seq"), None),
        P(("rows", "seq"), None),
        P(("rows", "seq"), None),
    )
    small = mesh.shape["rows"] == 4 and mesh.shape["seq"] == 8
    return jax.shard_map(
        body_planes if small else body_general,
        mesh=mesh,
        in_specs=placed,
        out_specs=(
            P("rows", "seq", None),
            P("rows", "seq", None),
            P("rows", "seq", None),
            P(("rows", "seq")),
            P(("rows", "seq"), None),
            P(("rows", "seq"), None),
            P(("rows", "seq"), None),
            P(("rows", "seq"), None),
            P(("rows", "seq")),
            P(("rows", "seq"), None),
            P(("rows", "seq"), None),
            P(("rows", "seq"), None),
            P(("rows", "seq"), None),
            P(("rows", "seq")),
            P(("rows", "seq"), None),
            P(("rows", "seq"), None),
            P(("rows", "seq"), None),
        ),
        check_vma=False,
    )
```

```python
import functools

import jax
import jax.numpy as jnp
from jax import lax
from jax.experimental import pallas as pl
from jax.experimental.pallas import tpu as pltpu
from jax.sharding import PartitionSpec as P

HEADS = 12


SCALE = 0.125
EPS = 1e-06
NEG = -1e30
ROW, SEQ = "rows", "seq"
BOTH = (ROW, SEQ)
EQ0 = "rhqk,rkhd->rqhd"
EQ1 = "rhqk,rqhd->rkhd"
EQ2 = "rld,de->rle"
EQ3 = "rld,rle->de"
EQ4 = "rle,de->rld"
EQ5 = "rqhd,rkhd->rhqk"
EQ6 = "rqhd,rqhd->rhq"


def running_sum(lengths):
    ids = jnp.arange(lengths.shape[1], dtype=jnp.int32)
    upto = (ids[None, :] <= ids[:, None]).astype(lengths.dtype)
    return jnp.sum(lengths[:, None, :] * upto[None], axis=2)


def rms_forward(values, gain_vector):
    inverse = lax.rsqrt(jnp.mean(values * values, axis=-1, keepdims=True) + EPS)
    return (values * inverse * gain_vector, inverse)


def rms_backward(values, inverse, gain_vector, upstream):
    normed = values * inverse
    gain_grad = jnp.sum(upstream * normed, axis=(0, 1))
    scaled = upstream * gain_vector
    input_grad = inverse * (scaled - normed * jnp.mean(scaled * normed, axis=-1, keepdims=True))
    return (input_grad, gain_grad)


def matmul(operand, weight):
    return jnp.einsum(EQ2, operand, weight, preferred_element_type=jnp.float32)


def matmul_back(upstream, weight):
    return jnp.einsum(EQ4, upstream, weight, preferred_element_type=jnp.float32)


def weight_grad(operand, upstream):
    return jnp.einsum(EQ3, operand, upstream, preferred_element_type=jnp.float32)


def split_heads(values):
    return values.reshape(values.shape[0], values.shape[1], HEADS, values.shape[2] // HEADS)


def segment_of(places, table_ends):
    return jnp.sum((places[None, :, None] >= table_ends[:, None, :]).astype(jnp.int32), axis=2)


def pair_mask(query_seg, query_pos, key_seg, key_pos, causal):
    same_pair = query_seg[:, :, None] == key_seg[:, None, :]
    if causal:
        same_pair = jnp.logical_and(same_pair, key_pos[None, None, :] <= query_pos[None, :, None])
    return same_pair


def over_blocks(advance_block, fold_state, arrays, block_width):
    piece_rows = arrays[0].shape[1]
    block_count = piece_rows // block_width
    stacked = tuple(
        (
            jnp.moveaxis(
                member.reshape((member.shape[0], block_count, block_width) + member.shape[2:]), 1, 0
            )
            for member in arrays
        )
    )

    def advance(carried, block_items):
        block_index, block_parts = block_items
        return (advance_block(carried, block_parts, block_index * block_width), None)

    fold_state, ignored = lax.scan(
        advance, fold_state, (jnp.arange(block_count, dtype=jnp.int32), stacked)
    )
    return fold_state


def forward_fold(query_heads, query_seg, query_pos, key_segment, causal, block_width):

    def advance_block(fold_state, parts, first_row):
        key_block, value_block = parts
        key_pos = first_row + jnp.arange(key_block.shape[1], dtype=jnp.int32)
        allowed = pair_mask(query_seg, query_pos, key_segment(key_pos), key_pos, causal)

        def compute(current):
            running_max, running_sum, accumulated = current
            scores = (
                jnp.einsum(
                    EQ5,
                    query_heads,
                    split_heads(key_block),
                    preferred_element_type=jnp.float32,
                )
                * SCALE
            )
            scores = jnp.where(allowed[:, None], scores, NEG)
            new_max = jnp.maximum(running_max, jnp.max(scores, axis=-1))
            weights = jnp.where(allowed[:, None], jnp.exp(scores - new_max[..., None]), 0.0)
            factor = jnp.exp(running_max - new_max)
            new_sum = running_sum * factor + jnp.sum(weights, axis=-1)
            update = jnp.einsum(
                EQ0,
                weights.astype(jnp.bfloat16),
                split_heads(value_block),
                preferred_element_type=jnp.float32,
            )
            return (
                new_max,
                new_sum,
                accumulated * jnp.transpose(factor, (0, 2, 1))[..., None] + update,
            )

        return compute(fold_state)

    def forward_fold_piece(fold_state, shard_piece, first_row):
        return over_blocks(advance_block, fold_state, shard_piece, block_width)

    return forward_fold_piece


def finish(fold_state):
    running_max, running_sum, accumulated = fold_state
    attended = accumulated / jnp.transpose(running_sum, (0, 2, 1))[..., None]
    return (attended, running_max + jnp.log(running_sum))


def query_grad_fold(
    query_heads,
    out_heads,
    log_total,
    row_delta,
    query_seg,
    query_pos,
    key_segment,
    causal,
    block_width,
):

    def advance_block(fold_state, parts, first_row):
        key_block, value_block = parts
        key_pos = first_row + jnp.arange(key_block.shape[1], dtype=jnp.int32)
        allowed = pair_mask(query_seg, query_pos, key_segment(key_pos), key_pos, causal)

        def compute(current):
            key_heads = split_heads(key_block)
            scores = (
                jnp.einsum(
                    EQ5, query_heads, key_heads, preferred_element_type=jnp.float32
                )
                * SCALE
            )
            scores = jnp.where(allowed[:, None], scores, NEG)
            probabilities = jnp.where(allowed[:, None], jnp.exp(scores - log_total[..., None]), 0.0)
            prob_grad = jnp.einsum(
                EQ5,
                out_heads,
                split_heads(value_block),
                preferred_element_type=jnp.float32,
            )
            score_grad = (probabilities * (prob_grad - row_delta[..., None])).astype(jnp.bfloat16)
            return current + SCALE * jnp.einsum(
                EQ0, score_grad, key_heads, preferred_element_type=jnp.float32
            )

        return compute(fold_state)

    def query_fold_piece(fold_state, shard_piece, first_row):
        return over_blocks(advance_block, fold_state, shard_piece, block_width)

    return query_fold_piece


def key_grad_fold(
    key_heads,
    value_heads,
    key_seg,
    key_pos,
    total_rows,
    delta_rows,
    query_segment,
    causal,
    block_width,
):

    def advance_block(fold_state, parts, first_row):
        query_block, out_block = parts
        piece_rows = query_block.shape[1]
        query_pos = first_row + jnp.arange(piece_rows, dtype=jnp.int32)
        allowed = pair_mask(query_segment(query_pos), query_pos, key_seg, key_pos, causal)
        total_block = lax.dynamic_slice_in_dim(total_rows, first_row, piece_rows, 2)
        delta_block = lax.dynamic_slice_in_dim(delta_rows, first_row, piece_rows, 2)

        def compute(current):
            key_acc, value_acc = current
            query_heads = split_heads(query_block)
            out_heads = split_heads(out_block)
            scores = (
                jnp.einsum(
                    EQ5, query_heads, key_heads, preferred_element_type=jnp.float32
                )
                * SCALE
            )
            scores = jnp.where(allowed[:, None], scores, NEG)
            probabilities = jnp.where(
                allowed[:, None], jnp.exp(scores - total_block[..., None]), 0.0
            )
            value_acc = value_acc + jnp.einsum(
                EQ1,
                probabilities.astype(jnp.bfloat16),
                out_heads,
                preferred_element_type=jnp.float32,
            )
            prob_grad = jnp.einsum(
                EQ5, out_heads, value_heads, preferred_element_type=jnp.float32
            )
            score_grad = (probabilities * (prob_grad - delta_block[..., None])).astype(jnp.bfloat16)
            key_acc = key_acc + SCALE * jnp.einsum(
                EQ1, score_grad, query_heads, preferred_element_type=jnp.float32
            )
            return (key_acc, value_acc)

        return compute(fold_state)

    def key_fold_piece(fold_state, shard_piece, first_row):
        return over_blocks(advance_block, fold_state, shard_piece, block_width)

    return key_fold_piece


def body_general(
    tokens,
    memory,
    out_grad,
    table_lengths,
    table_plots,
    self_gain,
    self_query,
    self_key,
    self_value,
    self_output,
    cross_gain,
    cross_query,
    cross_key,
    cross_value,
    cross_output,
    mlp_gain,
    mlp_gate,
    mlp_up,
    mlp_down,
):
    def whole(shard):
        return lax.all_gather(shard, BOTH, axis=0, tiled=True)

    all_self_gain = whole(self_gain)
    all_self_query = whole(self_query)
    all_self_key = whole(self_key)
    all_self_value = whole(self_value)
    all_self_output = whole(self_output)
    all_cross_gain = whole(cross_gain)
    all_cross_query = whole(cross_query)
    all_cross_key = whole(cross_key)
    all_cross_value = whole(cross_value)
    all_cross_output = whole(cross_output)
    all_mlp_gain = whole(mlp_gain)
    all_mlp_gate = whole(mlp_gate)
    all_mlp_up = whole(mlp_up)
    all_mlp_down = whole(mlp_down)
    seq_count = lax.axis_size(SEQ)
    seq_index = lax.axis_index(SEQ)
    row_count = tokens.shape[0]
    positions = tokens.shape[1]
    memory_cols = memory.shape[1]
    width = tokens.shape[2]
    head_size = width // HEADS
    query_pos = seq_index * positions + jnp.arange(positions, dtype=jnp.int32)
    memory_pos = seq_index * memory_cols + jnp.arange(memory_cols, dtype=jnp.int32)
    table_ends = running_sum(table_lengths)
    tables = table_lengths.shape[1]
    table_ids = jnp.arange(tables, dtype=jnp.int32)
    plot_width = memory_cols * seq_count // tables

    def token_segment(places):
        return segment_of(places, table_ends)

    def token_plot(places):
        segments = segment_of(places, table_ends)
        return jnp.sum(
            jnp.where(segments[:, :, None] == table_ids[None, None, :], table_plots[:, None, :], 0),
            axis=2,
        )

    def memory_plot(places):
        return (places // plot_width)[None, :]

    def start_state():
        return (
            jnp.full((row_count, HEADS, positions), NEG, jnp.float32),
            jnp.zeros((row_count, HEADS, positions), jnp.float32),
            jnp.zeros((row_count, positions, HEADS, head_size), jnp.float32),
        )

    values = tokens.astype(jnp.float32)
    normed_one, inverse_one = rms_forward(values, all_self_gain.astype(jnp.float32))
    input_one = normed_one.astype(jnp.bfloat16)
    queries = matmul(input_one, all_self_query).astype(jnp.bfloat16)
    key_rows = matmul(input_one, all_self_key).astype(jnp.bfloat16)
    value_rows = matmul(input_one, all_self_value).astype(jnp.bfloat16)
    query_seg = token_segment(query_pos)
    self_fold = forward_fold(
        split_heads(queries), query_seg, query_pos, token_segment, True, positions
    )
    self_out, self_total = finish(
        self_fold(
            start_state(),
            (
                lax.all_gather(key_rows, SEQ, axis=1, tiled=True),
                lax.all_gather(value_rows, SEQ, axis=1, tiled=True),
            ),
            jnp.int32(0),
        )
    )
    self_att = self_out.reshape(row_count, positions, width).astype(jnp.bfloat16)
    first_sum = values + matmul(self_att, all_self_output)
    normed_two, inverse_two = rms_forward(first_sum, all_cross_gain.astype(jnp.float32))
    input_two = normed_two.astype(jnp.bfloat16)
    cross_rows = matmul(input_two, all_cross_query).astype(jnp.bfloat16)
    memory_keys = matmul(memory, all_cross_key).astype(jnp.bfloat16)
    memory_rows = matmul(memory, all_cross_value).astype(jnp.bfloat16)
    query_plot = token_plot(query_pos)
    cross_fold = forward_fold(
        split_heads(cross_rows), query_plot, query_pos, memory_plot, False, memory_cols
    )
    cross_out, cross_total = finish(
        cross_fold(
            start_state(),
            (
                lax.all_gather(memory_keys, SEQ, axis=1, tiled=True),
                lax.all_gather(memory_rows, SEQ, axis=1, tiled=True),
            ),
            jnp.int32(0),
        )
    )
    cross_att = cross_out.reshape(row_count, positions, width).astype(jnp.bfloat16)
    second_sum = first_sum + matmul(cross_att, all_cross_output)
    normed_three, inverse_three = rms_forward(second_sum, all_mlp_gain.astype(jnp.float32))
    input_three = normed_three.astype(jnp.bfloat16)
    gate_pre = matmul(input_three, all_mlp_gate)
    up_pre = matmul(input_three, all_mlp_up)

    def gated_unit(gate_value, up_value):
        return jax.nn.gelu(gate_value, approximate=True) * up_value

    hidden_value, gated_back = jax.vjp(gated_unit, gate_pre, up_pre)
    hidden = hidden_value.astype(jnp.bfloat16)
    layer_out = (second_sum + matmul(hidden, all_mlp_down)).astype(jnp.bfloat16)
    upstream = out_grad.astype(jnp.float32)
    grad_down = weight_grad(hidden, out_grad)
    hidden_grad = matmul_back(out_grad, all_mlp_down)
    gate_grad, up_grad = gated_back(hidden_grad)
    gate_low = gate_grad.astype(jnp.bfloat16)
    up_low = up_grad.astype(jnp.bfloat16)
    grad_gate = weight_grad(input_three, gate_low)
    grad_up = weight_grad(input_three, up_low)
    three_grad = matmul_back(gate_low, all_mlp_gate) + matmul_back(
        up_low, all_mlp_up
    )
    part_three, grad_gain_three = rms_backward(
        second_sum, inverse_three, all_mlp_gain.astype(jnp.float32), three_grad
    )
    second_grad = upstream + part_three
    cross_branch = second_grad.astype(jnp.bfloat16)
    grad_cross_output = weight_grad(cross_att, cross_branch)
    cross_dout = matmul_back(cross_branch, all_cross_output).astype(jnp.bfloat16)
    cross_heads = split_heads(cross_dout)
    cross_delta = jnp.einsum(EQ6, cross_heads.astype(jnp.float32), cross_out)
    cross_total_all, cross_delta_all = (
        lax.all_gather(cross_total, SEQ, axis=2, tiled=True),
        lax.all_gather(cross_delta, SEQ, axis=2, tiled=True),
    )
    cross_query_fold = query_grad_fold(
        split_heads(cross_rows),
        cross_heads,
        cross_total,
        cross_delta,
        query_plot,
        query_pos,
        memory_plot,
        False,
        memory_cols,
    )
    cross_rows_grad = cross_query_fold(
        jnp.zeros((row_count, positions, HEADS, head_size), jnp.float32),
        (
            lax.all_gather(memory_keys, SEQ, axis=1, tiled=True),
            lax.all_gather(memory_rows, SEQ, axis=1, tiled=True),
        ),
        jnp.int32(0),
    )
    cross_rows_low = cross_rows_grad.reshape(row_count, positions, width).astype(jnp.bfloat16)
    memory_fold = key_grad_fold(
        split_heads(memory_keys),
        split_heads(memory_rows),
        memory_plot(memory_pos),
        memory_pos,
        cross_total_all,
        cross_delta_all,
        token_plot,
        False,
        positions,
    )
    memory_zero = jnp.zeros((row_count, memory_cols, HEADS, head_size), jnp.float32)
    memory_key_grad, memory_value_grad = memory_fold(
        (memory_zero, memory_zero),
        (
            lax.all_gather(cross_rows, SEQ, axis=1, tiled=True),
            lax.all_gather(cross_dout, SEQ, axis=1, tiled=True),
        ),
        jnp.int32(0),
    )
    memory_key_low = memory_key_grad.reshape(row_count, memory_cols, width).astype(jnp.bfloat16)
    memory_value_low = memory_value_grad.reshape(row_count, memory_cols, width).astype(jnp.bfloat16)
    grad_cross_query = weight_grad(input_two, cross_rows_low)
    grad_cross_key = weight_grad(memory, memory_key_low)
    grad_cross_value = weight_grad(memory, memory_value_low)
    memory_grad = (
        matmul_back(memory_key_low, all_cross_key)
        + matmul_back(memory_value_low, all_cross_value)
    ).astype(jnp.bfloat16)
    two_grad = matmul_back(cross_rows_low, all_cross_query)
    part_two, grad_gain_two = rms_backward(
        first_sum, inverse_two, all_cross_gain.astype(jnp.float32), two_grad
    )
    first_grad = second_grad + part_two
    self_branch = first_grad.astype(jnp.bfloat16)
    grad_self_output = weight_grad(self_att, self_branch)
    self_dout = matmul_back(self_branch, all_self_output).astype(jnp.bfloat16)
    self_heads = split_heads(self_dout)
    self_delta = jnp.einsum(EQ6, self_heads.astype(jnp.float32), self_out)
    self_total_all, self_delta_all = (
        lax.all_gather(self_total, SEQ, axis=2, tiled=True),
        lax.all_gather(self_delta, SEQ, axis=2, tiled=True),
    )
    self_query_fold = query_grad_fold(
        split_heads(queries),
        self_heads,
        self_total,
        self_delta,
        query_seg,
        query_pos,
        token_segment,
        True,
        positions,
    )
    queries_grad = self_query_fold(
        jnp.zeros((row_count, positions, HEADS, head_size), jnp.float32),
        (
            lax.all_gather(key_rows, SEQ, axis=1, tiled=True),
            lax.all_gather(value_rows, SEQ, axis=1, tiled=True),
        ),
        jnp.int32(0),
    )
    queries_low = queries_grad.reshape(row_count, positions, width).astype(jnp.bfloat16)
    self_key_fold = key_grad_fold(
        split_heads(key_rows),
        split_heads(value_rows),
        query_seg,
        query_pos,
        self_total_all,
        self_delta_all,
        token_segment,
        True,
        positions,
    )
    token_zero = jnp.zeros((row_count, positions, HEADS, head_size), jnp.float32)
    key_grad, value_grad = self_key_fold(
        (token_zero, token_zero),
        (
            lax.all_gather(queries, SEQ, axis=1, tiled=True),
            lax.all_gather(self_dout, SEQ, axis=1, tiled=True),
        ),
        jnp.int32(0),
    )
    key_low = key_grad.reshape(row_count, positions, width).astype(jnp.bfloat16)
    value_low = value_grad.reshape(row_count, positions, width).astype(jnp.bfloat16)
    grad_self_query = weight_grad(input_one, queries_low)
    grad_self_key = weight_grad(input_one, key_low)
    grad_self_value = weight_grad(input_one, value_low)
    one_grad = (
        matmul_back(queries_low, all_self_query)
        + matmul_back(key_low, all_self_key)
        + matmul_back(value_low, all_self_value)
    )
    part_one, grad_gain_one = rms_backward(
        values, inverse_one, all_self_gain.astype(jnp.float32), one_grad
    )
    tokens_grad = (first_grad + part_one).astype(jnp.bfloat16)
    summed = tuple(
        (
            lax.psum_scatter(grad_gain_one, BOTH, scatter_dimension=0, tiled=True),
            lax.psum_scatter(grad_self_query, BOTH, scatter_dimension=0, tiled=True),
            lax.psum_scatter(grad_self_key, BOTH, scatter_dimension=0, tiled=True),
            lax.psum_scatter(grad_self_value, BOTH, scatter_dimension=0, tiled=True),
            lax.psum_scatter(grad_self_output, BOTH, scatter_dimension=0, tiled=True),
            lax.psum_scatter(grad_gain_two, BOTH, scatter_dimension=0, tiled=True),
            lax.psum_scatter(grad_cross_query, BOTH, scatter_dimension=0, tiled=True),
            lax.psum_scatter(grad_cross_key, BOTH, scatter_dimension=0, tiled=True),
            lax.psum_scatter(grad_cross_value, BOTH, scatter_dimension=0, tiled=True),
            lax.psum_scatter(grad_cross_output, BOTH, scatter_dimension=0, tiled=True),
            lax.psum_scatter(grad_gain_three, BOTH, scatter_dimension=0, tiled=True),
            lax.psum_scatter(grad_gate, BOTH, scatter_dimension=0, tiled=True),
            lax.psum_scatter(grad_up, BOTH, scatter_dimension=0, tiled=True),
            lax.psum_scatter(grad_down, BOTH, scatter_dimension=0, tiled=True),
        )
    )
    return (layer_out, tokens_grad, memory_grad) + summed


MESH = pl.DeviceIdType.MESH
BF = jnp.bfloat16
F32 = jnp.float32
QW = 1152
VMEM_LIMIT = 60 * 1024 * 1024


def coords():
    r = lax.axis_index(ROW)
    s = lax.axis_index(SEQ)
    return lax.div(r, 2), lax.rem(r, 2), lax.rem(s, 2), lax.div(s, 2)


def dev(x, c, y, z):
    return {ROW: 2 * x + c, SEQ: 2 * z + y}


def remote(src, dst, send_sem, recv_sem, to):
    return pltpu.make_async_remote_copy(
        src_ref=src,
        dst_ref=dst,
        send_sem=send_sem,
        recv_sem=recv_sem,
        device_id=dev(*to),
        device_id_type=MESH,
    )


def owner_of(x, c, y, z):
    return lax.div(z, 2), lax.rem(z, 2), y, 2 * c + x


def source_of(x, c, y, z):
    return lax.rem(z, 2), lax.div(z, 2), y, 2 * x + c


def is_fixed(x, c, y, z):
    same = jnp.logical_and(lax.div(z, 2) == x, lax.rem(z, 2) == c)
    return jnp.logical_and(same, 2 * c + x == z)


def greet(me, pairs=(), z_line=False, moves=False):
    x, c, y, z = me
    bar = pltpu.get_barrier_semaphore()

    def hello(to):
        pl.semaphore_signal(bar, 1, device_id=dev(*to), device_id_type=MESH)

    count = len(pairs)
    for to in pairs:
        hello(to)
    if z_line:

        @pl.when(z > 0)
        def _():
            hello((x, c, y, z - 1))

        @pl.when(z < 3)
        def _():
            hello((x, c, y, z + 1))

        count = count + jnp.where(z > 0, 1, 0) + jnp.where(z < 3, 1, 0)
    if moves:
        away = jnp.logical_not(is_fixed(*me))

        @pl.when(away)
        def _():
            hello(owner_of(*me))
            hello(source_of(*me))

        count = count + jnp.where(away, 2, 0)
    pl.semaphore_wait(bar, count)


class Move:
    def __init__(self, me, src, dst, sems, back=False):
        self.me = me
        to = source_of(*me) if back else owner_of(*me)
        self.far = remote(src, dst, sems.at[0], sems.at[1], to)
        self.near = pltpu.make_async_copy(src, dst, sems.at[0])
        self.fixed = is_fixed(*me)

    def start(self):
        @pl.when(self.fixed)
        def _():
            self.near.start()

        @pl.when(jnp.logical_not(self.fixed))
        def _():
            self.far.start()

    def arrive(self):
        @pl.when(self.fixed)
        def _():
            self.near.wait()

        @pl.when(jnp.logical_not(self.fixed))
        def _():
            self.far.wait_recv()

    def finish(self):
        @pl.when(jnp.logical_not(self.fixed))
        def _():
            self.far.wait_send()


class Gather4:
    def __init__(self, me, buf, sems):
        x, c, y, z = me
        g = 2 * x + c
        self.g = g
        xp, cp = (1 - x, c, y, z), (x, 1 - c, y, z)
        far = 2 * (1 - x) + c
        self.x_own = remote(buf.at[g], buf.at[g], sems.at[0], sems.at[1], xp)
        self.c_own = remote(buf.at[g], buf.at[g], sems.at[2], sems.at[3], cp)
        self.c_far = remote(buf.at[far], buf.at[far], sems.at[4], sems.at[5], cp)

    def start(self):
        self.x_own.start()
        self.c_own.start()

    def forward(self):
        self.x_own.wait_recv()
        self.c_far.start()

    def arrive(self):
        self.c_own.wait_recv()
        self.c_far.wait_recv()

    def finish(self):
        self.x_own.wait_send()
        self.c_own.wait_send()
        self.c_far.wait_send()


class Gather8:
    def __init__(self, me, buf, sems):
        x, c, y, z = me
        xp, cp, yp = (1 - x, c, y, z), (x, 1 - c, y, z), (x, c, 1 - y, z)
        self.c = c

        def piece(px, pc, py):
            return buf.at[2 * (2 * px + pc) + py]

        def send(p, k, to):
            return remote(p, p, sems.at[2 * k], sems.at[2 * k + 1], to)

        own, at_x = piece(x, c, y), piece(1 - x, c, y)
        at_y, at_d = piece(x, c, 1 - y), piece(1 - x, c, 1 - y)
        self.x_own = send(own, 0, xp)
        self.y_own = send(own, 1, yp)
        self.c_own = send(own, 2, cp)
        self.c_x = send(at_x, 3, cp)
        self.c_y = send(at_y, 4, cp)
        self.c_d = send(at_d, 5, cp)
        self.d_by_y = send(at_x, 6, yp)
        self.d_by_x = send(at_y, 6, xp)

    def start(self):
        self.x_own.start()
        self.y_own.start()
        self.c_own.start()

    def forward(self):
        self.x_own.wait_recv()

        @pl.when(self.c == 0)
        def _():
            self.d_by_y.start()

        self.c_x.start()
        self.y_own.wait_recv()

        @pl.when(self.c == 1)
        def _():
            self.d_by_x.start()

        self.c_y.start()

    def forward_far(self):
        self.d_by_y.wait_recv()
        self.c_d.start()

    def arrive(self):
        for one in (self.c_own, self.c_x, self.c_y, self.c_d):
            one.wait_recv()

    def finish(self):
        for one in (self.x_own, self.y_own, self.c_own, self.c_x, self.c_y, self.c_d, self.d_by_y):
            one.wait_send()


QB = 256


def dot(a, b):
    return lax.dot_general(a, b, (((1,), (0,)), ((), ())), preferred_element_type=F32)


def dot_nt(a, b):
    return lax.dot_general(a, b, (((1,), (1,)), ((), ())), preferred_element_type=F32)


def dot_tn(a, b):
    return lax.dot_general(a, b, (((0,), (0,)), ((), ())), preferred_element_type=F32)


def masked(scores, info, lanes, causal):
    keys = scores.shape[0]
    if causal:
        pos = lax.broadcasted_iota(jnp.int32, scores.shape, 0)
        allowed = jnp.logical_and(pos >= info[1:2, lanes], pos <= info[0:1, lanes])
        return jnp.where(allowed, scores, NEG)
    plot = info[2:3, lanes]
    half = keys // 2
    low = jnp.where(plot == 0, 0.0, NEG)
    high = jnp.where(plot == 1, 0.0, NEG)
    return jnp.concatenate([scores[:half] + low, scores[half:] + high], axis=0)


class GatherPlane:
    def __init__(self, me, buf, sems):
        x, c, y, z = me

        def send(p, k, to):
            piece = buf.at[2 * p + y]
            return remote(piece, piece, sems.at[0, k], sems.at[1, k], to)

        yp = (x, c, 1 - y, z)
        self.along = [send(z, k - 1, (x, c, y, lax.rem(z + k, 4))) for k in (1, 2, 3)]
        self.across = [send(z, 3, yp)]
        self.across += [send(lax.rem(z + 4 - k, 4), 3 + k, yp) for k in (1, 2, 3)]

    def start(self):
        for one in self.along:
            one.start()
        self.across[0].start()

    def forward(self, k):
        self.along[k - 1].wait_recv()
        self.across[k].start()

    def arrive(self):
        for one in self.across:
            one.wait_recv()

    def finish(self):
        for one in self.along + self.across:
            one.wait_send()


class SumPlane:
    def __init__(self, me, parts, by_y, by_z, sems, lanes=None):
        x, c, y, z = me
        self.y, self.z = y, z
        lanes = slice(None) if lanes is None else lanes
        self.mine = [parts.at[2 * lax.rem(z + k, 4) + y, :, lanes] for k in range(4)]
        self.by_y = [by_y.at[lax.rem(z + k, 4), :, lanes] for k in range(4)]
        self.by_z = [by_z.at[k, :, lanes] for k in range(3)]

        def theirs(k):
            return parts.at[2 * lax.rem(z + k, 4) + 1 - y, :, lanes]

        yp = (x, c, 1 - y, z)
        self.across = [
            remote(theirs(k), self.by_y[k], sems.at[0, k], sems.at[1, k], yp) for k in range(4)
        ]
        self.along = [
            remote(
                self.mine[k],
                self.by_z[k - 1],
                sems.at[0, 3 + k],
                sems.at[1, 3 + k],
                (x, c, y, lax.rem(z + k, 4)),
            )
            for k in (1, 2, 3)
        ]

    def start(self):
        for k in (2, 1, 3, 0):
            self.across[k].start()

    def fold(self):
        for k in (2, 1, 3, 0):
            self.across[k].wait_recv()
            add_into(self.mine[k], self.by_y[k])
            if k:
                self.along[k - 1].start()

    def end(self):
        for k in (1, 2, 3):
            self.along[k - 1].wait_recv()
            add_into(self.mine[0], self.by_z[k - 1])

    def finish(self):
        for one in self.across + self.along:
            one.wait_send()


class Sum8:
    def __init__(self, me, parts, by_c, by_y, by_x, sems):
        x, c, y, z = me
        self.me, self.parts = me, parts
        self.by_c, self.by_y, self.by_x = by_c, by_y, by_x
        xp, cp, yp = (1 - x, c, y, z), (x, 1 - c, y, z), (x, c, 1 - y, z)

        def send(src, dst, k, to):
            return remote(src, dst, sems.at[0, k], sems.at[1, k], to)

        self.first = [
            send(parts.at[2 * (2 * px + 1 - c) + py], by_c.at[px, py], 2 * px + py, cp)
            for px in range(2)
            for py in range(2)
        ]
        self.second = [send(by_c.at[px, 1 - y], by_y.at[px], 4 + px, yp) for px in range(2)]
        self.third = send(by_y.at[1 - x], by_x, 6, xp)

    def start(self):
        for one in self.first:
            one.start()

    def to_y(self):
        x, c, y, z = self.me
        for one in self.first:
            one.wait_recv()
        for px in range(2):
            add_into(self.by_c.at[px, 1 - y], self.parts.at[2 * (2 * px + c) + 1 - y])
            self.second[px].start()

    def to_x(self):
        x, c, y, z = self.me
        for one in self.second:
            one.wait_recv()
        add_into(self.by_y.at[1 - x], self.by_c.at[1 - x, y])
        add_into(self.by_y.at[1 - x], self.parts.at[2 * (2 * (1 - x) + c) + y])
        self.third.start()

    def end(self):
        x, c, y, z = self.me
        self.third.wait_recv()
        return (
            self.parts[2 * (2 * x + c) + y].astype(F32)
            + self.by_c[x, y].astype(F32)
            + self.by_y[x].astype(F32)
            + self.by_x[...].astype(F32)
        )

    def finish(self):
        for one in self.first + self.second + [self.third]:
            one.wait_send()


class Sum4:
    def __init__(self, me, parts, by_c, by_x, sems):
        x, c, y, z = me
        self.me, self.parts, self.by_c, self.by_x = me, parts, by_c, by_x
        xp, cp = (1 - x, c, y, z), (x, 1 - c, y, z)
        self.first = [
            remote(parts.at[2 * px + 1 - c], by_c.at[px], sems.at[0, px], sems.at[1, px], cp)
            for px in range(2)
        ]
        self.second = remote(by_c.at[1 - x], by_x, sems.at[0, 2], sems.at[1, 2], xp)

    def start(self):
        for one in self.first:
            one.start()

    def to_x(self):
        x, c, y, z = self.me
        for one in self.first:
            one.wait_recv()
        add_into(self.by_c.at[1 - x], self.parts.at[2 * (1 - x) + c])
        self.second.start()

    def end(self):
        x, c, y, z = self.me
        self.second.wait_recv()
        return (
            self.parts[2 * x + c].astype(F32)
            + self.by_c[x].astype(F32)
            + self.by_x[...].astype(F32)
        )

    def finish(self):
        for one in self.first + [self.second]:
            one.wait_send()


def chunks(rows, step, run):
    def one(i, carry):
        run(pl.ds(pl.multiple_of(i * step, step), step))
        return carry

    lax.fori_loop(0, rows // step, one, 0)


def add_into(into, more, step=16):
    def run(rows):
        total = into[rows, :].astype(F32) + more[rows, :].astype(F32)
        into[rows, :] = total.astype(into.dtype)

    chunks(into.shape[0], step, run)


def dma(*shape):
    return pltpu.SemaphoreType.DMA(shape)


ANYWHERE = pl.BlockSpec(memory_space=pl.ANY)
IN_VMEM = pl.BlockSpec(memory_space=pltpu.VMEM)


def attend_head(h, info, qt, kv, kvt, out, lse, causal):
    keys = kv.shape[0]
    rows = slice(64 * h, 64 * h + 64)
    for b in range(512 // QB):
        lanes = slice(QB * b, QB * b + QB)
        top = keys * (b + 1) * QB // 512 if causal else keys
        scores = dot(kv[:top, rows], qt[rows, lanes])
        scores = masked(scores, info, lanes, causal)
        high = jnp.max(scores, axis=0, keepdims=True)
        weights = jnp.exp(scores - high)
        total = jnp.sum(weights, axis=0, keepdims=True)
        out[rows, lanes] = dot(kvt[192 + 64 * h : 256 + 64 * h, :top], weights.astype(BF)) / total
        lse[h : h + 1, lanes] = high + jnp.log(total)


def attend_back_head(h, info, qt, kv, kvt, outer_t, out, lse, dq, dkv, dk_acc, dv_acc, causal):
    keys = kv.shape[0]
    rows = slice(64 * h, 64 * h + 64)
    value_rows = slice(192 + 64 * h, 256 + 64 * h)
    for b in reversed(range(512 // QB)):
        lanes = slice(QB * b, QB * b + QB)
        top = keys * (b + 1) * QB // 512 if causal else keys
        query, outer = qt[rows, lanes], outer_t[rows, lanes]
        delta = jnp.sum(outer.astype(F32) * out[rows, lanes], axis=0, keepdims=True)
        scores = masked(dot(kv[:top, rows], query), info, lanes, causal)
        prob = jnp.exp(scores - lse[h : h + 1, lanes])
        grad = (prob * (dot(kv[:top, value_rows], outer) - delta)).astype(BF)
        dq[rows, lanes] = (SCALE * dot(kvt[rows, :top], grad)).astype(BF)
        dk_new = dot_nt(query, grad)
        dv_new = dot_nt(outer, prob.astype(BF))
        if b == 512 // QB - 1:
            dk_acc[...] = dk_new
            dv_acc[...] = dv_new
        else:
            dk_acc[:, :top] += dk_new
            dv_acc[:, :top] += dv_new
    dkv[rows, :] = dk_acc[...].astype(BF)
    dkv[value_rows, :] = dv_acc[...].astype(BF)


def norm(values, gain):
    inverse = lax.rsqrt(jnp.mean(values * values, axis=-1, keepdims=True) + EPS)
    return (values * inverse * gain).astype(BF)


def norm_back(values, gain, upstream):
    inverse = lax.rsqrt(jnp.mean(values * values, axis=-1, keepdims=True) + EPS)
    normed = values * inverse
    scaled = upstream * gain
    grad = inverse * (scaled - normed * jnp.mean(scaled * normed, axis=-1, keepdims=True))
    return grad, jnp.sum(upstream * normed, axis=0, keepdims=True)


def gelu_parts(u):
    root = 0.7978845608028654
    square = u * u
    bend = jnp.tanh(root * u * (1.0 + 0.044715 * square))
    half = 0.5 * (1.0 + bend)
    slope = half + 0.5 * u * (1.0 - bend * bend) * (root * (1.0 + 0.134145 * square))
    return u * half, slope


class Names:
    pass


def layer_kernel(names, *refs):
    R = Names()
    for name, ref in zip(names, refs, strict=True):
        setattr(R, name, ref)
    me = coords()
    x, c, y, z = me
    g = 2 * x + c
    s = 2 * z + y
    group = ((1 - x, c, y, z), (x, 1 - c, y, z), (1 - x, 1 - c, y, z))
    line = tuple((x, c, y, lax.rem(z + k, 4)) for k in (1, 2, 3))
    greet(me, group + line + ((x, c, 1 - y, z),), moves=True)

    there = owner_of(*me)
    there_g = 2 * there[0] + there[1]
    move_x = Move(me, R.tok, R.X.at[2 * there_g + y], R.s_move.at[0])
    move_t = Move(me, R.tab, R.TAB, R.s_move.at[1])
    move_m = Move(me, R.mem, R.M.at[2 * there_g + y], R.s_move.at[2])
    move_d = Move(me, R.dout, R.DO.at[there_g], R.s_move.at[3])
    move_x.start()
    move_t.start()
    near_dn = pltpu.make_async_copy(R.down, R.DN.at[s], R.s_near.at[0])
    near_dn.start()

    gains = R.gains[...].astype(F32)
    for k in range(4):
        narrow = slice(192 * k, 192 * k + 192)
        wide = slice(512 * k, 512 * k + 512)
        top = jnp.concatenate(
            [w[:, narrow].astype(F32) for w in (R.ck, R.cv, R.sk, R.sv, R.sq, R.cq)], axis=1
        )
        bottom = jnp.concatenate(
            [R.gate[:, wide].astype(F32), R.up[:, wide].astype(F32), gains], axis=1
        )
        R.stage[k] = jnp.concatenate([top, bottom], axis=0).astype(BF)
    parts = [
        remote(
            R.stage.at[2 * to[0] + to[1]], R.land.at[g], R.s_part.at[0, i], R.s_part.at[1, i], to
        )
        for i, to in enumerate(group)
    ]
    for one in parts:
        one.start()
    move_m.start()
    move_d.start()
    top = jnp.concatenate([R.so[...].astype(F32), R.co[:, :384].astype(F32)], axis=1)
    bottom = jnp.concatenate([R.co[:, 384:].astype(F32), R.cq[...].astype(F32)], axis=1)
    R.FL[g, s] = jnp.concatenate([top, bottom], axis=0).astype(BF)
    R.land[g] = R.stage[g]

    gather_x = Gather8(me, R.X, R.s_x)
    gather_m = Gather8(me, R.M, R.s_m)
    gather_d = Gather4(me, R.DO, R.s_d)
    gather_1 = GatherPlane(me, R.P1, R.s_1)
    gather_2 = GatherPlane(me, R.P2, R.s_2)
    gather_f = GatherPlane(me, R.FL.at[g], R.s_f)
    gather_n = GatherPlane(me, R.DN, R.s_n)
    gather_ff = Gather4(me, R.FL, R.s_ff)
    move_x.arrive()
    gather_x.start()
    for one in parts:
        one.wait_recv()
    tops, bottoms = [], []
    for r in range(4):
        piece = R.land[r].astype(F32)
        tops.append(jnp.concatenate([piece[:24], piece[24:, 1024:]], axis=1))
        bottoms.append(piece[24:, :1024])
    R.P1[s] = jnp.concatenate(tops, axis=0).astype(BF)
    gather_1.start()
    for one in parts:
        one.wait_send()
    R.P2[s] = jnp.concatenate(bottoms, axis=0).astype(BF)
    gather_x.forward()
    gather_x.forward_far()
    for k in (1, 3, 2):
        gather_1.forward(k)
    move_m.arrive()
    gather_m.start()
    gather_f.start()
    gather_1.arrive()
    move_d.arrive()
    gather_d.start()

    def unpack(pieces, whole, width):
        for zz in range(4):

            def one(i, carry):
                lanes = pl.ds(pl.multiple_of(i * 256, 256), 256)
                low = pieces[2 * zz, :, lanes].astype(F32)
                high = pieces[2 * zz + 1, :, lanes].astype(F32)
                for r in range(4):
                    rows = slice(24 * r, 24 * r + 24)
                    both = jnp.concatenate([low[rows], high[rows]], axis=0)
                    whole[192 * r + 48 * zz : 192 * r + 48 * zz + 48, lanes] = both.astype(BF)
                return carry

            lax.fori_loop(0, width // 256, one, 0)

    unpack(R.P1, R.W1, 1280)
    gather_1.finish()
    gain_rows = R.W1[:, 1152:1280].astype(F32).T
    gain_one, gain_two, gain_three = (gain_rows[i : i + 1] for i in range(3))
    gather_x.arrive()
    gather_m.forward()
    gather_m.forward_far()
    gather_d.forward()
    gather_2.start()
    near_dn.wait()
    gather_n.start()
    move_t.arrive()
    end_one, end_two = R.TAB[0:1, 0:1], R.TAB[1:2, 0:1]
    plot_one, plot_two = R.TAB[2:3, 0:1], R.TAB[3:4, 0:1]
    lane = lax.broadcasted_iota(jnp.int32, (1, 512), 1)
    for i in range(4):
        lanes = slice(128 * i, 128 * i + 128)
        R.info[0:1, lanes] = lane[:, :128] + (2 * i + y) * 128
    qpos = R.info[0:1, :]
    past_one, past_two = qpos >= end_one, qpos >= end_two
    R.info[1:2, :] = jnp.where(past_two, end_two, jnp.where(past_one, end_one, 0))
    R.info[2:3, :] = jnp.where(past_two, 0, jnp.where(past_one, plot_two, plot_one))

    def pair_rows(buf, i):
        return jnp.concatenate([buf[2 * i], buf[2 * i + 1]], axis=0)

    def mine_rows(buf):
        return jnp.concatenate([buf[2 * i + y] for i in range(4)], axis=0)

    def keys_values(i, operand, columns, natural, turned):
        rows = pl.ds(pl.multiple_of(i * 256, 256), 256)
        product = dot(operand, R.W1[:, columns])
        natural[rows, :] = product.astype(BF)
        turned[:, rows] = product.T.astype(BF)

    def first_norm(i, carry):
        x1 = norm(pair_rows(R.X, i).astype(F32), gain_one)
        R.X1[2 * i] = x1[:128]
        R.X1[2 * i + 1] = x1[128:]
        keys_values(i, x1, slice(384, 768), R.KV, R.KVT)
        return carry

    lax.fori_loop(0, 4, first_norm, 0)
    product = SCALE * dot(mine_rows(R.X1), R.W1[:, 768:1024])
    R.QT[...] = product.T[:192].astype(BF)
    for k in (1, 3, 2):
        gather_f.forward(k)

    for h in range(3):
        attend_head(h, R.info, R.QT, R.KV, R.KVT, R.OUT1, R.LSE1, True)
        if h == 0:
            gather_f.arrive()
            gather_ff.start()
        if h == 1:
            gather_2.forward(1)
            gather_n.forward(1)
            gather_2.forward(3)
            gather_n.forward(3)
    R.A4[g] = R.OUT1[...].astype(BF)
    share_a = Gather4(me, R.A4, R.s_a)
    share_a.start()
    gather_ff.forward()
    gather_2.forward(2)
    gather_n.forward(2)
    gather_m.arrive()

    def memory_pair(i, carry):
        keys_values(i, pair_rows(R.M, i), slice(0, 384), R.MKV, R.MKVT)
        return carry

    lax.fori_loop(0, 2, memory_pair, 0)
    share_a.forward()
    lax.fori_loop(2, 4, memory_pair, 0)
    gather_ff.arrive()

    def unpack_full(r, carry):
        for zz in range(4):
            low, high = R.FL[r, 2 * zz].astype(F32), R.FL[r, 2 * zz + 1].astype(F32)
            rows = pl.ds(pl.multiple_of(192 * r + 48 * zz, 16), 48)
            R.WF[rows, :QW] = jnp.concatenate([low[:24], high[:24]], axis=0).astype(BF)
            R.WF[rows, QW:] = jnp.concatenate([low[24:], high[24:]], axis=0).astype(BF)
        return carry

    lax.fori_loop(0, 4, unpack_full, 0)
    share_a.arrive()

    def project(pieces, weight, i):
        lanes = slice(256 * i, 256 * i + 256)
        turned = pieces[:, :, lanes].astype(F32).reshape(768, 256)
        return dot(turned.T.astype(BF), weight)

    for i in range(2):
        rows = slice(256 * i, 256 * i + 256)
        before = jnp.concatenate([R.X[4 * i + y], R.X[4 * i + 2 + y]], axis=0).astype(F32)
        first = before + project(R.A4, R.WF[:, :768], i)
        R.FIRST[rows, :] = first
        x2 = norm(first, gain_two)
        R.X2[rows, :] = x2
        product = SCALE * dot(x2, R.W1[:, 896:1152])
        R.CQT[:, rows] = product.T[64:].astype(BF)
    for h in range(3):
        attend_head(h, R.info, R.CQT, R.MKV, R.MKVT, R.OUT2, R.LSE2, False)
    R.C4[g] = R.OUT2[...].astype(BF)
    share_c = Gather4(me, R.C4, R.s_c)
    share_c.start()
    gather_2.arrive()
    unpack(R.P2, R.W2, 1024)
    gather_2.finish()
    share_c.forward()
    gather_d.arrive()
    gather_n.arrive()
    share_c.arrive()
    for i in range(2):
        rows = slice(256 * i, 256 * i + 256)
        second = R.FIRST[rows, :] + project(R.C4, R.WF[:, 768:1536], i)
        R.SECOND[rows, :] = second
        R.X3[rows, :] = norm(second, gain_three)

    sum_dx = Sum4(me, R.DXP, R.by_c_dx, R.by_x_dx, R.s_dx)
    sum_out = Sum4(me, R.OP, R.by_c_out, R.by_x_out, R.s_out)

    def feed(core):
        at = [pl.ds(pl.multiple_of((2 * px + core) * 128, 128), 128) for px in range(2)]
        x3 = jnp.concatenate([R.X3[rows, :] for rows in at], axis=0)
        gate, up = dot(x3, R.W2[:, :512]), dot(x3, R.W2[:, 512:])
        active, slope = gelu_parts(gate)
        hidden = (active * up).astype(BF)
        outer = jnp.concatenate([R.DO[2 * px + core] for px in range(2)], axis=0)
        w_down = R.DN[...].reshape(512, 768)
        hidden_grad = dot_nt(outer, w_down)
        gate_grad = (hidden_grad * up * slope).astype(BF)
        up_grad = (hidden_grad * active).astype(BF)
        dx3 = (dot_nt(gate_grad, R.W2[:, :512]) + dot_nt(up_grad, R.W2[:, 512:])).astype(BF)
        out = dot(hidden, w_down).astype(BF)
        for px in range(2):
            half = slice(128 * px, 128 * px + 128)
            R.H[at[px], :] = hidden[half]
            R.GG[at[px], :512] = gate_grad[half]
            R.GG[at[px], 512:] = up_grad[half]
            R.DXP[2 * px + core] = dx3[half]
            R.OP[2 * px + core] = out[half]

    feed(1 - c)
    sum_dx.start()
    feed(c)
    sum_dx.to_x()
    sum_out.start()
    own = pl.ds(pl.multiple_of(g * 128, 128), 128)
    own_block = 2 * g + y
    x3_t = R.X3[...].astype(F32).T.astype(BF)
    R.W2G[...] = dot(x3_t, R.GG[:, :512])
    part, gain_grad_three = norm_back(R.SECOND[own, :], gain_three, sum_dx.end())
    second_grad = R.DO[g].astype(F32) + part
    R.SGRAD[...] = second_grad
    R.DS4[g] = second_grad.astype(BF)
    share_s = Gather4(me, R.DS4, R.s_s)
    share_s.start()

    def pack(whole, pieces, start, width):
        for t in range(8):
            rows = [whole[(8 * r + t) * 24 : (8 * r + t) * 24 + 24, :] for r in range(4)]
            pieces[t, :, start : start + width] = jnp.concatenate(rows, axis=0).astype(BF)

    pack(R.W2G, R.P2, 0, 512)
    share_s.forward()
    R.W2G[...] = dot(x3_t, R.GG[:, 512:])
    pack(R.W2G, R.P2, 512, 512)
    hidden_t = R.H[...].astype(F32).T.astype(BF)
    d_down = dot(hidden_t, R.DO[...].reshape(512, 768)).astype(BF)
    for t in range(8):
        R.DNG[t] = d_down[64 * t : 64 * t + 64]
    total_2 = SumPlane(me, R.P2, R.by_y_2, R.by_z_2, R.s_g2)
    total_n = SumPlane(me, R.DNG, R.by_y_n, R.by_z_n, R.s_gn)
    share_s.arrive()
    total_2.start()
    total_n.start()

    dsec = R.DS4[...].reshape(512, 768)
    mine_192 = pl.ds(pl.multiple_of(g * 192, 16), 192)
    R.OUTER[...] = dot_nt(R.WF[mine_192, 768:1536], dsec).astype(BF)
    for h in range(3):
        attend_back_head(
            h, R.info, R.CQT, R.MKV, R.MKVT, R.OUTER, R.OUT2, R.LSE2, R.DCQT, R.MDKV, R.dk, R.dv, False
        )
    R.DC4[g] = R.DCQT[...]
    share_q = Gather4(me, R.DC4, R.s_q)
    share_q.start()
    sum_out.to_x()

    def pack_24(whole, pieces):
        for t in range(8):
            rows = whole[24 * t : 24 * t + 24]
            pieces[t] = jnp.concatenate([rows[:, :384], rows[:, 384:]], axis=0).astype(BF)

    pack_24(dot(R.C4[g], dsec), R.CO8)
    total_c = SumPlane(me, R.CO8, R.by_y_c, R.by_z_c, R.s_gc)
    total_c.start()
    total_2.fold()
    total_n.fold()

    def memory_grad_pair(i, carry):
        lanes = pl.ds(pl.multiple_of(i * 256, 256), 256)
        turned = dot(R.W1[:, :384], R.MDKV[:, lanes]).astype(BF)
        R.MG[2 * i] = turned[:, :128]
        R.MG[2 * i + 1] = turned[:, 128:]
        return carry

    lax.fori_loop(0, 2, memory_grad_pair, 0)
    share_q.forward()
    lax.fori_loop(2, 4, memory_grad_pair, 0)
    sum_m = Sum8(me, R.MG, R.by_c_m, R.by_y_m, R.by_x_m, R.s_gm)
    sum_m.start()
    share_q.arrive()

    for i in range(2):
        rows = slice(256 * i, 256 * i + 256)
        turned = R.DC4[:, :, rows].reshape(768, 256)
        dx2 = dot(R.WF[:, 1536:], turned).T
        part, ignored = norm_back(R.FIRST[rows, :], gain_two, dx2)
        R.DFIRST[rows, :] = (dsec[rows].astype(F32) + part).astype(BF)
    dx2 = dot(R.WF[:, 1536:], R.DC4[:, :, own].reshape(768, 128)).T
    part, gain_grad_two = norm_back(R.FIRST[own, :], gain_two, dx2)
    R.SGRAD[...] += part

    R.OUTER[...] = dot_nt(R.WF[mine_192, :768], R.DFIRST[...]).astype(BF)
    sum_m.to_y()
    for h in range(3):
        attend_back_head(
            h, R.info, R.QT, R.KV, R.KVT, R.OUTER, R.OUT1, R.LSE1, R.DQT, R.DKV, R.dk, R.dv, True
        )
        if h == 0:
            total_c.fold()
            sum_m.to_x()

    def token_grad_pair(i, carry):
        lanes = pl.ds(pl.multiple_of(i * 256, 256), 256)
        half = pl.ds(pl.multiple_of(i * 128, 128), 128)
        turned = dot(R.W1[:, 384:768], R.DKV[:, lanes])
        query = dot(R.W1[:, 768:960], R.DQT[:, half])
        R.TG[2 * i] = (turned[:, :128] + jnp.where(y == 0, query, 0.0)).astype(BF)
        R.TG[2 * i + 1] = (turned[:, 128:] + jnp.where(y == 1, query, 0.0)).astype(BF)
        return carry

    lax.fori_loop(0, 4, token_grad_pair, 0)
    sum_t = Sum8(me, R.TG, R.by_c_t, R.by_y_t, R.by_x_t, R.s_gt)
    sum_t.start()
    memory_t = dot(R.MDKV[...], R.M[...].reshape(1024, 768))
    R.W1G[...] = memory_t.T
    pack(R.W1G, R.P1, 0, 384)
    total_1a = SumPlane(me, R.P1, R.by_y_1, R.by_z_1, R.s_g1a, slice(0, 384))
    total_1a.start()
    sum_t.to_y()
    turned = dot(R.DKV[...], R.X1[...].reshape(1024, 768))
    R.W1G[...] = turned.T
    pack(R.W1G, R.P1, 384, 384)
    sum_t.to_x()
    R.TURN[:192, :] = dot(R.DQT[...], mine_rows(R.X1))
    R.TURN[192:, :] = dot(R.DCQT[...], R.X2[...])
    R.W1G[...] = R.TURN[...].T
    pack(R.W1G, R.P1, 768, 384)
    pack_24(dot(R.A4[g], R.DFIRST[...]), R.SO8)
    dx1 = sum_t.end().T
    part, gain_grad_one = norm_back(R.X[own_block].astype(F32), gain_one, dx1)
    gain_grads = jnp.concatenate(
        [gain_grad_one, gain_grad_two, gain_grad_three, jnp.zeros((125, 768), F32)], axis=0
    )
    R.GAINS[...] = gain_grads.T
    pack(R.GAINS, R.P1, 1152, 128)
    total_1b = SumPlane(me, R.P1, R.by_y_1, R.by_z_1, R.s_g1b, slice(384, 1280))
    total_s = SumPlane(me, R.SO8, R.by_y_s, R.by_z_s, R.s_gs)
    total_1b.start()
    total_s.start()
    R.TBLOCK[...] = (R.SGRAD[...] + part).astype(BF)
    R.LBLOCK[...] = (R.SECOND[own, :] + sum_out.end()).astype(BF)
    R.MBLOCK[...] = sum_m.end().T.astype(BF)
    back = [
        Move(me, src, dst, R.s_back.at[i], back=True)
        for i, (src, dst) in enumerate(
            ((R.TBLOCK, R.tokens_out), (R.LBLOCK, R.layer_out), (R.MBLOCK, R.memory_out))
        )
    ]
    for one in back:
        one.start()
    total_1a.fold()
    total_1b.fold()
    total_s.fold()
    total_2.end()
    total_n.end()
    total_c.end()
    total_1a.end()
    total_1b.end()
    first_rows = R.P1[s].astype(F32)
    last_rows = R.P2[s].astype(F32)
    for r in range(4):
        rows = slice(24 * r, 24 * r + 24)
        bottom = jnp.concatenate([last_rows[rows], first_rows[rows, 1152:]], axis=1)
        R.stage[r] = jnp.concatenate([first_rows[rows, :1152], bottom], axis=0).astype(BF)
    finals = [
        remote(
            R.stage.at[2 * to[0] + to[1]], R.quarters_out.at[g], R.s_last.at[0, i], R.s_last.at[1, i], to
        )
        for i, to in enumerate(group)
    ]
    for one in finals:
        one.start()
    total_s.end()
    near = [
        pltpu.make_async_copy(src, dst, R.s_near.at[1 + i])
        for i, (src, dst) in enumerate(
            (
                (R.stage.at[g], R.quarters_out.at[g]),
                (R.CO8.at[s], R.co_out),
                (R.SO8.at[s], R.so_out),
                (R.DNG.at[s], R.down_out),
            )
        )
    ]
    for one in near:
        one.start()
    for one in near:
        one.wait()
    for one in finals:
        one.wait_recv()
    for one in back:
        one.arrive()
        one.finish()
    for one in finals:
        one.wait_send()
    for one in (move_x, move_t, move_m, move_d):
        one.finish()
    for one in (gather_x, gather_m, gather_d, gather_f, gather_n, gather_ff):
        one.finish()
    for one in (share_a, share_c, share_s, share_q, sum_dx, sum_out, sum_m, sum_t):
        one.finish()
    for one in (total_1a, total_1b, total_2, total_n, total_c, total_s):
        one.finish()


def run_layer(inputs):
    n, d = 128, 768

    def low(*shape):
        return pltpu.VMEM(shape, BF)

    def full(*shape):
        return pltpu.VMEM(shape, F32)

    outs = dict(
        quarters_out=(4, 48, QW),
        co_out=(48, 384),
        so_out=(48, 384),
        down_out=(64, d),
        tokens_out=(n, d),
        layer_out=(n, d),
        memory_out=(n, d),
    )
    scratch = dict(
        stage=low(4, 48, QW), land=low(4, 48, QW),
        X=low(8, n, d), M=low(8, n, d), DO=low(4, n, d), TAB=pltpu.VMEM((8, 128), jnp.int32),
        P1=low(8, 96, 1280), P2=low(8, 96, 1024), FL=low(4, 8, 48, QW), DN=low(8, 64, d),
        W1=low(768, 1280), W2=low(768, 1024), WF=low(768, 2304),
        info=pltpu.VMEM((8, 512), jnp.int32),
        X1=low(8, n, d), X2=low(512, d), X3=low(512, d),
        KV=low(1024, 384), KVT=low(384, 1024), MKV=low(1024, 384), MKVT=low(384, 1024),
        QT=low(192, 512), CQT=low(192, 512), OUT1=full(192, 512), OUT2=full(192, 512),
        LSE1=full(8, 512), LSE2=full(8, 512),
        A4=low(4, 192, 512), C4=low(4, 192, 512), DC4=low(4, 192, 512),
        FIRST=full(512, d), SECOND=full(512, d),
        H=low(512, 512), GG=low(512, 1024), DXP=low(4, n, d), OP=low(4, n, d),
        by_c_dx=low(2, n, d), by_x_dx=low(n, d), by_c_out=low(2, n, d), by_x_out=low(n, d),
        W2G=full(768, 512), by_y_2=low(4, 96, 1024), by_z_2=low(3, 96, 1024),
        DNG=low(8, 64, d), by_y_n=low(4, 64, d), by_z_n=low(3, 64, d),
        SGRAD=full(n, d), DS4=low(4, n, d), OUTER=low(192, 512),
        DCQT=low(192, 512), DQT=low(192, 512), MDKV=low(384, 1024), DKV=low(384, 1024),
        dk=full(64, 1024), dv=full(64, 1024),
        CO8=low(8, 48, 384), by_y_c=low(4, 48, 384), by_z_c=low(3, 48, 384),
        SO8=low(8, 48, 384), by_y_s=low(4, 48, 384), by_z_s=low(3, 48, 384),
        MG=low(8, d, n), by_c_m=low(2, 2, d, n), by_y_m=low(2, d, n), by_x_m=low(d, n),
        TG=low(8, d, n), by_c_t=low(2, 2, d, n), by_y_t=low(2, d, n), by_x_t=low(d, n),
        DFIRST=low(512, d),
        W1G=full(768, 384), TURN=full(384, 768), GAINS=full(768, 128),
        by_y_1=low(4, 96, 1280), by_z_1=low(3, 96, 1280),
        TBLOCK=low(n, d), LBLOCK=low(n, d), MBLOCK=low(n, d),
        s_move=dma(4, 2), s_near=dma(5), s_part=dma(2, 3), s_last=dma(2, 3), s_back=dma(3, 2),
        s_x=dma(14), s_m=dma(14), s_d=dma(6), s_ff=dma(6),
        s_1=dma(2, 7), s_2=dma(2, 7), s_f=dma(2, 7), s_n=dma(2, 7),
        s_a=dma(6), s_c=dma(6), s_s=dma(6), s_q=dma(6),
        s_dx=dma(2, 3), s_out=dma(2, 3), s_gm=dma(2, 7), s_gt=dma(2, 7),
        s_g1a=dma(2, 7), s_g1b=dma(2, 7), s_g2=dma(2, 7), s_gn=dma(2, 7), s_gc=dma(2, 7), s_gs=dma(2, 7),
    )
    names = tuple(inputs) + tuple(outs) + tuple(scratch)
    return pl.pallas_call(
        functools.partial(layer_kernel, names),
        out_shape=tuple(jax.ShapeDtypeStruct(shape, BF) for shape in outs.values()),
        in_specs=[spec for _, spec in inputs.values()],
        out_specs=tuple([ANYWHERE] * len(outs)),
        scratch_shapes=list(scratch.values()),
        compiler_params=pltpu.CompilerParams(
            collective_id=1, has_side_effects=True, vmem_limit_bytes=VMEM_LIMIT
        ),
        name="layer",
    )(*[a for a, _ in inputs.values()])


def body_planes(
    tokens, memory, out_grad, table_lengths, table_plots,
    self_gain, self_query, self_key, self_value, self_output,
    cross_gain, cross_query, cross_key, cross_value, cross_output,
    mlp_gain, mlp_gate, mlp_up, mlp_down,
):
    gains = jnp.stack([self_gain, cross_gain, mlp_gain], axis=1)
    gains = jnp.pad(gains, ((0, 0), (0, 125)))
    ends = running_sum(table_lengths)
    tab = jnp.concatenate([ends[0], table_plots[0], jnp.zeros((4,), jnp.int32)])
    tab = jnp.broadcast_to(tab[:, None], (8, 128))
    oa, co, so, down, tokens_mine, layer_mine, memory_mine = run_layer(
        dict(
            tok=(tokens[0], ANYWHERE), mem=(memory[0], ANYWHERE), dout=(out_grad[0], ANYWHERE),
            tab=(tab, IN_VMEM), gains=(gains, IN_VMEM),
            sq=(self_query, IN_VMEM), sk=(self_key, IN_VMEM), sv=(self_value, IN_VMEM), so=(self_output, IN_VMEM),
            cq=(cross_query, IN_VMEM), ck=(cross_key, IN_VMEM), cv=(cross_value, IN_VMEM), co=(cross_output, IN_VMEM),
            gate=(mlp_gate, IN_VMEM), up=(mlp_up, IN_VMEM), down=(mlp_down, ANYWHERE),
        )
    )
    oa = oa.astype(F32)

    def columns(top, start, width):
        part = oa[:, 24 * top : 24 * top + 24, start : start + width]
        return jnp.moveaxis(part, 0, 1).reshape(24, 4 * width)

    def halves(a):
        a = a.astype(F32)
        return jnp.concatenate([a[:24], a[24:]], axis=1)

    gain_sum = jnp.sum(oa[:, 24:, 1024:1027], axis=0)
    return (
        layer_mine[None], tokens_mine[None], memory_mine[None],
        gain_sum[:, 0], columns(0, 768, 192), columns(0, 384, 192), columns(0, 576, 192), halves(so),
        gain_sum[:, 1], columns(0, 960, 192), columns(0, 0, 192), columns(0, 192, 192), halves(co),
        gain_sum[:, 2], columns(1, 0, 512), columns(1, 512, 512), down.astype(F32),
    )


def solution(mesh):
    placed = (
        P(ROW, SEQ, None),
        P(ROW, SEQ, None),
        P(ROW, SEQ, None),
        P(ROW, None),
        P(ROW, None),
        P(BOTH),
        P(BOTH, None),
        P(BOTH, None),
        P(BOTH, None),
        P(BOTH, None),
        P(BOTH),
        P(BOTH, None),
        P(BOTH, None),
        P(BOTH, None),
        P(BOTH, None),
        P(BOTH),
        P(BOTH, None),
        P(BOTH, None),
        P(BOTH, None),
    )
    small = mesh.shape[ROW] == 4 and mesh.shape[SEQ] == 8
    return jax.shard_map(
        body_planes if small else body_general,
        mesh=mesh,
        in_specs=placed,
        out_specs=(
            P(ROW, SEQ, None),
            P(ROW, SEQ, None),
            P(ROW, SEQ, None),
            P(BOTH),
            P(BOTH, None),
            P(BOTH, None),
            P(BOTH, None),
            P(BOTH, None),
            P(BOTH),
            P(BOTH, None),
            P(BOTH, None),
            P(BOTH, None),
            P(BOTH, None),
            P(BOTH),
            P(BOTH, None),
            P(BOTH, None),
            P(BOTH, None),
        ),
        check_vma=False,
    )
```

```python
import functools

import jax
import jax.numpy as jnp
from jax import lax
from jax.experimental import pallas as pl
from jax.experimental.pallas import tpu as pltpu
from jax.sharding import PartitionSpec as P

HEADS = 12


SCALE = 0.125
EPS = 1e-06
NEG = -1e30
ROW, SEQ = "rows", "seq"
BOTH = (ROW, SEQ)
EQ0 = "rhqk,rkhd->rqhd"
EQ1 = "rhqk,rqhd->rkhd"
EQ2 = "rld,de->rle"
EQ3 = "rld,rle->de"
EQ4 = "rle,de->rld"
EQ5 = "rqhd,rkhd->rhqk"
EQ6 = "rqhd,rqhd->rhq"


def running_sum(lengths):
    ids = jnp.arange(lengths.shape[1], dtype=jnp.int32)
    upto = (ids[None, :] <= ids[:, None]).astype(lengths.dtype)
    return jnp.sum(lengths[:, None, :] * upto[None], axis=2)


def rms_forward(values, gain_vector):
    inverse = lax.rsqrt(jnp.mean(values * values, axis=-1, keepdims=True) + EPS)
    return (values * inverse * gain_vector, inverse)


def rms_backward(values, inverse, gain_vector, upstream):
    normed = values * inverse
    gain_grad = jnp.sum(upstream * normed, axis=(0, 1))
    scaled = upstream * gain_vector
    input_grad = inverse * (scaled - normed * jnp.mean(scaled * normed, axis=-1, keepdims=True))
    return (input_grad, gain_grad)


def matmul(operand, weight):
    return jnp.einsum(EQ2, operand, weight, preferred_element_type=jnp.float32)


def matmul_back(upstream, weight):
    return jnp.einsum(EQ4, upstream, weight, preferred_element_type=jnp.float32)


def weight_grad(operand, upstream):
    return jnp.einsum(EQ3, operand, upstream, preferred_element_type=jnp.float32)


def split_heads(values):
    return values.reshape(values.shape[0], values.shape[1], HEADS, values.shape[2] // HEADS)


def segment_of(places, table_ends):
    return jnp.sum((places[None, :, None] >= table_ends[:, None, :]).astype(jnp.int32), axis=2)


def pair_mask(query_seg, query_pos, key_seg, key_pos, causal):
    same_pair = query_seg[:, :, None] == key_seg[:, None, :]
    if causal:
        same_pair = jnp.logical_and(same_pair, key_pos[None, None, :] <= query_pos[None, :, None])
    return same_pair


def over_blocks(advance_block, fold_state, arrays, block_width):
    piece_rows = arrays[0].shape[1]
    block_count = piece_rows // block_width
    stacked = tuple(
        (
            jnp.moveaxis(
                member.reshape((member.shape[0], block_count, block_width) + member.shape[2:]), 1, 0
            )
            for member in arrays
        )
    )

    def advance(carried, block_items):
        block_index, block_parts = block_items
        return (advance_block(carried, block_parts, block_index * block_width), None)

    fold_state, ignored = lax.scan(
        advance, fold_state, (jnp.arange(block_count, dtype=jnp.int32), stacked)
    )
    return fold_state


def forward_fold(query_heads, query_seg, query_pos, key_segment, causal, block_width):

    def advance_block(fold_state, parts, first_row):
        key_block, value_block = parts
        key_pos = first_row + jnp.arange(key_block.shape[1], dtype=jnp.int32)
        allowed = pair_mask(query_seg, query_pos, key_segment(key_pos), key_pos, causal)

        def compute(current):
            running_max, running_sum, accumulated = current
            scores = (
                jnp.einsum(
                    EQ5,
                    query_heads,
                    split_heads(key_block),
                    preferred_element_type=jnp.float32,
                )
                * SCALE
            )
            scores = jnp.where(allowed[:, None], scores, NEG)
            new_max = jnp.maximum(running_max, jnp.max(scores, axis=-1))
            weights = jnp.where(allowed[:, None], jnp.exp(scores - new_max[..., None]), 0.0)
            factor = jnp.exp(running_max - new_max)
            new_sum = running_sum * factor + jnp.sum(weights, axis=-1)
            update = jnp.einsum(
                EQ0,
                weights.astype(jnp.bfloat16),
                split_heads(value_block),
                preferred_element_type=jnp.float32,
            )
            return (
                new_max,
                new_sum,
                accumulated * jnp.transpose(factor, (0, 2, 1))[..., None] + update,
            )

        return compute(fold_state)

    def forward_fold_piece(fold_state, shard_piece, first_row):
        return over_blocks(advance_block, fold_state, shard_piece, block_width)

    return forward_fold_piece


def finish(fold_state):
    running_max, running_sum, accumulated = fold_state
    attended = accumulated / jnp.transpose(running_sum, (0, 2, 1))[..., None]
    return (attended, running_max + jnp.log(running_sum))


def query_grad_fold(
    query_heads,
    out_heads,
    log_total,
    row_delta,
    query_seg,
    query_pos,
    key_segment,
    causal,
    block_width,
):

    def advance_block(fold_state, parts, first_row):
        key_block, value_block = parts
        key_pos = first_row + jnp.arange(key_block.shape[1], dtype=jnp.int32)
        allowed = pair_mask(query_seg, query_pos, key_segment(key_pos), key_pos, causal)

        def compute(current):
            key_heads = split_heads(key_block)
            scores = (
                jnp.einsum(
                    EQ5, query_heads, key_heads, preferred_element_type=jnp.float32
                )
                * SCALE
            )
            scores = jnp.where(allowed[:, None], scores, NEG)
            probabilities = jnp.where(allowed[:, None], jnp.exp(scores - log_total[..., None]), 0.0)
            prob_grad = jnp.einsum(
                EQ5,
                out_heads,
                split_heads(value_block),
                preferred_element_type=jnp.float32,
            )
            score_grad = (probabilities * (prob_grad - row_delta[..., None])).astype(jnp.bfloat16)
            return current + SCALE * jnp.einsum(
                EQ0, score_grad, key_heads, preferred_element_type=jnp.float32
            )

        return compute(fold_state)

    def query_fold_piece(fold_state, shard_piece, first_row):
        return over_blocks(advance_block, fold_state, shard_piece, block_width)

    return query_fold_piece


def key_grad_fold(
    key_heads,
    value_heads,
    key_seg,
    key_pos,
    total_rows,
    delta_rows,
    query_segment,
    causal,
    block_width,
):

    def advance_block(fold_state, parts, first_row):
        query_block, out_block = parts
        piece_rows = query_block.shape[1]
        query_pos = first_row + jnp.arange(piece_rows, dtype=jnp.int32)
        allowed = pair_mask(query_segment(query_pos), query_pos, key_seg, key_pos, causal)
        total_block = lax.dynamic_slice_in_dim(total_rows, first_row, piece_rows, 2)
        delta_block = lax.dynamic_slice_in_dim(delta_rows, first_row, piece_rows, 2)

        def compute(current):
            key_acc, value_acc = current
            query_heads = split_heads(query_block)
            out_heads = split_heads(out_block)
            scores = (
                jnp.einsum(
                    EQ5, query_heads, key_heads, preferred_element_type=jnp.float32
                )
                * SCALE
            )
            scores = jnp.where(allowed[:, None], scores, NEG)
            probabilities = jnp.where(
                allowed[:, None], jnp.exp(scores - total_block[..., None]), 0.0
            )
            value_acc = value_acc + jnp.einsum(
                EQ1,
                probabilities.astype(jnp.bfloat16),
                out_heads,
                preferred_element_type=jnp.float32,
            )
            prob_grad = jnp.einsum(
                EQ5, out_heads, value_heads, preferred_element_type=jnp.float32
            )
            score_grad = (probabilities * (prob_grad - delta_block[..., None])).astype(jnp.bfloat16)
            key_acc = key_acc + SCALE * jnp.einsum(
                EQ1, score_grad, query_heads, preferred_element_type=jnp.float32
            )
            return (key_acc, value_acc)

        return compute(fold_state)

    def key_fold_piece(fold_state, shard_piece, first_row):
        return over_blocks(advance_block, fold_state, shard_piece, block_width)

    return key_fold_piece


def body_general(
    tokens,
    memory,
    out_grad,
    table_lengths,
    table_plots,
    self_gain,
    self_query,
    self_key,
    self_value,
    self_output,
    cross_gain,
    cross_query,
    cross_key,
    cross_value,
    cross_output,
    mlp_gain,
    mlp_gate,
    mlp_up,
    mlp_down,
):
    def whole(shard):
        return lax.all_gather(shard, BOTH, axis=0, tiled=True)

    all_self_gain = whole(self_gain)
    all_self_query = whole(self_query)
    all_self_key = whole(self_key)
    all_self_value = whole(self_value)
    all_self_output = whole(self_output)
    all_cross_gain = whole(cross_gain)
    all_cross_query = whole(cross_query)
    all_cross_key = whole(cross_key)
    all_cross_value = whole(cross_value)
    all_cross_output = whole(cross_output)
    all_mlp_gain = whole(mlp_gain)
    all_mlp_gate = whole(mlp_gate)
    all_mlp_up = whole(mlp_up)
    all_mlp_down = whole(mlp_down)
    seq_count = lax.axis_size(SEQ)
    seq_index = lax.axis_index(SEQ)
    row_count = tokens.shape[0]
    positions = tokens.shape[1]
    memory_cols = memory.shape[1]
    width = tokens.shape[2]
    head_size = width // HEADS
    query_pos = seq_index * positions + jnp.arange(positions, dtype=jnp.int32)
    memory_pos = seq_index * memory_cols + jnp.arange(memory_cols, dtype=jnp.int32)
    table_ends = running_sum(table_lengths)
    tables = table_lengths.shape[1]
    table_ids = jnp.arange(tables, dtype=jnp.int32)
    plot_width = memory_cols * seq_count // tables

    def token_segment(places):
        return segment_of(places, table_ends)

    def token_plot(places):
        segments = segment_of(places, table_ends)
        return jnp.sum(
            jnp.where(segments[:, :, None] == table_ids[None, None, :], table_plots[:, None, :], 0),
            axis=2,
        )

    def memory_plot(places):
        return (places // plot_width)[None, :]

    def start_state():
        return (
            jnp.full((row_count, HEADS, positions), NEG, jnp.float32),
            jnp.zeros((row_count, HEADS, positions), jnp.float32),
            jnp.zeros((row_count, positions, HEADS, head_size), jnp.float32),
        )

    values = tokens.astype(jnp.float32)
    normed_one, inverse_one = rms_forward(values, all_self_gain.astype(jnp.float32))
    input_one = normed_one.astype(jnp.bfloat16)
    queries = matmul(input_one, all_self_query).astype(jnp.bfloat16)
    key_rows = matmul(input_one, all_self_key).astype(jnp.bfloat16)
    value_rows = matmul(input_one, all_self_value).astype(jnp.bfloat16)
    query_seg = token_segment(query_pos)
    self_fold = forward_fold(
        split_heads(queries), query_seg, query_pos, token_segment, True, positions
    )
    self_out, self_total = finish(
        self_fold(
            start_state(),
            (
                lax.all_gather(key_rows, SEQ, axis=1, tiled=True),
                lax.all_gather(value_rows, SEQ, axis=1, tiled=True),
            ),
            jnp.int32(0),
        )
    )
    self_att = self_out.reshape(row_count, positions, width).astype(jnp.bfloat16)
    first_sum = values + matmul(self_att, all_self_output)
    normed_two, inverse_two = rms_forward(first_sum, all_cross_gain.astype(jnp.float32))
    input_two = normed_two.astype(jnp.bfloat16)
    cross_rows = matmul(input_two, all_cross_query).astype(jnp.bfloat16)
    memory_keys = matmul(memory, all_cross_key).astype(jnp.bfloat16)
    memory_rows = matmul(memory, all_cross_value).astype(jnp.bfloat16)
    query_plot = token_plot(query_pos)
    cross_fold = forward_fold(
        split_heads(cross_rows), query_plot, query_pos, memory_plot, False, memory_cols
    )
    cross_out, cross_total = finish(
        cross_fold(
            start_state(),
            (
                lax.all_gather(memory_keys, SEQ, axis=1, tiled=True),
                lax.all_gather(memory_rows, SEQ, axis=1, tiled=True),
            ),
            jnp.int32(0),
        )
    )
    cross_att = cross_out.reshape(row_count, positions, width).astype(jnp.bfloat16)
    second_sum = first_sum + matmul(cross_att, all_cross_output)
    normed_three, inverse_three = rms_forward(second_sum, all_mlp_gain.astype(jnp.float32))
    input_three = normed_three.astype(jnp.bfloat16)
    gate_pre = matmul(input_three, all_mlp_gate)
    up_pre = matmul(input_three, all_mlp_up)

    def gated_unit(gate_value, up_value):
        return jax.nn.gelu(gate_value, approximate=True) * up_value

    hidden_value, gated_back = jax.vjp(gated_unit, gate_pre, up_pre)
    hidden = hidden_value.astype(jnp.bfloat16)
    layer_out = (second_sum + matmul(hidden, all_mlp_down)).astype(jnp.bfloat16)
    upstream = out_grad.astype(jnp.float32)
    grad_down = weight_grad(hidden, out_grad)
    hidden_grad = matmul_back(out_grad, all_mlp_down)
    gate_grad, up_grad = gated_back(hidden_grad)
    gate_low = gate_grad.astype(jnp.bfloat16)
    up_low = up_grad.astype(jnp.bfloat16)
    grad_gate = weight_grad(input_three, gate_low)
    grad_up = weight_grad(input_three, up_low)
    three_grad = matmul_back(gate_low, all_mlp_gate) + matmul_back(
        up_low, all_mlp_up
    )
    part_three, grad_gain_three = rms_backward(
        second_sum, inverse_three, all_mlp_gain.astype(jnp.float32), three_grad
    )
    second_grad = upstream + part_three
    cross_branch = second_grad.astype(jnp.bfloat16)
    grad_cross_output = weight_grad(cross_att, cross_branch)
    cross_dout = matmul_back(cross_branch, all_cross_output).astype(jnp.bfloat16)
    cross_heads = split_heads(cross_dout)
    cross_delta = jnp.einsum(EQ6, cross_heads.astype(jnp.float32), cross_out)
    cross_total_all, cross_delta_all = (
        lax.all_gather(cross_total, SEQ, axis=2, tiled=True),
        lax.all_gather(cross_delta, SEQ, axis=2, tiled=True),
    )
    cross_query_fold = query_grad_fold(
        split_heads(cross_rows),
        cross_heads,
        cross_total,
        cross_delta,
        query_plot,
        query_pos,
        memory_plot,
        False,
        memory_cols,
    )
    cross_rows_grad = cross_query_fold(
        jnp.zeros((row_count, positions, HEADS, head_size), jnp.float32),
        (
            lax.all_gather(memory_keys, SEQ, axis=1, tiled=True),
            lax.all_gather(memory_rows, SEQ, axis=1, tiled=True),
        ),
        jnp.int32(0),
    )
    cross_rows_low = cross_rows_grad.reshape(row_count, positions, width).astype(jnp.bfloat16)
    memory_fold = key_grad_fold(
        split_heads(memory_keys),
        split_heads(memory_rows),
        memory_plot(memory_pos),
        memory_pos,
        cross_total_all,
        cross_delta_all,
        token_plot,
        False,
        positions,
    )
    memory_zero = jnp.zeros((row_count, memory_cols, HEADS, head_size), jnp.float32)
    memory_key_grad, memory_value_grad = memory_fold(
        (memory_zero, memory_zero),
        (
            lax.all_gather(cross_rows, SEQ, axis=1, tiled=True),
            lax.all_gather(cross_dout, SEQ, axis=1, tiled=True),
        ),
        jnp.int32(0),
    )
    memory_key_low = memory_key_grad.reshape(row_count, memory_cols, width).astype(jnp.bfloat16)
    memory_value_low = memory_value_grad.reshape(row_count, memory_cols, width).astype(jnp.bfloat16)
    grad_cross_query = weight_grad(input_two, cross_rows_low)
    grad_cross_key = weight_grad(memory, memory_key_low)
    grad_cross_value = weight_grad(memory, memory_value_low)
    memory_grad = (
        matmul_back(memory_key_low, all_cross_key)
        + matmul_back(memory_value_low, all_cross_value)
    ).astype(jnp.bfloat16)
    two_grad = matmul_back(cross_rows_low, all_cross_query)
    part_two, grad_gain_two = rms_backward(
        first_sum, inverse_two, all_cross_gain.astype(jnp.float32), two_grad
    )
    first_grad = second_grad + part_two
    self_branch = first_grad.astype(jnp.bfloat16)
    grad_self_output = weight_grad(self_att, self_branch)
    self_dout = matmul_back(self_branch, all_self_output).astype(jnp.bfloat16)
    self_heads = split_heads(self_dout)
    self_delta = jnp.einsum(EQ6, self_heads.astype(jnp.float32), self_out)
    self_total_all, self_delta_all = (
        lax.all_gather(self_total, SEQ, axis=2, tiled=True),
        lax.all_gather(self_delta, SEQ, axis=2, tiled=True),
    )
    self_query_fold = query_grad_fold(
        split_heads(queries),
        self_heads,
        self_total,
        self_delta,
        query_seg,
        query_pos,
        token_segment,
        True,
        positions,
    )
    queries_grad = self_query_fold(
        jnp.zeros((row_count, positions, HEADS, head_size), jnp.float32),
        (
            lax.all_gather(key_rows, SEQ, axis=1, tiled=True),
            lax.all_gather(value_rows, SEQ, axis=1, tiled=True),
        ),
        jnp.int32(0),
    )
    queries_low = queries_grad.reshape(row_count, positions, width).astype(jnp.bfloat16)
    self_key_fold = key_grad_fold(
        split_heads(key_rows),
        split_heads(value_rows),
        query_seg,
        query_pos,
        self_total_all,
        self_delta_all,
        token_segment,
        True,
        positions,
    )
    token_zero = jnp.zeros((row_count, positions, HEADS, head_size), jnp.float32)
    key_grad, value_grad = self_key_fold(
        (token_zero, token_zero),
        (
            lax.all_gather(queries, SEQ, axis=1, tiled=True),
            lax.all_gather(self_dout, SEQ, axis=1, tiled=True),
        ),
        jnp.int32(0),
    )
    key_low = key_grad.reshape(row_count, positions, width).astype(jnp.bfloat16)
    value_low = value_grad.reshape(row_count, positions, width).astype(jnp.bfloat16)
    grad_self_query = weight_grad(input_one, queries_low)
    grad_self_key = weight_grad(input_one, key_low)
    grad_self_value = weight_grad(input_one, value_low)
    one_grad = (
        matmul_back(queries_low, all_self_query)
        + matmul_back(key_low, all_self_key)
        + matmul_back(value_low, all_self_value)
    )
    part_one, grad_gain_one = rms_backward(
        values, inverse_one, all_self_gain.astype(jnp.float32), one_grad
    )
    tokens_grad = (first_grad + part_one).astype(jnp.bfloat16)
    summed = tuple(
        (
            lax.psum_scatter(grad_gain_one, BOTH, scatter_dimension=0, tiled=True),
            lax.psum_scatter(grad_self_query, BOTH, scatter_dimension=0, tiled=True),
            lax.psum_scatter(grad_self_key, BOTH, scatter_dimension=0, tiled=True),
            lax.psum_scatter(grad_self_value, BOTH, scatter_dimension=0, tiled=True),
            lax.psum_scatter(grad_self_output, BOTH, scatter_dimension=0, tiled=True),
            lax.psum_scatter(grad_gain_two, BOTH, scatter_dimension=0, tiled=True),
            lax.psum_scatter(grad_cross_query, BOTH, scatter_dimension=0, tiled=True),
            lax.psum_scatter(grad_cross_key, BOTH, scatter_dimension=0, tiled=True),
            lax.psum_scatter(grad_cross_value, BOTH, scatter_dimension=0, tiled=True),
            lax.psum_scatter(grad_cross_output, BOTH, scatter_dimension=0, tiled=True),
            lax.psum_scatter(grad_gain_three, BOTH, scatter_dimension=0, tiled=True),
            lax.psum_scatter(grad_gate, BOTH, scatter_dimension=0, tiled=True),
            lax.psum_scatter(grad_up, BOTH, scatter_dimension=0, tiled=True),
            lax.psum_scatter(grad_down, BOTH, scatter_dimension=0, tiled=True),
        )
    )
    return (layer_out, tokens_grad, memory_grad) + summed


MESH = pl.DeviceIdType.MESH
BF = jnp.bfloat16
F32 = jnp.float32
QW = 1152
VMEM_LIMIT = 60 * 1024 * 1024


def coords():
    r = lax.axis_index(ROW)
    s = lax.axis_index(SEQ)
    return lax.div(r, 2), lax.rem(r, 2), lax.rem(s, 2), lax.div(s, 2)


def dev(x, c, y, z):
    return {ROW: 2 * x + c, SEQ: 2 * z + y}


def remote(src, dst, send_sem, recv_sem, to):
    return pltpu.make_async_remote_copy(
        src_ref=src,
        dst_ref=dst,
        send_sem=send_sem,
        recv_sem=recv_sem,
        device_id=dev(*to),
        device_id_type=MESH,
    )


def owner_of(x, c, y, z):
    return lax.div(z, 2), lax.rem(z, 2), y, 2 * c + x


def source_of(x, c, y, z):
    return lax.rem(z, 2), lax.div(z, 2), y, 2 * x + c


def is_fixed(x, c, y, z):
    same = jnp.logical_and(lax.div(z, 2) == x, lax.rem(z, 2) == c)
    return jnp.logical_and(same, 2 * c + x == z)


def greet(me, pairs=(), z_line=False, moves=False):
    x, c, y, z = me
    bar = pltpu.get_barrier_semaphore()

    def hello(to):
        pl.semaphore_signal(bar, 1, device_id=dev(*to), device_id_type=MESH)

    count = len(pairs)
    for to in pairs:
        hello(to)
    if z_line:

        @pl.when(z > 0)
        def _():
            hello((x, c, y, z - 1))

        @pl.when(z < 3)
        def _():
            hello((x, c, y, z + 1))

        count = count + jnp.where(z > 0, 1, 0) + jnp.where(z < 3, 1, 0)
    if moves:
        away = jnp.logical_not(is_fixed(*me))

        @pl.when(away)
        def _():
            hello(owner_of(*me))
            hello(source_of(*me))

        count = count + jnp.where(away, 2, 0)
    pl.semaphore_wait(bar, count)


class Move:
    def __init__(self, me, src, dst, sems, back=False):
        self.me = me
        to = source_of(*me) if back else owner_of(*me)
        self.far = remote(src, dst, sems.at[0], sems.at[1], to)
        self.near = pltpu.make_async_copy(src, dst, sems.at[0])
        self.fixed = is_fixed(*me)

    def start(self):
        @pl.when(self.fixed)
        def _():
            self.near.start()

        @pl.when(jnp.logical_not(self.fixed))
        def _():
            self.far.start()

    def arrive(self):
        @pl.when(self.fixed)
        def _():
            self.near.wait()

        @pl.when(jnp.logical_not(self.fixed))
        def _():
            self.far.wait_recv()

    def finish(self):
        @pl.when(jnp.logical_not(self.fixed))
        def _():
            self.far.wait_send()


class Gather4:
    def __init__(self, me, buf, sems):
        x, c, y, z = me
        g = 2 * x + c
        self.g = g
        xp, cp = (1 - x, c, y, z), (x, 1 - c, y, z)
        far = 2 * (1 - x) + c
        self.x_own = remote(buf.at[g], buf.at[g], sems.at[0], sems.at[1], xp)
        self.c_own = remote(buf.at[g], buf.at[g], sems.at[2], sems.at[3], cp)
        self.c_far = remote(buf.at[far], buf.at[far], sems.at[4], sems.at[5], cp)

    def start(self):
        self.x_own.start()
        self.c_own.start()

    def forward(self):
        self.x_own.wait_recv()
        self.c_far.start()

    def arrive(self):
        self.c_own.wait_recv()
        self.c_far.wait_recv()

    def finish(self):
        self.x_own.wait_send()
        self.c_own.wait_send()
        self.c_far.wait_send()


class Gather8:
    def __init__(self, me, buf, sems):
        x, c, y, z = me
        xp, cp, yp = (1 - x, c, y, z), (x, 1 - c, y, z), (x, c, 1 - y, z)
        self.c = c

        def piece(px, pc, py):
            return buf.at[2 * (2 * px + pc) + py]

        def send(p, k, to):
            return remote(p, p, sems.at[2 * k], sems.at[2 * k + 1], to)

        own, at_x = piece(x, c, y), piece(1 - x, c, y)
        at_y, at_d = piece(x, c, 1 - y), piece(1 - x, c, 1 - y)
        self.x_own = send(own, 0, xp)
        self.y_own = send(own, 1, yp)
        self.c_own = send(own, 2, cp)
        self.c_x = send(at_x, 3, cp)
        self.c_y = send(at_y, 4, cp)
        self.c_d = send(at_d, 5, cp)
        self.d_by_y = send(at_x, 6, yp)
        self.d_by_x = send(at_y, 6, xp)

    def start(self):
        self.x_own.start()
        self.y_own.start()
        self.c_own.start()

    def forward(self):
        self.x_own.wait_recv()

        @pl.when(self.c == 0)
        def _():
            self.d_by_y.start()

        self.c_x.start()
        self.y_own.wait_recv()

        @pl.when(self.c == 1)
        def _():
            self.d_by_x.start()

        self.c_y.start()

    def forward_far(self):
        self.d_by_y.wait_recv()
        self.c_d.start()

    def arrive(self):
        for one in (self.c_own, self.c_x, self.c_y, self.c_d):
            one.wait_recv()

    def finish(self):
        for one in (self.x_own, self.y_own, self.c_own, self.c_x, self.c_y, self.c_d, self.d_by_y):
            one.wait_send()


QB = 256


def dot(a, b):
    return lax.dot_general(a, b, (((1,), (0,)), ((), ())), preferred_element_type=F32)


def dot_nt(a, b):
    return lax.dot_general(a, b, (((1,), (1,)), ((), ())), preferred_element_type=F32)


def dot_tn(a, b):
    return lax.dot_general(a, b, (((0,), (0,)), ((), ())), preferred_element_type=F32)


def masked(scores, info, lanes, causal):
    keys = scores.shape[0]
    if causal:
        pos = lax.broadcasted_iota(jnp.int32, scores.shape, 0)
        allowed = jnp.logical_and(pos >= info[1:2, lanes], pos <= info[0:1, lanes])
        return jnp.where(allowed, scores, NEG)
    plot = info[2:3, lanes]
    half = keys // 2
    low = jnp.where(plot == 0, 0.0, NEG)
    high = jnp.where(plot == 1, 0.0, NEG)
    return jnp.concatenate([scores[:half] + low, scores[half:] + high], axis=0)


class GatherPlane:
    def __init__(self, me, buf, sems):
        x, c, y, z = me

        def send(p, k, to):
            piece = buf.at[2 * p + y]
            return remote(piece, piece, sems.at[0, k], sems.at[1, k], to)

        yp = (x, c, 1 - y, z)
        self.along = [send(z, k - 1, (x, c, y, lax.rem(z + k, 4))) for k in (1, 2, 3)]
        self.across = [send(z, 3, yp)]
        self.across += [send(lax.rem(z + 4 - k, 4), 3 + k, yp) for k in (1, 2, 3)]

    def start(self):
        for one in self.along:
            one.start()
        self.across[0].start()

    def forward(self, k):
        self.along[k - 1].wait_recv()
        self.across[k].start()

    def arrive(self):
        for one in self.across:
            one.wait_recv()

    def finish(self):
        for one in self.along + self.across:
            one.wait_send()


class SumPlane:
    def __init__(self, me, parts, by_y, by_z, sems, lanes=None):
        x, c, y, z = me
        self.y, self.z = y, z
        lanes = slice(None) if lanes is None else lanes
        self.mine = [parts.at[2 * lax.rem(z + k, 4) + y, :, lanes] for k in range(4)]
        self.by_y = [by_y.at[lax.rem(z + k, 4), :, lanes] for k in range(4)]
        self.by_z = [by_z.at[k, :, lanes] for k in range(3)]

        def theirs(k):
            return parts.at[2 * lax.rem(z + k, 4) + 1 - y, :, lanes]

        yp = (x, c, 1 - y, z)
        self.across = [
            remote(theirs(k), self.by_y[k], sems.at[0, k], sems.at[1, k], yp) for k in range(4)
        ]
        self.along = [
            remote(
                self.mine[k],
                self.by_z[k - 1],
                sems.at[0, 3 + k],
                sems.at[1, 3 + k],
                (x, c, y, lax.rem(z + k, 4)),
            )
            for k in (1, 2, 3)
        ]

    def start(self):
        for k in (2, 1, 3, 0):
            self.across[k].start()

    def fold(self, steps=(2, 1, 3, 0)):
        for k in steps:
            self.across[k].wait_recv()
            add_into(self.mine[k], self.by_y[k])
            if k:
                self.along[k - 1].start()

    def end(self):
        for k in (1, 2, 3):
            self.along[k - 1].wait_recv()
            add_into(self.mine[0], self.by_z[k - 1])

    def finish(self):
        for one in self.across + self.along:
            one.wait_send()


class Sum8:
    def __init__(self, me, parts, by_c, by_x, by_y, sems):
        x, c, y, z = me
        self.me, self.parts = me, parts
        self.by_c, self.by_x, self.by_y = by_c, by_x, by_y
        xp, cp, yp = (1 - x, c, y, z), (x, 1 - c, y, z), (x, c, 1 - y, z)

        def send(src, dst, k, to):
            return remote(src, dst, sems.at[0, k], sems.at[1, k], to)

        self.order = [(1 - x, 1 - y), (1 - x, y), (x, 1 - y), (x, y)]
        self.first = [
            send(parts.at[2 * (2 * px + 1 - c) + py], by_c.at[px, py], k, cp)
            for k, (px, py) in enumerate(self.order)
        ]
        self.second = [
            send(by_c.at[1 - x, py], by_x.at[py], 4 + k, xp) for k, py in enumerate((1 - y, y))
        ]
        self.third = send(by_x.at[1 - y], by_y, 6, yp)

    def start(self):
        for one in self.first:
            one.start()

    def to_x(self):
        x, c, y, z = self.me
        for k, py in enumerate((1 - y, y)):
            self.first[k].wait_recv()
            add_into(self.by_c.at[1 - x, py], self.parts.at[2 * (2 * (1 - x) + c) + py])
            self.second[k].start()

    def to_y(self):
        x, c, y, z = self.me
        self.first[2].wait_recv()
        self.first[3].wait_recv()
        add_into(self.by_c.at[x, 1 - y], self.parts.at[2 * (2 * x + c) + 1 - y])
        self.second[0].wait_recv()
        add_into(self.by_x.at[1 - y], self.by_c.at[x, 1 - y])
        self.third.start()

    def end(self):
        x, c, y, z = self.me
        self.second[1].wait_recv()
        self.third.wait_recv()
        return (
            self.parts[2 * (2 * x + c) + y].astype(F32)
            + self.by_c[x, y].astype(F32)
            + self.by_x[y].astype(F32)
            + self.by_y[...].astype(F32)
        )

    def finish(self):
        for one in self.first + self.second + [self.third]:
            one.wait_send()


class Sum4:
    def __init__(self, me, parts, by_c, by_x, sems):
        x, c, y, z = me
        self.me, self.parts, self.by_c, self.by_x = me, parts, by_c, by_x
        xp, cp = (1 - x, c, y, z), (x, 1 - c, y, z)
        self.first = [
            remote(parts.at[2 * px + 1 - c], by_c.at[px], sems.at[0, px], sems.at[1, px], cp)
            for px in range(2)
        ]
        self.second = remote(by_c.at[1 - x], by_x, sems.at[0, 2], sems.at[1, 2], xp)

    def start(self):
        for one in self.first:
            one.start()

    def to_x(self):
        x, c, y, z = self.me
        for one in self.first:
            one.wait_recv()
        add_into(self.by_c.at[1 - x], self.parts.at[2 * (1 - x) + c])
        self.second.start()

    def end(self):
        x, c, y, z = self.me
        self.second.wait_recv()
        return (
            self.parts[2 * x + c].astype(F32)
            + self.by_c[x].astype(F32)
            + self.by_x[...].astype(F32)
        )

    def finish(self):
        for one in self.first + [self.second]:
            one.wait_send()


def chunks(rows, step, run):
    def one(i, carry):
        run(pl.ds(pl.multiple_of(i * step, step), step))
        return carry

    lax.fori_loop(0, rows // step, one, 0)


def add_into(into, more, step=16):
    def run(rows):
        total = into[rows, :].astype(F32) + more[rows, :].astype(F32)
        into[rows, :] = total.astype(into.dtype)

    chunks(into.shape[0], step, run)


def dma(*shape):
    return pltpu.SemaphoreType.DMA(shape)


ANYWHERE = pl.BlockSpec(memory_space=pl.ANY)
IN_VMEM = pl.BlockSpec(memory_space=pltpu.VMEM)


def attend_head(h, info, qt, kv, kvt, out, lse, causal):
    keys = kv.shape[0]
    rows = slice(64 * h, 64 * h + 64)
    for b in range(512 // QB):
        lanes = slice(QB * b, QB * b + QB)
        top = keys * (b + 1) * QB // 512 if causal else keys
        scores = dot(kv[:top, rows], qt[rows, lanes])
        scores = masked(scores, info, lanes, causal)
        high = jnp.max(scores, axis=0, keepdims=True)
        weights = jnp.exp(scores - high)
        total = jnp.sum(weights, axis=0, keepdims=True)
        out[rows, lanes] = dot(kvt[192 + 64 * h : 256 + 64 * h, :top], weights.astype(BF)) / total
        lse[h : h + 1, lanes] = high + jnp.log(total)


def attend_back_head(h, info, qt, kv, kvt, outer_t, out, lse, dq, dkv, dk_acc, dv_acc, causal):
    keys = kv.shape[0]
    rows = slice(64 * h, 64 * h + 64)
    value_rows = slice(192 + 64 * h, 256 + 64 * h)
    for b in reversed(range(512 // QB)):
        lanes = slice(QB * b, QB * b + QB)
        top = keys * (b + 1) * QB // 512 if causal else keys
        query, outer = qt[rows, lanes], outer_t[rows, lanes]
        delta = jnp.sum(outer.astype(F32) * out[rows, lanes], axis=0, keepdims=True)
        scores = masked(dot(kv[:top, rows], query), info, lanes, causal)
        prob = jnp.exp(scores - lse[h : h + 1, lanes])
        grad = (prob * (dot(kv[:top, value_rows], outer) - delta)).astype(BF)
        dq[rows, lanes] = (SCALE * dot(kvt[rows, :top], grad)).astype(BF)
        dk_new = dot_nt(query, grad)
        dv_new = dot_nt(outer, prob.astype(BF))
        if b == 512 // QB - 1:
            dk_acc[...] = dk_new
            dv_acc[...] = dv_new
        else:
            dk_acc[:, :top] += dk_new
            dv_acc[:, :top] += dv_new
    dkv[rows, :] = dk_acc[...].astype(BF)
    dkv[value_rows, :] = dv_acc[...].astype(BF)


def norm(values, gain):
    inverse = lax.rsqrt(jnp.mean(values * values, axis=-1, keepdims=True) + EPS)
    return (values * inverse * gain).astype(BF)


def norm_back(values, gain, upstream):
    inverse = lax.rsqrt(jnp.mean(values * values, axis=-1, keepdims=True) + EPS)
    normed = values * inverse
    scaled = upstream * gain
    grad = inverse * (scaled - normed * jnp.mean(scaled * normed, axis=-1, keepdims=True))
    return grad, jnp.sum(upstream * normed, axis=0, keepdims=True)


def gelu_parts(u):
    root = 0.7978845608028654
    square = u * u
    bend = jnp.tanh(root * u * (1.0 + 0.044715 * square))
    half = 0.5 * (1.0 + bend)
    slope = half + 0.5 * u * (1.0 - bend * bend) * (root * (1.0 + 0.134145 * square))
    return u * half, slope


class Names:
    pass


def layer_kernel(names, *refs):
    R = Names()
    for name, ref in zip(names, refs, strict=True):
        setattr(R, name, ref)
    me = coords()
    x, c, y, z = me
    g = 2 * x + c
    s = 2 * z + y
    group = ((1 - x, c, y, z), (1 - x, 1 - c, y, z), (x, 1 - c, y, z))
    line = tuple((x, c, y, lax.rem(z + k, 4)) for k in (1, 2, 3))
    greet(me, group + line + ((x, c, 1 - y, z),), moves=True)

    there = owner_of(*me)
    there_g = 2 * there[0] + there[1]
    move_x = Move(me, R.tok, R.X.at[2 * there_g + y], R.s_move.at[0])
    move_t = Move(me, R.tabs, R.TAB, R.s_move.at[1])
    move_m = Move(me, R.mem, R.M.at[2 * there_g + y], R.s_move.at[2])
    move_d = Move(me, R.dout, R.DO.at[there_g], R.s_move.at[3])
    move_x.start()
    near_dn = pltpu.make_async_copy(R.down, R.DN.at[s], R.s_near.at[0])
    near_dn.start()
    gains = R.gains[...].astype(F32)
    blank = jnp.zeros((24, 64), F32)
    for k in range(4):
        narrow = slice(192 * k, 192 * k + 192)
        top = [w[:, narrow].astype(F32) for w in (R.sk, R.sv, R.sq)] + [gains]
        bottom = [w[:, narrow].astype(F32) for w in (R.ck, R.cv, R.cq)] + [blank]
        R.stage_a[k] = jnp.concatenate(
            [jnp.concatenate(top, axis=1), jnp.concatenate(bottom, axis=1)], axis=0
        ).astype(BF)

    def to_group(stage, land, sems):
        return [
            remote(stage.at[2 * to[0] + to[1]], land.at[g], sems.at[0, i], sems.at[1, i], to)
            for i, to in enumerate(group)
        ]

    parts_a = to_group(R.stage_a, R.land_a, R.s_part_a)
    for one in parts_a:
        one.start()
    for t in range(2):
        length, plot = R.lengths[0, t], R.plots[0, t]
        start = R.lengths[0, 0] if t else 0
        R.tabs[t : t + 1, :] = jnp.full((1, 128), start + length, jnp.int32)
        R.tabs[2 + t : 3 + t, :] = jnp.full((1, 128), plot, jnp.int32)
    R.tabs[4:, :] = jnp.zeros((4, 128), jnp.int32)
    move_t.start()

    def halves_stacked(w):
        w = w[...].astype(F32)
        return jnp.concatenate([w[:, :384], w[:, 384:]], axis=0).astype(BF)

    R.FO[g, s] = halves_stacked(R.so)
    gather_o = GatherPlane(me, R.FO.at[g], R.s_fo)
    gather_o.start()
    R.FC[g, s] = halves_stacked(R.co)
    R.FQ[g, s] = halves_stacked(R.cq)
    gather_c = GatherPlane(me, R.FC.at[g], R.s_fc)
    gather_q = GatherPlane(me, R.FQ.at[g], R.s_fq)
    for k in range(4):
        wide = slice(512 * k, 512 * k + 512)
        R.stage_b[k, :24] = R.gate[:, wide]
        R.stage_b[k, 24:] = R.up[:, wide]
    R.land_a[g] = R.stage_a[g]
    R.land_b[g] = R.stage_b[g]
    gather_x = Gather8(me, R.X, R.s_x)
    gather_m = Gather8(me, R.M, R.s_m)
    gather_d = Gather4(me, R.DO, R.s_d)
    gather_a = GatherPlane(me, R.PA, R.s_a)
    gather_b = GatherPlane(me, R.PB, R.s_b)
    gather_2 = GatherPlane(me, R.P2, R.s_2)
    gather_n = GatherPlane(me, R.DN, R.s_n)
    whole_o = Gather4(me, R.FO, R.s_wo)
    whole_c = Gather4(me, R.FC, R.s_wc)
    whole_q = Gather4(me, R.FQ, R.s_wq)

    for one in parts_a:
        one.wait_recv()
    tops, bottoms = [], []
    for r in range(4):
        piece = R.land_a[r].astype(F32)
        tops.append(piece[:24])
        bottoms.append(piece[24:])
    R.PA[s] = jnp.concatenate(tops, axis=0).astype(BF)
    gather_a.start()
    R.PB[s] = jnp.concatenate(bottoms, axis=0).astype(BF)
    move_x.arrive()
    gather_x.start()
    parts_b = to_group(R.stage_b, R.land_b, R.s_part_b)
    for one in parts_b:
        one.start()
    for k in (1, 3, 2):
        gather_o.forward(k)
    gather_x.forward()
    move_m.start()
    for k in (1, 3, 2):
        gather_a.forward(k)
    gather_x.forward_far()
    gather_o.arrive()
    whole_o.start()
    gather_b.start()
    for one in parts_b:
        one.wait_recv()
    for half in range(2):
        rows = [R.land_b[r].astype(F32)[24 * half : 24 * half + 24] for r in range(4)]
        R.P2[s, :, 512 * half : 512 * half + 512] = jnp.concatenate(rows, axis=0).astype(BF)
    move_t.arrive()
    end_one, end_two = R.TAB[0:1, 0:1], R.TAB[1:2, 0:1]
    plot_one, plot_two = R.TAB[2:3, 0:1], R.TAB[3:4, 0:1]
    lane = lax.broadcasted_iota(jnp.int32, (1, 512), 1)
    for i in range(4):
        lanes = slice(128 * i, 128 * i + 128)
        R.info[0:1, lanes] = lane[:, :128] + (2 * i + y) * 128
    qpos = R.info[0:1, :]
    past_one, past_two = qpos >= end_one, qpos >= end_two
    R.info[1:2, :] = jnp.where(past_two, end_two, jnp.where(past_one, end_one, 0))
    R.info[2:3, :] = jnp.where(past_two, 0, jnp.where(past_one, plot_two, plot_one))

    def unpack(pieces, whole, width, step):
        for zz in range(4):

            def one(i, carry):
                lanes = pl.ds(pl.multiple_of(i * step, step), step)
                low = pieces[2 * zz, :, lanes].astype(F32)
                high = pieces[2 * zz + 1, :, lanes].astype(F32)
                for r in range(4):
                    rows = slice(24 * r, 24 * r + 24)
                    both = jnp.concatenate([low[rows], high[rows]], axis=0)
                    whole[192 * r + 48 * zz : 192 * r + 48 * zz + 48, lanes] = both.astype(BF)
                return carry

            lax.fori_loop(0, width // step, one, 0)

    gather_a.arrive()
    unpack(R.PA, R.WA, 640, 128)
    gain_rows = R.WA[:, 512:640].astype(F32).T
    gain_one, gain_two, gain_three = (gain_rows[64 + i : 65 + i] for i in range(3))

    def pair_rows(buf, i):
        return jnp.concatenate([buf[2 * i], buf[2 * i + 1]], axis=0)

    def mine_rows(buf):
        return jnp.concatenate([buf[2 * i + y] for i in range(4)], axis=0)

    def keys_values(i, operand, weight, natural, turned):
        rows = pl.ds(pl.multiple_of(i * 256, 256), 256)
        product = dot(operand, weight[:, :384])
        natural[rows, :] = product.astype(BF)
        turned[:, rows] = product.T.astype(BF)

    def first_norm(i, carry):
        x1 = norm(pair_rows(R.X, i).astype(F32), gain_one)
        R.X1[2 * i] = x1[:128]
        R.X1[2 * i + 1] = x1[128:]
        keys_values(i, x1, R.WA, R.KV, R.KVT)
        return carry

    gather_x.arrive()
    lax.fori_loop(0, 4, first_norm, 0)
    product = SCALE * dot(mine_rows(R.X1), R.WA[:, 384:640])
    R.QT[...] = product.T[:192].astype(BF)

    def share_heads(buf, sems):
        return [Gather4(me, buf.at[:, h], sems.at[h]) for h in range(3)]

    share_1 = share_heads(R.A4, R.s_share1)
    move_m.arrive()
    gather_m.start()
    move_d.start()
    for h in range(3):
        attend_head(h, R.info, R.QT, R.KV, R.KVT, R.OUT1, R.LSE1, True)
        R.A4[g, h] = R.OUT1[64 * h : 64 * h + 64, :].astype(BF)
        share_1[h].start()
        if h == 0:
            whole_o.forward()
            gather_b.forward(1)
            gather_b.forward(3)
        if h == 1:
            share_1[0].forward()
            gather_b.forward(2)
            gather_m.forward()
    gather_m.forward_far()
    gather_c.start()
    gather_2.start()
    near_dn.wait()
    share_1[1].forward()
    whole_o.arrive()

    def unpack_full(pieces, whole):
        def one(r, carry):
            for zz in range(4):
                low, high = pieces[r, 2 * zz].astype(F32), pieces[r, 2 * zz + 1].astype(F32)
                rows = pl.ds(pl.multiple_of(192 * r + 48 * zz, 16), 48)
                whole[rows, :384] = jnp.concatenate([low[:24], high[:24]], axis=0).astype(BF)
                whole[rows, 384:] = jnp.concatenate([low[24:], high[24:]], axis=0).astype(BF)
            return carry

        lax.fori_loop(0, 4, one, 0)

    unpack_full(R.FO, R.WO)
    share_1[2].forward()
    gather_b.arrive()
    unpack(R.PB, R.WB, 640, 128)
    for one in share_1:
        one.arrive()

    def project(pieces, weight, i):
        lanes = slice(256 * i, 256 * i + 256)
        turned = pieces[:, :, :, lanes].astype(F32).reshape(768, 256)
        return dot(turned.T.astype(BF), weight[...])

    for i in range(2):
        rows = slice(256 * i, 256 * i + 256)
        before = jnp.concatenate([R.X[4 * i + y], R.X[4 * i + 2 + y]], axis=0).astype(F32)
        first = before + project(R.A4, R.WO, i)
        R.FIRST[rows, :] = first
        x2 = norm(first, gain_two)
        R.X2[rows, :] = x2
        product = SCALE * dot(x2, R.WB[:, 384:640])
        R.CQT[:, rows] = product.T[:192].astype(BF)
    gather_m.arrive()

    def memory_pair(i, carry):
        keys_values(i, pair_rows(R.M, i), R.WB, R.MKV, R.MKVT)
        return carry

    lax.fori_loop(0, 4, memory_pair, 0)
    for k in (1, 3, 2):
        gather_c.forward(k)
    gather_n.start()
    gather_q.start()
    gather_c.arrive()
    whole_c.start()
    move_d.arrive()
    share_2 = share_heads(R.C4, R.s_share2)
    for h in range(3):
        attend_head(h, R.info, R.CQT, R.MKV, R.MKVT, R.OUT2, R.LSE2, False)
        R.C4[g, h] = R.OUT2[64 * h : 64 * h + 64, :].astype(BF)
        if h == 0:
            whole_c.forward()
        share_2[h].start()
        if h:
            share_2[h - 1].forward()
    gather_d.start()
    for k in (1, 3, 2):
        gather_2.forward(k)
    share_2[2].forward()
    whole_c.arrive()
    unpack_full(R.FC, R.WC)
    for one in share_2:
        one.arrive()
    for i in range(2):
        rows = slice(256 * i, 256 * i + 256)
        second = R.FIRST[rows, :] + project(R.C4, R.WC, i)
        R.SECOND[rows, :] = second
        R.X3[rows, :] = norm(second, gain_three)
    gather_d.forward()
    for k in (1, 3, 2):
        gather_n.forward(k)
    for k in (1, 3, 2):
        gather_q.forward(k)
    gather_2.arrive()
    unpack(R.P2, R.W2, 1024, 256)
    for one in parts_a + parts_b:
        one.wait_send()
    gather_2.finish()
    gather_a.finish()
    gather_b.finish()
    gather_d.arrive()
    gather_n.arrive()

    sum_dx = Sum4(me, R.DXP, R.by_c_dx, R.by_x_dx, R.s_dx)
    sum_out = Sum4(me, R.OP, R.by_c_out, R.by_x_out, R.s_out)

    def feed(core):
        at = [pl.ds(pl.multiple_of((2 * px + core) * 128, 128), 128) for px in range(2)]
        x3 = jnp.concatenate([R.X3[rows, :] for rows in at], axis=0)
        gate, up = dot(x3, R.W2[:, :512]), dot(x3, R.W2[:, 512:])
        active, slope = gelu_parts(gate)
        hidden = (active * up).astype(BF)
        outer = jnp.concatenate([R.DO[2 * px + core] for px in range(2)], axis=0)
        w_down = R.DN[...].reshape(512, 768)
        hidden_grad = dot_nt(outer, w_down)
        gate_grad = (hidden_grad * up * slope).astype(BF)
        up_grad = (hidden_grad * active).astype(BF)
        dx3 = (dot_nt(gate_grad, R.W2[:, :512]) + dot_nt(up_grad, R.W2[:, 512:])).astype(BF)
        out = dot(hidden, w_down).astype(BF)
        for px in range(2):
            half = slice(128 * px, 128 * px + 128)
            R.H[at[px], :] = hidden[half]
            R.GG[at[px], :512] = gate_grad[half]
            R.GG[at[px], 512:] = up_grad[half]
            R.DXP[2 * px + core] = dx3[half]
            R.OP[2 * px + core] = out[half]

    def pack(whole, pieces, start, width):
        for t in range(8):
            rows = [whole[(8 * r + t) * 24 : (8 * r + t) * 24 + 24, :] for r in range(4)]
            pieces[t, :, start : start + width] = jnp.concatenate(rows, axis=0).astype(BF)

    feed(1 - c)
    sum_dx.start()
    feed(c)
    sum_dx.to_x()
    sum_out.start()
    own = pl.ds(pl.multiple_of(g * 128, 128), 128)
    own_block = 2 * g + y
    x3_t = R.X3[...].astype(F32).T.astype(BF)
    total_2 = [
        SumPlane(me, R.P2, R.by_y_2, R.by_z_2, R.s_g2.at[i], slice(512 * i, 512 * i + 512))
        for i in range(2)
    ]
    for i in range(2):
        R.W2G[...] = dot(x3_t, R.GG[:, 512 * i : 512 * i + 512])
        pack(R.W2G, R.P2, 512 * i, 512)
        total_2[i].start()
    hidden_t = R.H[...].astype(F32).T.astype(BF)
    d_down = dot(hidden_t, R.DO[...].reshape(512, 768)).astype(BF)
    for t in range(8):
        R.DNG[t] = d_down[64 * t : 64 * t + 64]
    total_n = SumPlane(me, R.DNG, R.by_y_n, R.by_z_n, R.s_gn)
    total_n.start()
    part, gain_grad_three = norm_back(R.SECOND[own, :], gain_three, sum_dx.end())
    second_grad = R.DO[g].astype(F32) + part
    R.SGRAD[...] = second_grad
    R.DS4[g] = second_grad.astype(BF)
    share_s = Gather4(me, R.DS4, R.s_s)
    share_s.start()
    sum_out.to_x()
    gather_q.arrive()
    whole_q.start()
    share_s.forward()
    share_s.arrive()

    dsec = R.DS4[...].reshape(512, 768)
    mine_192 = pl.ds(pl.multiple_of(g * 192, 16), 192)
    R.OUTER[...] = dot_nt(R.WC[mine_192, :], dsec).astype(BF)
    share_3 = share_heads(R.DC4, R.s_share3)
    for h in range(3):
        attend_back_head(
            h, R.info, R.CQT, R.MKV, R.MKVT, R.OUTER, R.OUT2, R.LSE2, R.DCQT, R.MDKV, R.dk, R.dv, False
        )
        if h == 0:
            whole_q.forward()
        R.DC4[g, h] = R.DCQT[64 * h : 64 * h + 64, :]
        share_3[h].start()
        if h:
            share_3[h - 1].forward()

    def pack_24(whole, pieces):
        for t in range(8):
            rows = whole[24 * t : 24 * t + 24]
            pieces[t] = jnp.concatenate([rows[:, :384], rows[:, 384:]], axis=0).astype(BF)

    whole_q.arrive()
    unpack_full(R.FQ, R.WQ)
    pack_24(dot(R.C4[g].reshape(192, 512), dsec), R.CO8)
    total_c = SumPlane(me, R.CO8, R.by_y_c, R.by_z_c, R.s_gc)
    total_c.start()
    share_3[2].forward()
    for one in share_3:
        one.arrive()

    for i in range(2):
        rows = slice(256 * i, 256 * i + 256)
        dx2 = dot(R.WQ[...], R.DC4[:, :, :, rows].reshape(768, 256)).T
        part, ignored = norm_back(R.FIRST[rows, :], gain_two, dx2)
        R.DFIRST[rows, :] = (dsec[rows].astype(F32) + part).astype(BF)
    dx2 = dot(R.WQ[...], R.DC4[:, :, :, own].reshape(768, 128)).T
    part, gain_grad_two = norm_back(R.FIRST[own, :], gain_two, dx2)
    R.SGRAD[...] += part

    R.OUTER[...] = dot_nt(R.WO[mine_192, :], R.DFIRST[...]).astype(BF)
    for h in range(3):
        attend_back_head(
            h, R.info, R.QT, R.KV, R.KVT, R.OUTER, R.OUT1, R.LSE1, R.DQT, R.DKV, R.dk, R.dv, True
        )

    def token_grad_pair(i, carry):
        lanes = pl.ds(pl.multiple_of(i * 256, 256), 256)
        half = pl.ds(pl.multiple_of(i * 128, 128), 128)
        turned = dot(R.WA[:, :384], R.DKV[:, lanes])
        query = dot(R.WA[:, 384:576], R.DQT[:, half])
        R.TG[2 * i] = (turned[:, :128] + jnp.where(y == 0, query, 0.0)).astype(BF)
        R.TG[2 * i + 1] = (turned[:, 128:] + jnp.where(y == 1, query, 0.0)).astype(BF)
        return carry

    lax.fori_loop(0, 4, token_grad_pair, 0)
    sum_t = Sum8(me, R.TG, R.by_c_t, R.by_x_t, R.by_y_t, R.s_gt)
    sum_t.start()
    R.W1G[...] = dot(R.DKV[...], R.X1[...].reshape(1024, 768)).T
    pack(R.W1G, R.PA, 0, 384)
    total_a = SumPlane(me, R.PA, R.by_y_a, R.by_z_a, R.s_ga, slice(0, 384))
    sum_t.to_x()
    total_a.start()

    def memory_grad_pair(i, carry):
        lanes = pl.ds(pl.multiple_of(i * 256, 256), 256)
        turned = dot(R.WB[:, :384], R.MDKV[:, lanes]).astype(BF)
        R.MG[2 * i] = turned[:, :128]
        R.MG[2 * i + 1] = turned[:, 128:]
        return carry

    lax.fori_loop(0, 4, memory_grad_pair, 0)
    sum_m = Sum8(me, R.MG, R.by_c_m, R.by_x_m, R.by_y_m, R.s_gm)
    sum_m.start()
    R.W1G[...] = dot(R.MDKV[...], R.M[...].reshape(1024, 768)).T
    pack(R.W1G, R.PB, 0, 384)
    R.TURN[:192, :] = dot(R.DCQT[...], R.X2[...])
    R.TURN[192:, :] = jnp.zeros((64, 768), F32)
    pack(R.TURN[...].T, R.PB, 384, 256)
    total_b = SumPlane(me, R.PB, R.by_y_b, R.by_z_b, R.s_gb)
    R.TURN[:192, :] = dot(R.DQT[...], mine_rows(R.X1))
    pack_24(dot(R.A4[g].reshape(192, 512), R.DFIRST[...]), R.SO8)
    total_s = SumPlane(me, R.SO8, R.by_y_s, R.by_z_s, R.s_gs)
    for one in total_2:
        one.fold()
    total_n.fold()
    total_c.fold()
    sum_t.to_y()
    sum_m.to_x()
    total_b.start()
    total_s.start()
    total_a.fold()
    dx1 = sum_t.end().T
    part, gain_grad_one = norm_back(R.X[own_block].astype(F32), gain_one, dx1)
    R.TURN[192:193, :] = gain_grad_one
    R.TURN[193:194, :] = gain_grad_two
    R.TURN[194:195, :] = gain_grad_three
    pack(R.TURN[...].T, R.PA, 384, 256)
    total_g = SumPlane(me, R.PA, R.by_y_a, R.by_z_a, R.s_gg, slice(384, 640))
    total_g.start()
    R.TBLOCK[...] = (R.SGRAD[...] + part).astype(BF)
    R.LBLOCK[...] = (R.SECOND[own, :] + sum_out.end()).astype(BF)
    back = [
        Move(me, src, dst, R.s_back.at[i], back=True)
        for i, (src, dst) in enumerate(
            ((R.TBLOCK, R.tokens_out), (R.LBLOCK, R.layer_out), (R.MBLOCK, R.memory_out))
        )
    ]
    back[0].start()
    back[1].start()
    sum_m.to_y()
    total_b.fold()
    total_s.fold()
    total_g.fold()
    for one in total_2:
        one.end()
    rows_2 = R.P2[s].astype(F32)
    for r in range(4):
        rows = slice(24 * r, 24 * r + 24)
        R.stage_b[r] = jnp.concatenate([rows_2[rows, :512], rows_2[rows, 512:]], axis=0).astype(BF)
    last_b = to_group(R.stage_b, R.quarters_b, R.s_last_b)
    for one in last_b:
        one.start()
    R.MBLOCK[...] = sum_m.end().T.astype(BF)
    back[2].start()
    total_n.end()
    total_c.end()
    total_a.end()
    total_b.end()
    total_g.end()
    rows_a, rows_b = R.PA[s].astype(F32), R.PB[s].astype(F32)
    for r in range(4):
        rows = slice(24 * r, 24 * r + 24)
        R.stage_a[r] = jnp.concatenate([rows_a[rows], rows_b[rows]], axis=0).astype(BF)
    last_a = to_group(R.stage_a, R.quarters_a, R.s_last_a)
    for one in last_a:
        one.start()
    total_s.end()
    near = [
        pltpu.make_async_copy(src, dst, R.s_near.at[1 + i])
        for i, (src, dst) in enumerate(
            (
                (R.stage_a.at[g], R.quarters_a.at[g]),
                (R.stage_b.at[g], R.quarters_b.at[g]),
                (R.CO8.at[s], R.co_out),
                (R.SO8.at[s], R.so_out),
                (R.DNG.at[s], R.down_out),
            )
        )
    ]
    for one in near:
        one.start()
    for one in near:
        one.wait()
    for one in last_a + last_b:
        one.wait_recv()
    for one in back:
        one.arrive()
        one.finish()
    for one in last_a + last_b:
        one.wait_send()
    for one in (move_x, move_t, move_m, move_d):
        one.finish()
    for one in (gather_x, gather_m, gather_d, gather_o, gather_c, gather_q, gather_n):
        one.finish()
    for one in (whole_o, whole_c, whole_q, share_s, sum_dx, sum_out, sum_m, sum_t):
        one.finish()
    for one in share_1 + share_2 + share_3 + total_2:
        one.finish()
    for one in (total_a, total_g, total_b, total_n, total_c, total_s):
        one.finish()


def run_layer(inputs):
    n, d = 128, 768

    def low(*shape):
        return pltpu.VMEM(shape, BF)

    def full(*shape):
        return pltpu.VMEM(shape, F32)

    outs = dict(
        quarters_a=(4, 48, 640),
        quarters_b=(4, 48, 512),
        co_out=(48, 384),
        so_out=(48, 384),
        down_out=(64, d),
        tokens_out=(n, d),
        layer_out=(n, d),
        memory_out=(n, d),
    )
    scratch = dict(
        stage_a=low(4, 48, 640), land_a=low(4, 48, 640), stage_b=low(4, 48, 512), land_b=low(4, 48, 512),
        tabs=pltpu.VMEM((8, 128), jnp.int32), TAB=pltpu.VMEM((8, 128), jnp.int32),
        X=low(8, n, d), M=low(8, n, d), DO=low(4, n, d),
        PA=low(8, 96, 640), PB=low(8, 96, 640), P2=low(8, 96, 1024), DN=low(8, 64, d),
        FO=low(4, 8, 48, 384), FC=low(4, 8, 48, 384), FQ=low(4, 8, 48, 384),
        WA=low(768, 640), WB=low(768, 640), W2=low(768, 1024), WO=low(d, d), WC=low(d, d), WQ=low(d, d),
        info=pltpu.VMEM((8, 512), jnp.int32),
        X1=low(8, n, d), X2=low(512, d), X3=low(512, d),
        KV=low(1024, 384), KVT=low(384, 1024), MKV=low(1024, 384), MKVT=low(384, 1024),
        QT=low(192, 512), CQT=low(192, 512), OUT1=full(192, 512), OUT2=full(192, 512),
        LSE1=full(8, 512), LSE2=full(8, 512),
        A4=low(4, 3, 64, 512), C4=low(4, 3, 64, 512), DC4=low(4, 3, 64, 512),
        FIRST=full(512, d), SECOND=full(512, d),
        H=low(512, 512), GG=low(512, 1024), DXP=low(4, n, d), OP=low(4, n, d),
        by_c_dx=low(2, n, d), by_x_dx=low(n, d), by_c_out=low(2, n, d), by_x_out=low(n, d),
        W2G=full(768, 512), by_y_2=low(4, 96, 1024), by_z_2=low(3, 96, 1024),
        DNG=low(8, 64, d), by_y_n=low(4, 64, d), by_z_n=low(3, 64, d),
        SGRAD=full(n, d), DS4=low(4, n, d), OUTER=low(192, 512),
        DCQT=low(192, 512), DQT=low(192, 512), MDKV=low(384, 1024), DKV=low(384, 1024),
        dk=full(64, 1024), dv=full(64, 1024),
        CO8=low(8, 48, 384), by_y_c=low(4, 48, 384), by_z_c=low(3, 48, 384),
        SO8=low(8, 48, 384), by_y_s=low(4, 48, 384), by_z_s=low(3, 48, 384),
        MG=low(8, d, n), by_c_m=low(2, 2, d, n), by_x_m=low(2, d, n), by_y_m=low(d, n),
        TG=low(8, d, n), by_c_t=low(2, 2, d, n), by_x_t=low(2, d, n), by_y_t=low(d, n),
        DFIRST=low(512, d), W1G=full(768, 384), TURN=full(256, 768),
        by_y_a=low(4, 96, 640), by_z_a=low(3, 96, 640), by_y_b=low(4, 96, 640), by_z_b=low(3, 96, 640),
        TBLOCK=low(n, d), LBLOCK=low(n, d), MBLOCK=low(n, d),
        s_move=dma(4, 2), s_near=dma(6), s_part_a=dma(2, 3), s_part_b=dma(2, 3),
        s_last_a=dma(2, 3), s_last_b=dma(2, 3), s_back=dma(3, 2),
        s_x=dma(14), s_m=dma(14), s_d=dma(6), s_wo=dma(6), s_wc=dma(6), s_wq=dma(6), s_s=dma(6),
        s_a=dma(2, 7), s_b=dma(2, 7), s_2=dma(2, 7), s_n=dma(2, 7), s_fo=dma(2, 7), s_fc=dma(2, 7), s_fq=dma(2, 7),
        s_share1=dma(3, 6), s_share2=dma(3, 6), s_share3=dma(3, 6),
        s_dx=dma(2, 3), s_out=dma(2, 3), s_gm=dma(2, 7), s_gt=dma(2, 7),
        s_ga=dma(2, 7), s_gb=dma(2, 7), s_gg=dma(2, 7), s_g2=dma(2, 2, 7), s_gn=dma(2, 7), s_gc=dma(2, 7), s_gs=dma(2, 7),
    )
    names = tuple(inputs) + tuple(outs) + tuple(scratch)
    return pl.pallas_call(
        functools.partial(layer_kernel, names),
        out_shape=tuple(jax.ShapeDtypeStruct(shape, BF) for shape in outs.values()),
        in_specs=[spec for _, spec in inputs.values()],
        out_specs=tuple([ANYWHERE] * len(outs)),
        scratch_shapes=list(scratch.values()),
        compiler_params=pltpu.CompilerParams(
            collective_id=1, has_side_effects=True, vmem_limit_bytes=VMEM_LIMIT
        ),
        name="layer",
    )(*[a for a, _ in inputs.values()])


def outputs_kernel(
    qa, qb, co, so, down, tokens, layer, memory,
    layer_out, tokens_out, memory_out, gains_out,
    sq, sk, sv, so_out, cq, ck, cv, co_out, gate, up, down_out,
):
    layer_out[...] = layer[...]
    tokens_out[...] = tokens[...]
    memory_out[...] = memory[...]
    down_out[...] = down[...].astype(F32)
    gains = jnp.zeros((24, 128), F32)
    for k in range(4):
        piece = qa[k].astype(F32)
        gains = gains + piece[:24, 512:]
        narrow = slice(192 * k, 192 * k + 192)
        for row, outs in ((0, (sk, sv, sq)), (24, (ck, cv, cq))):
            for i, out in enumerate(outs):
                out[:, narrow] = piece[row : row + 24, 192 * i : 192 * i + 192]
        piece = qb[k].astype(F32)
        gate[:, 512 * k : 512 * k + 512] = piece[:24]
        up[:, 512 * k : 512 * k + 512] = piece[24:]
    gains_out[...] = gains
    for piece, out in ((so, so_out), (co, co_out)):
        rows = piece[...].astype(F32)
        out[:, :384] = rows[:24]
        out[:, 384:] = rows[24:]


def body_planes(
    tokens, memory, out_grad, table_lengths, table_plots,
    self_gain, self_query, self_key, self_value, self_output,
    cross_gain, cross_query, cross_key, cross_value, cross_output,
    mlp_gain, mlp_gate, mlp_up, mlp_down,
):
    gains = jnp.stack([self_gain, cross_gain, mlp_gain], axis=1)
    gains = jnp.pad(gains, ((0, 0), (0, 61)))
    in_smem = pl.BlockSpec(memory_space=pltpu.SMEM)
    results = run_layer(
        dict(
            tok=(tokens[0], ANYWHERE), mem=(memory[0], ANYWHERE), dout=(out_grad[0], ANYWHERE),
            lengths=(table_lengths, in_smem), plots=(table_plots, in_smem), gains=(gains, IN_VMEM),
            sq=(self_query, IN_VMEM), sk=(self_key, IN_VMEM), sv=(self_value, IN_VMEM), so=(self_output, IN_VMEM),
            cq=(cross_query, IN_VMEM), ck=(cross_key, IN_VMEM), cv=(cross_value, IN_VMEM), co=(cross_output, IN_VMEM),
            gate=(mlp_gate, IN_VMEM), up=(mlp_up, IN_VMEM), down=(mlp_down, ANYWHERE),
        )
    )
    block = jax.ShapeDtypeStruct((128, 768), BF)
    rows = jax.ShapeDtypeStruct((24, 768), F32)
    wide = jax.ShapeDtypeStruct((24, 2048), F32)
    outs = pl.pallas_call(
        outputs_kernel,
        out_shape=(block,) * 3
        + (jax.ShapeDtypeStruct((24, 128), F32),)
        + (rows,) * 8
        + (wide, wide, jax.ShapeDtypeStruct((64, 768), F32)),
        name="outputs",
    )(*results)
    layer, tokens_mine, memory_mine, gain_sums, sq, sk, sv, so, cq, ck, cv, co, gate, up, down = outs
    return (
        layer[None], tokens_mine[None], memory_mine[None],
        gain_sums[:, 64], sq, sk, sv, so,
        gain_sums[:, 65], cq, ck, cv, co,
        gain_sums[:, 66], gate, up, down,
    )


def solution(mesh):
    placed = (
        P(ROW, SEQ, None),
        P(ROW, SEQ, None),
        P(ROW, SEQ, None),
        P(ROW, None),
        P(ROW, None),
        P(BOTH),
        P(BOTH, None),
        P(BOTH, None),
        P(BOTH, None),
        P(BOTH, None),
        P(BOTH),
        P(BOTH, None),
        P(BOTH, None),
        P(BOTH, None),
        P(BOTH, None),
        P(BOTH),
        P(BOTH, None),
        P(BOTH, None),
        P(BOTH, None),
    )
    small = mesh.shape[ROW] == 4 and mesh.shape[SEQ] == 8
    return jax.shard_map(
        body_planes if small else body_general,
        mesh=mesh,
        in_specs=placed,
        out_specs=(
            P(ROW, SEQ, None),
            P(ROW, SEQ, None),
            P(ROW, SEQ, None),
            P(BOTH),
            P(BOTH, None),
            P(BOTH, None),
            P(BOTH, None),
            P(BOTH, None),
            P(BOTH),
            P(BOTH, None),
            P(BOTH, None),
            P(BOTH, None),
            P(BOTH, None),
            P(BOTH),
            P(BOTH, None),
            P(BOTH, None),
            P(BOTH, None),
        ),
        check_vma=False,
    )
```

```python
import functools

import jax
import jax.numpy as jnp
from jax import lax
from jax.experimental import pallas as pl
from jax.experimental.pallas import tpu as pltpu
from jax.sharding import PartitionSpec as P

HEADS = 12


SCALE = 0.125
EPS = 1e-06
NEG = -1e30
ROW, SEQ = "rows", "seq"
BOTH = (ROW, SEQ)
EQ0 = "rhqk,rkhd->rqhd"
EQ1 = "rhqk,rqhd->rkhd"
EQ2 = "rld,de->rle"
EQ3 = "rld,rle->de"
EQ4 = "rle,de->rld"
EQ5 = "rqhd,rkhd->rhqk"
EQ6 = "rqhd,rqhd->rhq"


def running_sum(lengths):
    ids = jnp.arange(lengths.shape[1], dtype=jnp.int32)
    upto = (ids[None, :] <= ids[:, None]).astype(lengths.dtype)
    return jnp.sum(lengths[:, None, :] * upto[None], axis=2)


def rms_forward(values, gain_vector):
    inverse = lax.rsqrt(jnp.mean(values * values, axis=-1, keepdims=True) + EPS)
    return (values * inverse * gain_vector, inverse)


def rms_backward(values, inverse, gain_vector, upstream):
    normed = values * inverse
    gain_grad = jnp.sum(upstream * normed, axis=(0, 1))
    scaled = upstream * gain_vector
    input_grad = inverse * (scaled - normed * jnp.mean(scaled * normed, axis=-1, keepdims=True))
    return (input_grad, gain_grad)


def matmul(operand, weight):
    return jnp.einsum(EQ2, operand, weight, preferred_element_type=jnp.float32)


def matmul_back(upstream, weight):
    return jnp.einsum(EQ4, upstream, weight, preferred_element_type=jnp.float32)


def weight_grad(operand, upstream):
    return jnp.einsum(EQ3, operand, upstream, preferred_element_type=jnp.float32)


def split_heads(values):
    return values.reshape(values.shape[0], values.shape[1], HEADS, values.shape[2] // HEADS)


def segment_of(places, table_ends):
    return jnp.sum((places[None, :, None] >= table_ends[:, None, :]).astype(jnp.int32), axis=2)


def pair_mask(query_seg, query_pos, key_seg, key_pos, causal):
    same_pair = query_seg[:, :, None] == key_seg[:, None, :]
    if causal:
        same_pair = jnp.logical_and(same_pair, key_pos[None, None, :] <= query_pos[None, :, None])
    return same_pair


def over_blocks(advance_block, fold_state, arrays, block_width):
    piece_rows = arrays[0].shape[1]
    block_count = piece_rows // block_width
    stacked = tuple(
        (
            jnp.moveaxis(
                member.reshape((member.shape[0], block_count, block_width) + member.shape[2:]), 1, 0
            )
            for member in arrays
        )
    )

    def advance(carried, block_items):
        block_index, block_parts = block_items
        return (advance_block(carried, block_parts, block_index * block_width), None)

    fold_state, ignored = lax.scan(
        advance, fold_state, (jnp.arange(block_count, dtype=jnp.int32), stacked)
    )
    return fold_state


def forward_fold(query_heads, query_seg, query_pos, key_segment, causal, block_width):

    def advance_block(fold_state, parts, first_row):
        key_block, value_block = parts
        key_pos = first_row + jnp.arange(key_block.shape[1], dtype=jnp.int32)
        allowed = pair_mask(query_seg, query_pos, key_segment(key_pos), key_pos, causal)

        def compute(current):
            running_max, running_sum, accumulated = current
            scores = (
                jnp.einsum(
                    EQ5,
                    query_heads,
                    split_heads(key_block),
                    preferred_element_type=jnp.float32,
                )
                * SCALE
            )
            scores = jnp.where(allowed[:, None], scores, NEG)
            new_max = jnp.maximum(running_max, jnp.max(scores, axis=-1))
            weights = jnp.where(allowed[:, None], jnp.exp(scores - new_max[..., None]), 0.0)
            factor = jnp.exp(running_max - new_max)
            new_sum = running_sum * factor + jnp.sum(weights, axis=-1)
            update = jnp.einsum(
                EQ0,
                weights.astype(jnp.bfloat16),
                split_heads(value_block),
                preferred_element_type=jnp.float32,
            )
            return (
                new_max,
                new_sum,
                accumulated * jnp.transpose(factor, (0, 2, 1))[..., None] + update,
            )

        return compute(fold_state)

    def forward_fold_piece(fold_state, shard_piece, first_row):
        return over_blocks(advance_block, fold_state, shard_piece, block_width)

    return forward_fold_piece


def finish(fold_state):
    running_max, running_sum, accumulated = fold_state
    attended = accumulated / jnp.transpose(running_sum, (0, 2, 1))[..., None]
    return (attended, running_max + jnp.log(running_sum))


def query_grad_fold(
    query_heads,
    out_heads,
    log_total,
    row_delta,
    query_seg,
    query_pos,
    key_segment,
    causal,
    block_width,
):

    def advance_block(fold_state, parts, first_row):
        key_block, value_block = parts
        key_pos = first_row + jnp.arange(key_block.shape[1], dtype=jnp.int32)
        allowed = pair_mask(query_seg, query_pos, key_segment(key_pos), key_pos, causal)

        def compute(current):
            key_heads = split_heads(key_block)
            scores = (
                jnp.einsum(
                    EQ5, query_heads, key_heads, preferred_element_type=jnp.float32
                )
                * SCALE
            )
            scores = jnp.where(allowed[:, None], scores, NEG)
            probabilities = jnp.where(allowed[:, None], jnp.exp(scores - log_total[..., None]), 0.0)
            prob_grad = jnp.einsum(
                EQ5,
                out_heads,
                split_heads(value_block),
                preferred_element_type=jnp.float32,
            )
            score_grad = (probabilities * (prob_grad - row_delta[..., None])).astype(jnp.bfloat16)
            return current + SCALE * jnp.einsum(
                EQ0, score_grad, key_heads, preferred_element_type=jnp.float32
            )

        return compute(fold_state)

    def query_fold_piece(fold_state, shard_piece, first_row):
        return over_blocks(advance_block, fold_state, shard_piece, block_width)

    return query_fold_piece


def key_grad_fold(
    key_heads,
    value_heads,
    key_seg,
    key_pos,
    total_rows,
    delta_rows,
    query_segment,
    causal,
    block_width,
):

    def advance_block(fold_state, parts, first_row):
        query_block, out_block = parts
        piece_rows = query_block.shape[1]
        query_pos = first_row + jnp.arange(piece_rows, dtype=jnp.int32)
        allowed = pair_mask(query_segment(query_pos), query_pos, key_seg, key_pos, causal)
        total_block = lax.dynamic_slice_in_dim(total_rows, first_row, piece_rows, 2)
        delta_block = lax.dynamic_slice_in_dim(delta_rows, first_row, piece_rows, 2)

        def compute(current):
            key_acc, value_acc = current
            query_heads = split_heads(query_block)
            out_heads = split_heads(out_block)
            scores = (
                jnp.einsum(
                    EQ5, query_heads, key_heads, preferred_element_type=jnp.float32
                )
                * SCALE
            )
            scores = jnp.where(allowed[:, None], scores, NEG)
            probabilities = jnp.where(
                allowed[:, None], jnp.exp(scores - total_block[..., None]), 0.0
            )
            value_acc = value_acc + jnp.einsum(
                EQ1,
                probabilities.astype(jnp.bfloat16),
                out_heads,
                preferred_element_type=jnp.float32,
            )
            prob_grad = jnp.einsum(
                EQ5, out_heads, value_heads, preferred_element_type=jnp.float32
            )
            score_grad = (probabilities * (prob_grad - delta_block[..., None])).astype(jnp.bfloat16)
            key_acc = key_acc + SCALE * jnp.einsum(
                EQ1, score_grad, query_heads, preferred_element_type=jnp.float32
            )
            return (key_acc, value_acc)

        return compute(fold_state)

    def key_fold_piece(fold_state, shard_piece, first_row):
        return over_blocks(advance_block, fold_state, shard_piece, block_width)

    return key_fold_piece


def body_general(
    tokens,
    memory,
    out_grad,
    table_lengths,
    table_plots,
    self_gain,
    self_query,
    self_key,
    self_value,
    self_output,
    cross_gain,
    cross_query,
    cross_key,
    cross_value,
    cross_output,
    mlp_gain,
    mlp_gate,
    mlp_up,
    mlp_down,
):
    def whole(shard):
        return lax.all_gather(shard, BOTH, axis=0, tiled=True)

    all_self_gain = whole(self_gain)
    all_self_query = whole(self_query)
    all_self_key = whole(self_key)
    all_self_value = whole(self_value)
    all_self_output = whole(self_output)
    all_cross_gain = whole(cross_gain)
    all_cross_query = whole(cross_query)
    all_cross_key = whole(cross_key)
    all_cross_value = whole(cross_value)
    all_cross_output = whole(cross_output)
    all_mlp_gain = whole(mlp_gain)
    all_mlp_gate = whole(mlp_gate)
    all_mlp_up = whole(mlp_up)
    all_mlp_down = whole(mlp_down)
    seq_count = lax.axis_size(SEQ)
    seq_index = lax.axis_index(SEQ)
    row_count = tokens.shape[0]
    positions = tokens.shape[1]
    memory_cols = memory.shape[1]
    width = tokens.shape[2]
    head_size = width // HEADS
    query_pos = seq_index * positions + jnp.arange(positions, dtype=jnp.int32)
    memory_pos = seq_index * memory_cols + jnp.arange(memory_cols, dtype=jnp.int32)
    table_ends = running_sum(table_lengths)
    tables = table_lengths.shape[1]
    table_ids = jnp.arange(tables, dtype=jnp.int32)
    plot_width = memory_cols * seq_count // tables

    def token_segment(places):
        return segment_of(places, table_ends)

    def token_plot(places):
        segments = segment_of(places, table_ends)
        return jnp.sum(
            jnp.where(segments[:, :, None] == table_ids[None, None, :], table_plots[:, None, :], 0),
            axis=2,
        )

    def memory_plot(places):
        return (places // plot_width)[None, :]

    def start_state():
        return (
            jnp.full((row_count, HEADS, positions), NEG, jnp.float32),
            jnp.zeros((row_count, HEADS, positions), jnp.float32),
            jnp.zeros((row_count, positions, HEADS, head_size), jnp.float32),
        )

    values = tokens.astype(jnp.float32)
    normed_one, inverse_one = rms_forward(values, all_self_gain.astype(jnp.float32))
    input_one = normed_one.astype(jnp.bfloat16)
    queries = matmul(input_one, all_self_query).astype(jnp.bfloat16)
    key_rows = matmul(input_one, all_self_key).astype(jnp.bfloat16)
    value_rows = matmul(input_one, all_self_value).astype(jnp.bfloat16)
    query_seg = token_segment(query_pos)
    self_fold = forward_fold(
        split_heads(queries), query_seg, query_pos, token_segment, True, positions
    )
    self_out, self_total = finish(
        self_fold(
            start_state(),
            (
                lax.all_gather(key_rows, SEQ, axis=1, tiled=True),
                lax.all_gather(value_rows, SEQ, axis=1, tiled=True),
            ),
            jnp.int32(0),
        )
    )
    self_att = self_out.reshape(row_count, positions, width).astype(jnp.bfloat16)
    first_sum = values + matmul(self_att, all_self_output)
    normed_two, inverse_two = rms_forward(first_sum, all_cross_gain.astype(jnp.float32))
    input_two = normed_two.astype(jnp.bfloat16)
    cross_rows = matmul(input_two, all_cross_query).astype(jnp.bfloat16)
    memory_keys = matmul(memory, all_cross_key).astype(jnp.bfloat16)
    memory_rows = matmul(memory, all_cross_value).astype(jnp.bfloat16)
    query_plot = token_plot(query_pos)
    cross_fold = forward_fold(
        split_heads(cross_rows), query_plot, query_pos, memory_plot, False, memory_cols
    )
    cross_out, cross_total = finish(
        cross_fold(
            start_state(),
            (
                lax.all_gather(memory_keys, SEQ, axis=1, tiled=True),
                lax.all_gather(memory_rows, SEQ, axis=1, tiled=True),
            ),
            jnp.int32(0),
        )
    )
    cross_att = cross_out.reshape(row_count, positions, width).astype(jnp.bfloat16)
    second_sum = first_sum + matmul(cross_att, all_cross_output)
    normed_three, inverse_three = rms_forward(second_sum, all_mlp_gain.astype(jnp.float32))
    input_three = normed_three.astype(jnp.bfloat16)
    gate_pre = matmul(input_three, all_mlp_gate)
    up_pre = matmul(input_three, all_mlp_up)

    def gated_unit(gate_value, up_value):
        return jax.nn.gelu(gate_value, approximate=True) * up_value

    hidden_value, gated_back = jax.vjp(gated_unit, gate_pre, up_pre)
    hidden = hidden_value.astype(jnp.bfloat16)
    layer_out = (second_sum + matmul(hidden, all_mlp_down)).astype(jnp.bfloat16)
    upstream = out_grad.astype(jnp.float32)
    grad_down = weight_grad(hidden, out_grad)
    hidden_grad = matmul_back(out_grad, all_mlp_down)
    gate_grad, up_grad = gated_back(hidden_grad)
    gate_low = gate_grad.astype(jnp.bfloat16)
    up_low = up_grad.astype(jnp.bfloat16)
    grad_gate = weight_grad(input_three, gate_low)
    grad_up = weight_grad(input_three, up_low)
    three_grad = matmul_back(gate_low, all_mlp_gate) + matmul_back(
        up_low, all_mlp_up
    )
    part_three, grad_gain_three = rms_backward(
        second_sum, inverse_three, all_mlp_gain.astype(jnp.float32), three_grad
    )
    second_grad = upstream + part_three
    cross_branch = second_grad.astype(jnp.bfloat16)
    grad_cross_output = weight_grad(cross_att, cross_branch)
    cross_dout = matmul_back(cross_branch, all_cross_output).astype(jnp.bfloat16)
    cross_heads = split_heads(cross_dout)
    cross_delta = jnp.einsum(EQ6, cross_heads.astype(jnp.float32), cross_out)
    cross_total_all, cross_delta_all = (
        lax.all_gather(cross_total, SEQ, axis=2, tiled=True),
        lax.all_gather(cross_delta, SEQ, axis=2, tiled=True),
    )
    cross_query_fold = query_grad_fold(
        split_heads(cross_rows),
        cross_heads,
        cross_total,
        cross_delta,
        query_plot,
        query_pos,
        memory_plot,
        False,
        memory_cols,
    )
    cross_rows_grad = cross_query_fold(
        jnp.zeros((row_count, positions, HEADS, head_size), jnp.float32),
        (
            lax.all_gather(memory_keys, SEQ, axis=1, tiled=True),
            lax.all_gather(memory_rows, SEQ, axis=1, tiled=True),
        ),
        jnp.int32(0),
    )
    cross_rows_low = cross_rows_grad.reshape(row_count, positions, width).astype(jnp.bfloat16)
    memory_fold = key_grad_fold(
        split_heads(memory_keys),
        split_heads(memory_rows),
        memory_plot(memory_pos),
        memory_pos,
        cross_total_all,
        cross_delta_all,
        token_plot,
        False,
        positions,
    )
    memory_zero = jnp.zeros((row_count, memory_cols, HEADS, head_size), jnp.float32)
    memory_key_grad, memory_value_grad = memory_fold(
        (memory_zero, memory_zero),
        (
            lax.all_gather(cross_rows, SEQ, axis=1, tiled=True),
            lax.all_gather(cross_dout, SEQ, axis=1, tiled=True),
        ),
        jnp.int32(0),
    )
    memory_key_low = memory_key_grad.reshape(row_count, memory_cols, width).astype(jnp.bfloat16)
    memory_value_low = memory_value_grad.reshape(row_count, memory_cols, width).astype(jnp.bfloat16)
    grad_cross_query = weight_grad(input_two, cross_rows_low)
    grad_cross_key = weight_grad(memory, memory_key_low)
    grad_cross_value = weight_grad(memory, memory_value_low)
    memory_grad = (
        matmul_back(memory_key_low, all_cross_key)
        + matmul_back(memory_value_low, all_cross_value)
    ).astype(jnp.bfloat16)
    two_grad = matmul_back(cross_rows_low, all_cross_query)
    part_two, grad_gain_two = rms_backward(
        first_sum, inverse_two, all_cross_gain.astype(jnp.float32), two_grad
    )
    first_grad = second_grad + part_two
    self_branch = first_grad.astype(jnp.bfloat16)
    grad_self_output = weight_grad(self_att, self_branch)
    self_dout = matmul_back(self_branch, all_self_output).astype(jnp.bfloat16)
    self_heads = split_heads(self_dout)
    self_delta = jnp.einsum(EQ6, self_heads.astype(jnp.float32), self_out)
    self_total_all, self_delta_all = (
        lax.all_gather(self_total, SEQ, axis=2, tiled=True),
        lax.all_gather(self_delta, SEQ, axis=2, tiled=True),
    )
    self_query_fold = query_grad_fold(
        split_heads(queries),
        self_heads,
        self_total,
        self_delta,
        query_seg,
        query_pos,
        token_segment,
        True,
        positions,
    )
    queries_grad = self_query_fold(
        jnp.zeros((row_count, positions, HEADS, head_size), jnp.float32),
        (
            lax.all_gather(key_rows, SEQ, axis=1, tiled=True),
            lax.all_gather(value_rows, SEQ, axis=1, tiled=True),
        ),
        jnp.int32(0),
    )
    queries_low = queries_grad.reshape(row_count, positions, width).astype(jnp.bfloat16)
    self_key_fold = key_grad_fold(
        split_heads(key_rows),
        split_heads(value_rows),
        query_seg,
        query_pos,
        self_total_all,
        self_delta_all,
        token_segment,
        True,
        positions,
    )
    token_zero = jnp.zeros((row_count, positions, HEADS, head_size), jnp.float32)
    key_grad, value_grad = self_key_fold(
        (token_zero, token_zero),
        (
            lax.all_gather(queries, SEQ, axis=1, tiled=True),
            lax.all_gather(self_dout, SEQ, axis=1, tiled=True),
        ),
        jnp.int32(0),
    )
    key_low = key_grad.reshape(row_count, positions, width).astype(jnp.bfloat16)
    value_low = value_grad.reshape(row_count, positions, width).astype(jnp.bfloat16)
    grad_self_query = weight_grad(input_one, queries_low)
    grad_self_key = weight_grad(input_one, key_low)
    grad_self_value = weight_grad(input_one, value_low)
    one_grad = (
        matmul_back(queries_low, all_self_query)
        + matmul_back(key_low, all_self_key)
        + matmul_back(value_low, all_self_value)
    )
    part_one, grad_gain_one = rms_backward(
        values, inverse_one, all_self_gain.astype(jnp.float32), one_grad
    )
    tokens_grad = (first_grad + part_one).astype(jnp.bfloat16)
    summed = tuple(
        (
            lax.psum_scatter(grad_gain_one, BOTH, scatter_dimension=0, tiled=True),
            lax.psum_scatter(grad_self_query, BOTH, scatter_dimension=0, tiled=True),
            lax.psum_scatter(grad_self_key, BOTH, scatter_dimension=0, tiled=True),
            lax.psum_scatter(grad_self_value, BOTH, scatter_dimension=0, tiled=True),
            lax.psum_scatter(grad_self_output, BOTH, scatter_dimension=0, tiled=True),
            lax.psum_scatter(grad_gain_two, BOTH, scatter_dimension=0, tiled=True),
            lax.psum_scatter(grad_cross_query, BOTH, scatter_dimension=0, tiled=True),
            lax.psum_scatter(grad_cross_key, BOTH, scatter_dimension=0, tiled=True),
            lax.psum_scatter(grad_cross_value, BOTH, scatter_dimension=0, tiled=True),
            lax.psum_scatter(grad_cross_output, BOTH, scatter_dimension=0, tiled=True),
            lax.psum_scatter(grad_gain_three, BOTH, scatter_dimension=0, tiled=True),
            lax.psum_scatter(grad_gate, BOTH, scatter_dimension=0, tiled=True),
            lax.psum_scatter(grad_up, BOTH, scatter_dimension=0, tiled=True),
            lax.psum_scatter(grad_down, BOTH, scatter_dimension=0, tiled=True),
        )
    )
    return (layer_out, tokens_grad, memory_grad) + summed


MESH = pl.DeviceIdType.MESH
BF = jnp.bfloat16
F32 = jnp.float32
QW = 1152
VMEM_LIMIT = 60 * 1024 * 1024


def coords():
    r = lax.axis_index(ROW)
    s = lax.axis_index(SEQ)
    return lax.div(r, 2), lax.rem(r, 2), lax.rem(s, 2), lax.div(s, 2)


def dev(x, c, y, z):
    return {ROW: 2 * x + c, SEQ: 2 * z + y}


def remote(src, dst, send_sem, recv_sem, to):
    return pltpu.make_async_remote_copy(
        src_ref=src,
        dst_ref=dst,
        send_sem=send_sem,
        recv_sem=recv_sem,
        device_id=dev(*to),
        device_id_type=MESH,
    )


def owner_of(x, c, y, z):
    return lax.div(z, 2), lax.rem(z, 2), y, 2 * c + x


def source_of(x, c, y, z):
    return lax.rem(z, 2), lax.div(z, 2), y, 2 * x + c


def is_fixed(x, c, y, z):
    same = jnp.logical_and(lax.div(z, 2) == x, lax.rem(z, 2) == c)
    return jnp.logical_and(same, 2 * c + x == z)


def greet(me, pairs=(), z_line=False, moves=False):
    x, c, y, z = me
    bar = pltpu.get_barrier_semaphore()

    def hello(to):
        pl.semaphore_signal(bar, 1, device_id=dev(*to), device_id_type=MESH)

    count = len(pairs)
    for to in pairs:
        hello(to)
    if z_line:

        @pl.when(z > 0)
        def _():
            hello((x, c, y, z - 1))

        @pl.when(z < 3)
        def _():
            hello((x, c, y, z + 1))

        count = count + jnp.where(z > 0, 1, 0) + jnp.where(z < 3, 1, 0)
    if moves:
        away = jnp.logical_not(is_fixed(*me))

        @pl.when(away)
        def _():
            hello(owner_of(*me))
            hello(source_of(*me))

        count = count + jnp.where(away, 2, 0)
    pl.semaphore_wait(bar, count)


class Move:
    def __init__(self, me, src, dst, sems, back=False):
        self.me = me
        to = source_of(*me) if back else owner_of(*me)
        self.far = remote(src, dst, sems.at[0], sems.at[1], to)
        self.near = pltpu.make_async_copy(src, dst, sems.at[0])
        self.fixed = is_fixed(*me)

    def start(self):
        @pl.when(self.fixed)
        def _():
            self.near.start()

        @pl.when(jnp.logical_not(self.fixed))
        def _():
            self.far.start()

    def arrive(self):
        @pl.when(self.fixed)
        def _():
            self.near.wait()

        @pl.when(jnp.logical_not(self.fixed))
        def _():
            self.far.wait_recv()

    def finish(self):
        @pl.when(jnp.logical_not(self.fixed))
        def _():
            self.far.wait_send()


class Gather4:
    def __init__(self, me, buf, sems):
        x, c, y, z = me
        g = 2 * x + c
        self.g = g
        xp, cp = (1 - x, c, y, z), (x, 1 - c, y, z)
        far = 2 * (1 - x) + c
        self.x_own = remote(buf.at[g], buf.at[g], sems.at[0], sems.at[1], xp)
        self.c_own = remote(buf.at[g], buf.at[g], sems.at[2], sems.at[3], cp)
        self.c_far = remote(buf.at[far], buf.at[far], sems.at[4], sems.at[5], cp)

    def start(self):
        self.x_own.start()
        self.c_own.start()

    def forward(self):
        self.x_own.wait_recv()
        self.c_far.start()

    def arrive(self):
        self.c_own.wait_recv()
        self.c_far.wait_recv()

    def finish(self):
        self.x_own.wait_send()
        self.c_own.wait_send()
        self.c_far.wait_send()


class Gather8:
    def __init__(self, me, buf, sems, split=False):
        x, c, y, z = me
        xp, cp, yp = (1 - x, c, y, z), (x, 1 - c, y, z), (x, c, 1 - y, z)
        def piece(px, pc, py):
            return buf.at[2 * (2 * px + pc) + py]

        def send(p, k, to):
            return remote(p, p, sems.at[2 * k], sems.at[2 * k + 1], to)

        own, at_x = piece(x, c, y), piece(1 - x, c, y)
        at_y, at_d = piece(x, c, 1 - y), piece(1 - x, c, 1 - y)
        self.x_own = send(own, 0, xp)
        self.y_own = send(own, 1, yp)
        self.c_own = send(own, 2, cp)
        self.c_x = send(at_x, 3, cp)
        self.c_y = send(at_y, 4, cp)
        self.c_d = send(at_d, 5, cp)
        self.d_by_x = send(at_y, 6, xp)
        self.d_by_y = send(at_x, 6, yp)
        self.by_y = jnp.logical_and(c == 0, split)

    def start(self):
        self.start_x()
        self.start_y()

    def start_x(self):
        self.x_own.start()
        self.c_own.start()

    def start_y(self):
        self.y_own.start()

    def forward(self):
        self.y_own.wait_recv()

        @pl.when(jnp.logical_not(self.by_y))
        def _():
            self.d_by_x.start()

        self.c_y.start()
        self.x_own.wait_recv()

        @pl.when(self.by_y)
        def _():
            self.d_by_y.start()

        self.c_x.start()

    def forward_far(self):
        self.d_by_x.wait_recv()
        self.c_d.start()

    def arrive(self):
        for one in (self.c_own, self.c_x, self.c_y, self.c_d):
            one.wait_recv()

    def finish(self):
        for one in (self.x_own, self.y_own, self.c_own, self.c_x, self.c_y, self.c_d, self.d_by_x):
            one.wait_send()


QB = 256


def dot(a, b):
    return lax.dot_general(a, b, (((1,), (0,)), ((), ())), preferred_element_type=F32)


def dot_nt(a, b):
    return lax.dot_general(a, b, (((1,), (1,)), ((), ())), preferred_element_type=F32)


def dot_tn(a, b):
    return lax.dot_general(a, b, (((0,), (0,)), ((), ())), preferred_element_type=F32)


def masked(scores, info, lanes, causal):
    keys = scores.shape[0]
    if causal:
        pos = lax.broadcasted_iota(jnp.int32, scores.shape, 0)
        allowed = jnp.logical_and(pos >= info[1:2, lanes], pos <= info[0:1, lanes])
        return jnp.where(allowed, scores, NEG)
    plot = info[2:3, lanes]
    half = keys // 2
    low = jnp.where(plot == 0, 0.0, NEG)
    high = jnp.where(plot == 1, 0.0, NEG)
    return jnp.concatenate([scores[:half] + low, scores[half:] + high], axis=0)


class GatherPlane:
    def __init__(self, me, buf, sems, lanes=None):
        x, c, y, z = me

        def send(p, k, to):
            piece = buf.at[2 * p + y] if lanes is None else buf.at[2 * p + y, :, lanes]
            return remote(piece, piece, sems.at[0, k], sems.at[1, k], to)

        yp = (x, c, 1 - y, z)
        self.along = [send(z, k - 1, (x, c, y, lax.rem(z + k, 4))) for k in (1, 2, 3)]
        self.across = [send(z, 3, yp)]
        self.across += [send(lax.rem(z + 4 - k, 4), 3 + k, yp) for k in (1, 2, 3)]

    def start_along(self):
        for one in self.along:
            one.start()

    def start_across(self):
        self.across[0].start()

    def forward(self, k):
        self.along[k - 1].wait_recv()
        self.across[k].start()

    def arrive(self):
        for one in self.across:
            one.wait_recv()

    def finish(self):
        for one in self.along + self.across:
            one.wait_send()


class GatherRelay:
    def __init__(self, me, buf, sems, lanes=None):
        self.me, self.buf, self.sems, self.lanes = me, buf, sems, lanes

    def piece(self, p, y):
        return self.buf.at[2 * p + y] if self.lanes is None else self.buf.at[2 * p + y, :, self.lanes]

    def send(self, p, k, to):
        piece = self.piece(p, self.me[2])
        return remote(piece, piece, self.sems.at[0, k + p], self.sems.at[1, k + p], to)

    def up(self, p):
        x, c, y, z = self.me
        return self.send(p, 0, (x, c, y, z + 1))

    def down(self, p):
        x, c, y, z = self.me
        return self.send(p, 4, (x, c, y, z - 1))

    def across(self, p):
        x, c, y, z = self.me
        return self.send(p, 8, (x, c, 1 - y, z))

    def start_along(self):
        z = self.me[3]

        @pl.when(z < 3)
        def _():
            self.up(z).start()

        @pl.when(z > 0)
        def _():
            self.down(z).start()

    def start_across(self):
        self.across(self.me[3]).start()

    def forward(self, k):
        z = self.me[3]

        @pl.when(z - k >= 0)
        def _():
            p = z - k
            self.up(p).wait_recv()
            if k < 3:

                @pl.when(z < 3)
                def _():
                    self.up(p).start()

            self.across(p).start()

        @pl.when(z + k <= 3)
        def _():
            p = z + k
            self.down(p).wait_recv()
            if k < 3:

                @pl.when(z > 0)
                def _():
                    self.down(p).start()

            self.across(p).start()

    def arrive(self):
        for p in range(4):
            self.across(p).wait_recv()

    def finish(self):
        z = self.me[3]
        for p in range(4):
            self.across(p).wait_send()

            @pl.when(jnp.logical_and(z < 3, p <= z))
            def _():
                self.up(p).wait_send()

            @pl.when(jnp.logical_and(z > 0, p >= z))
            def _():
                self.down(p).wait_send()


class SumPlane:
    def __init__(self, me, parts, by_y, by_z, sems, lanes=None):
        self.me, self.parts, self.by_y, self.by_z, self.sems = me, parts, by_y, by_z, sems
        self.lanes = slice(None) if lanes is None else lanes

    def mine(self, p):
        return self.parts.at[2 * p + self.me[2], :, self.lanes]

    def from_y(self, p):
        return self.by_y.at[p, :, self.lanes]

    def slot(self, k):
        return self.by_z.at[k, :, self.lanes]

    def across(self, p):
        x, c, y, z = self.me
        theirs = self.parts.at[2 * p + 1 - y, :, self.lanes]
        return remote(theirs, self.from_y(p), self.sems.at[0, p], self.sems.at[1, p], (x, c, 1 - y, z))

    def up_slot(self, p):
        return self.slot(p - 1)

    def down_slot(self, q):
        return self.slot(lax.rem(3 + q, 5))

    def up(self, p):
        x, c, y, z = self.me
        k = 3 + p
        return remote(self.mine(p), self.up_slot(p), self.sems.at[0, k], self.sems.at[1, k], (x, c, y, z + 1))

    def down(self, q):
        x, c, y, z = self.me
        k = 7 + q
        return remote(self.mine(q), self.down_slot(q), self.sems.at[0, k], self.sems.at[1, k], (x, c, y, z - 1))

    def start(self):
        for p in (3, 0, 2, 1):
            self.across(p).start()

    def fold(self, steps=(3, 0, 2, 1)):
        z = self.me[3]
        for p in steps:
            self.across(p).wait_recv()
            add_into(self.mine(p), self.from_y(p))
            if p > 0:

                @pl.when(z == 0)
                def _():
                    self.up(p).start()

            if p < 3:

                @pl.when(z == 3)
                def _():
                    self.down(p).start()

    def relay_up(self, p):
        self.up(p).wait_recv()
        add_into(self.mine(p), self.up_slot(p))
        self.up(p).start()

    def relay_down(self, q):
        self.down(q).wait_recv()
        add_into(self.mine(q), self.down_slot(q))
        self.down(q).start()

    def pass_one(self):
        z = self.me[3]

        @pl.when(z == 1)
        def _():
            self.relay_up(3)
            self.relay_up(2)

        @pl.when(z == 2)
        def _():
            self.relay_down(0)
            self.relay_down(1)

    def pass_two(self):
        z = self.me[3]

        @pl.when(z == 2)
        def _():
            self.relay_up(3)

        @pl.when(z == 1)
        def _():
            self.relay_down(0)

    def end(self):
        z = self.me[3]

        @pl.when(z > 0)
        def _():
            self.up(z).wait_recv()
            add_into(self.mine(z), self.up_slot(z))

        @pl.when(z < 3)
        def _():
            self.down(z).wait_recv()
            add_into(self.mine(z), self.down_slot(z))

    def finish(self):
        z = self.me[3]
        for p in range(4):
            self.across(p).wait_send()

            @pl.when(z < p)
            def _():
                self.up(p).wait_send()

            @pl.when(z > p)
            def _():
                self.down(p).wait_send()


class Sum8:
    def __init__(self, me, parts, by_c, by_x, by_y, sems):
        x, c, y, z = me
        self.me, self.parts = me, parts
        self.by_c, self.by_x, self.by_y = by_c, by_x, by_y
        xp, cp, yp = (1 - x, c, y, z), (x, 1 - c, y, z), (x, c, 1 - y, z)

        def send(src, dst, k, to):
            return remote(src, dst, sems.at[0, k], sems.at[1, k], to)

        self.order = [(1 - x, 1 - y), (1 - x, y), (x, 1 - y), (x, y)]
        self.first = [
            send(parts.at[2 * (2 * px + 1 - c) + py], by_c.at[px, py], k, cp)
            for k, (px, py) in enumerate(self.order)
        ]
        self.second = [
            send(by_c.at[1 - x, py], by_x.at[py], 4 + k, xp) for k, py in enumerate((1 - y, y))
        ]
        self.third = send(by_x.at[1 - y], by_y, 6, yp)

    def start(self):
        for one in self.first:
            one.start()

    def to_x(self):
        x, c, y, z = self.me
        for k, py in enumerate((1 - y, y)):
            self.first[k].wait_recv()
            add_into(self.by_c.at[1 - x, py], self.parts.at[2 * (2 * (1 - x) + c) + py])
            self.second[k].start()

    def to_y(self):
        x, c, y, z = self.me
        self.first[2].wait_recv()
        self.first[3].wait_recv()
        add_into(self.by_c.at[x, 1 - y], self.parts.at[2 * (2 * x + c) + 1 - y])
        self.second[0].wait_recv()
        add_into(self.by_x.at[1 - y], self.by_c.at[x, 1 - y])
        self.third.start()

    def end(self):
        x, c, y, z = self.me
        self.second[1].wait_recv()
        self.third.wait_recv()
        return (
            self.parts[2 * (2 * x + c) + y].astype(F32)
            + self.by_c[x, y].astype(F32)
            + self.by_x[y].astype(F32)
            + self.by_y[...].astype(F32)
        )

    def finish(self):
        for one in self.first + self.second + [self.third]:
            one.wait_send()


class Sum4:
    def __init__(self, me, parts, by_c, by_x, sems):
        x, c, y, z = me
        self.me, self.parts, self.by_c, self.by_x = me, parts, by_c, by_x
        xp, cp = (1 - x, c, y, z), (x, 1 - c, y, z)
        self.first = [
            remote(parts.at[2 * px + 1 - c], by_c.at[px], sems.at[0, px], sems.at[1, px], cp)
            for px in range(2)
        ]
        self.second = remote(by_c.at[1 - x], by_x, sems.at[0, 2], sems.at[1, 2], xp)

    def start(self):
        for one in self.first:
            one.start()

    def to_x(self):
        x, c, y, z = self.me
        for one in self.first:
            one.wait_recv()
        add_into(self.by_c.at[1 - x], self.parts.at[2 * (1 - x) + c])
        self.second.start()

    def end(self):
        x, c, y, z = self.me
        self.second.wait_recv()
        return (
            self.parts[2 * x + c].astype(F32)
            + self.by_c[x].astype(F32)
            + self.by_x[...].astype(F32)
        )

    def finish(self):
        for one in self.first + [self.second]:
            one.wait_send()


def chunks(rows, step, run):
    def one(i, carry):
        run(pl.ds(pl.multiple_of(i * step, step), step))
        return carry

    lax.fori_loop(0, rows // step, one, 0)


def add_into(into, more, step=16):
    def run(rows):
        total = into[rows, :].astype(F32) + more[rows, :].astype(F32)
        into[rows, :] = total.astype(into.dtype)

    chunks(into.shape[0], step, run)


def dma(*shape):
    return pltpu.SemaphoreType.DMA(shape)


ANYWHERE = pl.BlockSpec(memory_space=pl.ANY)
IN_VMEM = pl.BlockSpec(memory_space=pltpu.VMEM)


def attend_head(h, info, qt, kv, kvt, out, lse, causal):
    keys = kv.shape[0]
    rows = slice(64 * h, 64 * h + 64)
    for b in range(512 // QB):
        lanes = slice(QB * b, QB * b + QB)
        top = keys * (b + 1) * QB // 512 if causal else keys
        scores = dot(kv[:top, rows], qt[rows, lanes])
        scores = masked(scores, info, lanes, causal)
        high = jnp.max(scores, axis=0, keepdims=True)
        weights = jnp.exp(scores - high)
        total = jnp.sum(weights, axis=0, keepdims=True)
        out[rows, lanes] = dot(kvt[192 + 64 * h : 256 + 64 * h, :top], weights.astype(BF)) / total
        lse[h : h + 1, lanes] = high + jnp.log(total)


def attend_back_head(h, info, qt, kv, kvt, outer_t, out, lse, dq, dkv, dk_acc, dv_acc, causal):
    keys = kv.shape[0]
    rows = slice(64 * h, 64 * h + 64)
    value_rows = slice(192 + 64 * h, 256 + 64 * h)
    for b in reversed(range(512 // QB)):
        lanes = slice(QB * b, QB * b + QB)
        top = keys * (b + 1) * QB // 512 if causal else keys
        query, outer = qt[rows, lanes], outer_t[rows, lanes]
        delta = jnp.sum(outer.astype(F32) * out[rows, lanes], axis=0, keepdims=True)
        scores = masked(dot(kv[:top, rows], query), info, lanes, causal)
        prob = jnp.exp(scores - lse[h : h + 1, lanes])
        grad = (prob * (dot(kv[:top, value_rows], outer) - delta)).astype(BF)
        dq[rows, lanes] = (SCALE * dot(kvt[rows, :top], grad)).astype(BF)
        dk_new = dot_nt(query, grad)
        dv_new = dot_nt(outer, prob.astype(BF))
        if b == 512 // QB - 1:
            dk_acc[...] = dk_new
            dv_acc[...] = dv_new
        else:
            dk_acc[:, :top] += dk_new
            dv_acc[:, :top] += dv_new
    dkv[rows, :] = dk_acc[...].astype(BF)
    dkv[value_rows, :] = dv_acc[...].astype(BF)


def norm(values, gain):
    inverse = lax.rsqrt(jnp.mean(values * values, axis=-1, keepdims=True) + EPS)
    return (values * inverse * gain).astype(BF)


def norm_back(values, gain, upstream):
    inverse = lax.rsqrt(jnp.mean(values * values, axis=-1, keepdims=True) + EPS)
    normed = values * inverse
    scaled = upstream * gain
    grad = inverse * (scaled - normed * jnp.mean(scaled * normed, axis=-1, keepdims=True))
    return grad, jnp.sum(upstream * normed, axis=0, keepdims=True)


def gelu_parts(u):
    root = 0.7978845608028654
    square = u * u
    bend = jnp.tanh(root * u * (1.0 + 0.044715 * square))
    half = 0.5 * (1.0 + bend)
    slope = half + 0.5 * u * (1.0 - bend * bend) * (root * (1.0 + 0.134145 * square))
    return u * half, slope


class Names:
    pass


FETCHED = "gains sk sv sq ck cv so co cq gate up".split()


def layer_kernel(names, *refs):
    R = Names()
    for name, ref in zip(names, refs, strict=True):
        setattr(R, name, ref)
    me = coords()
    x, c, y, z = me
    g = 2 * x + c
    s = 2 * z + y
    group = ((1 - x, c, y, z), (1 - x, 1 - c, y, z), (x, 1 - c, y, z))
    line = tuple((x, c, y, lax.rem(z + k, 4)) for k in (1, 2, 3))
    fetch = [
        pltpu.make_async_copy(getattr(R, name), getattr(R, "v_" + name), R.s_fetch.at[i])
        for i, name in enumerate(FETCHED)
    ]
    for one in fetch:
        one.start()
    near_dn = pltpu.make_async_copy(R.down, R.DN.at[s], R.s_near.at[0])
    near_dn.start()
    greet(me, group + line + ((x, c, 1 - y, z),), moves=True)

    there = owner_of(*me)
    there_g = 2 * there[0] + there[1]
    move_x = Move(me, R.tok, R.X.at[2 * there_g + y], R.s_move.at[0])
    move_t = Move(me, R.tabs, R.TAB, R.s_move.at[1])
    move_m = Move(me, R.mem, R.M.at[2 * there_g + y], R.s_move.at[2])
    move_d = Move(me, R.dout, R.DO.at[there_g], R.s_move.at[3])
    for one in fetch[:6]:
        one.wait()
    gains = R.v_gains[...].astype(F32)
    for k in range(4):
        narrow = slice(192 * k, 192 * k + 192)
        row = [w[:, narrow].astype(F32) for w in (R.v_sk, R.v_sv, R.v_sq)] + [gains]
        row = jnp.concatenate(row + [w[:, narrow].astype(F32) for w in (R.v_ck, R.v_cv)], axis=1)
        R.stage_a[k] = jnp.concatenate([row[:, :512], row[:, 512:]], axis=0).astype(BF)

    def to_group(stage, land, sems):
        return [
            remote(stage.at[2 * to[0] + to[1]], land.at[g], sems.at[0, i], sems.at[1, i], to)
            for i, to in enumerate(group)
        ]

    parts_a = to_group(R.stage_a, R.land_a, R.s_part_a)
    for one in parts_a:
        one.start()
    move_x.start()
    for t in range(2):
        length, plot = R.lengths[0, t], R.plots[0, t]
        start = R.lengths[0, 0] if t else 0
        R.tabs[t : t + 1, :] = jnp.full((1, 128), start + length, jnp.int32)
        R.tabs[2 + t : 3 + t, :] = jnp.full((1, 128), plot, jnp.int32)
    R.tabs[4:, :] = jnp.zeros((4, 128), jnp.int32)
    move_t.start()

    def halves_stacked(w):
        w = w[...].astype(F32)
        return jnp.concatenate([w[:, :384], w[:, 384:]], axis=0).astype(BF)

    for one in fetch[6:]:
        one.wait()
    for k in range(4):
        wide = slice(512 * k, 512 * k + 512)
        R.stage_b[k, :24] = R.v_gate[:, wide]
        R.stage_b[k, 24:] = R.v_up[:, wide]
    R.land_a[g] = R.stage_a[g]
    R.land_b[g] = R.stage_b[g]
    gather_x = Gather8(me, R.X, R.s_x, True)
    gather_m = Gather8(me, R.M, R.s_m, True)
    gather_d = Gather4(me, R.DO, R.s_d)
    gather_a = GatherPlane(me, R.PA, R.s_a)
    gather_b = GatherPlane(me, R.PB, R.s_b, slice(0, 384))
    gather_o = GatherPlane(me, R.FO.at[g], R.s_fo)
    gather_c = GatherPlane(me, R.FC.at[g], R.s_fc)
    gather_q = GatherPlane(me, R.FQ.at[g], R.s_fq)
    gather_2 = GatherRelay(me, R.P2, R.s_2)
    gather_n = GatherRelay(me, R.DN, R.s_n)
    whole_o = Gather4(me, R.FO, R.s_wo)
    whole_c = Gather4(me, R.FC, R.s_wc)
    whole_q = Gather4(me, R.FQ, R.s_wq)

    R.FO[g, s] = halves_stacked(R.v_so)
    gather_o.start_along()
    gather_o.start_across()
    R.FQ[g, s] = halves_stacked(R.v_cq)
    R.FC[g, s] = halves_stacked(R.v_co)
    for one in parts_a:
        one.wait_recv()
    whole = []
    for r in range(4):
        piece = R.land_a[r].astype(F32)
        whole.append(jnp.concatenate([piece[:24], piece[24:]], axis=1))
    whole = jnp.concatenate(whole, axis=0).astype(BF)
    R.PA[s] = whole[:, :640]
    R.PB[s, :, :384] = whole[:, 640:]
    gather_a.start_across()
    gather_b.start_across()
    gather_q.start_across()
    gather_c.start_across()
    move_x.arrive()
    gather_x.start()
    gather_a.start_along()
    parts_b = to_group(R.stage_b, R.land_b, R.s_part_b)
    for one in parts_b:
        one.start()
    move_m.start()
    gather_b.start_along()
    gather_q.start_along()
    gather_c.start_along()
    move_d.start()
    gather_x.forward()
    for k in (1, 3, 2):
        gather_o.forward(k)
    gather_a.forward(1)
    for one in parts_b:
        one.wait_recv()
    for half in range(2):
        rows = [R.land_b[r].astype(F32)[24 * half : 24 * half + 24] for r in range(4)]
        R.P2[s, :, 512 * half : 512 * half + 512] = jnp.concatenate(rows, axis=0).astype(BF)
    gather_2.start_along()
    near_dn.wait()
    gather_x.forward_far()
    gather_o.arrive()
    whole_o.start()
    gather_a.forward(3)
    gather_a.forward(2)
    move_t.arrive()
    end_one, end_two = R.TAB[0:1, 0:1], R.TAB[1:2, 0:1]
    plot_one, plot_two = R.TAB[2:3, 0:1], R.TAB[3:4, 0:1]
    lane = lax.broadcasted_iota(jnp.int32, (1, 512), 1)
    for i in range(4):
        lanes = slice(128 * i, 128 * i + 128)
        R.info[0:1, lanes] = lane[:, :128] + (2 * i + y) * 128
    qpos = R.info[0:1, :]
    past_one, past_two = qpos >= end_one, qpos >= end_two
    R.info[1:2, :] = jnp.where(past_two, end_two, jnp.where(past_one, end_one, 0))
    R.info[2:3, :] = jnp.where(past_two, 0, jnp.where(past_one, plot_two, plot_one))

    def unpack(pieces, whole, width, step):
        for zz in range(4):

            def one(i, carry):
                lanes = pl.ds(pl.multiple_of(i * step, step), step)
                low = pieces[2 * zz, :, lanes].astype(F32)
                high = pieces[2 * zz + 1, :, lanes].astype(F32)
                for r in range(4):
                    rows = slice(24 * r, 24 * r + 24)
                    both = jnp.concatenate([low[rows], high[rows]], axis=0)
                    whole[192 * r + 48 * zz : 192 * r + 48 * zz + 48, lanes] = both.astype(BF)
                return carry

            lax.fori_loop(0, width // step, one, 0)

    gather_a.arrive()
    unpack(R.PA, R.WA, 640, 128)
    gain_rows = R.WA[:, 512:640].astype(F32).T
    gain_one, gain_two, gain_three = (gain_rows[64 + i : 65 + i] for i in range(3))

    def pair_rows(buf, i):
        return jnp.concatenate([buf[2 * i], buf[2 * i + 1]], axis=0)

    def mine_rows(buf):
        return jnp.concatenate([buf[2 * i + y] for i in range(4)], axis=0)

    def keys_values(i, operand, weight, natural, turned):
        rows = pl.ds(pl.multiple_of(i * 256, 256), 256)
        product = dot(operand, weight[:, :384])
        natural[rows, :] = product.astype(BF)
        turned[:, rows] = product.T.astype(BF)

    def first_norm(i, carry):
        x1 = norm(pair_rows(R.X, i).astype(F32), gain_one)
        R.X1[2 * i] = x1[:128]
        R.X1[2 * i + 1] = x1[128:]
        keys_values(i, x1, R.WA, R.KV, R.KVT)
        return carry

    gather_x.arrive()
    move_m.arrive()
    gather_m.start()
    whole_o.forward()
    lax.fori_loop(0, 4, first_norm, 0)
    product = SCALE * dot(mine_rows(R.X1), R.WA[:, 384:640])
    R.QT[...] = product.T[:192].astype(BF)

    def share_heads(buf, sems):
        return [Gather4(me, buf.at[:, h], sems.at[h]) for h in range(3)]

    share_1 = share_heads(R.A4, R.s_share1)
    for k in (1, 3, 2):
        gather_b.forward(k)
    for h in range(3):
        attend_head(h, R.info, R.QT, R.KV, R.KVT, R.OUT1, R.LSE1, True)
        R.A4[g, h] = R.OUT1[64 * h : 64 * h + 64, :].astype(BF)
        share_1[h].start()
    gather_m.forward()
    for k in (1, 3, 2):
        gather_q.forward(k)
    for k in (1, 3, 2):
        gather_c.forward(k)
    gather_2.start_across()
    gather_n.start_across()
    for h in range(3):
        share_1[h].forward()
    gather_m.forward_far()
    gather_2.forward(1)
    gather_n.start_along()
    whole_o.arrive()

    def unpack_full(pieces, whole):
        def one(r, carry):
            for zz in range(4):
                low, high = pieces[r, 2 * zz].astype(F32), pieces[r, 2 * zz + 1].astype(F32)
                rows = pl.ds(pl.multiple_of(192 * r + 48 * zz, 16), 48)
                whole[rows, :384] = jnp.concatenate([low[:24], high[:24]], axis=0).astype(BF)
                whole[rows, 384:] = jnp.concatenate([low[24:], high[24:]], axis=0).astype(BF)
            return carry

        lax.fori_loop(0, 4, one, 0)

    unpack_full(R.FO, R.WO)
    for one in share_1:
        one.arrive()

    def project(pieces, weight, i):
        lanes = slice(256 * i, 256 * i + 256)
        turned = pieces[:, :, :, lanes].astype(F32).reshape(768, 256)
        return dot(turned.T.astype(BF), weight[...])

    for i in range(2):
        rows = slice(256 * i, 256 * i + 256)
        before = jnp.concatenate([R.X[4 * i + y], R.X[4 * i + 2 + y]], axis=0).astype(F32)
        first = before + project(R.A4, R.WO, i)
        R.FIRST[rows, :] = first
        R.X2[rows, :] = norm(first, gain_two)
    gather_q.arrive()
    whole_q.start()
    gather_2.forward(2)
    gather_n.forward(1)
    gather_b.arrive()
    unpack(R.PB, R.WB, 384, 128)
    gather_c.arrive()
    whole_c.start()
    move_d.arrive()
    gather_d.start()
    gather_m.arrive()

    def memory_pair(i, carry):
        keys_values(i, pair_rows(R.M, i), R.WB, R.MKV, R.MKVT)
        return carry

    lax.fori_loop(0, 4, memory_pair, 0)
    whole_q.forward()
    gather_2.forward(3)
    gather_n.forward(2)
    whole_q.arrive()
    unpack_full(R.FQ, R.WQ)
    for k in range(4):

        @pl.when(g == k)
        def _():
            R.WCQ[...] = R.WQ[:, 192 * k : 192 * k + 192]

    for i in range(2):
        rows = slice(256 * i, 256 * i + 256)
        product = SCALE * dot(R.X2[rows, :], R.WCQ[...])
        R.CQT[:, rows] = product.T.astype(BF)
    share_2 = share_heads(R.C4, R.s_share2)
    for h in range(3):
        attend_head(h, R.info, R.CQT, R.MKV, R.MKVT, R.OUT2, R.LSE2, False)
        R.C4[g, h] = R.OUT2[64 * h : 64 * h + 64, :].astype(BF)
        share_2[h].start()
        if h == 0:
            whole_c.forward()
        if h == 1:
            gather_n.forward(3)
            gather_d.forward()
    for h in range(3):
        share_2[h].forward()
    whole_c.arrive()
    unpack_full(R.FC, R.WC)
    for one in share_2:
        one.arrive()
    for i in range(2):
        rows = slice(256 * i, 256 * i + 256)
        second = R.FIRST[rows, :] + project(R.C4, R.WC, i)
        R.SECOND[rows, :] = second
        R.X3[rows, :] = norm(second, gain_three)
    gather_2.arrive()
    unpack(R.P2, R.W2, 1024, 256)
    for one in parts_a + parts_b:
        one.wait_send()
    gather_2.finish()
    gather_a.finish()
    gather_b.finish()
    gather_d.arrive()
    gather_n.arrive()

    sum_dx = Sum4(me, R.DXP, R.by_c_dx, R.by_x_dx, R.s_dx)
    sum_out = Sum4(me, R.OP, R.by_c_out, R.by_x_out, R.s_out)

    def feed(core):
        at = [pl.ds(pl.multiple_of((2 * px + core) * 128, 128), 128) for px in range(2)]
        x3 = jnp.concatenate([R.X3[rows, :] for rows in at], axis=0)
        gate, up = dot(x3, R.W2[:, :512]), dot(x3, R.W2[:, 512:])
        active, slope = gelu_parts(gate)
        hidden = (active * up).astype(BF)
        outer = jnp.concatenate([R.DO[2 * px + core] for px in range(2)], axis=0)
        w_down = R.DN[...].reshape(512, 768)
        hidden_grad = dot_nt(outer, w_down)
        gate_grad = (hidden_grad * up * slope).astype(BF)
        up_grad = (hidden_grad * active).astype(BF)
        dx3 = (dot_nt(gate_grad, R.W2[:, :512]) + dot_nt(up_grad, R.W2[:, 512:])).astype(BF)
        out = dot(hidden, w_down).astype(BF)
        for px in range(2):
            half = slice(128 * px, 128 * px + 128)
            R.H[at[px], :] = hidden[half]
            R.GG[at[px], :512] = gate_grad[half]
            R.GG[at[px], 512:] = up_grad[half]
            R.DXP[2 * px + core] = dx3[half]
            R.OP[2 * px + core] = out[half]

    def pack(whole, pieces, start, width):
        for t in range(8):
            rows = [whole[(8 * r + t) * 24 : (8 * r + t) * 24 + 24, :] for r in range(4)]
            pieces[t, :, start : start + width] = jnp.concatenate(rows, axis=0).astype(BF)

    feed(1 - c)
    sum_dx.start()
    feed(c)
    sum_dx.to_x()
    sum_out.start()
    own = pl.ds(pl.multiple_of(g * 128, 128), 128)
    own_block = 2 * g + y
    x3_t = R.X3[...].astype(F32).T.astype(BF)
    total_2 = [
        SumPlane(me, R.P2, R.by_y_2, R.by_z_2, R.s_g2.at[i], slice(256 * i, 256 * i + 256))
        for i in range(4)
    ]
    for i in range(4):
        R.W2G[...] = dot(x3_t, R.GG[:, 256 * i : 256 * i + 256])
        pack(R.W2G, R.P2, 256 * i, 256)
        total_2[i].start()
    hidden_t = R.H[...].astype(F32).T.astype(BF)
    d_down = dot(hidden_t, R.DO[...].reshape(512, 768)).astype(BF)
    for t in range(8):
        R.DNG[t] = d_down[64 * t : 64 * t + 64]
    total_n = SumPlane(me, R.DNG, R.by_y_n, R.by_z_n, R.s_gn)
    total_n.start()
    part, gain_grad_three = norm_back(R.SECOND[own, :], gain_three, sum_dx.end())
    second_grad = R.DO[g].astype(F32) + part
    R.SGRAD[...] = second_grad
    R.DS4[g] = second_grad.astype(BF)
    share_s = Gather4(me, R.DS4, R.s_s)
    share_s.start()
    total_2[0].fold()
    share_s.forward()
    sum_out.to_x()
    total_2[1].fold()
    share_s.arrive()

    dsec = R.DS4[...].reshape(512, 768)
    mine_192 = pl.ds(pl.multiple_of(g * 192, 16), 192)
    R.OUTER[...] = dot_nt(R.WC[mine_192, :], dsec).astype(BF)
    share_3 = share_heads(R.DC4, R.s_share3)
    for h in range(3):
        attend_back_head(
            h, R.info, R.CQT, R.MKV, R.MKVT, R.OUTER, R.OUT2, R.LSE2, R.DCQT, R.MDKV, R.dk, R.dv, False
        )
        R.DC4[g, h] = R.DCQT[64 * h : 64 * h + 64, :]
        share_3[h].start()
        if h == 0:
            total_2[2].fold()
            total_2[0].pass_one()
        if h == 1:
            share_3[0].forward()
            total_2[1].pass_one()

    def pack_24(whole, pieces):
        for t in range(8):
            rows = whole[24 * t : 24 * t + 24]
            pieces[t] = jnp.concatenate([rows[:, :384], rows[:, 384:]], axis=0).astype(BF)

    def memory_grad_pair(i, carry):
        lanes = pl.ds(pl.multiple_of(i * 256, 256), 256)
        turned = dot(R.WB[:, :384], R.MDKV[:, lanes]).astype(BF)
        R.MG[2 * i] = turned[:, :128]
        R.MG[2 * i + 1] = turned[:, 128:]
        return carry

    total_2[3].fold()
    total_2[0].pass_two()
    lax.fori_loop(0, 4, memory_grad_pair, 0)
    sum_m = Sum8(me, R.MG, R.by_c_m, R.by_x_m, R.by_y_m, R.s_gm)
    share_3[1].forward()
    pack_24(dot(R.C4[g].reshape(192, 512), dsec), R.CO8)
    total_c = SumPlane(me, R.CO8, R.by_y_c, R.by_z_c, R.s_gc)
    total_c.start()
    R.W1G[...] = dot(R.MDKV[...], R.M[...].reshape(1024, 768)).T
    pack(R.W1G, R.PB, 0, 384)
    R.TURN[:192, :] = dot(R.DCQT[...], R.X2[...])
    R.TURN[192:, :] = jnp.zeros((64, 768), F32)
    pack(R.TURN[...].T, R.PB, 384, 256)
    total_b = SumPlane(me, R.PB, R.by_y_b, R.by_z_b, R.s_gb)
    total_b.start()
    share_3[2].forward()
    sum_m.start()
    back = [
        Move(me, src, dst, R.s_back.at[i], back=True)
        for i, (src, dst) in enumerate(
            ((R.TBLOCK, R.tokens_out), (R.LBLOCK, R.layer_out), (R.MBLOCK, R.memory_out))
        )
    ]
    R.LBLOCK[...] = (R.SECOND[own, :] + sum_out.end()).astype(BF)
    back[1].start()
    total_2[2].pass_one()
    total_2[1].pass_two()
    for one in share_3:
        one.arrive()

    for i in range(2):
        rows = slice(256 * i, 256 * i + 256)
        dx2 = dot(R.WQ[...], R.DC4[:, :, :, rows].reshape(768, 256)).T
        part, ignored = norm_back(R.FIRST[rows, :], gain_two, dx2)
        R.DFIRST[rows, :] = (dsec[rows].astype(F32) + part).astype(BF)
    dx2 = dot(R.WQ[...], R.DC4[:, :, :, own].reshape(768, 128)).T
    part, gain_grad_two = norm_back(R.FIRST[own, :], gain_two, dx2)
    R.SGRAD[...] += part

    R.OUTER[...] = dot_nt(R.WO[mine_192, :], R.DFIRST[...]).astype(BF)
    sum_m.to_x()
    total_n.fold()
    total_2[3].pass_one()
    for h in range(3):
        attend_back_head(
            h, R.info, R.QT, R.KV, R.KVT, R.OUTER, R.OUT1, R.LSE1, R.DQT, R.DKV, R.dk, R.dv, True
        )
        if h == 0:
            total_c.fold()
            total_2[2].pass_two()
        if h == 1:
            total_n.pass_one()
            total_2[3].pass_two()

    def token_grad_pair(i, carry):
        lanes = pl.ds(pl.multiple_of(i * 256, 256), 256)
        half = pl.ds(pl.multiple_of(i * 128, 128), 128)
        turned = dot(R.WA[:, :384], R.DKV[:, lanes])
        query = dot(R.WA[:, 384:576], R.DQT[:, half])
        R.TG[2 * i] = (turned[:, :128] + jnp.where(y == 0, query, 0.0)).astype(BF)
        R.TG[2 * i + 1] = (turned[:, 128:] + jnp.where(y == 1, query, 0.0)).astype(BF)
        return carry

    lax.fori_loop(0, 4, token_grad_pair, 0)
    sum_t = Sum8(me, R.TG, R.by_c_t, R.by_x_t, R.by_y_t, R.s_gt)
    sum_t.start()
    sum_m.to_y()
    R.W1G[...] = dot(R.DKV[...], R.X1[...].reshape(1024, 768)).T
    pack(R.W1G, R.PA, 0, 384)
    total_a = SumPlane(me, R.PA, R.by_y_a, R.by_z_a, R.s_ga, slice(0, 384))
    sum_t.to_x()
    total_a.start()
    R.TURN[:192, :] = dot(R.DQT[...], mine_rows(R.X1))
    pack_24(dot(R.A4[g].reshape(192, 512), R.DFIRST[...]), R.SO8)
    total_s = SumPlane(me, R.SO8, R.by_y_s, R.by_z_s, R.s_gs)
    total_b.fold()
    total_c.pass_one()
    total_n.pass_two()
    R.MBLOCK[...] = sum_m.end().T.astype(BF)
    back[2].start()
    sum_t.to_y()
    total_s.start()
    total_b.pass_one()
    total_c.pass_two()
    total_a.fold()
    dx1 = sum_t.end().T
    part, gain_grad_one = norm_back(R.X[own_block].astype(F32), gain_one, dx1)
    R.TURN[192:193, :] = gain_grad_one
    R.TURN[193:194, :] = gain_grad_two
    R.TURN[194:195, :] = gain_grad_three
    pack(R.TURN[...].T, R.PA, 384, 256)
    total_g = SumPlane(me, R.PA, R.by_y_a, R.by_z_a, R.s_gg, slice(384, 640))
    total_g.start()
    R.TBLOCK[...] = (R.SGRAD[...] + part).astype(BF)
    back[0].start()
    total_b.pass_two()
    for one in total_2:
        one.end()
    rows_2 = R.P2[s].astype(F32)
    for r in range(4):
        rows = slice(24 * r, 24 * r + 24)
        R.stage_b[r] = jnp.concatenate([rows_2[rows, :512], rows_2[rows, 512:]], axis=0).astype(BF)
    last_b = to_group(R.stage_b, R.quarters_b, R.s_last_b)
    for one in last_b:
        one.start()
    total_s.fold()
    total_a.pass_one()
    total_g.fold()
    total_n.end()
    total_c.end()
    total_a.pass_two()
    total_s.pass_one()
    total_g.pass_one()
    total_b.end()
    total_s.pass_two()
    total_g.pass_two()
    total_a.end()
    total_g.end()
    rows_a, rows_b = R.PA[s].astype(F32), R.PB[s].astype(F32)
    for r in range(4):
        rows = slice(24 * r, 24 * r + 24)
        R.stage_z[r] = jnp.concatenate([rows_a[rows], rows_b[rows]], axis=0).astype(BF)
    last_a = to_group(R.stage_z, R.quarters_a, R.s_last_a)
    for one in last_a:
        one.start()
    total_s.end()
    near = [
        pltpu.make_async_copy(src, dst, R.s_near.at[1 + i])
        for i, (src, dst) in enumerate(
            (
                (R.stage_z.at[g], R.quarters_a.at[g]),
                (R.stage_b.at[g], R.quarters_b.at[g]),
                (R.CO8.at[s], R.co_out),
                (R.SO8.at[s], R.so_out),
                (R.DNG.at[s], R.down_out),
            )
        )
    ]
    for one in near:
        one.start()
    for one in near:
        one.wait()
    for one in last_a + last_b:
        one.wait_recv()
    for one in back:
        one.arrive()
        one.finish()
    for one in last_a + last_b:
        one.wait_send()
    for one in (move_x, move_t, move_m, move_d):
        one.finish()
    for one in (gather_x, gather_m, gather_d, gather_o, gather_c, gather_q, gather_n):
        one.finish()
    for one in (whole_o, whole_c, whole_q, share_s, sum_dx, sum_out, sum_m, sum_t):
        one.finish()
    for one in share_1 + share_2 + share_3 + total_2:
        one.finish()
    for one in (total_a, total_g, total_b, total_n, total_c, total_s):
        one.finish()


def run_layer(inputs):
    n, d = 128, 768

    def low(*shape):
        return pltpu.VMEM(shape, BF)

    def full(*shape):
        return pltpu.VMEM(shape, F32)

    outs = dict(
        quarters_a=(4, 48, 640),
        quarters_b=(4, 48, 512),
        co_out=(48, 384),
        so_out=(48, 384),
        down_out=(64, d),
        tokens_out=(n, d),
        layer_out=(n, d),
        memory_out=(n, d),
    )
    scratch = dict(
        stage_a=low(4, 48, 512), land_a=low(4, 48, 512), stage_z=low(4, 48, 640), stage_b=low(4, 48, 512), land_b=low(4, 48, 512),
        **{"v_" + name: pltpu.VMEM(inputs[name][0].shape, BF) for name in FETCHED},
        s_fetch=dma(len(FETCHED)),
        tabs=pltpu.VMEM((8, 128), jnp.int32), TAB=pltpu.VMEM((8, 128), jnp.int32),
        X=low(8, n, d), M=low(8, n, d), DO=low(4, n, d),
        PA=low(8, 96, 640), PB=low(8, 96, 640), P2=low(8, 96, 1024), DN=low(8, 64, d),
        FO=low(4, 8, 48, 384), FC=low(4, 8, 48, 384), FQ=low(4, 8, 48, 384),
        WA=low(768, 640), WB=low(768, 384), WCQ=low(768, 192), W2=low(768, 1024), WO=low(d, d), WC=low(d, d), WQ=low(d, d),
        info=pltpu.VMEM((8, 512), jnp.int32),
        X1=low(8, n, d), X2=low(512, d), X3=low(512, d),
        KV=low(1024, 384), KVT=low(384, 1024), MKV=low(1024, 384), MKVT=low(384, 1024),
        QT=low(192, 512), CQT=low(192, 512), OUT1=full(192, 512), OUT2=full(192, 512),
        LSE1=full(8, 512), LSE2=full(8, 512),
        A4=low(4, 3, 64, 512), C4=low(4, 3, 64, 512), DC4=low(4, 3, 64, 512),
        FIRST=full(512, d), SECOND=full(512, d),
        H=low(512, 512), GG=low(512, 1024), DXP=low(4, n, d), OP=low(4, n, d),
        by_c_dx=low(2, n, d), by_x_dx=low(n, d), by_c_out=low(2, n, d), by_x_out=low(n, d),
        W2G=full(768, 256), by_y_2=low(4, 96, 1024), by_z_2=low(5, 96, 1024),
        DNG=low(8, 64, d), by_y_n=low(4, 64, d), by_z_n=low(5, 64, d),
        SGRAD=full(n, d), DS4=low(4, n, d), OUTER=low(192, 512),
        DCQT=low(192, 512), DQT=low(192, 512), MDKV=low(384, 1024), DKV=low(384, 1024),
        dk=full(64, 1024), dv=full(64, 1024),
        CO8=low(8, 48, 384), by_y_c=low(4, 48, 384), by_z_c=low(5, 48, 384),
        SO8=low(8, 48, 384), by_y_s=low(4, 48, 384), by_z_s=low(5, 48, 384),
        MG=low(8, d, n), by_c_m=low(2, 2, d, n), by_x_m=low(2, d, n), by_y_m=low(d, n),
        TG=low(8, d, n), by_c_t=low(2, 2, d, n), by_x_t=low(2, d, n), by_y_t=low(d, n),
        DFIRST=low(512, d), W1G=full(768, 384), TURN=full(256, 768),
        by_y_a=low(4, 96, 640), by_z_a=low(5, 96, 640), by_y_b=low(4, 96, 640), by_z_b=low(5, 96, 640),
        TBLOCK=low(n, d), LBLOCK=low(n, d), MBLOCK=low(n, d),
        s_move=dma(4, 2), s_near=dma(6), s_part_a=dma(2, 3), s_part_b=dma(2, 3),
        s_last_a=dma(2, 3), s_last_b=dma(2, 3), s_back=dma(3, 2),
        s_x=dma(14), s_m=dma(14), s_d=dma(6), s_wo=dma(6), s_wc=dma(6), s_wq=dma(6), s_s=dma(6),
        s_a=dma(2, 12), s_b=dma(2, 12), s_2=dma(2, 12), s_n=dma(2, 12), s_fo=dma(2, 12), s_fc=dma(2, 12), s_fq=dma(2, 12),
        s_share1=dma(3, 6), s_share2=dma(3, 6), s_share3=dma(3, 6),
        s_dx=dma(2, 3), s_out=dma(2, 3), s_gm=dma(2, 7), s_gt=dma(2, 7),
        s_ga=dma(2, 11), s_gb=dma(2, 11), s_gg=dma(2, 11), s_g2=dma(4, 2, 11), s_gn=dma(2, 11), s_gc=dma(2, 11), s_gs=dma(2, 11),
    )
    names = tuple(inputs) + tuple(outs) + tuple(scratch)
    return pl.pallas_call(
        functools.partial(layer_kernel, names),
        out_shape=tuple(jax.ShapeDtypeStruct(shape, BF) for shape in outs.values()),
        in_specs=[spec for _, spec in inputs.values()],
        out_specs=tuple([ANYWHERE] * len(outs)),
        scratch_shapes=list(scratch.values()),
        compiler_params=pltpu.CompilerParams(
            collective_id=1, has_side_effects=True, vmem_limit_bytes=VMEM_LIMIT
        ),
        name="layer",
    )(*[a for a, _ in inputs.values()])


def outputs_kernel(
    qa, qb, co, so, down, tokens, layer, memory,
    layer_out, tokens_out, memory_out, gains_out,
    sq, sk, sv, so_out, cq, ck, cv, co_out, gate, up, down_out,
):
    layer_out[...] = layer[...]
    tokens_out[...] = tokens[...]
    memory_out[...] = memory[...]
    down_out[...] = down[...].astype(F32)
    gains = jnp.zeros((24, 128), F32)
    for k in range(4):
        piece = qa[k].astype(F32)
        gains = gains + piece[:24, 512:]
        narrow = slice(192 * k, 192 * k + 192)
        for row, outs in ((0, (sk, sv, sq)), (24, (ck, cv, cq))):
            for i, out in enumerate(outs):
                out[:, narrow] = piece[row : row + 24, 192 * i : 192 * i + 192]
        piece = qb[k].astype(F32)
        gate[:, 512 * k : 512 * k + 512] = piece[:24]
        up[:, 512 * k : 512 * k + 512] = piece[24:]
    gains_out[...] = gains
    for piece, out in ((so, so_out), (co, co_out)):
        rows = piece[...].astype(F32)
        out[:, :384] = rows[:24]
        out[:, 384:] = rows[24:]


def body_planes(
    tokens, memory, out_grad, table_lengths, table_plots,
    self_gain, self_query, self_key, self_value, self_output,
    cross_gain, cross_query, cross_key, cross_value, cross_output,
    mlp_gain, mlp_gate, mlp_up, mlp_down,
):
    gains = jnp.stack([self_gain, cross_gain, mlp_gain], axis=1)
    gains = jnp.pad(gains, ((0, 0), (0, 61)))
    in_smem = pl.BlockSpec(memory_space=pltpu.SMEM)
    results = run_layer(
        dict(
            tok=(tokens[0], ANYWHERE), mem=(memory[0], ANYWHERE), dout=(out_grad[0], ANYWHERE),
            lengths=(table_lengths, in_smem), plots=(table_plots, in_smem), gains=(gains, ANYWHERE),
            sq=(self_query, ANYWHERE), sk=(self_key, ANYWHERE), sv=(self_value, ANYWHERE), so=(self_output, ANYWHERE),
            cq=(cross_query, ANYWHERE), ck=(cross_key, ANYWHERE), cv=(cross_value, ANYWHERE), co=(cross_output, ANYWHERE),
            gate=(mlp_gate, ANYWHERE), up=(mlp_up, ANYWHERE), down=(mlp_down, ANYWHERE),
        )
    )
    block = jax.ShapeDtypeStruct((128, 768), BF)
    rows = jax.ShapeDtypeStruct((24, 768), F32)
    wide = jax.ShapeDtypeStruct((24, 2048), F32)
    outs = pl.pallas_call(
        outputs_kernel,
        out_shape=(block,) * 3
        + (jax.ShapeDtypeStruct((24, 128), F32),)
        + (rows,) * 8
        + (wide, wide, jax.ShapeDtypeStruct((64, 768), F32)),
        name="outputs",
    )(*results)
    layer, tokens_mine, memory_mine, gain_sums, sq, sk, sv, so, cq, ck, cv, co, gate, up, down = outs
    return (
        layer[None], tokens_mine[None], memory_mine[None],
        gain_sums[:, 64], sq, sk, sv, so,
        gain_sums[:, 65], cq, ck, cv, co,
        gain_sums[:, 66], gate, up, down,
    )


def solution(mesh):
    placed = (
        P(ROW, SEQ, None),
        P(ROW, SEQ, None),
        P(ROW, SEQ, None),
        P(ROW, None),
        P(ROW, None),
        P(BOTH),
        P(BOTH, None),
        P(BOTH, None),
        P(BOTH, None),
        P(BOTH, None),
        P(BOTH),
        P(BOTH, None),
        P(BOTH, None),
        P(BOTH, None),
        P(BOTH, None),
        P(BOTH),
        P(BOTH, None),
        P(BOTH, None),
        P(BOTH, None),
    )
    small = mesh.shape[ROW] == 4 and mesh.shape[SEQ] == 8
    return jax.shard_map(
        body_planes if small else body_general,
        mesh=mesh,
        in_specs=placed,
        out_specs=(
            P(ROW, SEQ, None),
            P(ROW, SEQ, None),
            P(ROW, SEQ, None),
            P(BOTH),
            P(BOTH, None),
            P(BOTH, None),
            P(BOTH, None),
            P(BOTH, None),
            P(BOTH),
            P(BOTH, None),
            P(BOTH, None),
            P(BOTH, None),
            P(BOTH, None),
            P(BOTH),
            P(BOTH, None),
            P(BOTH, None),
            P(BOTH, None),
        ),
        check_vma=False,
    )
```

```python
import functools

import jax
import jax.numpy as jnp
from jax import lax
from jax.experimental import pallas as pl
from jax.experimental.pallas import tpu as pltpu
from jax.sharding import PartitionSpec as P

HEADS = 12


SCALE = 0.125
EPS = 1e-06
NEG = -1e30
ROW, SEQ = "rows", "seq"
BOTH = (ROW, SEQ)
EQ0 = "rhqk,rkhd->rqhd"
EQ1 = "rhqk,rqhd->rkhd"
EQ2 = "rld,de->rle"
EQ3 = "rld,rle->de"
EQ4 = "rle,de->rld"
EQ5 = "rqhd,rkhd->rhqk"
EQ6 = "rqhd,rqhd->rhq"


def running_sum(lengths):
    ids = jnp.arange(lengths.shape[1], dtype=jnp.int32)
    upto = (ids[None, :] <= ids[:, None]).astype(lengths.dtype)
    return jnp.sum(lengths[:, None, :] * upto[None], axis=2)


def rms_forward(values, gain_vector):
    inverse = lax.rsqrt(jnp.mean(values * values, axis=-1, keepdims=True) + EPS)
    return (values * inverse * gain_vector, inverse)


def rms_backward(values, inverse, gain_vector, upstream):
    normed = values * inverse
    gain_grad = jnp.sum(upstream * normed, axis=(0, 1))
    scaled = upstream * gain_vector
    input_grad = inverse * (scaled - normed * jnp.mean(scaled * normed, axis=-1, keepdims=True))
    return (input_grad, gain_grad)


def matmul(operand, weight):
    return jnp.einsum(EQ2, operand, weight, preferred_element_type=jnp.float32)


def matmul_back(upstream, weight):
    return jnp.einsum(EQ4, upstream, weight, preferred_element_type=jnp.float32)


def weight_grad(operand, upstream):
    return jnp.einsum(EQ3, operand, upstream, preferred_element_type=jnp.float32)


def split_heads(values):
    return values.reshape(values.shape[0], values.shape[1], HEADS, values.shape[2] // HEADS)


def segment_of(places, table_ends):
    return jnp.sum((places[None, :, None] >= table_ends[:, None, :]).astype(jnp.int32), axis=2)


def pair_mask(query_seg, query_pos, key_seg, key_pos, causal):
    same_pair = query_seg[:, :, None] == key_seg[:, None, :]
    if causal:
        same_pair = jnp.logical_and(same_pair, key_pos[None, None, :] <= query_pos[None, :, None])
    return same_pair


def over_blocks(advance_block, fold_state, arrays, block_width):
    piece_rows = arrays[0].shape[1]
    block_count = piece_rows // block_width
    stacked = tuple(
        (
            jnp.moveaxis(
                member.reshape((member.shape[0], block_count, block_width) + member.shape[2:]), 1, 0
            )
            for member in arrays
        )
    )

    def advance(carried, block_items):
        block_index, block_parts = block_items
        return (advance_block(carried, block_parts, block_index * block_width), None)

    fold_state, ignored = lax.scan(
        advance, fold_state, (jnp.arange(block_count, dtype=jnp.int32), stacked)
    )
    return fold_state


def forward_fold(query_heads, query_seg, query_pos, key_segment, causal, block_width):

    def advance_block(fold_state, parts, first_row):
        key_block, value_block = parts
        key_pos = first_row + jnp.arange(key_block.shape[1], dtype=jnp.int32)
        allowed = pair_mask(query_seg, query_pos, key_segment(key_pos), key_pos, causal)

        def compute(current):
            running_max, running_sum, accumulated = current
            scores = (
                jnp.einsum(
                    EQ5,
                    query_heads,
                    split_heads(key_block),
                    preferred_element_type=jnp.float32,
                )
                * SCALE
            )
            scores = jnp.where(allowed[:, None], scores, NEG)
            new_max = jnp.maximum(running_max, jnp.max(scores, axis=-1))
            weights = jnp.where(allowed[:, None], jnp.exp(scores - new_max[..., None]), 0.0)
            factor = jnp.exp(running_max - new_max)
            new_sum = running_sum * factor + jnp.sum(weights, axis=-1)
            update = jnp.einsum(
                EQ0,
                weights.astype(jnp.bfloat16),
                split_heads(value_block),
                preferred_element_type=jnp.float32,
            )
            return (
                new_max,
                new_sum,
                accumulated * jnp.transpose(factor, (0, 2, 1))[..., None] + update,
            )

        return compute(fold_state)

    def forward_fold_piece(fold_state, shard_piece, first_row):
        return over_blocks(advance_block, fold_state, shard_piece, block_width)

    return forward_fold_piece


def finish(fold_state):
    running_max, running_sum, accumulated = fold_state
    attended = accumulated / jnp.transpose(running_sum, (0, 2, 1))[..., None]
    return (attended, running_max + jnp.log(running_sum))


def query_grad_fold(
    query_heads,
    out_heads,
    log_total,
    row_delta,
    query_seg,
    query_pos,
    key_segment,
    causal,
    block_width,
):

    def advance_block(fold_state, parts, first_row):
        key_block, value_block = parts
        key_pos = first_row + jnp.arange(key_block.shape[1], dtype=jnp.int32)
        allowed = pair_mask(query_seg, query_pos, key_segment(key_pos), key_pos, causal)

        def compute(current):
            key_heads = split_heads(key_block)
            scores = (
                jnp.einsum(
                    EQ5, query_heads, key_heads, preferred_element_type=jnp.float32
                )
                * SCALE
            )
            scores = jnp.where(allowed[:, None], scores, NEG)
            probabilities = jnp.where(allowed[:, None], jnp.exp(scores - log_total[..., None]), 0.0)
            prob_grad = jnp.einsum(
                EQ5,
                out_heads,
                split_heads(value_block),
                preferred_element_type=jnp.float32,
            )
            score_grad = (probabilities * (prob_grad - row_delta[..., None])).astype(jnp.bfloat16)
            return current + SCALE * jnp.einsum(
                EQ0, score_grad, key_heads, preferred_element_type=jnp.float32
            )

        return compute(fold_state)

    def query_fold_piece(fold_state, shard_piece, first_row):
        return over_blocks(advance_block, fold_state, shard_piece, block_width)

    return query_fold_piece


def key_grad_fold(
    key_heads,
    value_heads,
    key_seg,
    key_pos,
    total_rows,
    delta_rows,
    query_segment,
    causal,
    block_width,
):

    def advance_block(fold_state, parts, first_row):
        query_block, out_block = parts
        piece_rows = query_block.shape[1]
        query_pos = first_row + jnp.arange(piece_rows, dtype=jnp.int32)
        allowed = pair_mask(query_segment(query_pos), query_pos, key_seg, key_pos, causal)
        total_block = lax.dynamic_slice_in_dim(total_rows, first_row, piece_rows, 2)
        delta_block = lax.dynamic_slice_in_dim(delta_rows, first_row, piece_rows, 2)

        def compute(current):
            key_acc, value_acc = current
            query_heads = split_heads(query_block)
            out_heads = split_heads(out_block)
            scores = (
                jnp.einsum(
                    EQ5, query_heads, key_heads, preferred_element_type=jnp.float32
                )
                * SCALE
            )
            scores = jnp.where(allowed[:, None], scores, NEG)
            probabilities = jnp.where(
                allowed[:, None], jnp.exp(scores - total_block[..., None]), 0.0
            )
            value_acc = value_acc + jnp.einsum(
                EQ1,
                probabilities.astype(jnp.bfloat16),
                out_heads,
                preferred_element_type=jnp.float32,
            )
            prob_grad = jnp.einsum(
                EQ5, out_heads, value_heads, preferred_element_type=jnp.float32
            )
            score_grad = (probabilities * (prob_grad - delta_block[..., None])).astype(jnp.bfloat16)
            key_acc = key_acc + SCALE * jnp.einsum(
                EQ1, score_grad, query_heads, preferred_element_type=jnp.float32
            )
            return (key_acc, value_acc)

        return compute(fold_state)

    def key_fold_piece(fold_state, shard_piece, first_row):
        return over_blocks(advance_block, fold_state, shard_piece, block_width)

    return key_fold_piece


def body_general(
    tokens,
    memory,
    out_grad,
    table_lengths,
    table_plots,
    self_gain,
    self_query,
    self_key,
    self_value,
    self_output,
    cross_gain,
    cross_query,
    cross_key,
    cross_value,
    cross_output,
    mlp_gain,
    mlp_gate,
    mlp_up,
    mlp_down,
):
    def whole(shard):
        return lax.all_gather(shard, BOTH, axis=0, tiled=True)

    all_self_gain = whole(self_gain)
    all_self_query = whole(self_query)
    all_self_key = whole(self_key)
    all_self_value = whole(self_value)
    all_self_output = whole(self_output)
    all_cross_gain = whole(cross_gain)
    all_cross_query = whole(cross_query)
    all_cross_key = whole(cross_key)
    all_cross_value = whole(cross_value)
    all_cross_output = whole(cross_output)
    all_mlp_gain = whole(mlp_gain)
    all_mlp_gate = whole(mlp_gate)
    all_mlp_up = whole(mlp_up)
    all_mlp_down = whole(mlp_down)
    seq_count = lax.axis_size(SEQ)
    seq_index = lax.axis_index(SEQ)
    row_count = tokens.shape[0]
    positions = tokens.shape[1]
    memory_cols = memory.shape[1]
    width = tokens.shape[2]
    head_size = width // HEADS
    query_pos = seq_index * positions + jnp.arange(positions, dtype=jnp.int32)
    memory_pos = seq_index * memory_cols + jnp.arange(memory_cols, dtype=jnp.int32)
    table_ends = running_sum(table_lengths)
    tables = table_lengths.shape[1]
    table_ids = jnp.arange(tables, dtype=jnp.int32)
    plot_width = memory_cols * seq_count // tables

    def token_segment(places):
        return segment_of(places, table_ends)

    def token_plot(places):
        segments = segment_of(places, table_ends)
        return jnp.sum(
            jnp.where(segments[:, :, None] == table_ids[None, None, :], table_plots[:, None, :], 0),
            axis=2,
        )

    def memory_plot(places):
        return (places // plot_width)[None, :]

    def start_state():
        return (
            jnp.full((row_count, HEADS, positions), NEG, jnp.float32),
            jnp.zeros((row_count, HEADS, positions), jnp.float32),
            jnp.zeros((row_count, positions, HEADS, head_size), jnp.float32),
        )

    values = tokens.astype(jnp.float32)
    normed_one, inverse_one = rms_forward(values, all_self_gain.astype(jnp.float32))
    input_one = normed_one.astype(jnp.bfloat16)
    queries = matmul(input_one, all_self_query).astype(jnp.bfloat16)
    key_rows = matmul(input_one, all_self_key).astype(jnp.bfloat16)
    value_rows = matmul(input_one, all_self_value).astype(jnp.bfloat16)
    query_seg = token_segment(query_pos)
    self_fold = forward_fold(
        split_heads(queries), query_seg, query_pos, token_segment, True, positions
    )
    self_out, self_total = finish(
        self_fold(
            start_state(),
            (
                lax.all_gather(key_rows, SEQ, axis=1, tiled=True),
                lax.all_gather(value_rows, SEQ, axis=1, tiled=True),
            ),
            jnp.int32(0),
        )
    )
    self_att = self_out.reshape(row_count, positions, width).astype(jnp.bfloat16)
    first_sum = values + matmul(self_att, all_self_output)
    normed_two, inverse_two = rms_forward(first_sum, all_cross_gain.astype(jnp.float32))
    input_two = normed_two.astype(jnp.bfloat16)
    cross_rows = matmul(input_two, all_cross_query).astype(jnp.bfloat16)
    memory_keys = matmul(memory, all_cross_key).astype(jnp.bfloat16)
    memory_rows = matmul(memory, all_cross_value).astype(jnp.bfloat16)
    query_plot = token_plot(query_pos)
    cross_fold = forward_fold(
        split_heads(cross_rows), query_plot, query_pos, memory_plot, False, memory_cols
    )
    cross_out, cross_total = finish(
        cross_fold(
            start_state(),
            (
                lax.all_gather(memory_keys, SEQ, axis=1, tiled=True),
                lax.all_gather(memory_rows, SEQ, axis=1, tiled=True),
            ),
            jnp.int32(0),
        )
    )
    cross_att = cross_out.reshape(row_count, positions, width).astype(jnp.bfloat16)
    second_sum = first_sum + matmul(cross_att, all_cross_output)
    normed_three, inverse_three = rms_forward(second_sum, all_mlp_gain.astype(jnp.float32))
    input_three = normed_three.astype(jnp.bfloat16)
    gate_pre = matmul(input_three, all_mlp_gate)
    up_pre = matmul(input_three, all_mlp_up)

    def gated_unit(gate_value, up_value):
        return jax.nn.gelu(gate_value, approximate=True) * up_value

    hidden_value, gated_back = jax.vjp(gated_unit, gate_pre, up_pre)
    hidden = hidden_value.astype(jnp.bfloat16)
    layer_out = (second_sum + matmul(hidden, all_mlp_down)).astype(jnp.bfloat16)
    upstream = out_grad.astype(jnp.float32)
    grad_down = weight_grad(hidden, out_grad)
    hidden_grad = matmul_back(out_grad, all_mlp_down)
    gate_grad, up_grad = gated_back(hidden_grad)
    gate_low = gate_grad.astype(jnp.bfloat16)
    up_low = up_grad.astype(jnp.bfloat16)
    grad_gate = weight_grad(input_three, gate_low)
    grad_up = weight_grad(input_three, up_low)
    three_grad = matmul_back(gate_low, all_mlp_gate) + matmul_back(
        up_low, all_mlp_up
    )
    part_three, grad_gain_three = rms_backward(
        second_sum, inverse_three, all_mlp_gain.astype(jnp.float32), three_grad
    )
    second_grad = upstream + part_three
    cross_branch = second_grad.astype(jnp.bfloat16)
    grad_cross_output = weight_grad(cross_att, cross_branch)
    cross_dout = matmul_back(cross_branch, all_cross_output).astype(jnp.bfloat16)
    cross_heads = split_heads(cross_dout)
    cross_delta = jnp.einsum(EQ6, cross_heads.astype(jnp.float32), cross_out)
    cross_total_all, cross_delta_all = (
        lax.all_gather(cross_total, SEQ, axis=2, tiled=True),
        lax.all_gather(cross_delta, SEQ, axis=2, tiled=True),
    )
    cross_query_fold = query_grad_fold(
        split_heads(cross_rows),
        cross_heads,
        cross_total,
        cross_delta,
        query_plot,
        query_pos,
        memory_plot,
        False,
        memory_cols,
    )
    cross_rows_grad = cross_query_fold(
        jnp.zeros((row_count, positions, HEADS, head_size), jnp.float32),
        (
            lax.all_gather(memory_keys, SEQ, axis=1, tiled=True),
            lax.all_gather(memory_rows, SEQ, axis=1, tiled=True),
        ),
        jnp.int32(0),
    )
    cross_rows_low = cross_rows_grad.reshape(row_count, positions, width).astype(jnp.bfloat16)
    memory_fold = key_grad_fold(
        split_heads(memory_keys),
        split_heads(memory_rows),
        memory_plot(memory_pos),
        memory_pos,
        cross_total_all,
        cross_delta_all,
        token_plot,
        False,
        positions,
    )
    memory_zero = jnp.zeros((row_count, memory_cols, HEADS, head_size), jnp.float32)
    memory_key_grad, memory_value_grad = memory_fold(
        (memory_zero, memory_zero),
        (
            lax.all_gather(cross_rows, SEQ, axis=1, tiled=True),
            lax.all_gather(cross_dout, SEQ, axis=1, tiled=True),
        ),
        jnp.int32(0),
    )
    memory_key_low = memory_key_grad.reshape(row_count, memory_cols, width).astype(jnp.bfloat16)
    memory_value_low = memory_value_grad.reshape(row_count, memory_cols, width).astype(jnp.bfloat16)
    grad_cross_query = weight_grad(input_two, cross_rows_low)
    grad_cross_key = weight_grad(memory, memory_key_low)
    grad_cross_value = weight_grad(memory, memory_value_low)
    memory_grad = (
        matmul_back(memory_key_low, all_cross_key)
        + matmul_back(memory_value_low, all_cross_value)
    ).astype(jnp.bfloat16)
    two_grad = matmul_back(cross_rows_low, all_cross_query)
    part_two, grad_gain_two = rms_backward(
        first_sum, inverse_two, all_cross_gain.astype(jnp.float32), two_grad
    )
    first_grad = second_grad + part_two
    self_branch = first_grad.astype(jnp.bfloat16)
    grad_self_output = weight_grad(self_att, self_branch)
    self_dout = matmul_back(self_branch, all_self_output).astype(jnp.bfloat16)
    self_heads = split_heads(self_dout)
    self_delta = jnp.einsum(EQ6, self_heads.astype(jnp.float32), self_out)
    self_total_all, self_delta_all = (
        lax.all_gather(self_total, SEQ, axis=2, tiled=True),
        lax.all_gather(self_delta, SEQ, axis=2, tiled=True),
    )
    self_query_fold = query_grad_fold(
        split_heads(queries),
        self_heads,
        self_total,
        self_delta,
        query_seg,
        query_pos,
        token_segment,
        True,
        positions,
    )
    queries_grad = self_query_fold(
        jnp.zeros((row_count, positions, HEADS, head_size), jnp.float32),
        (
            lax.all_gather(key_rows, SEQ, axis=1, tiled=True),
            lax.all_gather(value_rows, SEQ, axis=1, tiled=True),
        ),
        jnp.int32(0),
    )
    queries_low = queries_grad.reshape(row_count, positions, width).astype(jnp.bfloat16)
    self_key_fold = key_grad_fold(
        split_heads(key_rows),
        split_heads(value_rows),
        query_seg,
        query_pos,
        self_total_all,
        self_delta_all,
        token_segment,
        True,
        positions,
    )
    token_zero = jnp.zeros((row_count, positions, HEADS, head_size), jnp.float32)
    key_grad, value_grad = self_key_fold(
        (token_zero, token_zero),
        (
            lax.all_gather(queries, SEQ, axis=1, tiled=True),
            lax.all_gather(self_dout, SEQ, axis=1, tiled=True),
        ),
        jnp.int32(0),
    )
    key_low = key_grad.reshape(row_count, positions, width).astype(jnp.bfloat16)
    value_low = value_grad.reshape(row_count, positions, width).astype(jnp.bfloat16)
    grad_self_query = weight_grad(input_one, queries_low)
    grad_self_key = weight_grad(input_one, key_low)
    grad_self_value = weight_grad(input_one, value_low)
    one_grad = (
        matmul_back(queries_low, all_self_query)
        + matmul_back(key_low, all_self_key)
        + matmul_back(value_low, all_self_value)
    )
    part_one, grad_gain_one = rms_backward(
        values, inverse_one, all_self_gain.astype(jnp.float32), one_grad
    )
    tokens_grad = (first_grad + part_one).astype(jnp.bfloat16)
    summed = tuple(
        (
            lax.psum_scatter(grad_gain_one, BOTH, scatter_dimension=0, tiled=True),
            lax.psum_scatter(grad_self_query, BOTH, scatter_dimension=0, tiled=True),
            lax.psum_scatter(grad_self_key, BOTH, scatter_dimension=0, tiled=True),
            lax.psum_scatter(grad_self_value, BOTH, scatter_dimension=0, tiled=True),
            lax.psum_scatter(grad_self_output, BOTH, scatter_dimension=0, tiled=True),
            lax.psum_scatter(grad_gain_two, BOTH, scatter_dimension=0, tiled=True),
            lax.psum_scatter(grad_cross_query, BOTH, scatter_dimension=0, tiled=True),
            lax.psum_scatter(grad_cross_key, BOTH, scatter_dimension=0, tiled=True),
            lax.psum_scatter(grad_cross_value, BOTH, scatter_dimension=0, tiled=True),
            lax.psum_scatter(grad_cross_output, BOTH, scatter_dimension=0, tiled=True),
            lax.psum_scatter(grad_gain_three, BOTH, scatter_dimension=0, tiled=True),
            lax.psum_scatter(grad_gate, BOTH, scatter_dimension=0, tiled=True),
            lax.psum_scatter(grad_up, BOTH, scatter_dimension=0, tiled=True),
            lax.psum_scatter(grad_down, BOTH, scatter_dimension=0, tiled=True),
        )
    )
    return (layer_out, tokens_grad, memory_grad) + summed


MESH = pl.DeviceIdType.MESH
BF = jnp.bfloat16
F32 = jnp.float32
QW = 1152
VMEM_LIMIT = 60 * 1024 * 1024


def coords():
    r = lax.axis_index(ROW)
    s = lax.axis_index(SEQ)
    return lax.div(r, 2), lax.rem(r, 2), lax.rem(s, 2), lax.div(s, 2)


def dev(x, c, y, z):
    return {ROW: 2 * x + c, SEQ: 2 * z + y}


def remote(src, dst, send_sem, recv_sem, to):
    return pltpu.make_async_remote_copy(
        src_ref=src,
        dst_ref=dst,
        send_sem=send_sem,
        recv_sem=recv_sem,
        device_id=dev(*to),
        device_id_type=MESH,
    )


def owner_of(x, c, y, z):
    return lax.rem(z, 2), lax.div(z, 2), y, 2 * c + x


def is_fixed(x, c, y, z):
    return 2 * c + x == z


def greet(me, pairs=(), z_line=False, moves=False):
    x, c, y, z = me
    bar = pltpu.get_barrier_semaphore()

    def hello(to):
        pl.semaphore_signal(bar, 1, device_id=dev(*to), device_id_type=MESH)

    count = len(pairs)
    for to in pairs:
        hello(to)
    if z_line:

        @pl.when(z > 0)
        def _():
            hello((x, c, y, z - 1))

        @pl.when(z < 3)
        def _():
            hello((x, c, y, z + 1))

        count = count + jnp.where(z > 0, 1, 0) + jnp.where(z < 3, 1, 0)
    if moves:
        away = jnp.logical_not(is_fixed(*me))

        @pl.when(away)
        def _():
            hello(owner_of(*me))

        count = count + jnp.where(away, 1, 0)
    pl.semaphore_wait(bar, count)


class Move:
    def __init__(self, me, src, dst, sems):
        self.far = remote(src, dst, sems.at[0], sems.at[1], owner_of(*me))
        self.near = pltpu.make_async_copy(src, dst, sems.at[0])
        self.fixed = is_fixed(*me)

    def start(self):
        @pl.when(self.fixed)
        def _():
            self.near.start()

        @pl.when(jnp.logical_not(self.fixed))
        def _():
            self.far.start()

    def arrive(self):
        @pl.when(self.fixed)
        def _():
            self.near.wait()

        @pl.when(jnp.logical_not(self.fixed))
        def _():
            self.far.wait_recv()

    def finish(self):
        @pl.when(jnp.logical_not(self.fixed))
        def _():
            self.far.wait_send()


class Gather4:
    def __init__(self, me, buf, sems, tokens=False):
        x, c, y, z = me
        xp, cp = (1 - x, c, y, z), (x, 1 - c, y, z)
        g = x + 2 * c if tokens else 2 * x + c
        far = 1 - x + 2 * c if tokens else 2 * (1 - x) + c
        self.x_own = remote(buf.at[g], buf.at[g], sems.at[0], sems.at[1], xp)
        self.c_own = remote(buf.at[g], buf.at[g], sems.at[0], sems.at[2], cp)
        self.c_far = remote(buf.at[far], buf.at[far], sems.at[0], sems.at[3], cp)

    def start(self):
        self.x_own.start()
        self.c_own.start()

    def forward(self):
        self.x_own.wait_recv()
        self.c_far.start()

    def arrive(self):
        self.c_own.wait_recv()
        self.c_far.wait_recv()

    def finish(self):
        self.x_own.wait_send()
        self.c_own.wait_send()
        self.c_far.wait_send()


class Gather8:
    def __init__(self, me, buf, sems, split=False):
        x, c, y, z = me
        xp, cp, yp = (1 - x, c, y, z), (x, 1 - c, y, z), (x, c, 1 - y, z)
        def piece(px, pc, py):
            return buf.at[2 * (px + 2 * pc) + py]

        def send(p, k, to):
            return remote(p, p, sems.at[0], sems.at[1 + k], to)

        own, at_x = piece(x, c, y), piece(1 - x, c, y)
        at_y, at_d = piece(x, c, 1 - y), piece(1 - x, c, 1 - y)
        self.x_own = send(own, 0, xp)
        self.y_own = send(own, 1, yp)
        self.c_own = send(own, 2, cp)
        self.c_x = send(at_x, 3, cp)
        self.c_y = send(at_y, 4, cp)
        self.c_d = send(at_d, 5, cp)
        self.d_by_x = send(at_y, 6, xp)
        self.d_by_y = send(at_x, 6, yp)
        self.by_y = jnp.logical_and(c == 0, split)

    def start(self):
        self.start_x()
        self.start_y()

    def start_x(self):
        self.x_own.start()
        self.c_own.start()

    def start_y(self):
        self.y_own.start()

    def forward(self):
        self.y_own.wait_recv()

        @pl.when(jnp.logical_not(self.by_y))
        def _():
            self.d_by_x.start()

        self.c_y.start()
        self.x_own.wait_recv()

        @pl.when(self.by_y)
        def _():
            self.d_by_y.start()

        self.c_x.start()

    def forward_far(self):
        self.d_by_x.wait_recv()
        self.c_d.start()

    def arrive(self):
        for one in (self.c_own, self.c_x, self.c_y, self.c_d):
            one.wait_recv()

    def finish(self):
        for one in (self.x_own, self.y_own, self.c_own, self.c_x, self.c_y, self.c_d, self.d_by_x):
            one.wait_send()


QB = 256


def dot(a, b):
    return lax.dot_general(a, b, (((1,), (0,)), ((), ())), preferred_element_type=F32)


def dot_nt(a, b):
    return lax.dot_general(a, b, (((1,), (1,)), ((), ())), preferred_element_type=F32)


def dot_tn(a, b):
    return lax.dot_general(a, b, (((0,), (0,)), ((), ())), preferred_element_type=F32)


def masked(scores, info, lanes, causal):
    keys = scores.shape[0]
    if causal:
        pos = lax.broadcasted_iota(jnp.int32, scores.shape, 0)
        allowed = jnp.logical_and(pos >= info[1:2, lanes], pos <= info[0:1, lanes])
        return jnp.where(allowed, scores, NEG)
    plot = info[2:3, lanes]
    half = keys // 2
    low = jnp.where(plot == 0, 0.0, NEG)
    high = jnp.where(plot == 1, 0.0, NEG)
    return jnp.concatenate([scores[:half] + low, scores[half:] + high], axis=0)


class GatherPlane:
    def __init__(self, me, buf, sems, lanes=None):
        x, c, y, z = me

        def send(p, k, to):
            piece = buf.at[2 * p + y] if lanes is None else buf.at[2 * p + y, :, lanes]
            return remote(piece, piece, sems.at[0], sems.at[1 + k], to)

        yp = (x, c, 1 - y, z)
        self.along = [send(z, k - 1, (x, c, y, lax.rem(z + k, 4))) for k in (1, 2, 3)]
        self.across = [send(z, 3, yp)]
        self.across += [send(lax.rem(z + 4 - k, 4), 3 + k, yp) for k in (1, 2, 3)]

    def start_along(self):
        for one in self.along:
            one.start()

    def start_across(self):
        self.across[0].start()

    def forward(self, k):
        self.along[k - 1].wait_recv()
        self.across[k].start()

    def arrive(self):
        for one in self.across:
            one.wait_recv()

    def finish(self):
        for one in self.along + self.across:
            one.wait_send()


class GatherRelay:
    def __init__(self, me, buf, sems, lanes=None):
        self.me, self.buf, self.sems, self.lanes = me, buf, sems, lanes

    def piece(self, p, y):
        return self.buf.at[2 * p + y] if self.lanes is None else self.buf.at[2 * p + y, :, self.lanes]

    def send(self, p, k, to):
        piece = self.piece(p, self.me[2])
        return remote(piece, piece, self.sems.at[0], self.sems.at[1 + k + p], to)

    def up(self, p):
        x, c, y, z = self.me
        return self.send(p, 0, (x, c, y, z + 1))

    def down(self, p):
        x, c, y, z = self.me
        return self.send(p, 4, (x, c, y, z - 1))

    def across(self, p):
        x, c, y, z = self.me
        return self.send(p, 8, (x, c, 1 - y, z))

    def start_along(self):
        z = self.me[3]

        @pl.when(z < 3)
        def _():
            self.up(z).start()

        @pl.when(z > 0)
        def _():
            self.down(z).start()

    def start_across(self):
        self.across(self.me[3]).start()

    def forward(self, k):
        z = self.me[3]

        @pl.when(z - k >= 0)
        def _():
            p = z - k
            self.up(p).wait_recv()
            if k < 3:

                @pl.when(z < 3)
                def _():
                    self.up(p).start()

            self.across(p).start()

        @pl.when(z + k <= 3)
        def _():
            p = z + k
            self.down(p).wait_recv()
            if k < 3:

                @pl.when(z > 0)
                def _():
                    self.down(p).start()

            self.across(p).start()

    def arrive(self):
        for p in range(4):
            self.across(p).wait_recv()

    def finish(self):
        z = self.me[3]
        for p in range(4):
            self.across(p).wait_send()

            @pl.when(jnp.logical_and(z < 3, p <= z))
            def _():
                self.up(p).wait_send()

            @pl.when(jnp.logical_and(z > 0, p >= z))
            def _():
                self.down(p).wait_send()


class SumPlane:
    def __init__(self, me, parts, by_y, by_z, sems, lanes=None):
        self.me, self.parts, self.by_y, self.by_z, self.sems = me, parts, by_y, by_z, sems
        self.lanes = slice(None) if lanes is None else lanes

    def mine(self, p):
        return self.parts.at[2 * p + self.me[2], :, self.lanes]

    def from_y(self, p):
        return self.by_y.at[p, :, self.lanes]

    def slot(self, k):
        return self.by_z.at[k, :, self.lanes]

    def across(self, p):
        x, c, y, z = self.me
        theirs = self.parts.at[2 * p + 1 - y, :, self.lanes]
        return remote(theirs, self.from_y(p), self.sems.at[0], self.sems.at[1 + p], (x, c, 1 - y, z))

    def up_slot(self, p):
        return self.slot(p - 1)

    def down_slot(self, q):
        return self.slot(lax.rem(3 + q, 5))

    def up(self, p):
        x, c, y, z = self.me
        send, recv = self.sems.at[0], self.sems.at[4 + p]
        return remote(self.mine(p), self.up_slot(p), send, recv, (x, c, y, z + 1))

    def down(self, q):
        x, c, y, z = self.me
        send, recv = self.sems.at[0], self.sems.at[5 + lax.rem(3 + q, 5)]
        return remote(self.mine(q), self.down_slot(q), send, recv, (x, c, y, z - 1))

    def start(self):
        for p in (3, 0, 2, 1):
            self.across(p).start()

    def fold(self, steps=(3, 0, 2, 1)):
        z = self.me[3]
        for p in steps:
            self.across(p).wait_recv()
            add_into(self.mine(p), self.from_y(p))
            if p > 0:

                @pl.when(z == 0)
                def _():
                    self.up(p).start()

            if p < 3:

                @pl.when(z == 3)
                def _():
                    self.down(p).start()

    def relay_up(self, p):
        self.up(p).wait_recv()
        add_into(self.mine(p), self.up_slot(p))
        self.up(p).start()

    def relay_down(self, q):
        self.down(q).wait_recv()
        add_into(self.mine(q), self.down_slot(q))
        self.down(q).start()

    def pass_one(self):
        z = self.me[3]

        @pl.when(z == 1)
        def _():
            self.relay_up(3)
            self.relay_up(2)

        @pl.when(z == 2)
        def _():
            self.relay_down(0)
            self.relay_down(1)

    def pass_two(self):
        z = self.me[3]

        @pl.when(z == 2)
        def _():
            self.relay_up(3)

        @pl.when(z == 1)
        def _():
            self.relay_down(0)

    def end(self):
        z = self.me[3]

        @pl.when(z > 0)
        def _():
            self.up(z).wait_recv()
            add_into(self.mine(z), self.up_slot(z))

        @pl.when(z < 3)
        def _():
            self.down(z).wait_recv()
            add_into(self.mine(z), self.down_slot(z))

    def finish(self):
        z = self.me[3]
        for p in range(4):
            self.across(p).wait_send()

            @pl.when(z < p)
            def _():
                self.up(p).wait_send()

            @pl.when(z > p)
            def _():
                self.down(p).wait_send()


class SumPlaneDirect(SumPlane):
    def straight(self, k):
        x, c, y, z = self.me
        p = lax.rem(z + k, 4)
        send, recv = self.sems.at[0], self.sems.at[4 + k]
        return remote(self.mine(p), self.slot(k - 1), send, recv, (x, c, y, p))

    def start(self):
        for k in (2, 1, 3, 0):
            self.across(lax.rem(self.me[3] + k, 4)).start()

    def fold(self, steps=(2, 1, 3, 0)):
        for k in steps:
            p = lax.rem(self.me[3] + k, 4)
            self.across(p).wait_recv()
            add_into(self.mine(p), self.from_y(p))
            if k:
                self.straight(k).start()

    def pass_one(self):
        pass

    def pass_two(self):
        pass

    def end(self):
        for k in (1, 2, 3):
            self.straight(k).wait_recv()
            add_into(self.mine(self.me[3]), self.slot(k - 1))

    def finish(self):
        for p in range(4):
            self.across(p).wait_send()
        for k in (1, 2, 3):
            self.straight(k).wait_send()


class Sum8:
    def __init__(self, me, parts, by_c, by_x, by_y, sems):
        x, c, y, z = me
        self.me, self.parts = me, parts
        self.by_c, self.by_x, self.by_y = by_c, by_x, by_y
        xp, cp, yp = (1 - x, c, y, z), (x, 1 - c, y, z), (x, c, 1 - y, z)

        def send(src, dst, k, to):
            return remote(src, dst, sems.at[0], sems.at[1 + k], to)

        self.order = [(1 - x, 1 - y), (1 - x, y), (x, 1 - y), (x, y)]
        self.first = [
            send(parts.at[2 * (px + 2 * (1 - c)) + py], by_c.at[px, py], k, cp)
            for k, (px, py) in enumerate(self.order)
        ]
        self.second = [
            send(by_c.at[1 - x, py], by_x.at[py], 4 + k, xp) for k, py in enumerate((1 - y, y))
        ]
        self.third = send(by_x.at[1 - y], by_y, 6, yp)

    def start(self):
        for one in self.first:
            one.start()

    def to_x(self):
        x, c, y, z = self.me
        for k, py in enumerate((1 - y, y)):
            self.first[k].wait_recv()
            add_into(self.by_c.at[1 - x, py], self.parts.at[2 * (1 - x + 2 * c) + py])
            self.second[k].start()

    def to_y(self):
        x, c, y, z = self.me
        self.first[2].wait_recv()
        self.first[3].wait_recv()
        add_into(self.by_c.at[x, 1 - y], self.parts.at[2 * (x + 2 * c) + 1 - y])
        self.second[0].wait_recv()
        add_into(self.by_x.at[1 - y], self.by_c.at[x, 1 - y])
        self.third.start()

    def end(self):
        x, c, y, z = self.me
        self.second[1].wait_recv()
        self.third.wait_recv()
        return (
            self.parts[2 * (x + 2 * c) + y].astype(F32)
            + self.by_c[x, y].astype(F32)
            + self.by_x[y].astype(F32)
            + self.by_y[...].astype(F32)
        )

    def finish(self):
        for one in self.first + self.second + [self.third]:
            one.wait_send()


class Sum4:
    def __init__(self, me, parts, by_c, by_x, sems):
        x, c, y, z = me
        self.me, self.parts, self.by_c, self.by_x = me, parts, by_c, by_x
        xp, cp = (1 - x, c, y, z), (x, 1 - c, y, z)
        self.first = [
            remote(parts.at[px + 2 * (1 - c)], by_c.at[px], sems.at[0], sems.at[1 + px], cp)
            for px in range(2)
        ]
        self.second = remote(by_c.at[1 - x], by_x, sems.at[0], sems.at[3], xp)

    def start(self):
        for one in self.first:
            one.start()

    def to_x(self):
        x, c, y, z = self.me
        for one in self.first:
            one.wait_recv()
        add_into(self.by_c.at[1 - x], self.parts.at[1 - x + 2 * c])
        self.second.start()

    def end(self):
        x, c, y, z = self.me
        self.second.wait_recv()
        return (
            self.parts[x + 2 * c].astype(F32)
            + self.by_c[x].astype(F32)
            + self.by_x[...].astype(F32)
        )

    def finish(self):
        for one in self.first + [self.second]:
            one.wait_send()


def chunks(rows, step, run):
    def one(i, carry):
        run(pl.ds(pl.multiple_of(i * step, step), step))
        return carry

    lax.fori_loop(0, rows // step, one, 0)


def add_into(into, more, step=16):
    def run(rows):
        total = into[rows, :].astype(F32) + more[rows, :].astype(F32)
        into[rows, :] = total.astype(into.dtype)

    chunks(into.shape[0], step, run)


def dma(*shape):
    return pltpu.SemaphoreType.DMA(shape)


ANYWHERE = pl.BlockSpec(memory_space=pl.ANY)
IN_VMEM = pl.BlockSpec(memory_space=pltpu.VMEM)


def attend_head(h, info, qt, kv, kvt, out, lse, causal):
    keys = kv.shape[0]
    rows = slice(64 * h, 64 * h + 64)
    for b in range(512 // QB):
        lanes = slice(QB * b, QB * b + QB)
        top = keys * (b + 1) * QB // 512 if causal else keys
        scores = dot(kv[:top, rows], qt[rows, lanes])
        scores = masked(scores, info, lanes, causal)
        high = jnp.max(scores, axis=0, keepdims=True)
        weights = jnp.exp(scores - high)
        total = jnp.sum(weights, axis=0, keepdims=True)
        out[rows, lanes] = dot(kvt[192 + 64 * h : 256 + 64 * h, :top], weights.astype(BF)) / total
        lse[h : h + 1, lanes] = high + jnp.log(total)


def attend_back_head(h, info, qt, kv, kvt, outer_t, out, lse, dq, dkv, dk_acc, dv_acc, causal):
    keys = kv.shape[0]
    rows = slice(64 * h, 64 * h + 64)
    value_rows = slice(192 + 64 * h, 256 + 64 * h)
    for b in reversed(range(512 // QB)):
        lanes = slice(QB * b, QB * b + QB)
        top = keys * (b + 1) * QB // 512 if causal else keys
        query, outer = qt[rows, lanes], outer_t[rows, lanes]
        delta = jnp.sum(outer.astype(F32) * out[rows, lanes], axis=0, keepdims=True)
        scores = masked(dot(kv[:top, rows], query), info, lanes, causal)
        prob = jnp.exp(scores - lse[h : h + 1, lanes])
        grad = (prob * (dot(kv[:top, value_rows], outer) - delta)).astype(BF)
        dq[rows, lanes] = (SCALE * dot(kvt[rows, :top], grad)).astype(BF)
        dk_new = dot_nt(query, grad)
        dv_new = dot_nt(outer, prob.astype(BF))
        if b == 512 // QB - 1:
            dk_acc[...] = dk_new
            dv_acc[...] = dv_new
        else:
            dk_acc[:, :top] += dk_new
            dv_acc[:, :top] += dv_new
    dkv[rows, :] = dk_acc[...].astype(BF)
    dkv[value_rows, :] = dv_acc[...].astype(BF)


def norm(values, gain):
    inverse = lax.rsqrt(jnp.mean(values * values, axis=-1, keepdims=True) + EPS)
    return (values * inverse * gain).astype(BF)


def norm_back(values, gain, upstream):
    inverse = lax.rsqrt(jnp.mean(values * values, axis=-1, keepdims=True) + EPS)
    normed = values * inverse
    scaled = upstream * gain
    grad = inverse * (scaled - normed * jnp.mean(scaled * normed, axis=-1, keepdims=True))
    return grad, jnp.sum(upstream * normed, axis=0, keepdims=True)


def gelu_parts(u):
    root = 0.7978845608028654
    square = u * u
    bend = jnp.tanh(root * u * (1.0 + 0.044715 * square))
    half = 0.5 * (1.0 + bend)
    slope = half + 0.5 * u * (1.0 - bend * bend) * (root * (1.0 + 0.134145 * square))
    return u * half, slope


class Names:
    pass


FETCHED = ("sk", "sv", "sq", "ck", "cv", "so", "co", "cq", "gate", "up")


def layer_kernel(names, *refs):
    R = Names()
    for name, ref in zip(names, refs, strict=True):
        setattr(R, name, ref)
    me = coords()
    x, c, y, z = me
    g = 2 * x + c
    t = x + 2 * c
    s = 2 * z + y
    group = ((1 - x, c, y, z), (1 - x, 1 - c, y, z), (x, 1 - c, y, z))
    line = tuple((x, c, y, lax.rem(z + k, 4)) for k in (1, 2, 3))
    fetch = [
        pltpu.make_async_copy(getattr(R, name), getattr(R, "v_" + name), R.s_fetch.at[i])
        for i, name in enumerate(FETCHED)
    ]
    for one in fetch:
        one.start()
    near_dn = pltpu.make_async_copy(R.down, R.DN.at[s], R.s_near.at[0])
    near_dn.start()
    greet(me, group + line + ((x, c, 1 - y, z),), moves=True)

    move_x = Move(me, R.tok, R.X.at[s], R.s_move.at[0])
    move_t = Move(me, R.tabs, R.TAB, R.s_move.at[1])
    move_m = Move(me, R.mem, R.M.at[s], R.s_move.at[2])
    move_d = Move(me, R.dout, R.DO.at[z], R.s_move.at[3])
    for one in fetch[:5]:
        one.wait()
    row = lax.broadcasted_iota(jnp.int32, (8, 128), 0)
    gains = jnp.zeros((8, 128), F32)
    for i, one in enumerate((R.g1, R.g2, R.g3)):
        one = jnp.concatenate([one[...].astype(F32), jnp.zeros((1, 104), F32)], axis=1)
        gains = jnp.where(row == i, one, gains)
    gains = jnp.concatenate([gains, jnp.zeros((120, 128), F32)], axis=0).T[:24, :64]
    blank = jnp.zeros((24, 64), F32)
    for k in range(4):
        narrow = slice(192 * k, 192 * k + 192)
        row = [w[:, narrow].astype(F32) for w in (R.v_sk, R.v_sv, R.v_sq)] + [gains]
        row = jnp.concatenate(row + [w[:, narrow].astype(F32) for w in (R.v_ck, R.v_cv)], axis=1)
        R.stage_a[k] = jnp.concatenate([row[:, :512], row[:, 512:]], axis=0).astype(BF)

    def to_group(stage, land, sems):
        return [
            remote(stage.at[2 * to[0] + to[1]], land.at[g], sems.at[0], sems.at[1 + i], to)
            for i, to in enumerate(group)
        ]

    parts_a = to_group(R.stage_a, R.land_a, R.s_part_a)
    for one in parts_a:
        one.start()
    move_x.start()
    for i in range(2):
        length, plot = R.lengths[0, i], R.plots[0, i]
        start = R.lengths[0, 0] if i else 0
        R.tabs[i : i + 1, :] = jnp.full((1, 128), start + length, jnp.int32)
        R.tabs[2 + i : 3 + i, :] = jnp.full((1, 128), plot, jnp.int32)
    R.tabs[4:, :] = jnp.zeros((4, 128), jnp.int32)
    move_t.start()

    def halves_stacked(w):
        w = w[...].astype(F32)
        return jnp.concatenate([w[:, :384], w[:, 384:]], axis=0).astype(BF)

    for one in fetch[5:]:
        one.wait()
    for k in range(4):
        wide = slice(512 * k, 512 * k + 512)
        R.stage_b[k, :24] = R.v_gate[:, wide]
        R.stage_b[k, 24:] = R.v_up[:, wide]
    R.land_a[g] = R.stage_a[g]
    R.land_b[g] = R.stage_b[g]
    gather_x = Gather8(me, R.X, R.s_x, True)
    gather_m = Gather8(me, R.M, R.s_m, True)
    gather_d = Gather4(me, R.DO, R.s_d, tokens=True)
    gather_a = GatherPlane(me, R.PA, R.s_a)
    gather_b = GatherPlane(me, R.PB, R.s_b, slice(0, 384))
    gather_o = GatherPlane(me, R.FO.at[g], R.s_fo)
    gather_c = GatherPlane(me, R.FC.at[g], R.s_fc)
    gather_q = GatherPlane(me, R.FQ.at[g], R.s_fq)
    gather_2 = GatherRelay(me, R.P2, R.s_2)
    gather_n = GatherRelay(me, R.DN, R.s_n)
    whole_o = Gather4(me, R.FO, R.s_wo)
    whole_c = Gather4(me, R.FC, R.s_wc)
    whole_q = Gather4(me, R.FQ, R.s_wq)

    R.FO[g, s] = halves_stacked(R.v_so)
    gather_o.start_along()
    gather_o.start_across()
    R.FQ[g, s] = halves_stacked(R.v_cq)
    R.FC[g, s] = halves_stacked(R.v_co)
    for one in parts_a:
        one.wait_recv()
    whole = []
    for r in range(4):
        piece = R.land_a[r].astype(F32)
        whole.append(jnp.concatenate([piece[:24], piece[24:]], axis=1))
    whole = jnp.concatenate(whole, axis=0).astype(BF)
    R.PA[s] = whole[:, :640]
    R.PB[s, :, :384] = whole[:, 640:]
    gather_a.start_across()
    move_x.arrive()
    gather_x.start()
    gather_a.start_along()
    parts_b = to_group(R.stage_b, R.land_b, R.s_part_b)
    for one in parts_b:
        one.start()
    move_m.start()
    gather_b.start_along()
    gather_q.start_along()
    gather_c.start_along()
    move_d.start()
    for k in (1, 3, 2):
        gather_o.forward(k)
    gather_a.forward(1)
    gather_x.forward()
    gather_b.start_across()
    for one in parts_b:
        one.wait_recv()
    for half in range(2):
        rows = [R.land_b[r].astype(F32)[24 * half : 24 * half + 24] for r in range(4)]
        R.P2[s, :, 512 * half : 512 * half + 512] = jnp.concatenate(rows, axis=0).astype(BF)
    gather_2.start_along()
    near_dn.wait()
    gather_x.forward_far()
    gather_o.arrive()
    whole_o.start()
    gather_a.forward(3)
    gather_a.forward(2)
    gather_q.start_across()
    gather_c.start_across()
    move_t.arrive()
    end_one, end_two = R.TAB[0:1, 0:1], R.TAB[1:2, 0:1]
    plot_one, plot_two = R.TAB[2:3, 0:1], R.TAB[3:4, 0:1]
    lane = lax.broadcasted_iota(jnp.int32, (1, 512), 1)
    for i in range(4):
        lanes = slice(128 * i, 128 * i + 128)
        R.info[0:1, lanes] = lane[:, :128] + (2 * i + y) * 128
    qpos = R.info[0:1, :]
    past_one, past_two = qpos >= end_one, qpos >= end_two
    R.info[1:2, :] = jnp.where(past_two, end_two, jnp.where(past_one, end_one, 0))
    R.info[2:3, :] = jnp.where(past_two, 0, jnp.where(past_one, plot_two, plot_one))

    def unpack(pieces, whole, width, step):
        for zz in range(4):

            def one(i, carry):
                lanes = pl.ds(pl.multiple_of(i * step, step), step)
                low = pieces[2 * zz, :, lanes].astype(F32)
                high = pieces[2 * zz + 1, :, lanes].astype(F32)
                for r in range(4):
                    rows = slice(24 * r, 24 * r + 24)
                    both = jnp.concatenate([low[rows], high[rows]], axis=0)
                    whole[192 * r + 48 * zz : 192 * r + 48 * zz + 48, lanes] = both.astype(BF)
                return carry

            lax.fori_loop(0, width // step, one, 0)

    gather_a.arrive()
    unpack(R.PA, R.WA, 640, 128)
    gain_rows = R.WA[:, 512:640].astype(F32).T
    gain_one, gain_two, gain_three = (gain_rows[64 + i : 65 + i] for i in range(3))

    def pair_rows(buf, i):
        return jnp.concatenate([buf[2 * i], buf[2 * i + 1]], axis=0)

    def mine_rows(buf):
        return jnp.concatenate([buf[2 * i + y] for i in range(4)], axis=0)

    def keys_values(i, operand, weight, natural, turned):
        rows = pl.ds(pl.multiple_of(i * 256, 256), 256)
        product = dot(operand, weight[:, :384])
        natural[rows, :] = product.astype(BF)
        turned[:, rows] = product.T.astype(BF)

    def first_norm(i, carry):
        x1 = norm(pair_rows(R.X, i).astype(F32), gain_one)
        R.X1[2 * i] = x1[:128]
        R.X1[2 * i + 1] = x1[128:]
        keys_values(i, x1, R.WA, R.KV, R.KVT)
        return carry

    gather_x.arrive()
    lax.fori_loop(0, 4, first_norm, 0)
    product = SCALE * dot(mine_rows(R.X1), R.WA[:, 384:640])
    R.QT[...] = product.T[:192].astype(BF)

    def share_heads(buf, sems):
        return [Gather4(me, buf.at[:, h], sems.at[h]) for h in range(3)]

    share_1 = share_heads(R.A4, R.s_share1)
    move_m.arrive()
    gather_m.start()
    for h in range(3):
        attend_head(h, R.info, R.QT, R.KV, R.KVT, R.OUT1, R.LSE1, True)
        R.A4[g, h] = R.OUT1[64 * h : 64 * h + 64, :].astype(BF)
        share_1[h].start()
    for k in (1, 3, 2):
        gather_b.forward(k)
    for k in (1, 3, 2):
        gather_q.forward(k)
    whole_o.forward()
    for h in range(3):
        share_1[h].forward()
    gather_m.forward()
    for k in (1, 3, 2):
        gather_c.forward(k)
    gather_2.forward(1)
    gather_n.start_along()
    gather_2.start_across()
    gather_n.start_across()
    whole_o.arrive()

    def unpack_full(pieces, whole):
        def one(r, carry):
            for zz in range(4):
                low, high = pieces[r, 2 * zz].astype(F32), pieces[r, 2 * zz + 1].astype(F32)
                rows = pl.ds(pl.multiple_of(192 * r + 48 * zz, 16), 48)
                whole[rows, :384] = jnp.concatenate([low[:24], high[:24]], axis=0).astype(BF)
                whole[rows, 384:] = jnp.concatenate([low[24:], high[24:]], axis=0).astype(BF)
            return carry

        lax.fori_loop(0, 4, one, 0)

    unpack_full(R.FO, R.WO)
    for one in share_1:
        one.arrive()

    def project(pieces, weight, i):
        lanes = slice(256 * i, 256 * i + 256)
        turned = pieces[:, :, :, lanes].astype(F32).reshape(768, 256)
        return dot(turned.T.astype(BF), weight[...])

    for i in range(2):
        rows = slice(256 * i, 256 * i + 256)
        before = jnp.concatenate([R.X[4 * i + y], R.X[4 * i + 2 + y]], axis=0).astype(F32)
        first = before + project(R.A4, R.WO, i)
        R.FIRST[rows, :] = first
        R.X2[rows, :] = norm(first, gain_two)
    gather_q.arrive()
    whole_q.start()
    gather_m.forward_far()
    gather_b.arrive()
    unpack(R.PB, R.WB, 384, 128)
    gather_c.arrive()
    whole_c.start()
    move_d.arrive()
    gather_m.arrive()

    def memory_pair(i, carry):
        keys_values(i, pair_rows(R.M, i), R.WB, R.MKV, R.MKVT)
        return carry

    lax.fori_loop(0, 4, memory_pair, 0)
    gather_2.forward(2)
    gather_n.forward(1)
    whole_q.forward()
    whole_q.arrive()
    unpack_full(R.FQ, R.WQ)
    for k in range(4):

        @pl.when(g == k)
        def _():
            R.WCQ[...] = R.WQ[:, 192 * k : 192 * k + 192]

    for i in range(2):
        rows = slice(256 * i, 256 * i + 256)
        product = SCALE * dot(R.X2[rows, :], R.WCQ[...])
        R.CQT[:, rows] = product.T.astype(BF)
    share_2 = share_heads(R.C4, R.s_share2)
    for h in range(3):
        attend_head(h, R.info, R.CQT, R.MKV, R.MKVT, R.OUT2, R.LSE2, False)
        R.C4[g, h] = R.OUT2[64 * h : 64 * h + 64, :].astype(BF)
        share_2[h].start()
    gather_d.start()
    whole_c.forward()
    gather_2.forward(3)
    gather_n.forward(2)
    for h in range(3):
        share_2[h].forward()
    gather_n.forward(3)
    whole_c.arrive()
    unpack_full(R.FC, R.WC)
    for one in share_2:
        one.arrive()
    for i in range(2):
        rows = slice(256 * i, 256 * i + 256)
        second = R.FIRST[rows, :] + project(R.C4, R.WC, i)
        R.SECOND[rows, :] = second
        R.X3[rows, :] = norm(second, gain_three)
    gather_d.forward()
    gather_2.arrive()
    unpack(R.P2, R.W2, 1024, 256)
    for one in parts_a + parts_b:
        one.wait_send()
    gather_2.finish()
    gather_a.finish()
    gather_b.finish()
    gather_d.arrive()
    gather_n.arrive()

    sum_dx = Sum4(me, R.DXP, R.by_c_dx, R.by_x_dx, R.s_dx)
    sum_out = Sum4(me, R.OP, R.by_c_out, R.by_x_out, R.s_out)

    def feed(core):
        at = pl.ds(pl.multiple_of(core * 256, 256), 256)
        x3 = R.X3[at, :]
        gate, up = dot(x3, R.W2[:, :512]), dot(x3, R.W2[:, 512:])
        active, slope = gelu_parts(gate)
        hidden = (active * up).astype(BF)
        outer = jnp.concatenate([R.DO[2 * core + px] for px in range(2)], axis=0)
        w_down = R.DN[...].reshape(512, 768)
        hidden_grad = dot_nt(outer, w_down)
        gate_grad = (hidden_grad * up * slope).astype(BF)
        up_grad = (hidden_grad * active).astype(BF)
        dx3 = (dot_nt(gate_grad, R.W2[:, :512]) + dot_nt(up_grad, R.W2[:, 512:])).astype(BF)
        out = dot(hidden, w_down).astype(BF)
        R.H[at, :] = hidden
        R.GG[at, :512] = gate_grad
        R.GG[at, 512:] = up_grad
        for px in range(2):
            half = slice(128 * px, 128 * px + 128)
            R.DXP[2 * core + px] = dx3[half]
            R.OP[2 * core + px] = out[half]

    def pack(whole, pieces, start, width):
        for t in range(8):
            rows = [whole[(8 * r + t) * 24 : (8 * r + t) * 24 + 24, :] for r in range(4)]
            pieces[t, :, start : start + width] = jnp.concatenate(rows, axis=0).astype(BF)

    feed(1 - c)
    sum_dx.start()
    feed(c)
    sum_dx.to_x()
    sum_out.start()
    own = pl.ds(pl.multiple_of(t * 128, 128), 128)
    own_block = 2 * t + y
    x3_t = R.X3[...].astype(F32).T.astype(BF)
    total_2 = [
        SumPlaneDirect(me, R.P2, R.by_y_2, R.by_z_2, R.s_g2.at[i], slice(256 * i, 256 * i + 256))
        for i in range(4)
    ]
    for i in range(4):
        R.W2G[...] = dot(x3_t, R.GG[:, 256 * i : 256 * i + 256])
        pack(R.W2G, R.P2, 256 * i, 256)
        total_2[i].start()
    hidden_t = R.H[...].astype(F32).T.astype(BF)
    d_down = dot(hidden_t, R.DO[...].reshape(512, 768)).astype(BF)
    for i in range(8):
        R.DNG[i] = d_down[64 * i : 64 * i + 64]
    total_n = SumPlaneDirect(me, R.DNG, R.by_y_n, R.by_z_n, R.s_gn)
    total_n.start()
    part, gain_grad_three = norm_back(R.SECOND[own, :], gain_three, sum_dx.end())
    second_grad = R.DO[t].astype(F32) + part
    R.SGRAD[...] = second_grad
    R.DS4[t] = second_grad.astype(BF)
    share_s = Gather4(me, R.DS4, R.s_s, tokens=True)
    share_s.start()
    total_2[0].fold()
    share_s.forward()
    sum_out.to_x()
    total_2[1].fold()
    total_2[0].pass_one()
    share_s.arrive()

    dsec = R.DS4[...].reshape(512, 768)
    mine_192 = pl.ds(pl.multiple_of(g * 192, 16), 192)
    R.OUTER[...] = dot_nt(R.WC[mine_192, :], dsec).astype(BF)
    share_3 = share_heads(R.DC4, R.s_share3)
    for h in range(3):
        attend_back_head(
            h, R.info, R.CQT, R.MKV, R.MKVT, R.OUTER, R.OUT2, R.LSE2, R.DCQT, R.MDKV, R.dk, R.dv, False
        )
        R.DC4[g, h] = R.DCQT[64 * h : 64 * h + 64, :]
        share_3[h].start()
        if h == 0:
            total_2[2].fold()
        if h == 1:
            share_3[0].forward()
            total_2[0].pass_two()

    def pack_24(whole, pieces):
        for t in range(8):
            rows = whole[24 * t : 24 * t + 24]
            pieces[t] = jnp.concatenate([rows[:, :384], rows[:, 384:]], axis=0).astype(BF)

    def memory_grad_pair(i, carry):
        lanes = pl.ds(pl.multiple_of(i * 256, 256), 256)
        turned = dot(R.WB[:, :384], R.MDKV[:, lanes]).astype(BF)
        R.MG[2 * i] = turned[:, :128]
        R.MG[2 * i + 1] = turned[:, 128:]
        return carry

    total_2[3].fold()
    total_2[1].pass_one()
    lax.fori_loop(0, 4, memory_grad_pair, 0)
    sum_m = Sum8(me, R.MG, R.by_c_m, R.by_x_m, R.by_y_m, R.s_gm)
    share_3[1].forward()
    pack_24(dot(R.C4[g].reshape(192, 512), dsec), R.CO8)
    total_c = SumPlane(me, R.CO8, R.by_y_c, R.by_z_c, R.s_gc)
    total_c.start()
    R.W1G[...] = dot(R.MDKV[...], R.M[...].reshape(1024, 768)).T
    pack(R.W1G, R.PB, 0, 384)
    total_b = SumPlane(me, R.PB, R.by_y_b, R.by_z_b, R.s_gb, slice(0, 384))
    total_b.start()
    share_3[2].forward()
    sum_m.start()
    back = [
        Move(me, src, dst, R.s_back.at[i])
        for i, (src, dst) in enumerate(
            ((R.TBLOCK, R.tokens_out), (R.LBLOCK, R.layer_out), (R.MBLOCK, R.memory_out))
        )
    ]
    R.LBLOCK[...] = (R.SECOND[own, :] + sum_out.end()).astype(BF)
    back[1].start()
    total_2[2].pass_one()
    total_2[1].pass_two()
    for one in share_3:
        one.arrive()

    for i in range(2):
        rows = slice(256 * i, 256 * i + 256)
        dx2 = dot(R.WQ[...], R.DC4[:, :, :, rows].reshape(768, 256)).T
        part, ignored = norm_back(R.FIRST[rows, :], gain_two, dx2)
        R.DFIRST[rows, :] = (dsec[rows].astype(F32) + part).astype(BF)
    R.OUTER[...] = dot_nt(R.WO[mine_192, :], R.DFIRST[...]).astype(BF)
    sum_m.to_x()
    total_n.fold()
    total_2[3].pass_one()

    for h in range(3):
        attend_back_head(
            h, R.info, R.QT, R.KV, R.KVT, R.OUTER, R.OUT1, R.LSE1, R.DQT, R.DKV, R.dk, R.dv, True
        )

    def token_grad_pair(i, carry):
        lanes = pl.ds(pl.multiple_of(i * 256, 256), 256)
        half = pl.ds(pl.multiple_of(i * 128, 128), 128)
        turned = dot(R.WA[:, :384], R.DKV[:, lanes])
        query = dot(R.WA[:, 384:576], R.DQT[:, half])
        R.TG[2 * i] = (turned[:, :128] + jnp.where(y == 0, query, 0.0)).astype(BF)
        R.TG[2 * i + 1] = (turned[:, 128:] + jnp.where(y == 1, query, 0.0)).astype(BF)
        return carry

    lax.fori_loop(0, 4, token_grad_pair, 0)
    sum_t = Sum8(me, R.TG, R.by_c_t, R.by_x_t, R.by_y_t, R.s_gt)
    sum_t.start()
    pack_24(dot(R.A4[g].reshape(192, 512), R.DFIRST[...]), R.SO8)
    total_s = SumPlane(me, R.SO8, R.by_y_s, R.by_z_s, R.s_gs)
    total_s.start()
    dx2 = dot(R.WQ[...], R.DC4[:, :, :, own].reshape(768, 128)).T
    part, gain_grad_two = norm_back(R.FIRST[own, :], gain_two, dx2)
    R.SGRAD[...] += part
    sum_t.to_x()
    sum_m.to_y()
    total_c.fold()
    total_n.pass_one()
    total_2[2].pass_two()
    R.W1G[...] = dot(R.DKV[...], R.X1[...].reshape(1024, 768)).T
    pack(R.W1G, R.PA, 0, 384)
    total_a = SumPlane(me, R.PA, R.by_y_a, R.by_z_a, R.s_ga, slice(0, 384))
    R.TURN[:192, :] = dot(R.DQT[...], mine_rows(R.X1))
    R.TURN[192:, :] = dot(R.DCQT[...], R.X2[...])
    R.W1G[...] = R.TURN[...].T
    pack(R.W1G, R.PB, 384, 384)
    total_q = SumPlane(me, R.PB, R.by_y_b, R.by_z_b, R.s_gq, slice(384, 768))
    total_b.fold()
    total_2[3].pass_two()
    sum_t.to_y()
    total_a.start()
    total_q.start()
    total_c.pass_one()
    total_n.pass_two()
    total_s.fold()
    total_b.pass_one()
    R.MBLOCK[...] = sum_m.end().T.astype(BF)
    back[2].start()
    dx1 = sum_t.end().T
    part, gain_grad_one = norm_back(R.X[own_block].astype(F32), gain_one, dx1)
    R.TBLOCK[...] = (R.SGRAD[...] + part).astype(BF)
    back[0].start()
    R.GT[0:1, :] = gain_grad_one
    R.GT[1:2, :] = gain_grad_two
    R.GT[2:3, :] = gain_grad_three
    pack(R.GT[...].T, R.PG, 0, 128)
    total_g = SumPlane(me, R.PG, R.by_y_g, R.by_z_g, R.s_gg)
    total_g.start()
    total_c.pass_two()
    total_s.pass_one()
    total_b.pass_two()
    total_a.fold()
    for one in total_2:
        one.end()
    rows_2 = R.P2[s].astype(F32)
    for r in range(4):
        rows = slice(24 * r, 24 * r + 24)
        R.stage_b[r] = jnp.concatenate([rows_2[rows, :512], rows_2[rows, 512:]], axis=0).astype(BF)
    last_b = to_group(R.stage_b, R.quarters_b, R.s_last_b)
    for one in last_b:
        one.start()
    total_n.end()
    total_q.fold()
    total_s.pass_two()
    total_a.pass_one()
    total_g.fold()
    total_c.end()
    total_b.end()
    total_q.pass_one()
    total_a.pass_two()
    total_g.pass_one()
    total_s.end()
    total_q.pass_two()
    total_g.pass_two()
    total_a.end()
    total_q.end()
    total_g.end()
    rows_a, rows_b = R.PA[s, :, :384].astype(F32), R.PB[s].astype(F32)
    rows_g = R.PG[s].astype(F32)
    for r in range(4):
        rows = slice(24 * r, 24 * r + 24)
        top = [rows_a[rows], rows_b[rows, 384:576], rows_g[rows, :64]]
        bottom = [rows_b[rows, :384], rows_b[rows, 576:], blank]
        R.stage_z[r] = jnp.concatenate(
            [jnp.concatenate(top, axis=1), jnp.concatenate(bottom, axis=1)], axis=0
        ).astype(BF)
    last_a = to_group(R.stage_z, R.quarters_a, R.s_last_a)
    for one in last_a:
        one.start()
    near = [
        pltpu.make_async_copy(src, dst, R.s_near.at[1 + i])
        for i, (src, dst) in enumerate(
            (
                (R.stage_z.at[g], R.quarters_a.at[g]),
                (R.stage_b.at[g], R.quarters_b.at[g]),
                (R.CO8.at[s], R.co_out),
                (R.SO8.at[s], R.so_out),
                (R.DNG.at[s], R.down_out),
            )
        )
    ]
    for one in near:
        one.start()
    for one in near:
        one.wait()
    for one in last_a + last_b:
        one.wait_recv()
    for one in back:
        one.arrive()
        one.finish()
    for one in last_a + last_b:
        one.wait_send()
    for one in (move_x, move_t, move_m, move_d):
        one.finish()
    for one in (gather_x, gather_m, gather_d, gather_o, gather_c, gather_q, gather_n):
        one.finish()
    for one in (whole_o, whole_c, whole_q, share_s, sum_dx, sum_out, sum_m, sum_t):
        one.finish()
    for one in share_1 + share_2 + share_3 + total_2:
        one.finish()
    for one in (total_a, total_q, total_g, total_b, total_n, total_c, total_s):
        one.finish()


def run_layer(inputs):
    n, d = 128, 768

    def low(*shape):
        return pltpu.VMEM(shape, BF)

    def full(*shape):
        return pltpu.VMEM(shape, F32)

    outs = dict(
        quarters_a=(4, 48, 640),
        quarters_b=(4, 48, 512),
        co_out=(48, 384),
        so_out=(48, 384),
        down_out=(64, d),
        tokens_out=(n, d),
        layer_out=(n, d),
        memory_out=(n, d),
    )
    scratch = dict(
        stage_a=low(4, 48, 512), land_a=low(4, 48, 512), stage_z=low(4, 48, 640), stage_b=low(4, 48, 512), land_b=low(4, 48, 512),
        **{"v_" + name: pltpu.VMEM(inputs[name][0].shape, BF) for name in FETCHED},
        s_fetch=dma(len(FETCHED)),
        tabs=pltpu.VMEM((8, 128), jnp.int32), TAB=pltpu.VMEM((8, 128), jnp.int32),
        X=low(8, n, d), M=low(8, n, d), DO=low(4, n, d),
        PA=low(8, 96, 640), PB=low(8, 96, 768), PG=low(8, 96, 128), P2=low(8, 96, 1024), DN=low(8, 64, d),
        FO=low(4, 8, 48, 384), FC=low(4, 8, 48, 384), FQ=low(4, 8, 48, 384),
        WA=low(768, 640), WB=low(768, 384), WCQ=low(768, 192), W2=low(768, 1024), WO=low(d, d), WC=low(d, d), WQ=low(d, d),
        info=pltpu.VMEM((8, 512), jnp.int32),
        X1=low(8, n, d), X2=low(512, d), X3=low(512, d),
        KV=low(1024, 384), KVT=low(384, 1024), MKV=low(1024, 384), MKVT=low(384, 1024),
        QT=low(192, 512), CQT=low(192, 512), OUT1=full(192, 512), OUT2=full(192, 512),
        LSE1=full(8, 512), LSE2=full(8, 512),
        A4=low(4, 3, 64, 512), C4=low(4, 3, 64, 512), DC4=low(4, 3, 64, 512),
        FIRST=full(512, d), SECOND=full(512, d),
        H=low(512, 512), GG=low(512, 1024), DXP=low(4, n, d), OP=low(4, n, d),
        by_c_dx=low(2, n, d), by_x_dx=low(n, d), by_c_out=low(2, n, d), by_x_out=low(n, d),
        W2G=full(768, 256), by_y_2=low(4, 96, 1024), by_z_2=low(5, 96, 1024),
        DNG=low(8, 64, d), by_y_n=low(4, 64, d), by_z_n=low(5, 64, d),
        SGRAD=full(n, d), DS4=low(4, n, d), OUTER=low(192, 512),
        DCQT=low(192, 512), DQT=low(192, 512), MDKV=low(384, 1024), DKV=low(384, 1024),
        dk=full(64, 1024), dv=full(64, 1024),
        CO8=low(8, 48, 384), by_y_c=low(4, 48, 384), by_z_c=low(5, 48, 384),
        SO8=low(8, 48, 384), by_y_s=low(4, 48, 384), by_z_s=low(5, 48, 384),
        MG=low(8, d, n), by_c_m=low(2, 2, d, n), by_x_m=low(2, d, n), by_y_m=low(d, n),
        TG=low(8, d, n), by_c_t=low(2, 2, d, n), by_x_t=low(2, d, n), by_y_t=low(d, n),
        DFIRST=low(512, d), W1G=full(768, 384), TURN=full(384, 768), GT=full(128, 768),
        by_y_a=low(4, 96, 384), by_z_a=low(5, 96, 384), by_y_b=low(4, 96, 768), by_z_b=low(5, 96, 768),
        by_y_g=low(4, 96, 128), by_z_g=low(5, 96, 128),
        TBLOCK=low(n, d), LBLOCK=low(n, d), MBLOCK=low(n, d),
        s_move=dma(4, 2), s_near=dma(6), s_back=dma(3, 2),
        **{name: dma(4) for name in ("s_part_a", "s_part_b", "s_last_a", "s_last_b", "s_d", "s_wo", "s_wc", "s_wq", "s_s", "s_dx", "s_out")},
        **{name: dma(8) for name in ("s_x", "s_m", "s_gm", "s_gt", "s_a", "s_b", "s_fo", "s_fc", "s_fq")},
        s_2=dma(13), s_n=dma(13), s_share1=dma(3, 4), s_share2=dma(3, 4), s_share3=dma(3, 4), s_g2=dma(4, 10),
        **{name: dma(10) for name in ("s_ga", "s_gb", "s_gq", "s_gg", "s_gn", "s_gc", "s_gs")},
    )
    names = tuple(inputs) + tuple(outs) + tuple(scratch)
    return pl.pallas_call(
        functools.partial(layer_kernel, names),
        out_shape=tuple(jax.ShapeDtypeStruct(shape, BF) for shape in outs.values()),
        in_specs=[spec for _, spec in inputs.values()],
        out_specs=tuple([ANYWHERE] * len(outs)),
        scratch_shapes=list(scratch.values()),
        compiler_params=pltpu.CompilerParams(
            collective_id=1, has_side_effects=True, vmem_limit_bytes=VMEM_LIMIT
        ),
        name="layer",
    )(*[a for a, _ in inputs.values()])


def outputs_kernel(names, *refs):
    R = Names()
    for name, ref in zip(names, refs, strict=True):
        setattr(R, name, ref)

    def copies(pairs, sems):
        made = [pltpu.make_async_copy(a, b, sems.at[i]) for i, (a, b) in enumerate(pairs)]
        for one in made:
            one.start()
        return made

    arrive = copies(
        ((R.qa, R.v_qa), (R.qb, R.v_qb), (R.co, R.v_co), (R.so, R.v_so), (R.down, R.v_down)), R.s_in
    )
    blocks = copies([(getattr(R, n), getattr(R, "v_" + n)) for n in BLOCKS], R.s_block)
    for one in arrive:
        one.wait()
    gains = jnp.zeros((24, 128), F32)
    for k in range(4):
        piece = R.v_qa[k].astype(F32)
        gains = gains + piece[:24, 512:]
        narrow = slice(192 * k, 192 * k + 192)
        for row, outs in ((0, (R.w_sk, R.w_sv, R.w_sq)), (24, (R.w_ck, R.w_cv, R.w_cq))):
            for i, out in enumerate(outs):
                out[:, narrow] = piece[row : row + 24, 192 * i : 192 * i + 192]
        piece = R.v_qb[k].astype(F32)
        R.w_gate[:, 512 * k : 512 * k + 512] = piece[:24]
        R.w_up[:, 512 * k : 512 * k + 512] = piece[24:]
    for piece, out in ((R.v_so, R.w_so), (R.v_co, R.w_co)):
        rows = piece[...].astype(F32)
        out[:, :384] = rows[:24]
        out[:, 384:] = rows[24:]
    R.w_down[...] = R.v_down[...].astype(F32)
    turned = jnp.concatenate([gains, jnp.zeros((104, 128), F32)], axis=0).T
    for i, out in enumerate((R.w_g1, R.w_g2, R.w_g3)):
        out[...] = turned[64 + i : 65 + i, :24]
    leave = copies([(getattr(R, "w_" + n), getattr(R, "o_" + n)) for n in WEIGHTS], R.s_out)
    for one in blocks:
        one.wait()
    leave += copies([(getattr(R, "v_" + n), getattr(R, "o_" + n)) for n in BLOCKS], R.s_direct)
    for one in leave:
        one.wait()


BLOCKS = ("layer", "tokens", "memory")
WEIGHTS = ("g1", "sq", "sk", "sv", "so", "g2", "cq", "ck", "cv", "co", "g3", "gate", "up", "down")


def write_outputs(results):
    ins = ("qa", "qb", "co", "so", "down", "tokens", "layer", "memory")
    blocks = BLOCKS
    shapes = {name: (24, 768) for name in WEIGHTS}
    shapes |= {name: (1, 24) for name in ("g1", "g2", "g3")}
    shapes |= dict(gate=(24, 2048), up=(24, 2048), down=(64, 768))
    outs = [jax.ShapeDtypeStruct((128, 768), BF) for _ in blocks]
    outs += [jax.ShapeDtypeStruct(shapes[n], F32) for n in WEIGHTS]
    scratch = {"v_" + n: pltpu.VMEM(a.shape, BF) for n, a in zip(ins, results)}
    scratch |= {"w_" + n: pltpu.VMEM(shapes[n], F32) for n in WEIGHTS}
    scratch |= dict(s_in=dma(5), s_direct=dma(3), s_block=dma(3), s_out=dma(len(WEIGHTS)))
    names = ins + tuple("o_" + n for n in blocks + WEIGHTS) + tuple(scratch)
    return pl.pallas_call(
        functools.partial(outputs_kernel, names),
        out_shape=tuple(outs),
        in_specs=[ANYWHERE] * len(ins),
        out_specs=tuple([ANYWHERE] * len(outs)),
        scratch_shapes=list(scratch.values()),
        compiler_params=pltpu.CompilerParams(vmem_limit_bytes=VMEM_LIMIT),
        name="outputs",
    )(*results)


def body_planes(
    tokens, memory, out_grad, table_lengths, table_plots,
    self_gain, self_query, self_key, self_value, self_output,
    cross_gain, cross_query, cross_key, cross_value, cross_output,
    mlp_gain, mlp_gate, mlp_up, mlp_down,
):
    in_smem = pl.BlockSpec(memory_space=pltpu.SMEM)
    results = run_layer(
        dict(
            tok=(tokens[0], ANYWHERE), mem=(memory[0], ANYWHERE), dout=(out_grad[0], ANYWHERE),
            lengths=(table_lengths, in_smem), plots=(table_plots, in_smem), g1=(self_gain[None], IN_VMEM), g2=(cross_gain[None], IN_VMEM), g3=(mlp_gain[None], IN_VMEM),
            sq=(self_query, ANYWHERE), sk=(self_key, ANYWHERE), sv=(self_value, ANYWHERE), so=(self_output, ANYWHERE),
            cq=(cross_query, ANYWHERE), ck=(cross_key, ANYWHERE), cv=(cross_value, ANYWHERE), co=(cross_output, ANYWHERE),
            gate=(mlp_gate, ANYWHERE), up=(mlp_up, ANYWHERE), down=(mlp_down, ANYWHERE),
        )
    )
    outs = write_outputs(results)
    blocks = tuple(a[None] for a in outs[:3])
    return blocks + tuple(a[0] if a.shape[0] == 1 else a for a in outs[3:])


def solution(mesh):
    placed = (
        P(ROW, SEQ, None),
        P(ROW, SEQ, None),
        P(ROW, SEQ, None),
        P(ROW, None),
        P(ROW, None),
        P(BOTH),
        P(BOTH, None),
        P(BOTH, None),
        P(BOTH, None),
        P(BOTH, None),
        P(BOTH),
        P(BOTH, None),
        P(BOTH, None),
        P(BOTH, None),
        P(BOTH, None),
        P(BOTH),
        P(BOTH, None),
        P(BOTH, None),
        P(BOTH, None),
    )
    small = mesh.shape[ROW] == 4 and mesh.shape[SEQ] == 8
    return jax.shard_map(
        body_planes if small else body_general,
        mesh=mesh,
        in_specs=placed,
        out_specs=(
            P(ROW, SEQ, None),
            P(ROW, SEQ, None),
            P(ROW, SEQ, None),
            P(BOTH),
            P(BOTH, None),
            P(BOTH, None),
            P(BOTH, None),
            P(BOTH, None),
            P(BOTH),
            P(BOTH, None),
            P(BOTH, None),
            P(BOTH, None),
            P(BOTH, None),
            P(BOTH),
            P(BOTH, None),
            P(BOTH, None),
            P(BOTH, None),
        ),
        check_vma=False,
    )
```

```python
import functools

import jax
import jax.numpy as jnp
from jax import lax
from jax.experimental import pallas as pl
from jax.experimental.pallas import tpu as pltpu
from jax.sharding import PartitionSpec as P

HEADS = 12


SCALE = 0.125
EPS = 1e-06
NEG = -1e30
ROW, SEQ = "rows", "seq"
BOTH = (ROW, SEQ)
EQ0 = "rhqk,rkhd->rqhd"
EQ1 = "rhqk,rqhd->rkhd"
EQ2 = "rld,de->rle"
EQ3 = "rld,rle->de"
EQ4 = "rle,de->rld"
EQ5 = "rqhd,rkhd->rhqk"
EQ6 = "rqhd,rqhd->rhq"


def running_sum(lengths):
    ids = jnp.arange(lengths.shape[1], dtype=jnp.int32)
    upto = (ids[None, :] <= ids[:, None]).astype(lengths.dtype)
    return jnp.sum(lengths[:, None, :] * upto[None], axis=2)


def rms_forward(values, gain_vector):
    inverse = lax.rsqrt(jnp.mean(values * values, axis=-1, keepdims=True) + EPS)
    return (values * inverse * gain_vector, inverse)


def rms_backward(values, inverse, gain_vector, upstream):
    normed = values * inverse
    gain_grad = jnp.sum(upstream * normed, axis=(0, 1))
    scaled = upstream * gain_vector
    input_grad = inverse * (scaled - normed * jnp.mean(scaled * normed, axis=-1, keepdims=True))
    return (input_grad, gain_grad)


def matmul(operand, weight):
    return jnp.einsum(EQ2, operand, weight, preferred_element_type=jnp.float32)


def matmul_back(upstream, weight):
    return jnp.einsum(EQ4, upstream, weight, preferred_element_type=jnp.float32)


def weight_grad(operand, upstream):
    return jnp.einsum(EQ3, operand, upstream, preferred_element_type=jnp.float32)


def split_heads(values):
    return values.reshape(values.shape[0], values.shape[1], HEADS, values.shape[2] // HEADS)


def segment_of(places, table_ends):
    return jnp.sum((places[None, :, None] >= table_ends[:, None, :]).astype(jnp.int32), axis=2)


def pair_mask(query_seg, query_pos, key_seg, key_pos, causal):
    same_pair = query_seg[:, :, None] == key_seg[:, None, :]
    if causal:
        same_pair = jnp.logical_and(same_pair, key_pos[None, None, :] <= query_pos[None, :, None])
    return same_pair


def over_blocks(advance_block, fold_state, arrays, block_width):
    piece_rows = arrays[0].shape[1]
    block_count = piece_rows // block_width
    stacked = tuple(
        (
            jnp.moveaxis(
                member.reshape((member.shape[0], block_count, block_width) + member.shape[2:]), 1, 0
            )
            for member in arrays
        )
    )

    def advance(carried, block_items):
        block_index, block_parts = block_items
        return (advance_block(carried, block_parts, block_index * block_width), None)

    fold_state, ignored = lax.scan(
        advance, fold_state, (jnp.arange(block_count, dtype=jnp.int32), stacked)
    )
    return fold_state


def forward_fold(query_heads, query_seg, query_pos, key_segment, causal, block_width):

    def advance_block(fold_state, parts, first_row):
        key_block, value_block = parts
        key_pos = first_row + jnp.arange(key_block.shape[1], dtype=jnp.int32)
        allowed = pair_mask(query_seg, query_pos, key_segment(key_pos), key_pos, causal)

        def compute(current):
            running_max, running_sum, accumulated = current
            scores = (
                jnp.einsum(
                    EQ5,
                    query_heads,
                    split_heads(key_block),
                    preferred_element_type=jnp.float32,
                )
                * SCALE
            )
            scores = jnp.where(allowed[:, None], scores, NEG)
            new_max = jnp.maximum(running_max, jnp.max(scores, axis=-1))
            weights = jnp.where(allowed[:, None], jnp.exp(scores - new_max[..., None]), 0.0)
            factor = jnp.exp(running_max - new_max)
            new_sum = running_sum * factor + jnp.sum(weights, axis=-1)
            update = jnp.einsum(
                EQ0,
                weights.astype(jnp.bfloat16),
                split_heads(value_block),
                preferred_element_type=jnp.float32,
            )
            return (
                new_max,
                new_sum,
                accumulated * jnp.transpose(factor, (0, 2, 1))[..., None] + update,
            )

        return compute(fold_state)

    def forward_fold_piece(fold_state, shard_piece, first_row):
        return over_blocks(advance_block, fold_state, shard_piece, block_width)

    return forward_fold_piece


def finish(fold_state):
    running_max, running_sum, accumulated = fold_state
    attended = accumulated / jnp.transpose(running_sum, (0, 2, 1))[..., None]
    return (attended, running_max + jnp.log(running_sum))


def query_grad_fold(
    query_heads,
    out_heads,
    log_total,
    row_delta,
    query_seg,
    query_pos,
    key_segment,
    causal,
    block_width,
):

    def advance_block(fold_state, parts, first_row):
        key_block, value_block = parts
        key_pos = first_row + jnp.arange(key_block.shape[1], dtype=jnp.int32)
        allowed = pair_mask(query_seg, query_pos, key_segment(key_pos), key_pos, causal)

        def compute(current):
            key_heads = split_heads(key_block)
            scores = (
                jnp.einsum(
                    EQ5, query_heads, key_heads, preferred_element_type=jnp.float32
                )
                * SCALE
            )
            scores = jnp.where(allowed[:, None], scores, NEG)
            probabilities = jnp.where(allowed[:, None], jnp.exp(scores - log_total[..., None]), 0.0)
            prob_grad = jnp.einsum(
                EQ5,
                out_heads,
                split_heads(value_block),
                preferred_element_type=jnp.float32,
            )
            score_grad = (probabilities * (prob_grad - row_delta[..., None])).astype(jnp.bfloat16)
            return current + SCALE * jnp.einsum(
                EQ0, score_grad, key_heads, preferred_element_type=jnp.float32
            )

        return compute(fold_state)

    def query_fold_piece(fold_state, shard_piece, first_row):
        return over_blocks(advance_block, fold_state, shard_piece, block_width)

    return query_fold_piece


def key_grad_fold(
    key_heads,
    value_heads,
    key_seg,
    key_pos,
    total_rows,
    delta_rows,
    query_segment,
    causal,
    block_width,
):

    def advance_block(fold_state, parts, first_row):
        query_block, out_block = parts
        piece_rows = query_block.shape[1]
        query_pos = first_row + jnp.arange(piece_rows, dtype=jnp.int32)
        allowed = pair_mask(query_segment(query_pos), query_pos, key_seg, key_pos, causal)
        total_block = lax.dynamic_slice_in_dim(total_rows, first_row, piece_rows, 2)
        delta_block = lax.dynamic_slice_in_dim(delta_rows, first_row, piece_rows, 2)

        def compute(current):
            key_acc, value_acc = current
            query_heads = split_heads(query_block)
            out_heads = split_heads(out_block)
            scores = (
                jnp.einsum(
                    EQ5, query_heads, key_heads, preferred_element_type=jnp.float32
                )
                * SCALE
            )
            scores = jnp.where(allowed[:, None], scores, NEG)
            probabilities = jnp.where(
                allowed[:, None], jnp.exp(scores - total_block[..., None]), 0.0
            )
            value_acc = value_acc + jnp.einsum(
                EQ1,
                probabilities.astype(jnp.bfloat16),
                out_heads,
                preferred_element_type=jnp.float32,
            )
            prob_grad = jnp.einsum(
                EQ5, out_heads, value_heads, preferred_element_type=jnp.float32
            )
            score_grad = (probabilities * (prob_grad - delta_block[..., None])).astype(jnp.bfloat16)
            key_acc = key_acc + SCALE * jnp.einsum(
                EQ1, score_grad, query_heads, preferred_element_type=jnp.float32
            )
            return (key_acc, value_acc)

        return compute(fold_state)

    def key_fold_piece(fold_state, shard_piece, first_row):
        return over_blocks(advance_block, fold_state, shard_piece, block_width)

    return key_fold_piece


def body_general(
    tokens,
    memory,
    out_grad,
    table_lengths,
    table_plots,
    self_gain,
    self_query,
    self_key,
    self_value,
    self_output,
    cross_gain,
    cross_query,
    cross_key,
    cross_value,
    cross_output,
    mlp_gain,
    mlp_gate,
    mlp_up,
    mlp_down,
):
    def whole(shard):
        return lax.all_gather(shard, BOTH, axis=0, tiled=True)

    all_self_gain = whole(self_gain)
    all_self_query = whole(self_query)
    all_self_key = whole(self_key)
    all_self_value = whole(self_value)
    all_self_output = whole(self_output)
    all_cross_gain = whole(cross_gain)
    all_cross_query = whole(cross_query)
    all_cross_key = whole(cross_key)
    all_cross_value = whole(cross_value)
    all_cross_output = whole(cross_output)
    all_mlp_gain = whole(mlp_gain)
    all_mlp_gate = whole(mlp_gate)
    all_mlp_up = whole(mlp_up)
    all_mlp_down = whole(mlp_down)
    seq_count = lax.axis_size(SEQ)
    seq_index = lax.axis_index(SEQ)
    row_count = tokens.shape[0]
    positions = tokens.shape[1]
    memory_cols = memory.shape[1]
    width = tokens.shape[2]
    head_size = width // HEADS
    query_pos = seq_index * positions + jnp.arange(positions, dtype=jnp.int32)
    memory_pos = seq_index * memory_cols + jnp.arange(memory_cols, dtype=jnp.int32)
    table_ends = running_sum(table_lengths)
    tables = table_lengths.shape[1]
    table_ids = jnp.arange(tables, dtype=jnp.int32)
    plot_width = memory_cols * seq_count // tables

    def token_segment(places):
        return segment_of(places, table_ends)

    def token_plot(places):
        segments = segment_of(places, table_ends)
        return jnp.sum(
            jnp.where(segments[:, :, None] == table_ids[None, None, :], table_plots[:, None, :], 0),
            axis=2,
        )

    def memory_plot(places):
        return (places // plot_width)[None, :]

    def start_state():
        return (
            jnp.full((row_count, HEADS, positions), NEG, jnp.float32),
            jnp.zeros((row_count, HEADS, positions), jnp.float32),
            jnp.zeros((row_count, positions, HEADS, head_size), jnp.float32),
        )

    values = tokens.astype(jnp.float32)
    normed_one, inverse_one = rms_forward(values, all_self_gain.astype(jnp.float32))
    input_one = normed_one.astype(jnp.bfloat16)
    queries = matmul(input_one, all_self_query).astype(jnp.bfloat16)
    key_rows = matmul(input_one, all_self_key).astype(jnp.bfloat16)
    value_rows = matmul(input_one, all_self_value).astype(jnp.bfloat16)
    query_seg = token_segment(query_pos)
    self_fold = forward_fold(
        split_heads(queries), query_seg, query_pos, token_segment, True, positions
    )
    self_out, self_total = finish(
        self_fold(
            start_state(),
            (
                lax.all_gather(key_rows, SEQ, axis=1, tiled=True),
                lax.all_gather(value_rows, SEQ, axis=1, tiled=True),
            ),
            jnp.int32(0),
        )
    )
    self_att = self_out.reshape(row_count, positions, width).astype(jnp.bfloat16)
    first_sum = values + matmul(self_att, all_self_output)
    normed_two, inverse_two = rms_forward(first_sum, all_cross_gain.astype(jnp.float32))
    input_two = normed_two.astype(jnp.bfloat16)
    cross_rows = matmul(input_two, all_cross_query).astype(jnp.bfloat16)
    memory_keys = matmul(memory, all_cross_key).astype(jnp.bfloat16)
    memory_rows = matmul(memory, all_cross_value).astype(jnp.bfloat16)
    query_plot = token_plot(query_pos)
    cross_fold = forward_fold(
        split_heads(cross_rows), query_plot, query_pos, memory_plot, False, memory_cols
    )
    cross_out, cross_total = finish(
        cross_fold(
            start_state(),
            (
                lax.all_gather(memory_keys, SEQ, axis=1, tiled=True),
                lax.all_gather(memory_rows, SEQ, axis=1, tiled=True),
            ),
            jnp.int32(0),
        )
    )
    cross_att = cross_out.reshape(row_count, positions, width).astype(jnp.bfloat16)
    second_sum = first_sum + matmul(cross_att, all_cross_output)
    normed_three, inverse_three = rms_forward(second_sum, all_mlp_gain.astype(jnp.float32))
    input_three = normed_three.astype(jnp.bfloat16)
    gate_pre = matmul(input_three, all_mlp_gate)
    up_pre = matmul(input_three, all_mlp_up)

    def gated_unit(gate_value, up_value):
        return jax.nn.gelu(gate_value, approximate=True) * up_value

    hidden_value, gated_back = jax.vjp(gated_unit, gate_pre, up_pre)
    hidden = hidden_value.astype(jnp.bfloat16)
    layer_out = (second_sum + matmul(hidden, all_mlp_down)).astype(jnp.bfloat16)
    upstream = out_grad.astype(jnp.float32)
    grad_down = weight_grad(hidden, out_grad)
    hidden_grad = matmul_back(out_grad, all_mlp_down)
    gate_grad, up_grad = gated_back(hidden_grad)
    gate_low = gate_grad.astype(jnp.bfloat16)
    up_low = up_grad.astype(jnp.bfloat16)
    grad_gate = weight_grad(input_three, gate_low)
    grad_up = weight_grad(input_three, up_low)
    three_grad = matmul_back(gate_low, all_mlp_gate) + matmul_back(
        up_low, all_mlp_up
    )
    part_three, grad_gain_three = rms_backward(
        second_sum, inverse_three, all_mlp_gain.astype(jnp.float32), three_grad
    )
    second_grad = upstream + part_three
    cross_branch = second_grad.astype(jnp.bfloat16)
    grad_cross_output = weight_grad(cross_att, cross_branch)
    cross_dout = matmul_back(cross_branch, all_cross_output).astype(jnp.bfloat16)
    cross_heads = split_heads(cross_dout)
    cross_delta = jnp.einsum(EQ6, cross_heads.astype(jnp.float32), cross_out)
    cross_total_all, cross_delta_all = (
        lax.all_gather(cross_total, SEQ, axis=2, tiled=True),
        lax.all_gather(cross_delta, SEQ, axis=2, tiled=True),
    )
    cross_query_fold = query_grad_fold(
        split_heads(cross_rows),
        cross_heads,
        cross_total,
        cross_delta,
        query_plot,
        query_pos,
        memory_plot,
        False,
        memory_cols,
    )
    cross_rows_grad = cross_query_fold(
        jnp.zeros((row_count, positions, HEADS, head_size), jnp.float32),
        (
            lax.all_gather(memory_keys, SEQ, axis=1, tiled=True),
            lax.all_gather(memory_rows, SEQ, axis=1, tiled=True),
        ),
        jnp.int32(0),
    )
    cross_rows_low = cross_rows_grad.reshape(row_count, positions, width).astype(jnp.bfloat16)
    memory_fold = key_grad_fold(
        split_heads(memory_keys),
        split_heads(memory_rows),
        memory_plot(memory_pos),
        memory_pos,
        cross_total_all,
        cross_delta_all,
        token_plot,
        False,
        positions,
    )
    memory_zero = jnp.zeros((row_count, memory_cols, HEADS, head_size), jnp.float32)
    memory_key_grad, memory_value_grad = memory_fold(
        (memory_zero, memory_zero),
        (
            lax.all_gather(cross_rows, SEQ, axis=1, tiled=True),
            lax.all_gather(cross_dout, SEQ, axis=1, tiled=True),
        ),
        jnp.int32(0),
    )
    memory_key_low = memory_key_grad.reshape(row_count, memory_cols, width).astype(jnp.bfloat16)
    memory_value_low = memory_value_grad.reshape(row_count, memory_cols, width).astype(jnp.bfloat16)
    grad_cross_query = weight_grad(input_two, cross_rows_low)
    grad_cross_key = weight_grad(memory, memory_key_low)
    grad_cross_value = weight_grad(memory, memory_value_low)
    memory_grad = (
        matmul_back(memory_key_low, all_cross_key)
        + matmul_back(memory_value_low, all_cross_value)
    ).astype(jnp.bfloat16)
    two_grad = matmul_back(cross_rows_low, all_cross_query)
    part_two, grad_gain_two = rms_backward(
        first_sum, inverse_two, all_cross_gain.astype(jnp.float32), two_grad
    )
    first_grad = second_grad + part_two
    self_branch = first_grad.astype(jnp.bfloat16)
    grad_self_output = weight_grad(self_att, self_branch)
    self_dout = matmul_back(self_branch, all_self_output).astype(jnp.bfloat16)
    self_heads = split_heads(self_dout)
    self_delta = jnp.einsum(EQ6, self_heads.astype(jnp.float32), self_out)
    self_total_all, self_delta_all = (
        lax.all_gather(self_total, SEQ, axis=2, tiled=True),
        lax.all_gather(self_delta, SEQ, axis=2, tiled=True),
    )
    self_query_fold = query_grad_fold(
        split_heads(queries),
        self_heads,
        self_total,
        self_delta,
        query_seg,
        query_pos,
        token_segment,
        True,
        positions,
    )
    queries_grad = self_query_fold(
        jnp.zeros((row_count, positions, HEADS, head_size), jnp.float32),
        (
            lax.all_gather(key_rows, SEQ, axis=1, tiled=True),
            lax.all_gather(value_rows, SEQ, axis=1, tiled=True),
        ),
        jnp.int32(0),
    )
    queries_low = queries_grad.reshape(row_count, positions, width).astype(jnp.bfloat16)
    self_key_fold = key_grad_fold(
        split_heads(key_rows),
        split_heads(value_rows),
        query_seg,
        query_pos,
        self_total_all,
        self_delta_all,
        token_segment,
        True,
        positions,
    )
    token_zero = jnp.zeros((row_count, positions, HEADS, head_size), jnp.float32)
    key_grad, value_grad = self_key_fold(
        (token_zero, token_zero),
        (
            lax.all_gather(queries, SEQ, axis=1, tiled=True),
            lax.all_gather(self_dout, SEQ, axis=1, tiled=True),
        ),
        jnp.int32(0),
    )
    key_low = key_grad.reshape(row_count, positions, width).astype(jnp.bfloat16)
    value_low = value_grad.reshape(row_count, positions, width).astype(jnp.bfloat16)
    grad_self_query = weight_grad(input_one, queries_low)
    grad_self_key = weight_grad(input_one, key_low)
    grad_self_value = weight_grad(input_one, value_low)
    one_grad = (
        matmul_back(queries_low, all_self_query)
        + matmul_back(key_low, all_self_key)
        + matmul_back(value_low, all_self_value)
    )
    part_one, grad_gain_one = rms_backward(
        values, inverse_one, all_self_gain.astype(jnp.float32), one_grad
    )
    tokens_grad = (first_grad + part_one).astype(jnp.bfloat16)
    summed = tuple(
        (
            lax.psum_scatter(grad_gain_one, BOTH, scatter_dimension=0, tiled=True),
            lax.psum_scatter(grad_self_query, BOTH, scatter_dimension=0, tiled=True),
            lax.psum_scatter(grad_self_key, BOTH, scatter_dimension=0, tiled=True),
            lax.psum_scatter(grad_self_value, BOTH, scatter_dimension=0, tiled=True),
            lax.psum_scatter(grad_self_output, BOTH, scatter_dimension=0, tiled=True),
            lax.psum_scatter(grad_gain_two, BOTH, scatter_dimension=0, tiled=True),
            lax.psum_scatter(grad_cross_query, BOTH, scatter_dimension=0, tiled=True),
            lax.psum_scatter(grad_cross_key, BOTH, scatter_dimension=0, tiled=True),
            lax.psum_scatter(grad_cross_value, BOTH, scatter_dimension=0, tiled=True),
            lax.psum_scatter(grad_cross_output, BOTH, scatter_dimension=0, tiled=True),
            lax.psum_scatter(grad_gain_three, BOTH, scatter_dimension=0, tiled=True),
            lax.psum_scatter(grad_gate, BOTH, scatter_dimension=0, tiled=True),
            lax.psum_scatter(grad_up, BOTH, scatter_dimension=0, tiled=True),
            lax.psum_scatter(grad_down, BOTH, scatter_dimension=0, tiled=True),
        )
    )
    return (layer_out, tokens_grad, memory_grad) + summed


MESH = pl.DeviceIdType.MESH
BF = jnp.bfloat16
F32 = jnp.float32
QW = 1152
VMEM_LIMIT = 62 * 1024 * 1024


def coords():
    r = lax.axis_index(ROW)
    s = lax.axis_index(SEQ)
    return lax.div(r, 2), lax.rem(r, 2), lax.rem(s, 2), lax.div(s, 2)


def dev(x, c, y, z):
    return {ROW: 2 * x + c, SEQ: 2 * z + y}


def remote(src, dst, send_sem, recv_sem, to):
    return pltpu.make_async_remote_copy(
        src_ref=src,
        dst_ref=dst,
        send_sem=send_sem,
        recv_sem=recv_sem,
        device_id=dev(*to),
        device_id_type=MESH,
    )


def owner_of(x, c, y, z):
    return lax.rem(z, 2), lax.div(z, 2), y, 2 * c + x


def is_fixed(x, c, y, z):
    return 2 * c + x == z


def greet(me, pairs=(), z_line=False, moves=False):
    x, c, y, z = me
    bar = pltpu.get_barrier_semaphore()

    def hello(to):
        pl.semaphore_signal(bar, 1, device_id=dev(*to), device_id_type=MESH)

    count = len(pairs)
    for to in pairs:
        hello(to)
    if z_line:

        @pl.when(z > 0)
        def _():
            hello((x, c, y, z - 1))

        @pl.when(z < 3)
        def _():
            hello((x, c, y, z + 1))

        count = count + jnp.where(z > 0, 1, 0) + jnp.where(z < 3, 1, 0)
    if moves:
        away = jnp.logical_not(is_fixed(*me))

        @pl.when(away)
        def _():
            hello(owner_of(*me))

        count = count + jnp.where(away, 1, 0)
    pl.semaphore_wait(bar, count)


class Move:
    def __init__(self, me, src, dst, sems):
        self.far = remote(src, dst, sems.at[0], sems.at[1], owner_of(*me))
        self.near = pltpu.make_async_copy(src, dst, sems.at[0])
        self.fixed = is_fixed(*me)

    def start(self):
        @pl.when(self.fixed)
        def _():
            self.near.start()

        @pl.when(jnp.logical_not(self.fixed))
        def _():
            self.far.start()

    def arrive(self):
        @pl.when(self.fixed)
        def _():
            self.near.wait()

        @pl.when(jnp.logical_not(self.fixed))
        def _():
            self.far.wait_recv()

    def finish(self):
        @pl.when(jnp.logical_not(self.fixed))
        def _():
            self.far.wait_send()


class Gather4:
    def __init__(self, me, buf, sems, tokens=False):
        x, c, y, z = me
        xp, cp = (1 - x, c, y, z), (x, 1 - c, y, z)
        g = x + 2 * c if tokens else 2 * x + c
        far = 1 - x + 2 * c if tokens else 2 * (1 - x) + c
        self.x_own = remote(buf.at[g], buf.at[g], sems.at[0], sems.at[1], xp)
        self.c_own = remote(buf.at[g], buf.at[g], sems.at[0], sems.at[2], cp)
        self.c_far = remote(buf.at[far], buf.at[far], sems.at[0], sems.at[3], cp)

    def start(self):
        self.x_own.start()
        self.c_own.start()

    def forward(self):
        self.x_own.wait_recv()
        self.c_far.start()

    def arrive(self):
        self.c_own.wait_recv()
        self.c_far.wait_recv()

    def finish(self):
        self.x_own.wait_send()
        self.c_own.wait_send()
        self.c_far.wait_send()


class Gather8:
    def __init__(self, me, buf, sems, split=False):
        x, c, y, z = me
        xp, cp, yp = (1 - x, c, y, z), (x, 1 - c, y, z), (x, c, 1 - y, z)
        def piece(px, pc, py):
            return buf.at[2 * (px + 2 * pc) + py]

        def send(p, k, to):
            return remote(p, p, sems.at[0], sems.at[1 + k], to)

        own, at_x = piece(x, c, y), piece(1 - x, c, y)
        at_y, at_d = piece(x, c, 1 - y), piece(1 - x, c, 1 - y)
        self.x_own = send(own, 0, xp)
        self.y_own = send(own, 1, yp)
        self.c_own = send(own, 2, cp)
        self.c_x = send(at_x, 3, cp)
        self.c_y = send(at_y, 4, cp)
        self.c_d = send(at_d, 5, cp)
        self.d_by_x = send(at_y, 6, xp)
        self.d_by_y = send(at_x, 6, yp)
        self.by_y = jnp.logical_and(c == 0, split)

    def start(self):
        self.start_x()
        self.start_y()

    def start_x(self):
        self.x_own.start()
        self.c_own.start()

    def start_y(self):
        self.y_own.start()

    def forward(self):
        self.y_own.wait_recv()

        @pl.when(jnp.logical_not(self.by_y))
        def _():
            self.d_by_x.start()

        self.c_y.start()
        self.x_own.wait_recv()

        @pl.when(self.by_y)
        def _():
            self.d_by_y.start()

        self.c_x.start()

    def forward_far(self):
        self.d_by_x.wait_recv()
        self.c_d.start()

    def arrive(self):
        for one in (self.c_own, self.c_x, self.c_y, self.c_d):
            one.wait_recv()

    def finish(self):
        for one in (self.x_own, self.y_own, self.c_own, self.c_x, self.c_y, self.c_d, self.d_by_x):
            one.wait_send()


QB = 256


def dot(a, b):
    return lax.dot_general(a, b, (((1,), (0,)), ((), ())), preferred_element_type=F32)


def dot_nt(a, b):
    return lax.dot_general(a, b, (((1,), (1,)), ((), ())), preferred_element_type=F32)


def dot_tn(a, b):
    return lax.dot_general(a, b, (((0,), (0,)), ((), ())), preferred_element_type=F32)


def masked(scores, info, lanes, causal):
    keys = scores.shape[0]
    if causal:
        pos = lax.broadcasted_iota(jnp.int32, scores.shape, 0)
        allowed = jnp.logical_and(pos >= info[1:2, lanes], pos <= info[0:1, lanes])
        return jnp.where(allowed, scores, NEG)
    plot = info[2:3, lanes]
    half = keys // 2
    low = jnp.where(plot == 0, 0.0, NEG)
    high = jnp.where(plot == 1, 0.0, NEG)
    return jnp.concatenate([scores[:half] + low, scores[half:] + high], axis=0)


class GatherPlane:
    def __init__(self, me, buf, sems, lanes=None):
        x, c, y, z = me

        def send(p, k, to):
            piece = buf.at[2 * p + y] if lanes is None else buf.at[2 * p + y, :, lanes]
            return remote(piece, piece, sems.at[0], sems.at[1 + k], to)

        yp = (x, c, 1 - y, z)
        self.along = [send(z, k - 1, (x, c, y, lax.rem(z + k, 4))) for k in (1, 2, 3)]
        self.across = [send(z, 3, yp)]
        self.across += [send(lax.rem(z + 4 - k, 4), 3 + k, yp) for k in (1, 2, 3)]

    def start_along(self):
        for one in self.along:
            one.start()

    def start_across(self):
        self.across[0].start()

    def forward(self, k):
        self.along[k - 1].wait_recv()
        self.across[k].start()

    def arrive(self):
        for one in self.across:
            one.wait_recv()

    def finish(self):
        for one in self.along + self.across:
            one.wait_send()


class GatherRelay:
    def __init__(self, me, buf, sems, lanes=None):
        self.me, self.buf, self.sems, self.lanes = me, buf, sems, lanes

    def piece(self, p, y):
        return self.buf.at[2 * p + y] if self.lanes is None else self.buf.at[2 * p + y, :, self.lanes]

    def send(self, p, k, to):
        piece = self.piece(p, self.me[2])
        return remote(piece, piece, self.sems.at[0], self.sems.at[1 + k + p], to)

    def up(self, p):
        x, c, y, z = self.me
        return self.send(p, 0, (x, c, y, z + 1))

    def down(self, p):
        x, c, y, z = self.me
        return self.send(p, 4, (x, c, y, z - 1))

    def across(self, p):
        x, c, y, z = self.me
        return self.send(p, 8, (x, c, 1 - y, z))

    def start_along(self):
        z = self.me[3]

        @pl.when(z < 3)
        def _():
            self.up(z).start()

        @pl.when(z > 0)
        def _():
            self.down(z).start()

    def start_across(self):
        self.across(self.me[3]).start()

    def forward(self, k):
        z = self.me[3]

        @pl.when(z - k >= 0)
        def _():
            p = z - k
            self.up(p).wait_recv()
            if k < 3:

                @pl.when(z < 3)
                def _():
                    self.up(p).start()

            self.across(p).start()

        @pl.when(z + k <= 3)
        def _():
            p = z + k
            self.down(p).wait_recv()
            if k < 3:

                @pl.when(z > 0)
                def _():
                    self.down(p).start()

            self.across(p).start()

    def arrive(self):
        for p in range(4):
            self.across(p).wait_recv()

    def finish(self):
        z = self.me[3]
        for p in range(4):
            self.across(p).wait_send()

            @pl.when(jnp.logical_and(z < 3, p <= z))
            def _():
                self.up(p).wait_send()

            @pl.when(jnp.logical_and(z > 0, p >= z))
            def _():
                self.down(p).wait_send()


class SumPlane:
    def __init__(self, me, parts, by_y, by_z, sems, lanes=None):
        self.me, self.parts, self.by_y, self.by_z, self.sems = me, parts, by_y, by_z, sems
        self.lanes = slice(None) if lanes is None else lanes

    def mine(self, p):
        return self.parts.at[2 * p + self.me[2], :, self.lanes]

    def from_y(self, p):
        return self.by_y.at[p, :, self.lanes]

    def slot(self, k):
        return self.by_z.at[k, :, self.lanes]

    def across(self, p):
        x, c, y, z = self.me
        theirs = self.parts.at[2 * p + 1 - y, :, self.lanes]
        return remote(theirs, self.from_y(p), self.sems.at[0], self.sems.at[1 + p], (x, c, 1 - y, z))

    def up_slot(self, p):
        return self.slot(p - 1)

    def down_slot(self, q):
        return self.slot(lax.rem(3 + q, 5))

    def up(self, p):
        x, c, y, z = self.me
        send, recv = self.sems.at[0], self.sems.at[4 + p]
        return remote(self.mine(p), self.up_slot(p), send, recv, (x, c, y, z + 1))

    def down(self, q):
        x, c, y, z = self.me
        send, recv = self.sems.at[0], self.sems.at[5 + lax.rem(3 + q, 5)]
        return remote(self.mine(q), self.down_slot(q), send, recv, (x, c, y, z - 1))

    def start(self):
        for p in (3, 0, 2, 1):
            self.across(p).start()

    def fold(self, steps=(3, 0, 2, 1)):
        z = self.me[3]
        for p in steps:
            self.across(p).wait_recv()
            add_into(self.mine(p), self.from_y(p))
            if p > 0:

                @pl.when(z == 0)
                def _():
                    self.up(p).start()

            if p < 3:

                @pl.when(z == 3)
                def _():
                    self.down(p).start()

    def relay_up(self, p):
        self.up(p).wait_recv()
        add_into(self.mine(p), self.up_slot(p))
        self.up(p).start()

    def relay_down(self, q):
        self.down(q).wait_recv()
        add_into(self.mine(q), self.down_slot(q))
        self.down(q).start()

    def pass_one(self):
        z = self.me[3]

        @pl.when(z == 1)
        def _():
            self.relay_up(3)
            self.relay_up(2)

        @pl.when(z == 2)
        def _():
            self.relay_down(0)
            self.relay_down(1)

    def pass_two(self):
        z = self.me[3]

        @pl.when(z == 2)
        def _():
            self.relay_up(3)

        @pl.when(z == 1)
        def _():
            self.relay_down(0)

    def end(self):
        z = self.me[3]

        @pl.when(z > 0)
        def _():
            self.up(z).wait_recv()
            add_into(self.mine(z), self.up_slot(z))

        @pl.when(z < 3)
        def _():
            self.down(z).wait_recv()
            add_into(self.mine(z), self.down_slot(z))

    def finish(self):
        z = self.me[3]
        for p in range(4):
            self.across(p).wait_send()

            @pl.when(z < p)
            def _():
                self.up(p).wait_send()

            @pl.when(z > p)
            def _():
                self.down(p).wait_send()


class SumPlaneDirect(SumPlane):
    def straight(self, k):
        x, c, y, z = self.me
        p = lax.rem(z + k, 4)
        send, recv = self.sems.at[0], self.sems.at[4 + k]
        return remote(self.mine(p), self.slot(k - 1), send, recv, (x, c, y, p))

    def start(self):
        for k in (2, 1, 3, 0):
            self.across(lax.rem(self.me[3] + k, 4)).start()

    def fold(self, steps=(2, 1, 3, 0)):
        for k in steps:
            p = lax.rem(self.me[3] + k, 4)
            self.across(p).wait_recv()
            add_into(self.mine(p), self.from_y(p))
            if k:
                self.straight(k).start()

    def pass_one(self):
        pass

    def pass_two(self):
        pass

    def end(self):
        for k in (1, 2, 3):
            self.straight(k).wait_recv()
            add_into(self.mine(self.me[3]), self.slot(k - 1))

    def finish(self):
        for p in range(4):
            self.across(p).wait_send()
        for k in (1, 2, 3):
            self.straight(k).wait_send()


class Sum8:
    def __init__(self, me, parts, by_c, by_x, by_y, sems):
        x, c, y, z = me
        self.me, self.parts = me, parts
        self.by_c, self.by_x, self.by_y = by_c, by_x, by_y
        xp, cp, yp = (1 - x, c, y, z), (x, 1 - c, y, z), (x, c, 1 - y, z)

        def send(src, dst, k, to):
            return remote(src, dst, sems.at[0], sems.at[1 + k], to)

        self.order = [(1 - x, 1 - y), (1 - x, y), (x, 1 - y), (x, y)]
        self.first = [
            send(parts.at[2 * (px + 2 * (1 - c)) + py], by_c.at[px, py], k, cp)
            for k, (px, py) in enumerate(self.order)
        ]
        self.second = [
            send(by_c.at[1 - x, py], by_x.at[py], 4 + k, xp) for k, py in enumerate((1 - y, y))
        ]
        self.third = send(by_x.at[1 - y], by_y, 6, yp)

    def start(self):
        for one in self.first:
            one.start()

    def to_x(self):
        x, c, y, z = self.me
        for k, py in enumerate((1 - y, y)):
            self.first[k].wait_recv()
            add_into(self.by_c.at[1 - x, py], self.parts.at[2 * (1 - x + 2 * c) + py])
            self.second[k].start()

    def to_y(self):
        x, c, y, z = self.me
        self.first[2].wait_recv()
        self.first[3].wait_recv()
        add_into(self.by_c.at[x, 1 - y], self.parts.at[2 * (x + 2 * c) + 1 - y])
        self.second[0].wait_recv()
        add_into(self.by_x.at[1 - y], self.by_c.at[x, 1 - y])
        self.third.start()

    def end(self):
        x, c, y, z = self.me
        self.second[1].wait_recv()
        self.third.wait_recv()
        return (
            self.parts[2 * (x + 2 * c) + y].astype(F32)
            + self.by_c[x, y].astype(F32)
            + self.by_x[y].astype(F32)
            + self.by_y[...].astype(F32)
        )

    def finish(self):
        for one in self.first + self.second + [self.third]:
            one.wait_send()


class Sum4:
    def __init__(self, me, parts, by_c, by_x, sems):
        x, c, y, z = me
        self.me, self.parts, self.by_c, self.by_x = me, parts, by_c, by_x
        xp, cp = (1 - x, c, y, z), (x, 1 - c, y, z)
        self.first = [
            remote(parts.at[px + 2 * (1 - c)], by_c.at[px], sems.at[0], sems.at[1 + px], cp)
            for px in range(2)
        ]
        self.second = remote(by_c.at[1 - x], by_x, sems.at[0], sems.at[3], xp)

    def start(self):
        for one in self.first:
            one.start()

    def to_x(self):
        x, c, y, z = self.me
        for one in self.first:
            one.wait_recv()
        add_into(self.by_c.at[1 - x], self.parts.at[1 - x + 2 * c])
        self.second.start()

    def end(self):
        x, c, y, z = self.me
        self.second.wait_recv()
        return (
            self.parts[x + 2 * c].astype(F32)
            + self.by_c[x].astype(F32)
            + self.by_x[...].astype(F32)
        )

    def finish(self):
        for one in self.first + [self.second]:
            one.wait_send()


def chunks(rows, step, run):
    def one(i, carry):
        run(pl.ds(pl.multiple_of(i * step, step), step))
        return carry

    lax.fori_loop(0, rows // step, one, 0)


def add_into(into, more, step=16):
    def run(rows):
        total = into[rows, :].astype(F32) + more[rows, :].astype(F32)
        into[rows, :] = total.astype(into.dtype)

    chunks(into.shape[0], step, run)


def dma(*shape):
    return pltpu.SemaphoreType.DMA(shape)


ANYWHERE = pl.BlockSpec(memory_space=pl.ANY)
IN_VMEM = pl.BlockSpec(memory_space=pltpu.VMEM)


def attend_head(h, info, qt, kv, kvt, out, lse, causal):
    keys = kv.shape[0]
    rows = slice(64 * h, 64 * h + 64)
    for b in range(512 // QB):
        lanes = slice(QB * b, QB * b + QB)
        top = keys * (b + 1) * QB // 512 if causal else keys
        scores = dot(kv[:top, rows], qt[rows, lanes])
        scores = masked(scores, info, lanes, causal)
        high = jnp.max(scores, axis=0, keepdims=True)
        weights = jnp.exp(scores - high)
        total = jnp.sum(weights, axis=0, keepdims=True)
        out[rows, lanes] = dot(kvt[192 + 64 * h : 256 + 64 * h, :top], weights.astype(BF)) / total
        lse[h : h + 1, lanes] = high + jnp.log(total)


def attend_back_head(h, info, qt, kv, kvt, outer_t, out, lse, dq, dkv, dk_acc, dv_acc, causal):
    keys = kv.shape[0]
    rows = slice(64 * h, 64 * h + 64)
    value_rows = slice(192 + 64 * h, 256 + 64 * h)
    for b in reversed(range(512 // QB)):
        lanes = slice(QB * b, QB * b + QB)
        top = keys * (b + 1) * QB // 512 if causal else keys
        query, outer = qt[rows, lanes], outer_t[rows, lanes]
        delta = jnp.sum(outer.astype(F32) * out[rows, lanes], axis=0, keepdims=True)
        scores = masked(dot(kv[:top, rows], query), info, lanes, causal)
        prob = jnp.exp(scores - lse[h : h + 1, lanes])
        grad = (prob * (dot(kv[:top, value_rows], outer) - delta)).astype(BF)
        dq[rows, lanes] = (SCALE * dot(kvt[rows, :top], grad)).astype(BF)
        dk_new = dot_nt(query, grad)
        dv_new = dot_nt(outer, prob.astype(BF))
        if b == 512 // QB - 1:
            dk_acc[...] = dk_new
            dv_acc[...] = dv_new
        else:
            dk_acc[:, :top] += dk_new
            dv_acc[:, :top] += dv_new
    dkv[rows, :] = dk_acc[...].astype(BF)
    dkv[value_rows, :] = dv_acc[...].astype(BF)


def norm(values, gain):
    inverse = lax.rsqrt(jnp.mean(values * values, axis=-1, keepdims=True) + EPS)
    return (values * inverse * gain).astype(BF)


def norm_back(values, gain, upstream):
    inverse = lax.rsqrt(jnp.mean(values * values, axis=-1, keepdims=True) + EPS)
    normed = values * inverse
    scaled = upstream * gain
    grad = inverse * (scaled - normed * jnp.mean(scaled * normed, axis=-1, keepdims=True))
    return grad, jnp.sum(upstream * normed, axis=0, keepdims=True)


def gelu_parts(u):
    root = 0.7978845608028654
    square = u * u
    bend = jnp.tanh(root * u * (1.0 + 0.044715 * square))
    half = 0.5 * (1.0 + bend)
    slope = half + 0.5 * u * (1.0 - bend * bend) * (root * (1.0 + 0.134145 * square))
    return u * half, slope


class Names:
    pass


FETCHED = ("sk", "sv", "sq", "ck", "cv", "so", "co", "cq", "gate", "up")


def layer_kernel(names, *refs):
    R = Names()
    for name, ref in zip(names, refs, strict=True):
        setattr(R, name, ref)
    me = coords()
    x, c, y, z = me
    g = 2 * x + c
    t = x + 2 * c
    s = 2 * z + y
    group = ((1 - x, c, y, z), (1 - x, 1 - c, y, z), (x, 1 - c, y, z))
    line = tuple((x, c, y, lax.rem(z + k, 4)) for k in (1, 2, 3))
    fetch = [
        pltpu.make_async_copy(getattr(R, name), getattr(R, "v_" + name), R.s_fetch.at[i])
        for i, name in enumerate(FETCHED)
    ]
    for one in fetch:
        one.start()
    near_dn = pltpu.make_async_copy(R.down, R.DN.at[s], R.s_near.at[0])
    near_dn.start()
    greet(me, group + line + ((x, c, 1 - y, z),), moves=True)

    move_x = Move(me, R.tok, R.X.at[s], R.s_move.at[0])
    move_t = Move(me, R.tabs, R.TAB, R.s_move.at[1])
    move_m = Move(me, R.mem, R.M.at[s], R.s_move.at[2])
    move_d = Move(me, R.dout, R.DO.at[z], R.s_move.at[3])
    for one in fetch[:5]:
        one.wait()
    row = lax.broadcasted_iota(jnp.int32, (8, 128), 0)
    gains = jnp.zeros((8, 128), F32)
    for i, one in enumerate((R.g1, R.g2, R.g3)):
        one = jnp.concatenate([one[...].astype(F32), jnp.zeros((1, 104), F32)], axis=1)
        gains = jnp.where(row == i, one, gains)
    gains = jnp.concatenate([gains, jnp.zeros((120, 128), F32)], axis=0).T[:24, :64]
    blank = jnp.zeros((24, 64), F32)
    for k in range(4):
        narrow = slice(192 * k, 192 * k + 192)
        row = [w[:, narrow].astype(F32) for w in (R.v_sk, R.v_sv, R.v_sq)] + [gains]
        row = jnp.concatenate(row + [w[:, narrow].astype(F32) for w in (R.v_ck, R.v_cv)], axis=1)
        R.stage_a[k] = jnp.concatenate([row[:, :512], row[:, 512:]], axis=0).astype(BF)

    def to_group(stage, land, sems):
        return [
            remote(stage.at[2 * to[0] + to[1]], land.at[g], sems.at[0], sems.at[1 + i], to)
            for i, to in enumerate(group)
        ]

    parts_a = to_group(R.stage_a, R.land_a, R.s_part_a)
    for one in parts_a:
        one.start()
    move_x.start()
    for i in range(2):
        length, plot = R.lengths[0, i], R.plots[0, i]
        start = R.lengths[0, 0] if i else 0
        R.tabs[i : i + 1, :] = jnp.full((1, 128), start + length, jnp.int32)
        R.tabs[2 + i : 3 + i, :] = jnp.full((1, 128), plot, jnp.int32)
    R.tabs[4:, :] = jnp.zeros((4, 128), jnp.int32)
    move_t.start()

    def halves_stacked(w):
        w = w[...].astype(F32)
        return jnp.concatenate([w[:, :384], w[:, 384:]], axis=0).astype(BF)

    for one in fetch[5:]:
        one.wait()
    for k in range(4):
        wide = slice(512 * k, 512 * k + 512)
        R.stage_b[k, :24] = R.v_gate[:, wide]
        R.stage_b[k, 24:] = R.v_up[:, wide]
    R.land_a[g] = R.stage_a[g]
    R.land_b[g] = R.stage_b[g]
    gather_x = Gather8(me, R.X, R.s_x, True)
    gather_m = Gather8(me, R.M, R.s_m, True)
    gather_d = Gather4(me, R.DO, R.s_d, tokens=True)
    gather_a = GatherPlane(me, R.PA, R.s_a)
    gather_b = GatherPlane(me, R.PB, R.s_b, slice(0, 384))
    gather_o = GatherPlane(me, R.FO.at[g], R.s_fo)
    gather_c = GatherPlane(me, R.FC.at[g], R.s_fc)
    gather_q = GatherPlane(me, R.FQ.at[g], R.s_fq)
    gather_2 = GatherRelay(me, R.P2, R.s_2)
    gather_n = GatherRelay(me, R.DN, R.s_n)
    whole_o = Gather4(me, R.FO, R.s_wo)
    whole_c = Gather4(me, R.FC, R.s_wc)
    whole_q = Gather4(me, R.FQ, R.s_wq)

    R.FO[g, s] = halves_stacked(R.v_so)
    gather_o.start_along()
    gather_o.start_across()
    R.FQ[g, s] = halves_stacked(R.v_cq)
    R.FC[g, s] = halves_stacked(R.v_co)
    gather_q.start_across()
    gather_c.start_across()
    near_dn.wait()
    gather_n.start_across()
    for one in parts_a:
        one.wait_recv()
    whole = []
    for r in range(4):
        piece = R.land_a[r].astype(F32)
        whole.append(jnp.concatenate([piece[:24], piece[24:]], axis=1))
    whole = jnp.concatenate(whole, axis=0).astype(BF)
    R.PA[s] = whole[:, :640]
    R.PB[s, :, :384] = whole[:, 640:]
    gather_a.start_across()
    gather_a.start_along()
    move_x.arrive()
    gather_x.start()
    parts_b = to_group(R.stage_b, R.land_b, R.s_part_b)
    for one in parts_b:
        one.start()
    move_m.start()
    gather_b.start_along()
    gather_q.start_along()
    gather_c.start_along()
    move_d.start()
    gather_x.forward()
    gather_a.forward(1)
    for k in (1, 3, 2):
        gather_o.forward(k)
    for one in parts_b:
        one.wait_recv()
    for half in range(2):
        rows = [R.land_b[r].astype(F32)[24 * half : 24 * half + 24] for r in range(4)]
        R.P2[s, :, 512 * half : 512 * half + 512] = jnp.concatenate(rows, axis=0).astype(BF)
    gather_2.start_along()
    gather_x.forward_far()
    gather_o.arrive()
    whole_o.start()
    gather_a.forward(3)
    gather_a.forward(2)
    gather_b.start_across()
    move_t.arrive()
    end_one, end_two = R.TAB[0:1, 0:1], R.TAB[1:2, 0:1]
    plot_one, plot_two = R.TAB[2:3, 0:1], R.TAB[3:4, 0:1]
    lane = lax.broadcasted_iota(jnp.int32, (1, 512), 1)
    for i in range(4):
        lanes = slice(128 * i, 128 * i + 128)
        R.info[0:1, lanes] = lane[:, :128] + (2 * i + y) * 128
    qpos = R.info[0:1, :]
    past_one, past_two = qpos >= end_one, qpos >= end_two
    R.info[1:2, :] = jnp.where(past_two, end_two, jnp.where(past_one, end_one, 0))
    R.info[2:3, :] = jnp.where(past_two, 0, jnp.where(past_one, plot_two, plot_one))

    def unpack(pieces, whole, width, step):
        for zz in range(4):

            def one(i, carry):
                lanes = pl.ds(pl.multiple_of(i * step, step), step)
                low = pieces[2 * zz, :, lanes].astype(F32)
                high = pieces[2 * zz + 1, :, lanes].astype(F32)
                for r in range(4):
                    rows = slice(24 * r, 24 * r + 24)
                    both = jnp.concatenate([low[rows], high[rows]], axis=0)
                    whole[192 * r + 48 * zz : 192 * r + 48 * zz + 48, lanes] = both.astype(BF)
                return carry

            lax.fori_loop(0, width // step, one, 0)

    gather_a.arrive()
    unpack(R.PA, R.WA, 640, 128)
    gain_rows = R.WA[:, 512:640].astype(F32).T
    gain_one, gain_two, gain_three = (gain_rows[64 + i : 65 + i] for i in range(3))

    def pair_rows(buf, i):
        return jnp.concatenate([buf[2 * i], buf[2 * i + 1]], axis=0)

    def mine_rows(buf):
        return jnp.concatenate([buf[2 * i + y] for i in range(4)], axis=0)

    def keys_values(i, operand, weight, natural, turned):
        rows = pl.ds(pl.multiple_of(i * 256, 256), 256)
        product = dot(operand, weight[:, :384])
        natural[rows, :] = product.astype(BF)
        turned[:, rows] = product.T.astype(BF)

    def first_norm(i, carry):
        x1 = norm(pair_rows(R.X, i).astype(F32), gain_one)
        R.X1[2 * i] = x1[:128]
        R.X1[2 * i + 1] = x1[128:]
        keys_values(i, x1, R.WA, R.KV, R.KVT)
        return carry

    gather_x.arrive()
    lax.fori_loop(0, 4, first_norm, 0)
    product = SCALE * dot(mine_rows(R.X1), R.WA[:, 384:640])
    R.QT[...] = product.T[:192].astype(BF)

    def share_heads(buf, sems):
        return [Gather4(me, buf.at[:, h], sems.at[h]) for h in range(3)]

    share_1 = share_heads(R.A4, R.s_share1)
    move_m.arrive()
    gather_m.start()
    for h in range(3):
        attend_head(h, R.info, R.QT, R.KV, R.KVT, R.OUT1, R.LSE1, True)
        R.A4[g, h] = R.OUT1[64 * h : 64 * h + 64, :].astype(BF)
        share_1[h].start()
    for k in (1, 3, 2):
        gather_b.forward(k)
    for k in (1, 3, 2):
        gather_q.forward(k)
    whole_o.forward()
    for h in range(3):
        share_1[h].forward()
    gather_m.forward()
    for k in (1, 3, 2):
        gather_c.forward(k)
    gather_2.forward(1)
    gather_n.start_along()
    gather_2.start_across()
    whole_o.arrive()

    def unpack_full(pieces, whole):
        def one(r, carry):
            for zz in range(4):
                low, high = pieces[r, 2 * zz].astype(F32), pieces[r, 2 * zz + 1].astype(F32)
                rows = pl.ds(pl.multiple_of(192 * r + 48 * zz, 16), 48)
                whole[rows, :384] = jnp.concatenate([low[:24], high[:24]], axis=0).astype(BF)
                whole[rows, 384:] = jnp.concatenate([low[24:], high[24:]], axis=0).astype(BF)
            return carry

        lax.fori_loop(0, 4, one, 0)

    unpack_full(R.FO, R.WO)
    for one in share_1:
        one.arrive()

    def project(pieces, weight, i):
        lanes = slice(256 * i, 256 * i + 256)
        turned = pieces[:, :, :, lanes].astype(F32).reshape(768, 256)
        return dot(turned.T.astype(BF), weight[...])

    for i in range(2):
        rows = slice(256 * i, 256 * i + 256)
        before = jnp.concatenate([R.X[4 * i + y], R.X[4 * i + 2 + y]], axis=0).astype(F32)
        first = before + project(R.A4, R.WO, i)
        R.FIRST[rows, :] = first
        R.X2[rows, :] = norm(first, gain_two)
    gather_q.arrive()
    whole_q.start()
    gather_m.forward_far()
    gather_2.forward(2)
    gather_n.forward(1)
    gather_b.arrive()
    unpack(R.PB, R.WB, 384, 128)
    gather_c.arrive()
    whole_c.start()
    move_d.arrive()
    gather_m.arrive()

    def memory_pair(i, carry):
        keys_values(i, pair_rows(R.M, i), R.WB, R.MKV, R.MKVT)
        return carry

    lax.fori_loop(0, 4, memory_pair, 0)
    whole_q.forward()
    whole_q.arrive()
    unpack_full(R.FQ, R.WQ)
    for k in range(4):

        @pl.when(g == k)
        def _():
            R.WCQ[...] = R.WQ[:, 192 * k : 192 * k + 192]

    for i in range(2):
        rows = slice(256 * i, 256 * i + 256)
        product = SCALE * dot(R.X2[rows, :], R.WCQ[...])
        R.CQT[:, rows] = product.T.astype(BF)
    share_2 = share_heads(R.C4, R.s_share2)
    for h in range(3):
        attend_head(h, R.info, R.CQT, R.MKV, R.MKVT, R.OUT2, R.LSE2, False)
        R.C4[g, h] = R.OUT2[64 * h : 64 * h + 64, :].astype(BF)
        share_2[h].start()
        if h == 1:
            gather_2.forward(3)
            gather_n.forward(2)
    gather_d.start()
    whole_c.forward()
    share_2[0].forward()
    share_2[1].forward()
    gather_n.forward(3)
    share_2[2].forward()
    whole_c.arrive()
    unpack_full(R.FC, R.WC)
    for one in share_2:
        one.arrive()
    for i in range(2):
        rows = slice(256 * i, 256 * i + 256)
        second = R.FIRST[rows, :] + project(R.C4, R.WC, i)
        R.SECOND[rows, :] = second
        R.X3[rows, :] = norm(second, gain_three)
    gather_d.forward()
    gather_2.arrive()
    unpack(R.P2, R.W2, 1024, 256)
    for one in parts_a + parts_b:
        one.wait_send()
    gather_2.finish()
    gather_a.finish()
    gather_b.finish()
    sum_dx = Sum4(me, R.DXP, R.by_c_dx, R.by_x_dx, R.s_dx)
    sum_out = Sum4(me, R.OP, R.by_c_out, R.by_x_out, R.s_out)

    def feed_in(core):
        at = pl.ds(pl.multiple_of(core * 256, 256), 256)
        x3 = R.X3[at, :]
        gate, up = dot(x3, R.W2[:, :512]), dot(x3, R.W2[:, 512:])
        active, slope = gelu_parts(gate)
        R.ACTIVE[at, :] = active.astype(BF)
        R.FALL[at, :] = (up * slope).astype(BF)
        R.H[at, :] = (active * up).astype(BF)

    def feed_out(core):
        at = pl.ds(pl.multiple_of(core * 256, 256), 256)
        outer = jnp.concatenate([R.DO[2 * core + px] for px in range(2)], axis=0)
        w_down = R.DN[...].reshape(512, 768)
        hidden_grad = dot_nt(outer, w_down)
        gate_grad = (hidden_grad * R.FALL[at, :].astype(F32)).astype(BF)
        up_grad = (hidden_grad * R.ACTIVE[at, :].astype(F32)).astype(BF)
        dx3 = (dot_nt(gate_grad, R.W2[:, :512]) + dot_nt(up_grad, R.W2[:, 512:])).astype(BF)
        R.GG[at, :512] = gate_grad
        R.GG[at, 512:] = up_grad
        for px in range(2):
            R.DXP[2 * core + px] = dx3[128 * px : 128 * px + 128]

    def feed_sum(core):
        at = pl.ds(pl.multiple_of(core * 256, 256), 256)
        out = dot(R.H[at, :], R.DN[...].reshape(512, 768)).astype(BF)
        for px in range(2):
            R.OP[2 * core + px] = out[128 * px : 128 * px + 128]

    def pack(whole, pieces, start, width):
        for t in range(8):
            rows = [whole[(8 * r + t) * 24 : (8 * r + t) * 24 + 24, :] for r in range(4)]
            pieces[t, :, start : start + width] = jnp.concatenate(rows, axis=0).astype(BF)

    feed_in(1 - c)
    feed_in(c)
    R.X3T[...] = R.X3[...].astype(F32).T.astype(BF)
    gather_n.arrive()
    gather_d.arrive()
    feed_out(1 - c)
    sum_dx.start()
    feed_out(c)
    sum_dx.to_x()
    own = pl.ds(pl.multiple_of(t * 128, 128), 128)
    own_block = 2 * t + y
    total_2 = [
        SumPlaneDirect(me, R.P2, R.by_y_2, R.by_z_2, R.s_g2.at[i], slice(256 * i, 256 * i + 256))
        for i in range(4)
    ]
    for i in range(4):
        R.W2G[...] = dot(R.X3T[...], R.GG[:, 256 * i : 256 * i + 256])
        pack(R.W2G, R.P2, 256 * i, 256)
        total_2[i].start()
    hidden_t = R.H[...].astype(F32).T.astype(BF)
    d_down = dot(hidden_t, R.DO[...].reshape(512, 768)).astype(BF)
    for i in range(8):
        R.DNG[i] = d_down[64 * i : 64 * i + 64]
    total_n = SumPlaneDirect(me, R.DNG, R.by_y_n, R.by_z_n, R.s_gn)
    total_n.start()
    feed_sum(1 - c)
    feed_sum(c)
    sum_out.start()
    part, gain_grad_three = norm_back(R.SECOND[own, :], gain_three, sum_dx.end())
    second_grad = R.DO[t].astype(F32) + part
    R.SGRAD[...] = second_grad
    R.DS4[t] = second_grad.astype(BF)
    share_s = Gather4(me, R.DS4, R.s_s, tokens=True)
    share_s.start()
    total_2[0].fold()
    share_s.forward()
    sum_out.to_x()
    total_2[1].fold()
    total_2[0].pass_one()
    share_s.arrive()

    dsec = R.DS4[...].reshape(512, 768)
    mine_192 = pl.ds(pl.multiple_of(g * 192, 16), 192)
    R.OUTER[...] = dot_nt(R.WC[mine_192, :], dsec).astype(BF)
    share_3 = share_heads(R.DC4, R.s_share3)
    for h in range(3):
        attend_back_head(
            h, R.info, R.CQT, R.MKV, R.MKVT, R.OUTER, R.OUT2, R.LSE2, R.DCQT, R.MDKV, R.dk, R.dv, False
        )
        R.DC4[g, h] = R.DCQT[64 * h : 64 * h + 64, :]
        share_3[h].start()
        if h == 0:
            total_2[2].fold()
        if h == 1:
            share_3[0].forward()
            total_2[0].pass_two()

    def pack_24(whole, pieces):
        for t in range(8):
            rows = whole[24 * t : 24 * t + 24]
            pieces[t] = jnp.concatenate([rows[:, :384], rows[:, 384:]], axis=0).astype(BF)

    def memory_grad_pair(i, carry):
        lanes = pl.ds(pl.multiple_of(i * 256, 256), 256)
        turned = dot(R.WB[:, :384], R.MDKV[:, lanes]).astype(BF)
        R.MG[2 * i] = turned[:, :128]
        R.MG[2 * i + 1] = turned[:, 128:]
        return carry

    total_2[3].fold()
    total_2[1].pass_one()
    lax.fori_loop(0, 4, memory_grad_pair, 0)
    sum_m = Sum8(me, R.MG, R.by_c_m, R.by_x_m, R.by_y_m, R.s_gm)
    share_3[1].forward()
    pack_24(dot(R.C4[g].reshape(192, 512), dsec), R.CO8)
    total_c = SumPlane(me, R.CO8, R.by_y_c, R.by_z_c, R.s_gc)
    total_c.start()
    R.W1G[...] = dot(R.MDKV[...], R.M[...].reshape(1024, 768)).T
    pack(R.W1G, R.PB, 0, 384)
    total_b = SumPlane(me, R.PB, R.by_y_b, R.by_z_b, R.s_gb, slice(0, 384))
    total_b.start()
    share_3[2].forward()
    sum_m.start()
    back = [
        Move(me, src, dst, R.s_back.at[i])
        for i, (src, dst) in enumerate(
            ((R.TBLOCK, R.tokens_out), (R.LBLOCK, R.layer_out), (R.MBLOCK, R.memory_out))
        )
    ]
    R.LBLOCK[...] = (R.SECOND[own, :] + sum_out.end()).astype(BF)
    back[1].start()
    total_2[2].pass_one()
    total_2[1].pass_two()
    for one in share_3:
        one.arrive()

    for i in range(2):
        rows = slice(256 * i, 256 * i + 256)
        dx2 = dot(R.WQ[...], R.DC4[:, :, :, rows].reshape(768, 256)).T
        part, ignored = norm_back(R.FIRST[rows, :], gain_two, dx2)
        R.DFIRST[rows, :] = (dsec[rows].astype(F32) + part).astype(BF)
    R.OUTER[...] = dot_nt(R.WO[mine_192, :], R.DFIRST[...]).astype(BF)
    sum_m.to_x()
    total_n.fold()
    total_2[3].pass_one()

    for h in range(3):
        attend_back_head(
            h, R.info, R.QT, R.KV, R.KVT, R.OUTER, R.OUT1, R.LSE1, R.DQT, R.DKV, R.dk, R.dv, True
        )

    def token_grad_pair(i, carry):
        lanes = pl.ds(pl.multiple_of(i * 256, 256), 256)
        half = pl.ds(pl.multiple_of(i * 128, 128), 128)
        turned = dot(R.WA[:, :384], R.DKV[:, lanes])
        query = dot(R.WA[:, 384:576], R.DQT[:, half])
        R.TG[2 * i] = (turned[:, :128] + jnp.where(y == 0, query, 0.0)).astype(BF)
        R.TG[2 * i + 1] = (turned[:, 128:] + jnp.where(y == 1, query, 0.0)).astype(BF)
        return carry

    lax.fori_loop(0, 4, token_grad_pair, 0)
    sum_t = Sum8(me, R.TG, R.by_c_t, R.by_x_t, R.by_y_t, R.s_gt)
    sum_t.start()
    pack_24(dot(R.A4[g].reshape(192, 512), R.DFIRST[...]), R.SO8)
    total_s = SumPlane(me, R.SO8, R.by_y_s, R.by_z_s, R.s_gs)
    dx2 = dot(R.WQ[...], R.DC4[:, :, :, own].reshape(768, 128)).T
    part, gain_grad_two = norm_back(R.FIRST[own, :], gain_two, dx2)
    R.SGRAD[...] += part
    sum_t.to_x()
    sum_m.to_y()
    total_c.fold()
    total_n.pass_one()
    total_2[2].pass_two()
    R.W1G[...] = dot(R.DKV[...], R.X1[...].reshape(1024, 768)).T
    pack(R.W1G, R.PA, 0, 384)
    total_a = SumPlane(me, R.PA, R.by_y_a, R.by_z_a, R.s_ga, slice(0, 384))
    total_a.start()
    R.TURN[:192, :] = dot(R.DQT[...], mine_rows(R.X1))
    R.TURN[192:, :] = dot(R.DCQT[...], R.X2[...])
    R.W1G[...] = R.TURN[...].T
    pack(R.W1G, R.PB, 384, 384)
    total_q = SumPlaneDirect(me, R.PB, R.by_y_b, R.by_z_b, R.s_gq, slice(384, 768))
    total_b.fold()
    total_2[3].pass_two()
    sum_t.to_y()
    total_q.start()
    total_s.start()
    total_c.pass_one()
    total_n.pass_two()
    total_b.pass_one()
    R.MBLOCK[...] = sum_m.end().T.astype(BF)
    back[2].start()
    total_a.fold()
    total_c.pass_two()
    total_b.pass_two()
    dx1 = sum_t.end().T
    part, gain_grad_one = norm_back(R.X[own_block].astype(F32), gain_one, dx1)
    R.TBLOCK[...] = (R.SGRAD[...] + part).astype(BF)
    back[0].start()
    R.GT[0:1, :] = gain_grad_one
    R.GT[1:2, :] = gain_grad_two
    R.GT[2:3, :] = gain_grad_three
    pack(R.GT[...].T, R.PG, 0, 128)
    total_g = SumPlaneDirect(me, R.PG, R.by_y_g, R.by_z_g, R.s_gg)
    total_g.start()
    for one in total_2:
        one.end()
    rows_2 = R.P2[s].astype(F32)
    for r in range(4):
        rows = slice(24 * r, 24 * r + 24)
        R.stage_b[r] = jnp.concatenate([rows_2[rows, :512], rows_2[rows, 512:]], axis=0).astype(BF)
    last_b = to_group(R.stage_b, R.quarters_b, R.s_last_b)
    for one in last_b:
        one.start()
    total_n.end()
    total_a.pass_one()
    total_q.fold()
    total_a.pass_two()
    total_s.fold()
    total_c.end()
    total_b.end()
    total_q.pass_one()
    total_g.fold()
    total_s.pass_one()
    total_a.end()
    rows_a, rows_b = R.PA[s, :, :384].astype(F32), R.PB[s, :, :384].astype(F32)
    for r in range(4):
        rows = slice(24 * r, 24 * r + 24)
        R.stage_z[r] = jnp.concatenate([rows_a[rows], rows_b[rows]], axis=0).astype(BF)
    last_a = to_group(R.stage_z, R.quarters_a, R.s_last_a)
    for one in last_a:
        one.start()
    total_q.pass_two()
    total_g.pass_one()
    total_s.pass_two()
    total_g.pass_two()
    total_q.end()
    total_g.end()
    rows_q = R.PB[s, :, 384:].astype(F32)
    rows_g = R.PG[s].astype(F32)
    for r in range(4):
        rows = slice(24 * r, 24 * r + 24)
        both = [rows_q[rows, :192], rows_g[rows, :64], rows_q[rows, 192:], blank]
        both = jnp.concatenate(both, axis=1)
        R.stage_q[r] = jnp.concatenate([both[:, :256], both[:, 256:]], axis=0).astype(BF)
    last_q = to_group(R.stage_q, R.quarters_q, R.s_last_q)
    for one in last_q:
        one.start()
    total_s.end()
    near = [
        pltpu.make_async_copy(src, dst, R.s_near.at[1 + i])
        for i, (src, dst) in enumerate(
            (
                (R.stage_z.at[g], R.quarters_a.at[g]),
                (R.stage_q.at[g], R.quarters_q.at[g]),
                (R.stage_b.at[g], R.quarters_b.at[g]),
                (R.CO8.at[s], R.co_out),
                (R.SO8.at[s], R.so_out),
                (R.DNG.at[s], R.down_out),
            )
        )
    ]
    for one in near:
        one.start()
    for one in near:
        one.wait()
    for one in last_a + last_b + last_q:
        one.wait_recv()
    for one in back:
        one.arrive()
        one.finish()
    for one in last_a + last_b + last_q:
        one.wait_send()
    for one in (move_x, move_t, move_m, move_d):
        one.finish()
    for one in (gather_x, gather_m, gather_d, gather_o, gather_c, gather_q, gather_n):
        one.finish()
    for one in (whole_o, whole_c, whole_q, share_s, sum_dx, sum_out, sum_m, sum_t):
        one.finish()
    for one in share_1 + share_2 + share_3 + total_2:
        one.finish()
    for one in (total_a, total_q, total_g, total_b, total_n, total_c, total_s):
        one.finish()


def run_layer(inputs):
    n, d = 128, 768

    def low(*shape):
        return pltpu.VMEM(shape, BF)

    def full(*shape):
        return pltpu.VMEM(shape, F32)

    outs = dict(
        quarters_a=(4, 48, 384),
        quarters_b=(4, 48, 512),
        quarters_q=(4, 48, 256),
        co_out=(48, 384),
        so_out=(48, 384),
        down_out=(64, d),
        tokens_out=(n, d),
        layer_out=(n, d),
        memory_out=(n, d),
    )
    scratch = dict(
        stage_a=low(4, 48, 512), land_a=low(4, 48, 512), stage_z=low(4, 48, 384), stage_q=low(4, 48, 256), stage_b=low(4, 48, 512), land_b=low(4, 48, 512),
        **{"v_" + name: pltpu.VMEM(inputs[name][0].shape, BF) for name in FETCHED},
        s_fetch=dma(len(FETCHED)),
        tabs=pltpu.VMEM((8, 128), jnp.int32), TAB=pltpu.VMEM((8, 128), jnp.int32),
        X=low(8, n, d), M=low(8, n, d), DO=low(4, n, d),
        PA=low(8, 96, 640), PB=low(8, 96, 768), PG=low(8, 96, 128), P2=low(8, 96, 1024), DN=low(8, 64, d),
        FO=low(4, 8, 48, 384), FC=low(4, 8, 48, 384), FQ=low(4, 8, 48, 384),
        WA=low(768, 640), WB=low(768, 384), WCQ=low(768, 192), W2=low(768, 1024), WO=low(d, d), WC=low(d, d), WQ=low(d, d),
        info=pltpu.VMEM((8, 512), jnp.int32),
        X1=low(8, n, d), X2=low(512, d), X3=low(512, d),
        KV=low(1024, 384), KVT=low(384, 1024), MKV=low(1024, 384), MKVT=low(384, 1024),
        QT=low(192, 512), CQT=low(192, 512), OUT1=full(192, 512), OUT2=full(192, 512),
        LSE1=full(8, 512), LSE2=full(8, 512),
        A4=low(4, 3, 64, 512), C4=low(4, 3, 64, 512), DC4=low(4, 3, 64, 512),
        FIRST=full(512, d), SECOND=full(512, d),
        H=low(512, 512), ACTIVE=low(512, 512), FALL=low(512, 512), X3T=low(768, 512), GG=low(512, 1024), DXP=low(4, n, d), OP=low(4, n, d),
        by_c_dx=low(2, n, d), by_x_dx=low(n, d), by_c_out=low(2, n, d), by_x_out=low(n, d),
        W2G=full(768, 256), by_y_2=low(4, 96, 1024), by_z_2=low(5, 96, 1024),
        DNG=low(8, 64, d), by_y_n=low(4, 64, d), by_z_n=low(5, 64, d),
        SGRAD=full(n, d), DS4=low(4, n, d), OUTER=low(192, 512),
        DCQT=low(192, 512), DQT=low(192, 512), MDKV=low(384, 1024), DKV=low(384, 1024),
        dk=full(64, 1024), dv=full(64, 1024),
        CO8=low(8, 48, 384), by_y_c=low(4, 48, 384), by_z_c=low(5, 48, 384),
        SO8=low(8, 48, 384), by_y_s=low(4, 48, 384), by_z_s=low(5, 48, 384),
        MG=low(8, d, n), by_c_m=low(2, 2, d, n), by_x_m=low(2, d, n), by_y_m=low(d, n),
        TG=low(8, d, n), by_c_t=low(2, 2, d, n), by_x_t=low(2, d, n), by_y_t=low(d, n),
        DFIRST=low(512, d), W1G=full(768, 384), TURN=full(384, 768), GT=full(128, 768),
        by_y_a=low(4, 96, 384), by_z_a=low(5, 96, 384), by_y_b=low(4, 96, 768), by_z_b=low(5, 96, 768),
        by_y_g=low(4, 96, 128), by_z_g=low(5, 96, 128),
        TBLOCK=low(n, d), LBLOCK=low(n, d), MBLOCK=low(n, d),
        s_move=dma(4, 2), s_near=dma(7), s_back=dma(3, 2),
        **{name: dma(4) for name in ("s_part_a", "s_part_b", "s_last_a", "s_last_b", "s_last_q", "s_d", "s_wo", "s_wc", "s_wq", "s_s", "s_dx", "s_out")},
        **{name: dma(8) for name in ("s_x", "s_m", "s_gm", "s_gt", "s_a", "s_b", "s_fo", "s_fc", "s_fq")},
        s_2=dma(13), s_n=dma(13), s_share1=dma(3, 4), s_share2=dma(3, 4), s_share3=dma(3, 4), s_g2=dma(4, 10),
        **{name: dma(10) for name in ("s_ga", "s_gb", "s_gq", "s_gg", "s_gn", "s_gc", "s_gs")},
    )
    names = tuple(inputs) + tuple(outs) + tuple(scratch)
    return pl.pallas_call(
        functools.partial(layer_kernel, names),
        out_shape=tuple(jax.ShapeDtypeStruct(shape, BF) for shape in outs.values()),
        in_specs=[spec for _, spec in inputs.values()],
        out_specs=tuple([ANYWHERE] * len(outs)),
        scratch_shapes=list(scratch.values()),
        compiler_params=pltpu.CompilerParams(
            collective_id=1, has_side_effects=True, vmem_limit_bytes=VMEM_LIMIT
        ),
        name="layer",
    )(*[a for a, _ in inputs.values()])


def outputs_kernel(names, *refs):
    R = Names()
    for name, ref in zip(names, refs, strict=True):
        setattr(R, name, ref)

    def copies(pairs, sems):
        made = [pltpu.make_async_copy(a, b, sems.at[i]) for i, (a, b) in enumerate(pairs)]
        for one in made:
            one.start()
        return made

    arrive = copies(
        ((R.qa, R.v_qa), (R.qb, R.v_qb), (R.qq, R.v_qq), (R.co, R.v_co), (R.so, R.v_so), (R.down, R.v_down)), R.s_in
    )
    blocks = copies([(getattr(R, n), getattr(R, "v_" + n)) for n in BLOCKS], R.s_block)
    for one in arrive:
        one.wait()
    gains = jnp.zeros((24, 128), F32)
    for k in range(4):
        piece, last = R.v_qa[k].astype(F32), R.v_qq[k].astype(F32)
        gains = gains + last[:24, 128:]
        narrow = slice(192 * k, 192 * k + 192)
        R.w_sk[:, narrow] = piece[:24, :192]
        R.w_sv[:, narrow] = piece[:24, 192:]
        R.w_ck[:, narrow] = piece[24:, :192]
        R.w_cv[:, narrow] = piece[24:, 192:]
        R.w_sq[:, narrow] = last[:24, :192]
        R.w_cq[:, narrow] = last[24:, :192]
        piece = R.v_qb[k].astype(F32)
        R.w_gate[:, 512 * k : 512 * k + 512] = piece[:24]
        R.w_up[:, 512 * k : 512 * k + 512] = piece[24:]
    for piece, out in ((R.v_so, R.w_so), (R.v_co, R.w_co)):
        rows = piece[...].astype(F32)
        out[:, :384] = rows[:24]
        out[:, 384:] = rows[24:]
    R.w_down[...] = R.v_down[...].astype(F32)
    turned = jnp.concatenate([gains, jnp.zeros((104, 128), F32)], axis=0).T
    for i, out in enumerate((R.w_g1, R.w_g2, R.w_g3)):
        out[...] = turned[64 + i : 65 + i, :24]
    leave = copies([(getattr(R, "w_" + n), getattr(R, "o_" + n)) for n in WEIGHTS], R.s_out)
    for one in blocks:
        one.wait()
    leave += copies([(getattr(R, "v_" + n), getattr(R, "o_" + n)) for n in BLOCKS], R.s_direct)
    for one in leave:
        one.wait()


BLOCKS = ("layer", "tokens", "memory")
WEIGHTS = ("g1", "sq", "sk", "sv", "so", "g2", "cq", "ck", "cv", "co", "g3", "gate", "up", "down")


def write_outputs(results):
    ins = ("qa", "qb", "qq", "co", "so", "down", "tokens", "layer", "memory")
    blocks = BLOCKS
    shapes = {name: (24, 768) for name in WEIGHTS}
    shapes |= {name: (1, 24) for name in ("g1", "g2", "g3")}
    shapes |= dict(gate=(24, 2048), up=(24, 2048), down=(64, 768))
    outs = [jax.ShapeDtypeStruct((128, 768), BF) for _ in blocks]
    outs += [jax.ShapeDtypeStruct(shapes[n], F32) for n in WEIGHTS]
    scratch = {"v_" + n: pltpu.VMEM(a.shape, BF) for n, a in zip(ins, results)}
    scratch |= {"w_" + n: pltpu.VMEM(shapes[n], F32) for n in WEIGHTS}
    scratch |= dict(s_in=dma(6), s_direct=dma(3), s_block=dma(3), s_out=dma(len(WEIGHTS)))
    names = ins + tuple("o_" + n for n in blocks + WEIGHTS) + tuple(scratch)
    return pl.pallas_call(
        functools.partial(outputs_kernel, names),
        out_shape=tuple(outs),
        in_specs=[ANYWHERE] * len(ins),
        out_specs=tuple([ANYWHERE] * len(outs)),
        scratch_shapes=list(scratch.values()),
        compiler_params=pltpu.CompilerParams(vmem_limit_bytes=VMEM_LIMIT),
        name="outputs",
    )(*results)


def body_planes(
    tokens, memory, out_grad, table_lengths, table_plots,
    self_gain, self_query, self_key, self_value, self_output,
    cross_gain, cross_query, cross_key, cross_value, cross_output,
    mlp_gain, mlp_gate, mlp_up, mlp_down,
):
    in_smem = pl.BlockSpec(memory_space=pltpu.SMEM)
    results = run_layer(
        dict(
            tok=(tokens[0], ANYWHERE), mem=(memory[0], ANYWHERE), dout=(out_grad[0], ANYWHERE),
            lengths=(table_lengths, in_smem), plots=(table_plots, in_smem), g1=(self_gain[None], IN_VMEM), g2=(cross_gain[None], IN_VMEM), g3=(mlp_gain[None], IN_VMEM),
            sq=(self_query, ANYWHERE), sk=(self_key, ANYWHERE), sv=(self_value, ANYWHERE), so=(self_output, ANYWHERE),
            cq=(cross_query, ANYWHERE), ck=(cross_key, ANYWHERE), cv=(cross_value, ANYWHERE), co=(cross_output, ANYWHERE),
            gate=(mlp_gate, ANYWHERE), up=(mlp_up, ANYWHERE), down=(mlp_down, ANYWHERE),
        )
    )
    outs = write_outputs(results)
    blocks = tuple(a[None] for a in outs[:3])
    return blocks + tuple(a[0] if a.shape[0] == 1 else a for a in outs[3:])


def solution(mesh):
    placed = (
        P(ROW, SEQ, None),
        P(ROW, SEQ, None),
        P(ROW, SEQ, None),
        P(ROW, None),
        P(ROW, None),
        P(BOTH),
        P(BOTH, None),
        P(BOTH, None),
        P(BOTH, None),
        P(BOTH, None),
        P(BOTH),
        P(BOTH, None),
        P(BOTH, None),
        P(BOTH, None),
        P(BOTH, None),
        P(BOTH),
        P(BOTH, None),
        P(BOTH, None),
        P(BOTH, None),
    )
    small = mesh.shape[ROW] == 4 and mesh.shape[SEQ] == 8
    return jax.shard_map(
        body_planes if small else body_general,
        mesh=mesh,
        in_specs=placed,
        out_specs=(
            P(ROW, SEQ, None),
            P(ROW, SEQ, None),
            P(ROW, SEQ, None),
            P(BOTH),
            P(BOTH, None),
            P(BOTH, None),
            P(BOTH, None),
            P(BOTH, None),
            P(BOTH),
            P(BOTH, None),
            P(BOTH, None),
            P(BOTH, None),
            P(BOTH, None),
            P(BOTH),
            P(BOTH, None),
            P(BOTH, None),
            P(BOTH, None),
        ),
        check_vma=False,
    )
```

```python
import functools

import jax
import jax.numpy as jnp
from jax import lax
from jax.experimental import pallas as pl
from jax.experimental.pallas import tpu as pltpu
from jax.sharding import PartitionSpec as P

HEADS = 12


SCALE = 0.125
EPS = 1e-06
NEG = -1e30
ROW, SEQ = "rows", "seq"
BOTH = (ROW, SEQ)
EQ0 = "rhqk,rkhd->rqhd"
EQ1 = "rhqk,rqhd->rkhd"
EQ2 = "rld,de->rle"
EQ3 = "rld,rle->de"
EQ4 = "rle,de->rld"
EQ5 = "rqhd,rkhd->rhqk"
EQ6 = "rqhd,rqhd->rhq"


def running_sum(lengths):
    ids = jnp.arange(lengths.shape[1], dtype=jnp.int32)
    upto = (ids[None, :] <= ids[:, None]).astype(lengths.dtype)
    return jnp.sum(lengths[:, None, :] * upto[None], axis=2)


def rms_forward(values, gain_vector):
    inverse = lax.rsqrt(jnp.mean(values * values, axis=-1, keepdims=True) + EPS)
    return (values * inverse * gain_vector, inverse)


def rms_backward(values, inverse, gain_vector, upstream):
    normed = values * inverse
    gain_grad = jnp.sum(upstream * normed, axis=(0, 1))
    scaled = upstream * gain_vector
    input_grad = inverse * (scaled - normed * jnp.mean(scaled * normed, axis=-1, keepdims=True))
    return (input_grad, gain_grad)


def matmul(operand, weight):
    return jnp.einsum(EQ2, operand, weight, preferred_element_type=jnp.float32)


def matmul_back(upstream, weight):
    return jnp.einsum(EQ4, upstream, weight, preferred_element_type=jnp.float32)


def weight_grad(operand, upstream):
    return jnp.einsum(EQ3, operand, upstream, preferred_element_type=jnp.float32)


def split_heads(values):
    return values.reshape(values.shape[0], values.shape[1], HEADS, values.shape[2] // HEADS)


def segment_of(places, table_ends):
    return jnp.sum((places[None, :, None] >= table_ends[:, None, :]).astype(jnp.int32), axis=2)


def pair_mask(query_seg, query_pos, key_seg, key_pos, causal):
    same_pair = query_seg[:, :, None] == key_seg[:, None, :]
    if causal:
        same_pair = jnp.logical_and(same_pair, key_pos[None, None, :] <= query_pos[None, :, None])
    return same_pair


def over_blocks(advance_block, fold_state, arrays, block_width):
    piece_rows = arrays[0].shape[1]
    block_count = piece_rows // block_width
    stacked = tuple(
        (
            jnp.moveaxis(
                member.reshape((member.shape[0], block_count, block_width) + member.shape[2:]), 1, 0
            )
            for member in arrays
        )
    )

    def advance(carried, block_items):
        block_index, block_parts = block_items
        return (advance_block(carried, block_parts, block_index * block_width), None)

    fold_state, ignored = lax.scan(
        advance, fold_state, (jnp.arange(block_count, dtype=jnp.int32), stacked)
    )
    return fold_state


def forward_fold(query_heads, query_seg, query_pos, key_segment, causal, block_width):

    def advance_block(fold_state, parts, first_row):
        key_block, value_block = parts
        key_pos = first_row + jnp.arange(key_block.shape[1], dtype=jnp.int32)
        allowed = pair_mask(query_seg, query_pos, key_segment(key_pos), key_pos, causal)

        def compute(current):
            running_max, running_sum, accumulated = current
            scores = (
                jnp.einsum(
                    EQ5,
                    query_heads,
                    split_heads(key_block),
                    preferred_element_type=jnp.float32,
                )
                * SCALE
            )
            scores = jnp.where(allowed[:, None], scores, NEG)
            new_max = jnp.maximum(running_max, jnp.max(scores, axis=-1))
            weights = jnp.where(allowed[:, None], jnp.exp(scores - new_max[..., None]), 0.0)
            factor = jnp.exp(running_max - new_max)
            new_sum = running_sum * factor + jnp.sum(weights, axis=-1)
            update = jnp.einsum(
                EQ0,
                weights.astype(jnp.bfloat16),
                split_heads(value_block),
                preferred_element_type=jnp.float32,
            )
            return (
                new_max,
                new_sum,
                accumulated * jnp.transpose(factor, (0, 2, 1))[..., None] + update,
            )

        return compute(fold_state)

    def forward_fold_piece(fold_state, shard_piece, first_row):
        return over_blocks(advance_block, fold_state, shard_piece, block_width)

    return forward_fold_piece


def finish(fold_state):
    running_max, running_sum, accumulated = fold_state
    attended = accumulated / jnp.transpose(running_sum, (0, 2, 1))[..., None]
    return (attended, running_max + jnp.log(running_sum))


def query_grad_fold(
    query_heads,
    out_heads,
    log_total,
    row_delta,
    query_seg,
    query_pos,
    key_segment,
    causal,
    block_width,
):

    def advance_block(fold_state, parts, first_row):
        key_block, value_block = parts
        key_pos = first_row + jnp.arange(key_block.shape[1], dtype=jnp.int32)
        allowed = pair_mask(query_seg, query_pos, key_segment(key_pos), key_pos, causal)

        def compute(current):
            key_heads = split_heads(key_block)
            scores = (
                jnp.einsum(
                    EQ5, query_heads, key_heads, preferred_element_type=jnp.float32
                )
                * SCALE
            )
            scores = jnp.where(allowed[:, None], scores, NEG)
            probabilities = jnp.where(allowed[:, None], jnp.exp(scores - log_total[..., None]), 0.0)
            prob_grad = jnp.einsum(
                EQ5,
                out_heads,
                split_heads(value_block),
                preferred_element_type=jnp.float32,
            )
            score_grad = (probabilities * (prob_grad - row_delta[..., None])).astype(jnp.bfloat16)
            return current + SCALE * jnp.einsum(
                EQ0, score_grad, key_heads, preferred_element_type=jnp.float32
            )

        return compute(fold_state)

    def query_fold_piece(fold_state, shard_piece, first_row):
        return over_blocks(advance_block, fold_state, shard_piece, block_width)

    return query_fold_piece


def key_grad_fold(
    key_heads,
    value_heads,
    key_seg,
    key_pos,
    total_rows,
    delta_rows,
    query_segment,
    causal,
    block_width,
):

    def advance_block(fold_state, parts, first_row):
        query_block, out_block = parts
        piece_rows = query_block.shape[1]
        query_pos = first_row + jnp.arange(piece_rows, dtype=jnp.int32)
        allowed = pair_mask(query_segment(query_pos), query_pos, key_seg, key_pos, causal)
        total_block = lax.dynamic_slice_in_dim(total_rows, first_row, piece_rows, 2)
        delta_block = lax.dynamic_slice_in_dim(delta_rows, first_row, piece_rows, 2)

        def compute(current):
            key_acc, value_acc = current
            query_heads = split_heads(query_block)
            out_heads = split_heads(out_block)
            scores = (
                jnp.einsum(
                    EQ5, query_heads, key_heads, preferred_element_type=jnp.float32
                )
                * SCALE
            )
            scores = jnp.where(allowed[:, None], scores, NEG)
            probabilities = jnp.where(
                allowed[:, None], jnp.exp(scores - total_block[..., None]), 0.0
            )
            value_acc = value_acc + jnp.einsum(
                EQ1,
                probabilities.astype(jnp.bfloat16),
                out_heads,
                preferred_element_type=jnp.float32,
            )
            prob_grad = jnp.einsum(
                EQ5, out_heads, value_heads, preferred_element_type=jnp.float32
            )
            score_grad = (probabilities * (prob_grad - delta_block[..., None])).astype(jnp.bfloat16)
            key_acc = key_acc + SCALE * jnp.einsum(
                EQ1, score_grad, query_heads, preferred_element_type=jnp.float32
            )
            return (key_acc, value_acc)

        return compute(fold_state)

    def key_fold_piece(fold_state, shard_piece, first_row):
        return over_blocks(advance_block, fold_state, shard_piece, block_width)

    return key_fold_piece


def body_general(
    tokens,
    memory,
    out_grad,
    table_lengths,
    table_plots,
    self_gain,
    self_query,
    self_key,
    self_value,
    self_output,
    cross_gain,
    cross_query,
    cross_key,
    cross_value,
    cross_output,
    mlp_gain,
    mlp_gate,
    mlp_up,
    mlp_down,
):
    def whole(shard):
        return lax.all_gather(shard, BOTH, axis=0, tiled=True)

    all_self_gain = whole(self_gain)
    all_self_query = whole(self_query)
    all_self_key = whole(self_key)
    all_self_value = whole(self_value)
    all_self_output = whole(self_output)
    all_cross_gain = whole(cross_gain)
    all_cross_query = whole(cross_query)
    all_cross_key = whole(cross_key)
    all_cross_value = whole(cross_value)
    all_cross_output = whole(cross_output)
    all_mlp_gain = whole(mlp_gain)
    all_mlp_gate = whole(mlp_gate)
    all_mlp_up = whole(mlp_up)
    all_mlp_down = whole(mlp_down)
    seq_count = lax.axis_size(SEQ)
    seq_index = lax.axis_index(SEQ)
    row_count = tokens.shape[0]
    positions = tokens.shape[1]
    memory_cols = memory.shape[1]
    width = tokens.shape[2]
    head_size = width // HEADS
    query_pos = seq_index * positions + jnp.arange(positions, dtype=jnp.int32)
    memory_pos = seq_index * memory_cols + jnp.arange(memory_cols, dtype=jnp.int32)
    table_ends = running_sum(table_lengths)
    tables = table_lengths.shape[1]
    table_ids = jnp.arange(tables, dtype=jnp.int32)
    plot_width = memory_cols * seq_count // tables

    def token_segment(places):
        return segment_of(places, table_ends)

    def token_plot(places):
        segments = segment_of(places, table_ends)
        return jnp.sum(
            jnp.where(segments[:, :, None] == table_ids[None, None, :], table_plots[:, None, :], 0),
            axis=2,
        )

    def memory_plot(places):
        return (places // plot_width)[None, :]

    def start_state():
        return (
            jnp.full((row_count, HEADS, positions), NEG, jnp.float32),
            jnp.zeros((row_count, HEADS, positions), jnp.float32),
            jnp.zeros((row_count, positions, HEADS, head_size), jnp.float32),
        )

    values = tokens.astype(jnp.float32)
    normed_one, inverse_one = rms_forward(values, all_self_gain.astype(jnp.float32))
    input_one = normed_one.astype(jnp.bfloat16)
    queries = matmul(input_one, all_self_query).astype(jnp.bfloat16)
    key_rows = matmul(input_one, all_self_key).astype(jnp.bfloat16)
    value_rows = matmul(input_one, all_self_value).astype(jnp.bfloat16)
    query_seg = token_segment(query_pos)
    self_fold = forward_fold(
        split_heads(queries), query_seg, query_pos, token_segment, True, positions
    )
    self_out, self_total = finish(
        self_fold(
            start_state(),
            (
                lax.all_gather(key_rows, SEQ, axis=1, tiled=True),
                lax.all_gather(value_rows, SEQ, axis=1, tiled=True),
            ),
            jnp.int32(0),
        )
    )
    self_att = self_out.reshape(row_count, positions, width).astype(jnp.bfloat16)
    first_sum = values + matmul(self_att, all_self_output)
    normed_two, inverse_two = rms_forward(first_sum, all_cross_gain.astype(jnp.float32))
    input_two = normed_two.astype(jnp.bfloat16)
    cross_rows = matmul(input_two, all_cross_query).astype(jnp.bfloat16)
    memory_keys = matmul(memory, all_cross_key).astype(jnp.bfloat16)
    memory_rows = matmul(memory, all_cross_value).astype(jnp.bfloat16)
    query_plot = token_plot(query_pos)
    cross_fold = forward_fold(
        split_heads(cross_rows), query_plot, query_pos, memory_plot, False, memory_cols
    )
    cross_out, cross_total = finish(
        cross_fold(
            start_state(),
            (
                lax.all_gather(memory_keys, SEQ, axis=1, tiled=True),
                lax.all_gather(memory_rows, SEQ, axis=1, tiled=True),
            ),
            jnp.int32(0),
        )
    )
    cross_att = cross_out.reshape(row_count, positions, width).astype(jnp.bfloat16)
    second_sum = first_sum + matmul(cross_att, all_cross_output)
    normed_three, inverse_three = rms_forward(second_sum, all_mlp_gain.astype(jnp.float32))
    input_three = normed_three.astype(jnp.bfloat16)
    gate_pre = matmul(input_three, all_mlp_gate)
    up_pre = matmul(input_three, all_mlp_up)

    def gated_unit(gate_value, up_value):
        return jax.nn.gelu(gate_value, approximate=True) * up_value

    hidden_value, gated_back = jax.vjp(gated_unit, gate_pre, up_pre)
    hidden = hidden_value.astype(jnp.bfloat16)
    layer_out = (second_sum + matmul(hidden, all_mlp_down)).astype(jnp.bfloat16)
    upstream = out_grad.astype(jnp.float32)
    grad_down = weight_grad(hidden, out_grad)
    hidden_grad = matmul_back(out_grad, all_mlp_down)
    gate_grad, up_grad = gated_back(hidden_grad)
    gate_low = gate_grad.astype(jnp.bfloat16)
    up_low = up_grad.astype(jnp.bfloat16)
    grad_gate = weight_grad(input_three, gate_low)
    grad_up = weight_grad(input_three, up_low)
    three_grad = matmul_back(gate_low, all_mlp_gate) + matmul_back(
        up_low, all_mlp_up
    )
    part_three, grad_gain_three = rms_backward(
        second_sum, inverse_three, all_mlp_gain.astype(jnp.float32), three_grad
    )
    second_grad = upstream + part_three
    cross_branch = second_grad.astype(jnp.bfloat16)
    grad_cross_output = weight_grad(cross_att, cross_branch)
    cross_dout = matmul_back(cross_branch, all_cross_output).astype(jnp.bfloat16)
    cross_heads = split_heads(cross_dout)
    cross_delta = jnp.einsum(EQ6, cross_heads.astype(jnp.float32), cross_out)
    cross_total_all, cross_delta_all = (
        lax.all_gather(cross_total, SEQ, axis=2, tiled=True),
        lax.all_gather(cross_delta, SEQ, axis=2, tiled=True),
    )
    cross_query_fold = query_grad_fold(
        split_heads(cross_rows),
        cross_heads,
        cross_total,
        cross_delta,
        query_plot,
        query_pos,
        memory_plot,
        False,
        memory_cols,
    )
    cross_rows_grad = cross_query_fold(
        jnp.zeros((row_count, positions, HEADS, head_size), jnp.float32),
        (
            lax.all_gather(memory_keys, SEQ, axis=1, tiled=True),
            lax.all_gather(memory_rows, SEQ, axis=1, tiled=True),
        ),
        jnp.int32(0),
    )
    cross_rows_low = cross_rows_grad.reshape(row_count, positions, width).astype(jnp.bfloat16)
    memory_fold = key_grad_fold(
        split_heads(memory_keys),
        split_heads(memory_rows),
        memory_plot(memory_pos),
        memory_pos,
        cross_total_all,
        cross_delta_all,
        token_plot,
        False,
        positions,
    )
    memory_zero = jnp.zeros((row_count, memory_cols, HEADS, head_size), jnp.float32)
    memory_key_grad, memory_value_grad = memory_fold(
        (memory_zero, memory_zero),
        (
            lax.all_gather(cross_rows, SEQ, axis=1, tiled=True),
            lax.all_gather(cross_dout, SEQ, axis=1, tiled=True),
        ),
        jnp.int32(0),
    )
    memory_key_low = memory_key_grad.reshape(row_count, memory_cols, width).astype(jnp.bfloat16)
    memory_value_low = memory_value_grad.reshape(row_count, memory_cols, width).astype(jnp.bfloat16)
    grad_cross_query = weight_grad(input_two, cross_rows_low)
    grad_cross_key = weight_grad(memory, memory_key_low)
    grad_cross_value = weight_grad(memory, memory_value_low)
    memory_grad = (
        matmul_back(memory_key_low, all_cross_key)
        + matmul_back(memory_value_low, all_cross_value)
    ).astype(jnp.bfloat16)
    two_grad = matmul_back(cross_rows_low, all_cross_query)
    part_two, grad_gain_two = rms_backward(
        first_sum, inverse_two, all_cross_gain.astype(jnp.float32), two_grad
    )
    first_grad = second_grad + part_two
    self_branch = first_grad.astype(jnp.bfloat16)
    grad_self_output = weight_grad(self_att, self_branch)
    self_dout = matmul_back(self_branch, all_self_output).astype(jnp.bfloat16)
    self_heads = split_heads(self_dout)
    self_delta = jnp.einsum(EQ6, self_heads.astype(jnp.float32), self_out)
    self_total_all, self_delta_all = (
        lax.all_gather(self_total, SEQ, axis=2, tiled=True),
        lax.all_gather(self_delta, SEQ, axis=2, tiled=True),
    )
    self_query_fold = query_grad_fold(
        split_heads(queries),
        self_heads,
        self_total,
        self_delta,
        query_seg,
        query_pos,
        token_segment,
        True,
        positions,
    )
    queries_grad = self_query_fold(
        jnp.zeros((row_count, positions, HEADS, head_size), jnp.float32),
        (
            lax.all_gather(key_rows, SEQ, axis=1, tiled=True),
            lax.all_gather(value_rows, SEQ, axis=1, tiled=True),
        ),
        jnp.int32(0),
    )
    queries_low = queries_grad.reshape(row_count, positions, width).astype(jnp.bfloat16)
    self_key_fold = key_grad_fold(
        split_heads(key_rows),
        split_heads(value_rows),
        query_seg,
        query_pos,
        self_total_all,
        self_delta_all,
        token_segment,
        True,
        positions,
    )
    token_zero = jnp.zeros((row_count, positions, HEADS, head_size), jnp.float32)
    key_grad, value_grad = self_key_fold(
        (token_zero, token_zero),
        (
            lax.all_gather(queries, SEQ, axis=1, tiled=True),
            lax.all_gather(self_dout, SEQ, axis=1, tiled=True),
        ),
        jnp.int32(0),
    )
    key_low = key_grad.reshape(row_count, positions, width).astype(jnp.bfloat16)
    value_low = value_grad.reshape(row_count, positions, width).astype(jnp.bfloat16)
    grad_self_query = weight_grad(input_one, queries_low)
    grad_self_key = weight_grad(input_one, key_low)
    grad_self_value = weight_grad(input_one, value_low)
    one_grad = (
        matmul_back(queries_low, all_self_query)
        + matmul_back(key_low, all_self_key)
        + matmul_back(value_low, all_self_value)
    )
    part_one, grad_gain_one = rms_backward(
        values, inverse_one, all_self_gain.astype(jnp.float32), one_grad
    )
    tokens_grad = (first_grad + part_one).astype(jnp.bfloat16)
    summed = tuple(
        (
            lax.psum_scatter(grad_gain_one, BOTH, scatter_dimension=0, tiled=True),
            lax.psum_scatter(grad_self_query, BOTH, scatter_dimension=0, tiled=True),
            lax.psum_scatter(grad_self_key, BOTH, scatter_dimension=0, tiled=True),
            lax.psum_scatter(grad_self_value, BOTH, scatter_dimension=0, tiled=True),
            lax.psum_scatter(grad_self_output, BOTH, scatter_dimension=0, tiled=True),
            lax.psum_scatter(grad_gain_two, BOTH, scatter_dimension=0, tiled=True),
            lax.psum_scatter(grad_cross_query, BOTH, scatter_dimension=0, tiled=True),
            lax.psum_scatter(grad_cross_key, BOTH, scatter_dimension=0, tiled=True),
            lax.psum_scatter(grad_cross_value, BOTH, scatter_dimension=0, tiled=True),
            lax.psum_scatter(grad_cross_output, BOTH, scatter_dimension=0, tiled=True),
            lax.psum_scatter(grad_gain_three, BOTH, scatter_dimension=0, tiled=True),
            lax.psum_scatter(grad_gate, BOTH, scatter_dimension=0, tiled=True),
            lax.psum_scatter(grad_up, BOTH, scatter_dimension=0, tiled=True),
            lax.psum_scatter(grad_down, BOTH, scatter_dimension=0, tiled=True),
        )
    )
    return (layer_out, tokens_grad, memory_grad) + summed


MESH = pl.DeviceIdType.MESH
BF = jnp.bfloat16
F32 = jnp.float32
QW = 1152
VMEM_LIMIT = 62 * 1024 * 1024


def coords():
    r = lax.axis_index(ROW)
    s = lax.axis_index(SEQ)
    return lax.div(r, 2), lax.rem(r, 2), lax.rem(s, 2), lax.div(s, 2)


def dev(x, c, y, z):
    return {ROW: 2 * x + c, SEQ: 2 * z + y}


def remote(src, dst, send_sem, recv_sem, to):
    return pltpu.make_async_remote_copy(
        src_ref=src,
        dst_ref=dst,
        send_sem=send_sem,
        recv_sem=recv_sem,
        device_id=dev(*to),
        device_id_type=MESH,
    )


def owner_of(x, c, y, z):
    return lax.rem(z, 2), lax.div(z, 2), y, 2 * c + x


def is_fixed(x, c, y, z):
    return 2 * c + x == z


def greet(me, pairs=(), z_line=False, moves=False):
    x, c, y, z = me
    bar = pltpu.get_barrier_semaphore()

    def hello(to):
        pl.semaphore_signal(bar, 1, device_id=dev(*to), device_id_type=MESH)

    count = len(pairs)
    for to in pairs:
        hello(to)
    if z_line:

        @pl.when(z > 0)
        def _():
            hello((x, c, y, z - 1))

        @pl.when(z < 3)
        def _():
            hello((x, c, y, z + 1))

        count = count + jnp.where(z > 0, 1, 0) + jnp.where(z < 3, 1, 0)
    if moves:
        away = jnp.logical_not(is_fixed(*me))

        @pl.when(away)
        def _():
            hello(owner_of(*me))

        count = count + jnp.where(away, 1, 0)
    pl.semaphore_wait(bar, count)


class Move:
    def __init__(self, me, src, dst, sems):
        self.far = remote(src, dst, sems.at[0], sems.at[1], owner_of(*me))
        self.near = pltpu.make_async_copy(src, dst, sems.at[0])
        self.fixed = is_fixed(*me)

    def start(self):
        @pl.when(self.fixed)
        def _():
            self.near.start()

        @pl.when(jnp.logical_not(self.fixed))
        def _():
            self.far.start()

    def arrive(self):
        @pl.when(self.fixed)
        def _():
            self.near.wait()

        @pl.when(jnp.logical_not(self.fixed))
        def _():
            self.far.wait_recv()

    def finish(self):
        @pl.when(jnp.logical_not(self.fixed))
        def _():
            self.far.wait_send()


class Gather4:
    def __init__(self, me, buf, sems, tokens=False):
        x, c, y, z = me
        xp, cp = (1 - x, c, y, z), (x, 1 - c, y, z)
        g = x + 2 * c if tokens else 2 * x + c
        far = 1 - x + 2 * c if tokens else 2 * (1 - x) + c
        self.x_own = remote(buf.at[g], buf.at[g], sems.at[0], sems.at[1], xp)
        self.c_own = remote(buf.at[g], buf.at[g], sems.at[0], sems.at[2], cp)
        self.c_far = remote(buf.at[far], buf.at[far], sems.at[0], sems.at[3], cp)

    def start(self):
        self.x_own.start()
        self.c_own.start()

    def forward(self):
        self.x_own.wait_recv()
        self.c_far.start()

    def arrive(self):
        self.c_own.wait_recv()
        self.c_far.wait_recv()

    def finish(self):
        self.x_own.wait_send()
        self.c_own.wait_send()
        self.c_far.wait_send()


class Gather8:
    def __init__(self, me, buf, sems, split=False):
        x, c, y, z = me
        xp, cp, yp = (1 - x, c, y, z), (x, 1 - c, y, z), (x, c, 1 - y, z)
        def piece(px, pc, py):
            return buf.at[2 * (px + 2 * pc) + py]

        def send(p, k, to):
            return remote(p, p, sems.at[0], sems.at[1 + k], to)

        own, at_x = piece(x, c, y), piece(1 - x, c, y)
        at_y, at_d = piece(x, c, 1 - y), piece(1 - x, c, 1 - y)
        self.x_own = send(own, 0, xp)
        self.y_own = send(own, 1, yp)
        self.c_own = send(own, 2, cp)
        self.c_x = send(at_x, 3, cp)
        self.c_y = send(at_y, 4, cp)
        self.c_d = send(at_d, 5, cp)
        self.d_by_x = send(at_y, 6, xp)
        self.d_by_y = send(at_x, 6, yp)
        self.by_y = jnp.logical_and(c == 0, split)

    def start(self):
        self.start_x()
        self.start_y()

    def start_x(self):
        self.x_own.start()
        self.c_own.start()

    def start_y(self):
        self.y_own.start()

    def forward(self):
        self.y_own.wait_recv()

        @pl.when(jnp.logical_not(self.by_y))
        def _():
            self.d_by_x.start()

        self.c_y.start()
        self.x_own.wait_recv()

        @pl.when(self.by_y)
        def _():
            self.d_by_y.start()

        self.c_x.start()

    def forward_far(self):
        self.d_by_x.wait_recv()
        self.c_d.start()

    def arrive(self):
        for one in (self.c_own, self.c_x, self.c_y, self.c_d):
            one.wait_recv()

    def finish(self):
        for one in (self.x_own, self.y_own, self.c_own, self.c_x, self.c_y, self.c_d, self.d_by_x):
            one.wait_send()


QB = 256


def dot(a, b):
    return lax.dot_general(a, b, (((1,), (0,)), ((), ())), preferred_element_type=F32)


def dot_nt(a, b):
    return lax.dot_general(a, b, (((1,), (1,)), ((), ())), preferred_element_type=F32)


def dot_tn(a, b):
    return lax.dot_general(a, b, (((0,), (0,)), ((), ())), preferred_element_type=F32)


def masked(scores, info, lanes, causal):
    keys = scores.shape[0]
    if causal:
        pos = lax.broadcasted_iota(jnp.int32, scores.shape, 0)
        allowed = jnp.logical_and(pos >= info[1:2, lanes], pos <= info[0:1, lanes])
        return jnp.where(allowed, scores, NEG)
    plot = info[2:3, lanes]
    half = keys // 2
    low = jnp.where(plot == 0, 0.0, NEG)
    high = jnp.where(plot == 1, 0.0, NEG)
    return jnp.concatenate([scores[:half] + low, scores[half:] + high], axis=0)


class GatherPlane:
    def __init__(self, me, buf, sems, lanes=None):
        x, c, y, z = me

        def send(p, k, to):
            piece = buf.at[2 * p + y] if lanes is None else buf.at[2 * p + y, :, lanes]
            return remote(piece, piece, sems.at[0], sems.at[1 + k], to)

        yp = (x, c, 1 - y, z)
        self.along = [send(z, k - 1, (x, c, y, lax.rem(z + k, 4))) for k in (1, 2, 3)]
        self.across = [send(z, 3, yp)]
        self.across += [send(lax.rem(z + 4 - k, 4), 3 + k, yp) for k in (1, 2, 3)]

    def start_along(self):
        for one in self.along:
            one.start()

    def start_across(self):
        self.across[0].start()

    def forward(self, k):
        self.along[k - 1].wait_recv()
        self.across[k].start()

    def arrive(self):
        for one in self.across:
            one.wait_recv()

    def finish(self):
        for one in self.along + self.across:
            one.wait_send()


class GatherRelay:
    def __init__(self, me, buf, sems, lanes=None):
        self.me, self.buf, self.sems, self.lanes = me, buf, sems, lanes

    def piece(self, p, y):
        return self.buf.at[2 * p + y] if self.lanes is None else self.buf.at[2 * p + y, :, self.lanes]

    def send(self, p, k, to):
        piece = self.piece(p, self.me[2])
        return remote(piece, piece, self.sems.at[0], self.sems.at[1 + k + p], to)

    def up(self, p):
        x, c, y, z = self.me
        return self.send(p, 0, (x, c, y, z + 1))

    def down(self, p):
        x, c, y, z = self.me
        return self.send(p, 4, (x, c, y, z - 1))

    def across(self, p):
        x, c, y, z = self.me
        return self.send(p, 8, (x, c, 1 - y, z))

    def start_along(self):
        z = self.me[3]

        @pl.when(z < 3)
        def _():
            self.up(z).start()

        @pl.when(z > 0)
        def _():
            self.down(z).start()

    def start_across(self):
        self.across(self.me[3]).start()

    def forward(self, k):
        z = self.me[3]

        @pl.when(z - k >= 0)
        def _():
            p = z - k
            self.up(p).wait_recv()
            if k < 3:

                @pl.when(z < 3)
                def _():
                    self.up(p).start()

            self.across(p).start()

        @pl.when(z + k <= 3)
        def _():
            p = z + k
            self.down(p).wait_recv()
            if k < 3:

                @pl.when(z > 0)
                def _():
                    self.down(p).start()

            self.across(p).start()

    def arrive(self):
        for p in range(4):
            self.across(p).wait_recv()

    def finish(self):
        z = self.me[3]
        for p in range(4):
            self.across(p).wait_send()

            @pl.when(jnp.logical_and(z < 3, p <= z))
            def _():
                self.up(p).wait_send()

            @pl.when(jnp.logical_and(z > 0, p >= z))
            def _():
                self.down(p).wait_send()


class SumPlane:
    def __init__(self, me, parts, by_y, by_z, sems, lanes=None):
        self.me, self.parts, self.by_y, self.by_z, self.sems = me, parts, by_y, by_z, sems
        self.lanes = slice(None) if lanes is None else lanes

    def mine(self, p):
        return self.parts.at[2 * p + self.me[2], :, self.lanes]

    def from_y(self, p):
        return self.by_y.at[p, :, self.lanes]

    def slot(self, k):
        return self.by_z.at[k, :, self.lanes]

    def across(self, p):
        x, c, y, z = self.me
        theirs = self.parts.at[2 * p + 1 - y, :, self.lanes]
        return remote(theirs, self.from_y(p), self.sems.at[0], self.sems.at[1 + p], (x, c, 1 - y, z))

    def up_slot(self, p):
        return self.slot(p - 1)

    def down_slot(self, q):
        return self.slot(lax.rem(3 + q, 5))

    def up(self, p):
        x, c, y, z = self.me
        send, recv = self.sems.at[0], self.sems.at[4 + p]
        return remote(self.mine(p), self.up_slot(p), send, recv, (x, c, y, z + 1))

    def down(self, q):
        x, c, y, z = self.me
        send, recv = self.sems.at[0], self.sems.at[5 + lax.rem(3 + q, 5)]
        return remote(self.mine(q), self.down_slot(q), send, recv, (x, c, y, z - 1))

    def start(self):
        for p in (3, 0, 2, 1):
            self.across(p).start()

    def fold(self, steps=(3, 0, 2, 1)):
        z = self.me[3]
        for p in steps:
            self.across(p).wait_recv()
            add_into(self.mine(p), self.from_y(p))
            if p > 0:

                @pl.when(z == 0)
                def _():
                    self.up(p).start()

            if p < 3:

                @pl.when(z == 3)
                def _():
                    self.down(p).start()

    def relay_up(self, p):
        self.up(p).wait_recv()
        add_into(self.mine(p), self.up_slot(p))
        self.up(p).start()

    def relay_down(self, q):
        self.down(q).wait_recv()
        add_into(self.mine(q), self.down_slot(q))
        self.down(q).start()

    def pass_one(self):
        z = self.me[3]

        @pl.when(z == 1)
        def _():
            self.relay_up(3)
            self.relay_up(2)

        @pl.when(z == 2)
        def _():
            self.relay_down(0)
            self.relay_down(1)

    def pass_two(self):
        z = self.me[3]

        @pl.when(z == 2)
        def _():
            self.relay_up(3)

        @pl.when(z == 1)
        def _():
            self.relay_down(0)

    def end(self):
        z = self.me[3]

        @pl.when(z > 0)
        def _():
            self.up(z).wait_recv()
            add_into(self.mine(z), self.up_slot(z))

        @pl.when(z < 3)
        def _():
            self.down(z).wait_recv()
            add_into(self.mine(z), self.down_slot(z))

    def finish(self):
        z = self.me[3]
        for p in range(4):
            self.across(p).wait_send()

            @pl.when(z < p)
            def _():
                self.up(p).wait_send()

            @pl.when(z > p)
            def _():
                self.down(p).wait_send()


class SumPlaneDirect(SumPlane):
    def straight(self, k):
        x, c, y, z = self.me
        p = lax.rem(z + k, 4)
        send, recv = self.sems.at[0], self.sems.at[4 + k]
        return remote(self.mine(p), self.slot(k - 1), send, recv, (x, c, y, p))

    def start(self):
        for k in (2, 1, 3, 0):
            self.across(lax.rem(self.me[3] + k, 4)).start()

    def fold(self, steps=(2, 1, 3, 0)):
        for k in steps:
            p = lax.rem(self.me[3] + k, 4)
            self.across(p).wait_recv()
            add_into(self.mine(p), self.from_y(p))
            if k:
                self.straight(k).start()

    def pass_one(self):
        pass

    def pass_two(self):
        pass

    def end(self):
        for k in (1, 2, 3):
            self.straight(k).wait_recv()
            add_into(self.mine(self.me[3]), self.slot(k - 1))

    def finish(self):
        for p in range(4):
            self.across(p).wait_send()
        for k in (1, 2, 3):
            self.straight(k).wait_send()


class Sum8:
    def __init__(self, me, parts, by_c, by_x, by_y, sems):
        x, c, y, z = me
        self.me, self.parts = me, parts
        self.by_c, self.by_x, self.by_y = by_c, by_x, by_y
        xp, cp, yp = (1 - x, c, y, z), (x, 1 - c, y, z), (x, c, 1 - y, z)

        def send(src, dst, k, to):
            return remote(src, dst, sems.at[0], sems.at[1 + k], to)

        self.order = [(1 - x, 1 - y), (1 - x, y), (x, 1 - y), (x, y)]
        self.first = [
            send(parts.at[2 * (px + 2 * (1 - c)) + py], by_c.at[px, py], k, cp)
            for k, (px, py) in enumerate(self.order)
        ]
        self.second = [
            send(by_c.at[1 - x, py], by_x.at[py], 4 + k, xp) for k, py in enumerate((1 - y, y))
        ]
        self.third = send(by_x.at[1 - y], by_y, 6, yp)

    def start(self):
        for one in self.first:
            one.start()

    def to_x(self):
        x, c, y, z = self.me
        for k, py in enumerate((1 - y, y)):
            self.first[k].wait_recv()
            add_into(self.by_c.at[1 - x, py], self.parts.at[2 * (1 - x + 2 * c) + py])
            self.second[k].start()

    def to_y(self):
        x, c, y, z = self.me
        self.first[2].wait_recv()
        self.first[3].wait_recv()
        add_into(self.by_c.at[x, 1 - y], self.parts.at[2 * (x + 2 * c) + 1 - y])
        self.second[0].wait_recv()
        add_into(self.by_x.at[1 - y], self.by_c.at[x, 1 - y])
        self.third.start()

    def end(self):
        x, c, y, z = self.me
        self.second[1].wait_recv()
        self.third.wait_recv()
        return (
            self.parts[2 * (x + 2 * c) + y].astype(F32)
            + self.by_c[x, y].astype(F32)
            + self.by_x[y].astype(F32)
            + self.by_y[...].astype(F32)
        )

    def finish(self):
        for one in self.first + self.second + [self.third]:
            one.wait_send()


class Sum4:
    def __init__(self, me, parts, by_c, by_x, sems):
        x, c, y, z = me
        self.me, self.parts, self.by_c, self.by_x = me, parts, by_c, by_x
        xp, cp = (1 - x, c, y, z), (x, 1 - c, y, z)
        self.first = [
            remote(parts.at[px + 2 * (1 - c)], by_c.at[px], sems.at[0], sems.at[1 + px], cp)
            for px in range(2)
        ]
        self.second = remote(by_c.at[1 - x], by_x, sems.at[0], sems.at[3], xp)

    def start(self):
        for one in self.first:
            one.start()

    def to_x(self):
        x, c, y, z = self.me
        for one in self.first:
            one.wait_recv()
        add_into(self.by_c.at[1 - x], self.parts.at[1 - x + 2 * c])
        self.second.start()

    def end(self):
        x, c, y, z = self.me
        self.second.wait_recv()
        return (
            self.parts[x + 2 * c].astype(F32)
            + self.by_c[x].astype(F32)
            + self.by_x[...].astype(F32)
        )

    def finish(self):
        for one in self.first + [self.second]:
            one.wait_send()


def chunks(rows, step, run):
    def one(i, carry):
        run(pl.ds(pl.multiple_of(i * step, step), step))
        return carry

    lax.fori_loop(0, rows // step, one, 0)


def add_into(into, more, step=16):
    def run(rows):
        total = into[rows, :].astype(F32) + more[rows, :].astype(F32)
        into[rows, :] = total.astype(into.dtype)

    chunks(into.shape[0], step, run)


def dma(*shape):
    return pltpu.SemaphoreType.DMA(shape)


ANYWHERE = pl.BlockSpec(memory_space=pl.ANY)
IN_VMEM = pl.BlockSpec(memory_space=pltpu.VMEM)


def attend_head(h, info, qt, kv, kvt, out, lse, causal):
    keys = kv.shape[0]
    rows = slice(64 * h, 64 * h + 64)
    for b in range(512 // QB):
        lanes = slice(QB * b, QB * b + QB)
        top = keys * (b + 1) * QB // 512 if causal else keys
        scores = dot(kv[:top, rows], qt[rows, lanes])
        scores = masked(scores, info, lanes, causal)
        high = jnp.max(scores, axis=0, keepdims=True)
        weights = jnp.exp(scores - high)
        total = jnp.sum(weights, axis=0, keepdims=True)
        out[rows, lanes] = dot(kvt[192 + 64 * h : 256 + 64 * h, :top], weights.astype(BF)) / total
        lse[h : h + 1, lanes] = high + jnp.log(total)


def attend_back_head(h, info, qt, kv, kvt, outer_t, out, lse, dq, dkv, dk_acc, dv_acc, causal):
    keys = kv.shape[0]
    rows = slice(64 * h, 64 * h + 64)
    value_rows = slice(192 + 64 * h, 256 + 64 * h)
    for b in reversed(range(512 // QB)):
        lanes = slice(QB * b, QB * b + QB)
        top = keys * (b + 1) * QB // 512 if causal else keys
        query, outer = qt[rows, lanes], outer_t[rows, lanes]
        delta = jnp.sum(outer.astype(F32) * out[rows, lanes], axis=0, keepdims=True)
        scores = masked(dot(kv[:top, rows], query), info, lanes, causal)
        prob = jnp.exp(scores - lse[h : h + 1, lanes])
        grad = (prob * (dot(kv[:top, value_rows], outer) - delta)).astype(BF)
        dq[rows, lanes] = (SCALE * dot(kvt[rows, :top], grad)).astype(BF)
        dk_new = dot_nt(query, grad)
        dv_new = dot_nt(outer, prob.astype(BF))
        if b == 512 // QB - 1:
            dk_acc[...] = dk_new
            dv_acc[...] = dv_new
        else:
            dk_acc[:, :top] += dk_new
            dv_acc[:, :top] += dv_new
    dkv[rows, :] = dk_acc[...].astype(BF)
    dkv[value_rows, :] = dv_acc[...].astype(BF)


def norm(values, gain):
    inverse = lax.rsqrt(jnp.mean(values * values, axis=-1, keepdims=True) + EPS)
    return (values * inverse * gain).astype(BF)


def norm_back(values, gain, upstream):
    inverse = lax.rsqrt(jnp.mean(values * values, axis=-1, keepdims=True) + EPS)
    normed = values * inverse
    scaled = upstream * gain
    grad = inverse * (scaled - normed * jnp.mean(scaled * normed, axis=-1, keepdims=True))
    return grad, jnp.sum(upstream * normed, axis=0, keepdims=True)


def gelu_parts(u):
    root = 0.7978845608028654
    square = u * u
    bend = jnp.tanh(root * u * (1.0 + 0.044715 * square))
    half = 0.5 * (1.0 + bend)
    slope = half + 0.5 * u * (1.0 - bend * bend) * (root * (1.0 + 0.134145 * square))
    return u * half, slope


class Names:
    pass


FETCHED = ("sk", "sv", "sq", "ck", "cv", "so", "co", "cq", "gate", "up")


def layer_kernel(names, *refs):
    R = Names()
    for name, ref in zip(names, refs, strict=True):
        setattr(R, name, ref)
    me = coords()
    x, c, y, z = me
    g = 2 * x + c
    t = x + 2 * c
    s = 2 * z + y
    group = ((1 - x, c, y, z), (1 - x, 1 - c, y, z), (x, 1 - c, y, z))
    line = tuple((x, c, y, lax.rem(z + k, 4)) for k in (1, 2, 3))
    fetch = [
        pltpu.make_async_copy(getattr(R, name), getattr(R, "v_" + name), R.s_fetch.at[i])
        for i, name in enumerate(FETCHED)
    ]
    for one in fetch:
        one.start()
    near_dn = pltpu.make_async_copy(R.down, R.DN.at[s], R.s_near.at[0])
    near_dn.start()
    greet(me, group + line + ((x, c, 1 - y, z),), moves=True)

    move_x = Move(me, R.tok, R.X.at[s], R.s_move.at[0])
    move_t = Move(me, R.tabs, R.TAB, R.s_move.at[1])
    move_m = Move(me, R.mem, R.M.at[s], R.s_move.at[2])
    move_d = Move(me, R.dout, R.DO.at[z], R.s_move.at[3])
    for one in fetch[:5]:
        one.wait()
    row = lax.broadcasted_iota(jnp.int32, (8, 128), 0)
    gains = jnp.zeros((8, 128), F32)
    for i, one in enumerate((R.g1, R.g2, R.g3)):
        one = jnp.concatenate([one[...].astype(F32), jnp.zeros((1, 104), F32)], axis=1)
        gains = jnp.where(row == i, one, gains)
    gains = jnp.concatenate([gains, jnp.zeros((120, 128), F32)], axis=0).T[:24, :64]
    blank = jnp.zeros((24, 64), F32)
    for k in range(4):
        narrow = slice(192 * k, 192 * k + 192)
        row = [w[:, narrow].astype(F32) for w in (R.v_sk, R.v_sv, R.v_sq)] + [gains]
        row = jnp.concatenate(row + [w[:, narrow].astype(F32) for w in (R.v_ck, R.v_cv)], axis=1)
        R.stage_a[k] = jnp.concatenate([row[:, :512], row[:, 512:]], axis=0).astype(BF)

    def to_group(stage, land, sems):
        return [
            remote(stage.at[2 * to[0] + to[1]], land.at[g], sems.at[0], sems.at[1 + i], to)
            for i, to in enumerate(group)
        ]

    parts_a = to_group(R.stage_a, R.land_a, R.s_part_a)
    for one in parts_a:
        one.start()
    move_x.start()
    for i in range(2):
        length, plot = R.lengths[0, i], R.plots[0, i]
        start = R.lengths[0, 0] if i else 0
        R.tabs[i : i + 1, :] = jnp.full((1, 128), start + length, jnp.int32)
        R.tabs[2 + i : 3 + i, :] = jnp.full((1, 128), plot, jnp.int32)
    R.tabs[4:, :] = jnp.zeros((4, 128), jnp.int32)
    move_t.start()

    def halves_stacked(w):
        w = w[...].astype(F32)
        return jnp.concatenate([w[:, :384], w[:, 384:]], axis=0).astype(BF)

    for one in fetch[5:]:
        one.wait()
    for k in range(4):
        wide = slice(512 * k, 512 * k + 512)
        R.stage_b[k, :24] = R.v_gate[:, wide]
        R.stage_b[k, 24:] = R.v_up[:, wide]
    R.land_a[g] = R.stage_a[g]
    R.land_b[g] = R.stage_b[g]
    gather_x = Gather8(me, R.X, R.s_x, True)
    gather_m = Gather8(me, R.M, R.s_m, True)
    gather_d = Gather4(me, R.DO, R.s_d, tokens=True)
    gather_a = GatherPlane(me, R.PA, R.s_a)
    gather_b = GatherPlane(me, R.PB, R.s_b, slice(0, 384))
    gather_o = GatherPlane(me, R.FO.at[g], R.s_fo)
    gather_c = GatherPlane(me, R.FC.at[g], R.s_fc)
    gather_q = GatherPlane(me, R.FQ.at[g], R.s_fq)
    gather_2 = GatherRelay(me, R.P2, R.s_2)
    gather_n = GatherRelay(me, R.DN, R.s_n)
    whole_o = Gather4(me, R.FO, R.s_wo)
    whole_c = Gather4(me, R.FC, R.s_wc)
    whole_q = Gather4(me, R.FQ, R.s_wq)

    R.FO[g, s] = halves_stacked(R.v_so)
    gather_o.start_along()
    gather_o.start_across()
    R.FQ[g, s] = halves_stacked(R.v_cq)
    R.FC[g, s] = halves_stacked(R.v_co)
    gather_q.start_across()
    gather_c.start_across()
    near_dn.wait()
    gather_n.start_across()
    for one in parts_a:
        one.wait_recv()
    whole = []
    for r in range(4):
        piece = R.land_a[r].astype(F32)
        whole.append(jnp.concatenate([piece[:24], piece[24:]], axis=1))
    whole = jnp.concatenate(whole, axis=0).astype(BF)
    R.PA[s] = whole[:, :640]
    R.PB[s, :, :384] = whole[:, 640:]
    gather_a.start_across()
    gather_a.start_along()
    gather_b.start_across()
    move_x.arrive()
    gather_x.start()
    parts_b = to_group(R.stage_b, R.land_b, R.s_part_b)
    for one in parts_b:
        one.start()
    move_m.start()
    gather_b.start_along()
    gather_q.start_along()
    gather_c.start_along()
    move_d.start()
    gather_x.forward()
    gather_a.forward(1)
    for k in (1, 3, 2):
        gather_o.forward(k)
    for one in parts_b:
        one.wait_recv()
    for half in range(2):
        rows = [R.land_b[r].astype(F32)[24 * half : 24 * half + 24] for r in range(4)]
        R.P2[s, :, 512 * half : 512 * half + 512] = jnp.concatenate(rows, axis=0).astype(BF)
    gather_2.start_along()
    gather_x.forward_far()
    gather_o.arrive()
    whole_o.start()
    gather_a.forward(3)
    gather_a.forward(2)
    gather_2.start_across()
    move_t.arrive()
    end_one, end_two = R.TAB[0:1, 0:1], R.TAB[1:2, 0:1]
    plot_one, plot_two = R.TAB[2:3, 0:1], R.TAB[3:4, 0:1]
    lane = lax.broadcasted_iota(jnp.int32, (1, 512), 1)
    for i in range(4):
        lanes = slice(128 * i, 128 * i + 128)
        R.info[0:1, lanes] = lane[:, :128] + (2 * i + y) * 128
    qpos = R.info[0:1, :]
    past_one, past_two = qpos >= end_one, qpos >= end_two
    R.info[1:2, :] = jnp.where(past_two, end_two, jnp.where(past_one, end_one, 0))
    R.info[2:3, :] = jnp.where(past_two, 0, jnp.where(past_one, plot_two, plot_one))

    def unpack(pieces, whole, width, step):
        for zz in range(4):

            def one(i, carry):
                lanes = pl.ds(pl.multiple_of(i * step, step), step)
                low = pieces[2 * zz, :, lanes].astype(F32)
                high = pieces[2 * zz + 1, :, lanes].astype(F32)
                for r in range(4):
                    rows = slice(24 * r, 24 * r + 24)
                    both = jnp.concatenate([low[rows], high[rows]], axis=0)
                    whole[192 * r + 48 * zz : 192 * r + 48 * zz + 48, lanes] = both.astype(BF)
                return carry

            lax.fori_loop(0, width // step, one, 0)

    gather_a.arrive()
    unpack(R.PA, R.WA, 640, 128)
    gain_rows = R.WA[:, 512:640].astype(F32).T
    gain_one, gain_two, gain_three = (gain_rows[64 + i : 65 + i] for i in range(3))

    def pair_rows(buf, i):
        return jnp.concatenate([buf[2 * i], buf[2 * i + 1]], axis=0)

    def mine_rows(buf):
        return jnp.concatenate([buf[2 * i + y] for i in range(4)], axis=0)

    def keys_values(i, operand, weight, natural, turned):
        rows = pl.ds(pl.multiple_of(i * 256, 256), 256)
        product = dot(operand, weight[:, :384])
        natural[rows, :] = product.astype(BF)
        turned[:, rows] = product.T.astype(BF)

    def first_norm(i, carry):
        x1 = norm(pair_rows(R.X, i).astype(F32), gain_one)
        R.X1[2 * i] = x1[:128]
        R.X1[2 * i + 1] = x1[128:]
        keys_values(i, x1, R.WA, R.KV, R.KVT)
        return carry

    gather_x.arrive()
    lax.fori_loop(0, 4, first_norm, 0)
    product = SCALE * dot(mine_rows(R.X1), R.WA[:, 384:640])
    R.QT[...] = product.T[:192].astype(BF)

    def share_heads(buf, sems):
        return [Gather4(me, buf.at[:, h], sems.at[h]) for h in range(3)]

    share_1 = share_heads(R.A4, R.s_share1)
    move_m.arrive()
    gather_m.start()
    for h in range(3):
        attend_head(h, R.info, R.QT, R.KV, R.KVT, R.OUT1, R.LSE1, True)
        R.A4[g, h] = R.OUT1[64 * h : 64 * h + 64, :].astype(BF)
        share_1[h].start()
    for k in (1, 3, 2):
        gather_b.forward(k)
    for k in (1, 3, 2):
        gather_q.forward(k)
    whole_o.forward()
    for h in range(3):
        share_1[h].forward()
    gather_m.forward()
    for k in (1, 3, 2):
        gather_c.forward(k)
    gather_2.forward(1)
    gather_n.start_along()
    whole_o.arrive()

    def unpack_full(pieces, whole):
        def one(r, carry):
            for zz in range(4):
                low, high = pieces[r, 2 * zz].astype(F32), pieces[r, 2 * zz + 1].astype(F32)
                rows = pl.ds(pl.multiple_of(192 * r + 48 * zz, 16), 48)
                whole[rows, :384] = jnp.concatenate([low[:24], high[:24]], axis=0).astype(BF)
                whole[rows, 384:] = jnp.concatenate([low[24:], high[24:]], axis=0).astype(BF)
            return carry

        lax.fori_loop(0, 4, one, 0)

    unpack_full(R.FO, R.WO)
    for one in share_1:
        one.arrive()

    def project(pieces, weight, i):
        lanes = slice(256 * i, 256 * i + 256)
        turned = pieces[:, :, :, lanes].astype(F32).reshape(768, 256)
        return dot(turned.T.astype(BF), weight[...])

    for i in range(2):
        rows = slice(256 * i, 256 * i + 256)
        before = jnp.concatenate([R.X[4 * i + y], R.X[4 * i + 2 + y]], axis=0).astype(F32)
        first = before + project(R.A4, R.WO, i)
        R.FIRST[rows, :] = first
        R.X2[rows, :] = norm(first, gain_two)
    gather_q.arrive()
    whole_q.start()
    gather_m.forward_far()
    gather_2.forward(2)
    gather_n.forward(1)
    gather_b.arrive()
    unpack(R.PB, R.WB, 384, 128)
    gather_c.arrive()
    whole_c.start()
    move_d.arrive()
    gather_m.arrive()

    def memory_pair(i, carry):
        keys_values(i, pair_rows(R.M, i), R.WB, R.MKV, R.MKVT)
        return carry

    lax.fori_loop(0, 4, memory_pair, 0)
    whole_q.forward()
    whole_q.arrive()
    unpack_full(R.FQ, R.WQ)
    for k in range(4):

        @pl.when(g == k)
        def _():
            R.WCQ[...] = R.WQ[:, 192 * k : 192 * k + 192]

    for i in range(2):
        rows = slice(256 * i, 256 * i + 256)
        product = SCALE * dot(R.X2[rows, :], R.WCQ[...])
        R.CQT[:, rows] = product.T.astype(BF)
    share_2 = share_heads(R.C4, R.s_share2)
    for h in range(3):
        attend_head(h, R.info, R.CQT, R.MKV, R.MKVT, R.OUT2, R.LSE2, False)
        R.C4[g, h] = R.OUT2[64 * h : 64 * h + 64, :].astype(BF)
        share_2[h].start()
        if h == 1:
            gather_2.forward(3)
            gather_n.forward(2)
    gather_d.start()
    whole_c.forward()
    share_2[0].forward()
    share_2[1].forward()
    gather_n.forward(3)
    share_2[2].forward()
    whole_c.arrive()
    unpack_full(R.FC, R.WC)
    for one in share_2:
        one.arrive()
    for i in range(2):
        rows = slice(256 * i, 256 * i + 256)
        second = R.FIRST[rows, :] + project(R.C4, R.WC, i)
        R.SECOND[rows, :] = second
        R.X3[rows, :] = norm(second, gain_three)
    gather_d.forward()
    gather_2.arrive()
    unpack(R.P2, R.W2, 1024, 256)
    for one in parts_a + parts_b:
        one.wait_send()
    gather_2.finish()
    gather_a.finish()
    gather_b.finish()
    sum_dx = Sum4(me, R.DXP, R.by_c_dx, R.by_x_dx, R.s_dx)
    sum_out = Sum4(me, R.OP, R.by_c_out, R.by_x_out, R.s_out)

    def feed_in(core):
        at = pl.ds(pl.multiple_of(core * 256, 256), 256)
        x3 = R.X3[at, :]
        gate, up = dot(x3, R.W2[:, :512]), dot(x3, R.W2[:, 512:])
        active, slope = gelu_parts(gate)
        R.ACTIVE[at, :] = active.astype(BF)
        R.FALL[at, :] = (up * slope).astype(BF)
        R.H[at, :] = (active * up).astype(BF)

    def feed_out(core):
        at = pl.ds(pl.multiple_of(core * 256, 256), 256)
        outer = jnp.concatenate([R.DO[2 * core + px] for px in range(2)], axis=0)
        w_down = R.DN[...].reshape(512, 768)
        hidden_grad = dot_nt(outer, w_down)
        gate_grad = (hidden_grad * R.FALL[at, :].astype(F32)).astype(BF)
        up_grad = (hidden_grad * R.ACTIVE[at, :].astype(F32)).astype(BF)
        dx3 = (dot_nt(gate_grad, R.W2[:, :512]) + dot_nt(up_grad, R.W2[:, 512:])).astype(BF)
        R.GG[at, :512] = gate_grad
        R.GG[at, 512:] = up_grad
        for px in range(2):
            R.DXP[2 * core + px] = dx3[128 * px : 128 * px + 128]

    def feed_sum(core):
        at = pl.ds(pl.multiple_of(core * 256, 256), 256)
        out = dot(R.H[at, :], R.DN[...].reshape(512, 768)).astype(BF)
        for px in range(2):
            R.OP[2 * core + px] = out[128 * px : 128 * px + 128]

    def pack(whole, pieces, start, width):
        for t in range(8):
            rows = [whole[(8 * r + t) * 24 : (8 * r + t) * 24 + 24, :] for r in range(4)]
            pieces[t, :, start : start + width] = jnp.concatenate(rows, axis=0).astype(BF)

    feed_in(1 - c)
    feed_in(c)
    R.X3T[...] = R.X3[...].astype(F32).T.astype(BF)
    gather_n.arrive()
    gather_d.arrive()
    feed_out(1 - c)
    sum_dx.start()
    feed_out(c)
    sum_dx.to_x()
    own = pl.ds(pl.multiple_of(t * 128, 128), 128)
    own_block = 2 * t + y
    total_2 = [
        SumPlaneDirect(me, R.P2, R.by_y_2, R.by_z_2, R.s_g2.at[i], slice(256 * i, 256 * i + 256))
        for i in range(4)
    ]
    for i in range(4):
        R.W2G[...] = dot(R.X3T[...], R.GG[:, 256 * i : 256 * i + 256])
        pack(R.W2G, R.P2, 256 * i, 256)
        total_2[i].start()
    hidden_t = R.H[...].astype(F32).T.astype(BF)
    d_down = dot(hidden_t, R.DO[...].reshape(512, 768)).astype(BF)
    for i in range(8):
        R.DNG[i] = d_down[64 * i : 64 * i + 64]
    total_n = SumPlaneDirect(me, R.DNG, R.by_y_n, R.by_z_n, R.s_gn)
    total_n.start()
    feed_sum(1 - c)
    feed_sum(c)
    sum_out.start()
    part, gain_grad_three = norm_back(R.SECOND[own, :], gain_three, sum_dx.end())
    second_grad = R.DO[t].astype(F32) + part
    R.SGRAD[...] = second_grad
    R.DS4[t] = second_grad.astype(BF)
    share_s = Gather4(me, R.DS4, R.s_s, tokens=True)
    share_s.start()
    total_2[0].fold()
    share_s.forward()
    sum_out.to_x()
    total_2[1].fold()
    total_2[0].pass_one()
    share_s.arrive()

    dsec = R.DS4[...].reshape(512, 768)
    mine_192 = pl.ds(pl.multiple_of(g * 192, 16), 192)
    R.OUTER[...] = dot_nt(R.WC[mine_192, :], dsec).astype(BF)
    share_3 = share_heads(R.DC4, R.s_share3)
    for h in range(3):
        attend_back_head(
            h, R.info, R.CQT, R.MKV, R.MKVT, R.OUTER, R.OUT2, R.LSE2, R.DCQT, R.MDKV, R.dk, R.dv, False
        )
        R.DC4[g, h] = R.DCQT[64 * h : 64 * h + 64, :]
        share_3[h].start()
        if h == 0:
            total_2[2].fold()
        if h == 1:
            share_3[0].forward()
            total_2[0].pass_two()

    def pack_24(whole, pieces):
        for t in range(8):
            rows = whole[24 * t : 24 * t + 24]
            pieces[t] = jnp.concatenate([rows[:, :384], rows[:, 384:]], axis=0).astype(BF)

    def memory_grad_pair(i, carry):
        lanes = pl.ds(pl.multiple_of(i * 256, 256), 256)
        turned = dot(R.WB[:, :384], R.MDKV[:, lanes]).astype(BF)
        R.MG[2 * i] = turned[:, :128]
        R.MG[2 * i + 1] = turned[:, 128:]
        return carry

    total_2[3].fold()
    total_2[1].pass_one()
    lax.fori_loop(0, 4, memory_grad_pair, 0)
    sum_m = Sum8(me, R.MG, R.by_c_m, R.by_x_m, R.by_y_m, R.s_gm)
    share_3[1].forward()
    pack_24(dot(R.C4[g].reshape(192, 512), dsec), R.CO8)
    total_c = SumPlane(me, R.CO8, R.by_y_c, R.by_z_c, R.s_gc)
    total_c.start()
    R.W1G[...] = dot(R.MDKV[...], R.M[...].reshape(1024, 768)).T
    pack(R.W1G, R.PB, 0, 384)
    total_b = SumPlaneDirect(me, R.PB, R.by_y_b, R.by_z_b, R.s_gb, slice(0, 384))
    total_b.start()
    share_3[2].forward()
    sum_m.start()
    back = [
        Move(me, src, dst, R.s_back.at[i])
        for i, (src, dst) in enumerate(
            ((R.TBLOCK, R.tokens_out), (R.LBLOCK, R.layer_out), (R.MBLOCK, R.memory_out))
        )
    ]
    R.LBLOCK[...] = (R.SECOND[own, :] + sum_out.end()).astype(BF)
    back[1].start()
    total_2[2].pass_one()
    total_2[1].pass_two()
    for one in share_3:
        one.arrive()

    for i in range(2):
        rows = slice(256 * i, 256 * i + 256)
        dx2 = dot(R.WQ[...], R.DC4[:, :, :, rows].reshape(768, 256)).T
        part, ignored = norm_back(R.FIRST[rows, :], gain_two, dx2)
        R.DFIRST[rows, :] = (dsec[rows].astype(F32) + part).astype(BF)
    R.OUTER[...] = dot_nt(R.WO[mine_192, :], R.DFIRST[...]).astype(BF)
    sum_m.to_x()
    total_n.fold()
    total_2[3].pass_one()

    for h in range(3):
        attend_back_head(
            h, R.info, R.QT, R.KV, R.KVT, R.OUTER, R.OUT1, R.LSE1, R.DQT, R.DKV, R.dk, R.dv, True
        )

    def token_grad_pair(i, carry):
        lanes = pl.ds(pl.multiple_of(i * 256, 256), 256)
        half = pl.ds(pl.multiple_of(i * 128, 128), 128)
        turned = dot(R.WA[:, :384], R.DKV[:, lanes])
        query = dot(R.WA[:, 384:576], R.DQT[:, half])
        R.TG[2 * i] = (turned[:, :128] + jnp.where(y == 0, query, 0.0)).astype(BF)
        R.TG[2 * i + 1] = (turned[:, 128:] + jnp.where(y == 1, query, 0.0)).astype(BF)
        return carry

    lax.fori_loop(0, 4, token_grad_pair, 0)
    sum_t = Sum8(me, R.TG, R.by_c_t, R.by_x_t, R.by_y_t, R.s_gt)
    sum_t.start()
    pack_24(dot(R.A4[g].reshape(192, 512), R.DFIRST[...]), R.SO8)
    total_s = SumPlane(me, R.SO8, R.by_y_s, R.by_z_s, R.s_gs)
    dx2 = dot(R.WQ[...], R.DC4[:, :, :, own].reshape(768, 128)).T
    part, gain_grad_two = norm_back(R.FIRST[own, :], gain_two, dx2)
    R.SGRAD[...] += part
    sum_t.to_x()
    sum_m.to_y()
    total_c.fold()
    total_n.pass_one()
    total_2[2].pass_two()
    R.W1G[...] = dot(R.DKV[...], R.X1[...].reshape(1024, 768)).T
    pack(R.W1G, R.PA, 0, 384)
    total_a = SumPlane(me, R.PA, R.by_y_a, R.by_z_a, R.s_ga, slice(0, 384))
    total_a.start()
    R.TURN[:192, :] = dot(R.DQT[...], mine_rows(R.X1))
    R.TURN[192:, :] = dot(R.DCQT[...], R.X2[...])
    R.W1G[...] = R.TURN[...].T
    pack(R.W1G, R.PB, 384, 384)
    total_q = SumPlaneDirect(me, R.PB, R.by_y_b, R.by_z_b, R.s_gq, slice(384, 768))
    total_b.fold()
    total_2[3].pass_two()
    sum_t.to_y()
    total_q.start()
    total_s.start()
    total_c.pass_one()
    total_n.pass_two()
    total_b.pass_one()
    R.MBLOCK[...] = sum_m.end().T.astype(BF)
    back[2].start()
    total_a.fold()
    total_c.pass_two()
    total_b.pass_two()
    dx1 = sum_t.end().T
    part, gain_grad_one = norm_back(R.X[own_block].astype(F32), gain_one, dx1)
    R.TBLOCK[...] = (R.SGRAD[...] + part).astype(BF)
    back[0].start()
    R.GT[0:1, :] = gain_grad_one
    R.GT[1:2, :] = gain_grad_two
    R.GT[2:3, :] = gain_grad_three
    pack(R.GT[...].T, R.PG, 0, 128)
    total_g = SumPlaneDirect(me, R.PG, R.by_y_g, R.by_z_g, R.s_gg)
    total_g.start()
    for one in total_2:
        one.end()
    rows_2 = R.P2[s].astype(F32)
    for r in range(4):
        rows = slice(24 * r, 24 * r + 24)
        R.stage_b[r] = jnp.concatenate([rows_2[rows, :512], rows_2[rows, 512:]], axis=0).astype(BF)
    last_b = to_group(R.stage_b, R.quarters_b, R.s_last_b)
    for one in last_b:
        one.start()
    total_n.end()
    total_a.pass_one()
    total_q.fold()
    total_a.pass_two()
    total_s.fold()
    total_c.end()
    total_b.end()
    total_q.pass_one()
    total_g.fold()
    total_s.pass_one()
    total_a.end()
    rows_a, rows_b = R.PA[s, :, :384].astype(F32), R.PB[s, :, :384].astype(F32)
    for r in range(4):
        rows = slice(24 * r, 24 * r + 24)
        R.stage_z[r] = jnp.concatenate([rows_a[rows], rows_b[rows]], axis=0).astype(BF)
    last_a = to_group(R.stage_z, R.quarters_a, R.s_last_a)
    for one in last_a:
        one.start()
    total_q.pass_two()
    total_g.pass_one()
    total_s.pass_two()
    total_g.pass_two()
    total_q.end()
    total_g.end()
    rows_q = R.PB[s, :, 384:].astype(F32)
    rows_g = R.PG[s].astype(F32)
    for r in range(4):
        rows = slice(24 * r, 24 * r + 24)
        both = [rows_q[rows, :192], rows_g[rows, :64], rows_q[rows, 192:], blank]
        both = jnp.concatenate(both, axis=1)
        R.stage_q[r] = jnp.concatenate([both[:, :256], both[:, 256:]], axis=0).astype(BF)
    last_q = to_group(R.stage_q, R.quarters_q, R.s_last_q)
    for one in last_q:
        one.start()
    total_s.end()
    near = [
        pltpu.make_async_copy(src, dst, R.s_near.at[1 + i])
        for i, (src, dst) in enumerate(
            (
                (R.stage_z.at[g], R.quarters_a.at[g]),
                (R.stage_q.at[g], R.quarters_q.at[g]),
                (R.stage_b.at[g], R.quarters_b.at[g]),
                (R.CO8.at[s], R.co_out),
                (R.SO8.at[s], R.so_out),
                (R.DNG.at[s], R.down_out),
            )
        )
    ]
    for one in near:
        one.start()
    for one in near:
        one.wait()
    for one in last_a + last_b + last_q:
        one.wait_recv()
    for one in back:
        one.arrive()
        one.finish()
    for one in last_a + last_b + last_q:
        one.wait_send()
    for one in (move_x, move_t, move_m, move_d):
        one.finish()
    for one in (gather_x, gather_m, gather_d, gather_o, gather_c, gather_q, gather_n):
        one.finish()
    for one in (whole_o, whole_c, whole_q, share_s, sum_dx, sum_out, sum_m, sum_t):
        one.finish()
    for one in share_1 + share_2 + share_3 + total_2:
        one.finish()
    for one in (total_a, total_q, total_g, total_b, total_n, total_c, total_s):
        one.finish()


def run_layer(inputs):
    n, d = 128, 768

    def low(*shape):
        return pltpu.VMEM(shape, BF)

    def full(*shape):
        return pltpu.VMEM(shape, F32)

    outs = dict(
        quarters_a=(4, 48, 384),
        quarters_b=(4, 48, 512),
        quarters_q=(4, 48, 256),
        co_out=(48, 384),
        so_out=(48, 384),
        down_out=(64, d),
        tokens_out=(n, d),
        layer_out=(n, d),
        memory_out=(n, d),
    )
    scratch = dict(
        stage_a=low(4, 48, 512), land_a=low(4, 48, 512), stage_z=low(4, 48, 384), stage_q=low(4, 48, 256), stage_b=low(4, 48, 512), land_b=low(4, 48, 512),
        **{"v_" + name: pltpu.VMEM(inputs[name][0].shape, BF) for name in FETCHED},
        s_fetch=dma(len(FETCHED)),
        tabs=pltpu.VMEM((8, 128), jnp.int32), TAB=pltpu.VMEM((8, 128), jnp.int32),
        X=low(8, n, d), M=low(8, n, d), DO=low(4, n, d),
        PA=low(8, 96, 640), PB=low(8, 96, 768), PG=low(8, 96, 128), P2=low(8, 96, 1024), DN=low(8, 64, d),
        FO=low(4, 8, 48, 384), FC=low(4, 8, 48, 384), FQ=low(4, 8, 48, 384),
        WA=low(768, 640), WB=low(768, 384), WCQ=low(768, 192), W2=low(768, 1024), WO=low(d, d), WC=low(d, d), WQ=low(d, d),
        info=pltpu.VMEM((8, 512), jnp.int32),
        X1=low(8, n, d), X2=low(512, d), X3=low(512, d),
        KV=low(1024, 384), KVT=low(384, 1024), MKV=low(1024, 384), MKVT=low(384, 1024),
        QT=low(192, 512), CQT=low(192, 512), OUT1=full(192, 512), OUT2=full(192, 512),
        LSE1=full(8, 512), LSE2=full(8, 512),
        A4=low(4, 3, 64, 512), C4=low(4, 3, 64, 512), DC4=low(4, 3, 64, 512),
        FIRST=full(512, d), SECOND=full(512, d),
        H=low(512, 512), ACTIVE=low(512, 512), FALL=low(512, 512), X3T=low(768, 512), GG=low(512, 1024), DXP=low(4, n, d), OP=low(4, n, d),
        by_c_dx=low(2, n, d), by_x_dx=low(n, d), by_c_out=low(2, n, d), by_x_out=low(n, d),
        W2G=full(768, 256), by_y_2=low(4, 96, 1024), by_z_2=low(5, 96, 1024),
        DNG=low(8, 64, d), by_y_n=low(4, 64, d), by_z_n=low(5, 64, d),
        SGRAD=full(n, d), DS4=low(4, n, d), OUTER=low(192, 512),
        DCQT=low(192, 512), DQT=low(192, 512), MDKV=low(384, 1024), DKV=low(384, 1024),
        dk=full(64, 1024), dv=full(64, 1024),
        CO8=low(8, 48, 384), by_y_c=low(4, 48, 384), by_z_c=low(5, 48, 384),
        SO8=low(8, 48, 384), by_y_s=low(4, 48, 384), by_z_s=low(5, 48, 384),
        MG=low(8, d, n), by_c_m=low(2, 2, d, n), by_x_m=low(2, d, n), by_y_m=low(d, n),
        TG=low(8, d, n), by_c_t=low(2, 2, d, n), by_x_t=low(2, d, n), by_y_t=low(d, n),
        DFIRST=low(512, d), W1G=full(768, 384), TURN=full(384, 768), GT=full(128, 768),
        by_y_a=low(4, 96, 384), by_z_a=low(5, 96, 384), by_y_b=low(4, 96, 768), by_z_b=low(5, 96, 768),
        by_y_g=low(4, 96, 128), by_z_g=low(5, 96, 128),
        TBLOCK=low(n, d), LBLOCK=low(n, d), MBLOCK=low(n, d),
        s_move=dma(4, 2), s_near=dma(7), s_back=dma(3, 2),
        **{name: dma(4) for name in ("s_part_a", "s_part_b", "s_last_a", "s_last_b", "s_last_q", "s_d", "s_wo", "s_wc", "s_wq", "s_s", "s_dx", "s_out")},
        **{name: dma(8) for name in ("s_x", "s_m", "s_gm", "s_gt", "s_a", "s_b", "s_fo", "s_fc", "s_fq")},
        s_2=dma(13), s_n=dma(13), s_share1=dma(3, 4), s_share2=dma(3, 4), s_share3=dma(3, 4), s_g2=dma(4, 10),
        **{name: dma(10) for name in ("s_ga", "s_gb", "s_gq", "s_gg", "s_gn", "s_gc", "s_gs")},
    )
    names = tuple(inputs) + tuple(outs) + tuple(scratch)
    return pl.pallas_call(
        functools.partial(layer_kernel, names),
        out_shape=tuple(jax.ShapeDtypeStruct(shape, BF) for shape in outs.values()),
        in_specs=[spec for _, spec in inputs.values()],
        out_specs=tuple([ANYWHERE] * len(outs)),
        scratch_shapes=list(scratch.values()),
        compiler_params=pltpu.CompilerParams(
            collective_id=1, has_side_effects=True, vmem_limit_bytes=VMEM_LIMIT
        ),
        name="layer",
    )(*[a for a, _ in inputs.values()])


def outputs_kernel(names, *refs):
    R = Names()
    for name, ref in zip(names, refs, strict=True):
        setattr(R, name, ref)

    def copies(pairs, sems):
        made = [pltpu.make_async_copy(a, b, sems.at[i]) for i, (a, b) in enumerate(pairs)]
        for one in made:
            one.start()
        return made

    arrive = copies(
        ((R.qa, R.v_qa), (R.qb, R.v_qb), (R.qq, R.v_qq), (R.co, R.v_co), (R.so, R.v_so), (R.down, R.v_down)), R.s_in
    )
    blocks = copies([(getattr(R, n), getattr(R, "v_" + n)) for n in BLOCKS], R.s_block)
    for one in arrive:
        one.wait()
    gains = jnp.zeros((24, 128), F32)
    for k in range(4):
        piece, last = R.v_qa[k].astype(F32), R.v_qq[k].astype(F32)
        gains = gains + last[:24, 128:]
        narrow = slice(192 * k, 192 * k + 192)
        R.w_sk[:, narrow] = piece[:24, :192]
        R.w_sv[:, narrow] = piece[:24, 192:]
        R.w_ck[:, narrow] = piece[24:, :192]
        R.w_cv[:, narrow] = piece[24:, 192:]
        R.w_sq[:, narrow] = last[:24, :192]
        R.w_cq[:, narrow] = last[24:, :192]
        piece = R.v_qb[k].astype(F32)
        R.w_gate[:, 512 * k : 512 * k + 512] = piece[:24]
        R.w_up[:, 512 * k : 512 * k + 512] = piece[24:]
    for piece, out in ((R.v_so, R.w_so), (R.v_co, R.w_co)):
        rows = piece[...].astype(F32)
        out[:, :384] = rows[:24]
        out[:, 384:] = rows[24:]
    R.w_down[...] = R.v_down[...].astype(F32)
    turned = jnp.concatenate([gains, jnp.zeros((104, 128), F32)], axis=0).T
    for i, out in enumerate((R.w_g1, R.w_g2, R.w_g3)):
        out[...] = turned[64 + i : 65 + i, :24]
    leave = copies([(getattr(R, "w_" + n), getattr(R, "o_" + n)) for n in WEIGHTS], R.s_out)
    for one in blocks:
        one.wait()
    leave += copies([(getattr(R, "v_" + n), getattr(R, "o_" + n)) for n in BLOCKS], R.s_direct)
    for one in leave:
        one.wait()


BLOCKS = ("layer", "tokens", "memory")
WEIGHTS = ("g1", "sq", "sk", "sv", "so", "g2", "cq", "ck", "cv", "co", "g3", "gate", "up", "down")


def write_outputs(results):
    ins = ("qa", "qb", "qq", "co", "so", "down", "tokens", "layer", "memory")
    blocks = BLOCKS
    shapes = {name: (24, 768) for name in WEIGHTS}
    shapes |= {name: (1, 24) for name in ("g1", "g2", "g3")}
    shapes |= dict(gate=(24, 2048), up=(24, 2048), down=(64, 768))
    outs = [jax.ShapeDtypeStruct((128, 768), BF) for _ in blocks]
    outs += [jax.ShapeDtypeStruct(shapes[n], F32) for n in WEIGHTS]
    scratch = {"v_" + n: pltpu.VMEM(a.shape, BF) for n, a in zip(ins, results)}
    scratch |= {"w_" + n: pltpu.VMEM(shapes[n], F32) for n in WEIGHTS}
    scratch |= dict(s_in=dma(6), s_direct=dma(3), s_block=dma(3), s_out=dma(len(WEIGHTS)))
    names = ins + tuple("o_" + n for n in blocks + WEIGHTS) + tuple(scratch)
    return pl.pallas_call(
        functools.partial(outputs_kernel, names),
        out_shape=tuple(outs),
        in_specs=[ANYWHERE] * len(ins),
        out_specs=tuple([ANYWHERE] * len(outs)),
        scratch_shapes=list(scratch.values()),
        compiler_params=pltpu.CompilerParams(vmem_limit_bytes=VMEM_LIMIT),
        name="outputs",
    )(*results)


def body_planes(
    tokens, memory, out_grad, table_lengths, table_plots,
    self_gain, self_query, self_key, self_value, self_output,
    cross_gain, cross_query, cross_key, cross_value, cross_output,
    mlp_gain, mlp_gate, mlp_up, mlp_down,
):
    in_smem = pl.BlockSpec(memory_space=pltpu.SMEM)
    results = run_layer(
        dict(
            tok=(tokens[0], ANYWHERE), mem=(memory[0], ANYWHERE), dout=(out_grad[0], ANYWHERE),
            lengths=(table_lengths, in_smem), plots=(table_plots, in_smem), g1=(self_gain[None], IN_VMEM), g2=(cross_gain[None], IN_VMEM), g3=(mlp_gain[None], IN_VMEM),
            sq=(self_query, ANYWHERE), sk=(self_key, ANYWHERE), sv=(self_value, ANYWHERE), so=(self_output, ANYWHERE),
            cq=(cross_query, ANYWHERE), ck=(cross_key, ANYWHERE), cv=(cross_value, ANYWHERE), co=(cross_output, ANYWHERE),
            gate=(mlp_gate, ANYWHERE), up=(mlp_up, ANYWHERE), down=(mlp_down, ANYWHERE),
        )
    )
    outs = write_outputs(results)
    blocks = tuple(a[None] for a in outs[:3])
    return blocks + tuple(a[0] if a.shape[0] == 1 else a for a in outs[3:])


def solution(mesh):
    placed = (
        P(ROW, SEQ, None),
        P(ROW, SEQ, None),
        P(ROW, SEQ, None),
        P(ROW, None),
        P(ROW, None),
        P(BOTH),
        P(BOTH, None),
        P(BOTH, None),
        P(BOTH, None),
        P(BOTH, None),
        P(BOTH),
        P(BOTH, None),
        P(BOTH, None),
        P(BOTH, None),
        P(BOTH, None),
        P(BOTH),
        P(BOTH, None),
        P(BOTH, None),
        P(BOTH, None),
    )
    small = mesh.shape[ROW] == 4 and mesh.shape[SEQ] == 8
    return jax.shard_map(
        body_planes if small else body_general,
        mesh=mesh,
        in_specs=placed,
        out_specs=(
            P(ROW, SEQ, None),
            P(ROW, SEQ, None),
            P(ROW, SEQ, None),
            P(BOTH),
            P(BOTH, None),
            P(BOTH, None),
            P(BOTH, None),
            P(BOTH, None),
            P(BOTH),
            P(BOTH, None),
            P(BOTH, None),
            P(BOTH, None),
            P(BOTH, None),
            P(BOTH),
            P(BOTH, None),
            P(BOTH, None),
            P(BOTH, None),
        ),
        check_vma=False,
    )
```
